32 devices in a mesh: groups: 2 (over y), ctx: 16 (over z, x, core).
Axes of the slice: x: 2, y: 2, z: 4, core: 2. Of those that a mesh axis runs over, the one named last changes fastest.
Arguments:
- queries: bfloat16 [4096, 4096], P(('groups', 'ctx')), parts along dimension 0, may hold values from -12 to 12
- context_keys: bfloat16 [32, 2048, 512], P('groups', 'ctx'), parts along dimension 0, may hold values from -6 to 6
- context_values: bfloat16 [32, 2048, 512], P('groups', 'ctx'), parts along dimension 0, may hold values from -6 to 6
- forward_output: bfloat16 [4096, 4096], P(('groups', 'ctx')), parts along dimension 0, may hold values from -6 to 6
- output_cotangent: bfloat16 [4096, 4096], P(('groups', 'ctx')), parts along dimension 0, may hold values from -48 to 48
- verticals: int32 [8, 8], P('groups'), parts along dimension 0, may hold values from 0 to 511, as said below
- offsets: int32 [8, 3], P('groups'), parts along dimension 0, may hold values from 1 to 10, as said below
- slab_index: int32 [2], P('groups'), parts along dimension 0, may hold values from 1 to 15
Outputs:
- query_grad: bfloat16 [4096, 4096], P(('groups', 'ctx')), parts along dimension 0
- key_gradient: bfloat16 [32, 2048, 512], P('groups', 'ctx'), parts along dimension 0
- value_gradient: bfloat16 [32, 2048, 512], P('groups', 'ctx'), parts along dimension 0
The draws below stay inside these ranges and needn't reach their ends.
There are 2 independent parts, one for each index of `groups`. The reference program is written for one: setup_inputs(seed, part) draws one part's arguments, and reference() takes and returns one part's arrays. A program takes and returns all parts, laid end to end along the dimension named above; each array names one. Nothing has to cross between parts.
Inputs may be any that keep to these rules, and one draw needn't show every extreme that they name: `verticals`: each row holds 8 distinct block numbers; the first of every row is 0, and some row names the last block. Each row holds 3 distinct offsets; some row names 10.
All inputs are finite; a program needn't handle non-finite values.
Results may differ from the reference program's by a relative error of at most 0.0051.
Values may be sent and summed in bfloat16 or wider, within the bound.
No kernel may reach another device: no remote copies, remote signals or barrier semaphores. Data moves between devices by JAX's collectives and lax.ppermute only.
A program may use at most 128 MiB of HBM per device.

```python
import math
import jax
import jax.numpy as jnp
from jax import lax

HEAD_SIZE = 128
QUERY_HEADS = 32
KEY_VALUE_HEADS = 4
MASK_BLOCK_SIZE = 64
SLAB_COUNT = 16
SLASH_RANGE = 11
NV = 8
SLASH_COUNT = 3
SLAB_QUERY_ROWS = 2048


def draw_queries(key, part):
    random_seed_key = jax.random.fold_in(key, 5)
    unmasked_rows = jnp.clip(jax.random.normal(random_seed_key, (SLAB_QUERY_ROWS, QUERY_HEADS * HEAD_SIZE), jnp.float32), -6.0, 6.0)
    return unmasked_rows.astype(jnp.bfloat16)


def draw_context_keys(key, part):
    random_seed_key = jax.random.fold_in(key, 6)
    unmasked_rows = jnp.clip(jax.random.normal(random_seed_key, (SLAB_COUNT, SLAB_QUERY_ROWS, KEY_VALUE_HEADS * HEAD_SIZE), jnp.float32), -6.0, 6.0)
    return unmasked_rows.astype(jnp.bfloat16)


def draw_verticals(key, part):
    block_count_all = SLAB_COUNT * SLAB_QUERY_ROWS // MASK_BLOCK_SIZE
    per_head_seeds = jax.random.split(jax.random.fold_in(key, 9), KEY_VALUE_HEADS)

    def one_head(head_key):
        shuffled = jax.random.permutation(head_key, block_count_all - 2) + 1
        return shuffled[:NV - 1]
    remaining_slabs = jax.vmap(one_head)(per_head_seeds).astype(jnp.int32)
    selected_blocks = jax.random.randint(jax.random.fold_in(key, 10), (), 0, KEY_VALUE_HEADS)
    remaining_slabs = remaining_slabs.at[:, 0].set(jnp.where(jnp.arange(KEY_VALUE_HEADS) == selected_blocks, block_count_all - 1, remaining_slabs[:, 0]).astype(jnp.int32))
    return jnp.concatenate([jnp.zeros((KEY_VALUE_HEADS, 1), jnp.int32), remaining_slabs], axis=1).astype(jnp.int32)


def draw_offsets(key, part):
    per_head_seeds = jax.random.split(jax.random.fold_in(key, 21), KEY_VALUE_HEADS)

    def one_head(head_key):
        shuffled = jax.random.permutation(head_key, SLASH_RANGE - 2) + 1
        return shuffled[:SLASH_COUNT]
    chosen_rows = jax.vmap(one_head)(per_head_seeds).astype(jnp.int32)
    farthest_head = jax.random.randint(jax.random.fold_in(key, 22), (), 0, KEY_VALUE_HEADS)
    chosen_rows = chosen_rows.at[:, 0].set(jnp.where(jnp.arange(KEY_VALUE_HEADS) == farthest_head, SLASH_RANGE - 1, chosen_rows[:, 0]).astype(jnp.int32))
    return chosen_rows.astype(jnp.int32)


def level_of(rng, dims, cuts, least, high):
    level = 1.0
    for position, parts in cuts:
        steps = jax.random.uniform(jax.random.fold_in(jax.random.fold_in(rng, 6), position), (parts,), jnp.float32, least / len(cuts), high / len(cuts))
        level = level * jnp.repeat(jnp.exp(steps), dims[position] // parts).reshape((-1,) + (1,) * (len(dims) - 1 - position))
    return level


def gaussian(rng, dims, deviation, reach, cuts=(), held_as=jnp.bfloat16):
    factor_of = level_of(rng, dims, cuts, -0.22, 0.18) if cuts else 1.0
    values = jax.random.normal(rng, dims, jnp.float32) * deviation * factor_of
    return jnp.minimum(jnp.maximum(values, -reach), reach).astype(held_as)


def setup_inputs(seed: int = 0, part: int = 0) -> dict:
    key_of = jax.random.split(jax.random.key(seed), 9)
    part_splits = jax.random.split(jax.random.fold_in(key_of[8], part), 9)
    queries = draw_queries(jax.random.fold_in(jax.random.fold_in(key_of[8], part), 71), part)
    context_keys = draw_context_keys(jax.random.fold_in(jax.random.fold_in(key_of[8], part), 71), part)
    context_values = gaussian(part_splits[2], (SLAB_COUNT, SLAB_QUERY_ROWS, KEY_VALUE_HEADS * HEAD_SIZE), 1.0, 6.0, ((1, 16),))
    forward_output = gaussian(part_splits[3], (SLAB_QUERY_ROWS, QUERY_HEADS * HEAD_SIZE), 1.0, 6.0, ((0, 16),))
    output_cotangent = gaussian(part_splits[4], (SLAB_QUERY_ROWS, QUERY_HEADS * HEAD_SIZE), 8.0, 48.0, ((0, 16),))
    verticals = draw_verticals(jax.random.fold_in(jax.random.fold_in(key_of[8], part), 71), part)
    offsets = draw_offsets(jax.random.fold_in(jax.random.fold_in(key_of[8], part), 71), part)
    slab_index = jax.random.randint(part_splits[7], (1,), 1, SLAB_COUNT).astype(jnp.int32)
    return dict(queries=queries, context_keys=context_keys, context_values=context_values, forward_output=forward_output, output_cotangent=output_cotangent, verticals=verticals, offsets=offsets, slab_index=slab_index)


def lowered(source):
    return lax.optimization_barrier(source.astype(jnp.bfloat16)).astype(jnp.float32)

def reference(queries, context_keys, context_values, forward_output, output_cotangent, verticals, offsets, slab_index):
    query_per_key_head = QUERY_HEADS // KEY_VALUE_HEADS
    blocks_per_slab = SLAB_QUERY_ROWS // MASK_BLOCK_SIZE
    context_blocks = SLAB_COUNT * blocks_per_slab
    scaling = 1.0 / math.sqrt(HEAD_SIZE)
    first_block = (slab_index[0] * blocks_per_slab).astype(jnp.int32)
    key_pieces = context_keys.reshape(context_blocks, MASK_BLOCK_SIZE, KEY_VALUE_HEADS, HEAD_SIZE).transpose(2, 0, 1, 3)
    value_pieces = context_values.reshape(context_blocks, MASK_BLOCK_SIZE, KEY_VALUE_HEADS, HEAD_SIZE).transpose(2, 0, 1, 3)
    query_pieces = queries.reshape(blocks_per_slab, MASK_BLOCK_SIZE, KEY_VALUE_HEADS, query_per_key_head, HEAD_SIZE)
    gradient_pieces = output_cotangent.reshape(blocks_per_slab, MASK_BLOCK_SIZE, KEY_VALUE_HEADS, query_per_key_head, HEAD_SIZE)
    output_pieces = forward_output.reshape(blocks_per_slab, MASK_BLOCK_SIZE, KEY_VALUE_HEADS, query_per_key_head, HEAD_SIZE)
    head_numbers = jnp.arange(KEY_VALUE_HEADS, dtype=jnp.int32)[:, None]
    lower_tri = jnp.arange(MASK_BLOCK_SIZE)[:, None] >= jnp.arange(MASK_BLOCK_SIZE)[None, :]
    zero_gradients = jnp.zeros((KEY_VALUE_HEADS, context_blocks, MASK_BLOCK_SIZE, HEAD_SIZE), jnp.float32)

    def one_block(running, block_index):
        key_gradient_sum, value_gradient_sum = running
        present_slab = first_block + block_index
        slash_blocks = (present_slab - offsets).astype(jnp.int32)
        collide = jnp.any(slash_blocks[:, :, None] == verticals[:, None, :], axis=2)
        slash_valid = (offsets > 0) & jnp.logical_not(collide)
        vertical_valid = verticals < present_slab
        diagonal_mask = jnp.zeros((KEY_VALUE_HEADS, 1), jnp.int32) + present_slab
        cand_blocks = jnp.concatenate([diagonal_mask, verticals.astype(jnp.int32), slash_blocks], axis=1).astype(jnp.int32)
        candidate_valid = jnp.concatenate([jnp.ones((KEY_VALUE_HEADS, 1), jnp.bool_), vertical_valid, slash_valid], axis=1)
        cand_keys = key_pieces[head_numbers, cand_blocks].astype(jnp.float32)
        cand_values = value_pieces[head_numbers, cand_blocks].astype(jnp.float32)
        causal = (cand_blocks < present_slab)[:, None, :, None] | lower_tri[None, :, None, :]
        visible = candidate_valid[:, None, :, None] & causal
        q_block = lax.dynamic_index_in_dim(query_pieces, block_index, 0, keepdims=False).astype(jnp.float32)
        grad_block = lax.dynamic_index_in_dim(gradient_pieces, block_index, 0, keepdims=False).astype(jnp.float32)
        out_block = lax.dynamic_index_in_dim(output_pieces, block_index, 0, keepdims=False).astype(jnp.float32)
        scores = jnp.einsum('rhgd,hctd->hrgct', q_block, cand_keys) * scaling
        masked = jnp.where(visible[:, :, None], scores, -jnp.inf)
        row_max = lax.optimization_barrier(jnp.max(masked, axis=(3, 4), keepdims=True))
        row_sum = lax.optimization_barrier(jnp.sum(jnp.exp(masked - row_max), axis=(3, 4), keepdims=True))
        weights = jnp.exp(masked - (row_max + jnp.log(row_sum)))
        delta_rows = lax.optimization_barrier(jnp.sum(grad_block * out_block, axis=-1))
        weight_grad = jnp.einsum('rhgd,hctd->hrgct', grad_block, cand_values)
        score_grad = weights * (weight_grad - jnp.transpose(delta_rows, (1, 0, 2))[:, :, :, None, None])
        weights_low = lowered(weights)
        score_low = lowered(score_grad)
        value_part = jnp.einsum('hrgct,rhgd->hctd', weights_low, grad_block)
        key_part = jnp.einsum('hrgct,rhgd->hctd', score_low, q_block) * scaling
        query_part = jnp.einsum('hrgct,hctd->rhgd', score_low, cand_keys) * scaling
        key_gradient_sum = key_gradient_sum.at[head_numbers, cand_blocks].add(key_part)
        value_gradient_sum = value_gradient_sum.at[head_numbers, cand_blocks].add(value_part)
        return ((key_gradient_sum, value_gradient_sum), query_part)
    (key_gradient_sum, value_gradient_sum), query_parts = lax.scan(one_block, (zero_gradients, zero_gradients), jnp.arange(blocks_per_slab, dtype=jnp.int32))
    query_grad = query_parts.reshape(SLAB_QUERY_ROWS, QUERY_HEADS * HEAD_SIZE).astype(jnp.bfloat16)
    key_gradient = key_gradient_sum.transpose(1, 2, 0, 3).reshape(SLAB_COUNT, SLAB_QUERY_ROWS, KEY_VALUE_HEADS * HEAD_SIZE).astype(jnp.bfloat16)
    value_gradient = value_gradient_sum.transpose(1, 2, 0, 3).reshape(SLAB_COUNT, SLAB_QUERY_ROWS, KEY_VALUE_HEADS * HEAD_SIZE).astype(jnp.bfloat16)
    return (query_grad, key_gradient, value_gradient)
```

```python
import functools
import math

import jax
import jax.numpy as jnp
from jax import lax
from jax.experimental import pallas as pl
from jax.experimental.pallas import tpu as pltpu
from jax.sharding import PartitionSpec as P

BLOCK = 64
WDEV = 5
VMEM_LIMIT = 40 * 1024 * 1024
BF16 = jnp.bfloat16
F32 = jnp.float32


def from_behind(shard, by):
    peers = lax.axis_size("ctx")
    return lax.ppermute(shard, "ctx", [(i, (i + by) % peers) for i in range(peers)])


def pack_kernel(place, verts, keys, values, *rest, devices, heads, nv, per_device):
    sends, picked, sems, pick_sems = rest[:WDEV], rest[WDEV], rest[WDEV + 1], rest[WDEV + 2]
    slab, me = place[0], place[1]
    head_dim = picked.shape[2]
    copies = []
    for distance in range(1, WDEV + 1):
        region = slab - (me + distance >= devices).astype(jnp.int32)
        for kv, source in enumerate((keys, values)):
            copy = pltpu.make_async_copy(
                source.at[region], sends[distance - 1].at[kv], sems.at[distance - 1, kv]
            )
            copy.start()
            copies.append(copy)
    picked[...] = jnp.zeros_like(picked)
    slab_blocks = per_device * devices

    def unit_copy(h, m, kv, source):
        inner = verts[h, m] % slab_blocks
        region = verts[h, m] // slab_blocks
        row = pl.multiple_of((inner % per_device) * BLOCK, BLOCK)
        unit = h * nv + m
        return pltpu.make_async_copy(
            source.at[region, pl.ds(row, BLOCK), pl.ds(h * head_dim, head_dim)],
            picked.at[kv, pl.ds(unit * BLOCK, BLOCK), :],
            pick_sems.at[kv, unit],
        )

    def owned(h, m):
        return (verts[h, m] % slab_blocks) // per_device == me

    for h in range(heads):
        for m in range(nv):

            @pl.when(owned(h, m))
            def _():
                unit_copy(h, m, 0, keys).start()
                unit_copy(h, m, 1, values).start()

    for h in range(heads):
        for m in range(nv):

            @pl.when(owned(h, m))
            def _():
                unit_copy(h, m, 0, keys).wait()
                unit_copy(h, m, 1, values).wait()

    for copy in copies:
        copy.wait()


def pack(place, verticals, keys, values, devices):
    regions, rows, features = keys.shape
    heads, nv = verticals.shape
    head_dim = features // heads
    smem = pl.BlockSpec(memory_space=pltpu.SMEM)
    hbm = pl.BlockSpec(memory_space=pl.ANY)
    return pl.pallas_call(
        functools.partial(
            pack_kernel, devices=devices, heads=heads, nv=nv, per_device=rows // BLOCK
        ),
        in_specs=[smem, smem, hbm, hbm],
        out_specs=[hbm] * WDEV + [pl.BlockSpec(memory_space=pltpu.VMEM)],
        out_shape=[jax.ShapeDtypeStruct((2, rows, features), BF16)] * WDEV
        + [jax.ShapeDtypeStruct((2, heads * nv * BLOCK, head_dim), BF16)],
        scratch_shapes=[
            pltpu.SemaphoreType.DMA((WDEV, 2)),
            pltpu.SemaphoreType.DMA((2, heads * nv)),
        ],
        compiler_params=pltpu.CompilerParams(vmem_limit_bytes=VMEM_LIMIT),
    )(place, verticals, keys, values)


def attend_kernel(
    place, verts, offs, q, grad, out, keys, values, vert, *rest,
    devices, heads, nv, ns, per_device,
):
    recv = rest[:WDEV]
    dq, near, home, vgrad = rest[WDEV : WDEV + 4]
    (win, vkv, kc, vc, qs, gs, s_ref, dp_ref, w_ref, ds_ref, nacc, vacc, sems) = rest[WDEV + 4 :]
    h, j = pl.program_id(0), pl.program_id(1)
    slab, me = place[0], place[1]
    head_dim = kc.shape[1]
    group = q.shape[1] // head_dim
    cand = 1 + nv + ns
    scaling = 1.0 / math.sqrt(head_dim)
    rows = per_device * BLOCK
    block = slab * (per_device * devices) + me * per_device + j
    lanes = pl.ds(pl.multiple_of(h * head_dim, head_dim), head_dim)

    @pl.when((h == 0) & (j == 0))
    def _():
        copies = [
            pltpu.make_async_copy(
                recv[d - 1], win.at[:, pl.ds((WDEV - d) * rows, rows), :], sems.at[d - 1]
            )
            for d in range(1, WDEV + 1)
        ]
        own_rows = pl.ds(WDEV * rows, rows)
        copies.append(pltpu.make_async_copy(keys.at[slab], win.at[0, own_rows, :], sems.at[WDEV]))
        copies.append(
            pltpu.make_async_copy(values.at[slab], win.at[1, own_rows, :], sems.at[WDEV + 1])
        )
        copies.append(pltpu.make_async_copy(vert, vkv, sems.at[WDEV + 2]))
        for copy in copies:
            copy.start()
        nacc[...] = jnp.zeros_like(nacc)
        for copy in copies:
            copy.wait()

    own_at = pl.multiple_of((WDEV * per_device + j) * BLOCK, BLOCK)
    slash_at = [
        pl.multiple_of((WDEV * per_device + j - offs[h, s]) * BLOCK, BLOCK) for s in range(ns)
    ]
    vert_at = pl.multiple_of(h * (nv * BLOCK), nv * BLOCK)
    valid = [None]
    for m in range(nv):
        valid.append(verts[h, m] < block)
    for s in range(ns):
        collide = verts[h, 0] == block - offs[h, s]
        for m in range(1, nv):
            collide = collide | (verts[h, m] == block - offs[h, s])
        valid.append((offs[h, s] > 0) & jnp.logical_not(collide))
    for kv, to in enumerate((kc, vc)):
        to[0:BLOCK, :] = win[kv, pl.ds(own_at, BLOCK), lanes]
        to[BLOCK : (1 + nv) * BLOCK, :] = vkv[kv, pl.ds(vert_at, nv * BLOCK), :]
        for s in range(ns):
            to[(1 + nv + s) * BLOCK : (2 + nv + s) * BLOCK, :] = win[
                kv, pl.ds(slash_at[s], BLOCK), lanes
            ]
    products = []
    for g in range(group):
        cols = slice(g * head_dim, (g + 1) * head_dim)
        qs[g * BLOCK : (g + 1) * BLOCK, :] = q[:, cols]
        gs[g * BLOCK : (g + 1) * BLOCK, :] = grad[:, cols]
        products.append(grad[:, cols].astype(F32) * out[:, cols].astype(F32))
    width = group * BLOCK
    delta = jnp.sum(jnp.transpose(jnp.concatenate(products, axis=0)), axis=0, keepdims=True)

    nt = (((1,), (1,)), ((), ()))
    s_ref[...] = lax.dot_general(kc[...], qs[...], nt, preferred_element_type=F32)
    dp_ref[...] = lax.dot_general(vc[...], gs[...], nt, preferred_element_type=F32)

    log2_scale = scaling * math.log2(math.e)
    neg = jnp.float32(-jnp.inf)
    key_at = lax.broadcasted_iota(jnp.int32, (BLOCK, width), 0)
    row_at = lax.broadcasted_iota(jnp.int32, (BLOCK, width), 1) % BLOCK
    s_ref[0:BLOCK, :] = jnp.where(key_at <= row_at, s_ref[0:BLOCK, :], neg)

    def scaled(c):
        t = s_ref[c * BLOCK : (c + 1) * BLOCK, :] * log2_scale
        if c > 0:
            t = t + jnp.where(valid[c], jnp.float32(0), neg)
        return t

    def fold(x, op):
        y = x[0:8, :]
        for r in range(1, BLOCK // 8):
            y = op(y, x[r * 8 : (r + 1) * 8, :])
        return y

    top = fold(scaled(0), jnp.maximum)
    for c in range(1, cand):
        top = jnp.maximum(top, fold(scaled(c), jnp.maximum))
    top = jnp.max(top, axis=0, keepdims=True)
    total = jnp.zeros((8, width), F32)
    for c in range(cand):
        p = jnp.exp2(scaled(c) - top)
        s_ref[c * BLOCK : (c + 1) * BLOCK, :] = p
        total = total + fold(p, jnp.add)
    inverse = 1.0 / jnp.sum(total, axis=0, keepdims=True)
    for c in range(cand):
        span = slice(c * BLOCK, (c + 1) * BLOCK)
        w = s_ref[span, :] * inverse
        w_ref[span, :] = w.astype(BF16)
        ds_ref[span, :] = (w * (dp_ref[span, :] - delta)).astype(BF16)

    dv = jnp.dot(w_ref[...], gs[...], preferred_element_type=F32)
    dk = jnp.dot(ds_ref[...], qs[...], preferred_element_type=F32) * scaling
    dqt = lax.dot_general(
        kc[...], ds_ref[...], (((0,), (0,)), ((), ())), preferred_element_type=F32
    )
    dqr = (jnp.transpose(dqt) * scaling).astype(BF16)
    for g in range(group):
        dq[:, g * head_dim : (g + 1) * head_dim] = dqr[g * BLOCK : (g + 1) * BLOCK, :]

    for kv, part in enumerate((dk, dv)):
        nacc[kv, pl.ds(own_at, BLOCK), lanes] += part[0:BLOCK]
        for s in range(ns):
            nacc[kv, pl.ds(slash_at[s], BLOCK), lanes] += part[
                (1 + nv + s) * BLOCK : (2 + nv + s) * BLOCK
            ]
        verticals_part = part[BLOCK : (1 + nv) * BLOCK]

        @pl.when(j == 0)
        def _():
            vacc[kv] = verticals_part

        @pl.when(j > 0)
        def _():
            vacc[kv] += verticals_part

    @pl.when(j == per_device - 1)
    def _():
        for kv in range(2):
            vgrad[kv, pl.ds(vert_at, nv * BLOCK), :] = vacc[kv].astype(BF16)
            home[kv, :, lanes] = nacc[kv, WDEV * rows :, lanes]
            for d in range(1, WDEV + 1):
                near[d - 1, kv, :, lanes] = nacc[
                    kv, (WDEV - d) * rows : (WDEV - d + 1) * rows, lanes
                ].astype(BF16)


def attend(place, verticals, offsets, queries, cotangent, output, keys, values, vert, recv, devices):
    rows, width = queries.shape
    features = keys.shape[2]
    heads, nv = verticals.shape
    ns = offsets.shape[1]
    head_dim = features // heads
    group = width // features
    per_device = rows // BLOCK
    cand = 1 + nv + ns
    smem = pl.BlockSpec(memory_space=pltpu.SMEM)
    hbm = pl.BlockSpec(memory_space=pl.ANY)
    tile = pl.BlockSpec((BLOCK, group * head_dim), lambda h, j: (j, h))

    def whole(shape):
        return pl.BlockSpec(shape, lambda h, j: (0,) * len(shape))

    near_shape = (WDEV, 2, rows, features)
    home_shape = (2, rows, features)
    vert_shape = (2, heads * nv * BLOCK, head_dim)
    return pl.pallas_call(
        functools.partial(
            attend_kernel, devices=devices, heads=heads, nv=nv, ns=ns, per_device=per_device
        ),
        grid=(heads, per_device),
        in_specs=[smem] * 3 + [tile] * 3 + [hbm] * (3 + WDEV),
        out_specs=[tile, whole(near_shape), whole(home_shape), whole(vert_shape)],
        out_shape=[
            jax.ShapeDtypeStruct((rows, width), BF16),
            jax.ShapeDtypeStruct(near_shape, BF16),
            jax.ShapeDtypeStruct(home_shape, F32),
            jax.ShapeDtypeStruct(vert_shape, BF16),
        ],
        scratch_shapes=[
            pltpu.VMEM((2, (WDEV + 1) * rows, features), BF16),
            pltpu.VMEM(vert_shape, BF16),
            pltpu.VMEM((cand * BLOCK, head_dim), BF16),
            pltpu.VMEM((cand * BLOCK, head_dim), BF16),
            pltpu.VMEM((group * BLOCK, head_dim), BF16),
            pltpu.VMEM((group * BLOCK, head_dim), BF16),
            pltpu.VMEM((cand * BLOCK, group * BLOCK), F32),
            pltpu.VMEM((cand * BLOCK, group * BLOCK), F32),
            pltpu.VMEM((cand * BLOCK, group * BLOCK), BF16),
            pltpu.VMEM((cand * BLOCK, group * BLOCK), BF16),
            pltpu.VMEM((2, (WDEV + 1) * rows, features), F32),
            pltpu.VMEM((2, nv * BLOCK, head_dim), F32),
            pltpu.SemaphoreType.DMA((WDEV + 3,)),
        ],
        compiler_params=pltpu.CompilerParams(vmem_limit_bytes=VMEM_LIMIT),
    )(place, verticals, offsets, queries, cotangent, output, keys, values, vert, *recv)


def assemble_kernel(place, verts, home, *rest, devices, heads, nv, per_device):
    back = rest[:WDEV]
    vert, key_out, value_out, acc = rest[WDEV:]
    slab, me = place[0], place[1]
    head_dim = vert.shape[2]
    slab_blocks = per_device * devices
    acc[0] = home[...]
    acc[1] = jnp.zeros_like(home)
    for d in range(1, WDEV + 1):
        slot = (me + d >= devices).astype(jnp.int32)
        acc[slot] += back[d - 1][...].astype(F32)
    key_out[...] = jnp.zeros_like(key_out)
    value_out[...] = jnp.zeros_like(value_out)
    outs = (key_out, value_out)
    for h in range(heads):
        lanes = slice(h * head_dim, (h + 1) * head_dim)
        for m in range(nv):
            inner = verts[h, m] % slab_blocks
            region = verts[h, m] // slab_blocks
            row = pl.multiple_of((inner % per_device) * BLOCK, BLOCK)
            at = (h * nv + m) * BLOCK

            @pl.when(inner // per_device == me)
            def _():
                close = (region == slab) | (region == slab - 1)

                @pl.when(close)
                def _():
                    for kv in range(2):
                        acc[slab - region, kv, pl.ds(row, BLOCK), lanes] += vert[
                            kv, at : at + BLOCK, :
                        ].astype(F32)

                @pl.when(jnp.logical_not(close))
                def _():
                    for kv in range(2):
                        outs[kv][region, pl.ds(row, BLOCK), lanes] = vert[kv, at : at + BLOCK, :]

    for kv in range(2):
        outs[kv][slab] = acc[0, kv].astype(BF16)
        outs[kv][slab - 1] = acc[1, kv].astype(BF16)


def assemble(place, verticals, home, back, vert, regions, devices):
    _, rows, features = home.shape
    heads, nv = verticals.shape
    smem = pl.BlockSpec(memory_space=pltpu.SMEM)
    vmem = pl.BlockSpec(memory_space=pltpu.VMEM)
    return pl.pallas_call(
        functools.partial(
            assemble_kernel, devices=devices, heads=heads, nv=nv, per_device=rows // BLOCK
        ),
        in_specs=[smem] * 2 + [vmem] * (2 + WDEV),
        out_specs=[vmem] * 2,
        out_shape=[jax.ShapeDtypeStruct((regions, rows, features), BF16)] * 2,
        scratch_shapes=[pltpu.VMEM((2, 2, rows, features), F32)],
        compiler_params=pltpu.CompilerParams(vmem_limit_bytes=VMEM_LIMIT),
    )(place, verticals, home, *back, vert)


def shards(
    queries,
    context_keys,
    context_values,
    forward_output,
    output_cotangent,
    verticals,
    offsets,
    slab_index,
):
    devices = lax.axis_size("ctx")
    me = lax.axis_index("ctx")
    regions = context_keys.shape[0]
    place = jnp.stack([slab_index[0], me.astype(jnp.int32)])
    *sends, picked = pack(place, verticals, context_keys, context_values, devices)
    vert = lax.psum(picked, "ctx")
    recv = [from_behind(sends[d - 1], d) for d in range(1, WDEV + 1)]
    query_grad, near, home, vgrad = attend(
        place, verticals, offsets, queries, output_cotangent, forward_output,
        context_keys, context_values, vert, recv, devices,
    )
    flat = vgrad.reshape(devices, -1, vgrad.shape[-1])
    shares = lax.all_to_all(flat, "ctx", 0, 0, tiled=True)
    summed = jnp.sum(shares.astype(F32), axis=0).astype(BF16)
    vert_sum = lax.all_gather(summed, "ctx", axis=0, tiled=True).reshape(vgrad.shape)
    back = [from_behind(near[d - 1], -d) for d in range(1, WDEV + 1)]
    key_gradient, value_gradient = assemble(
        place, verticals, home, back, vert_sum, regions, devices
    )
    return query_grad, key_gradient, value_gradient


def solution(mesh):
    in_specs = (
        P(("groups", "ctx"), None),
        P("groups", "ctx", None),
        P("groups", "ctx", None),
        P(("groups", "ctx"), None),
        P(("groups", "ctx"), None),
        P("groups", None),
        P("groups", None),
        P("groups"),
    )
    out_specs = (P(("groups", "ctx"), None), P("groups", "ctx", None), P("groups", "ctx", None))
    return jax.shard_map(shards, mesh=mesh, in_specs=in_specs, out_specs=out_specs, check_vma=False)
```

```python
import functools
import math

import jax
import jax.numpy as jnp
from jax import lax
from jax.experimental import pallas as pl
from jax.experimental.pallas import tpu as pltpu
from jax.sharding import PartitionSpec as P

BLOCK = 64
WDEV = 5
VMEM_LIMIT = 60 * 1024 * 1024
BF16 = jnp.bfloat16
F32 = jnp.float32


def from_behind(shard, by):
    peers = lax.axis_size("ctx")
    return lax.ppermute(shard, "ctx", [(i, (i + by) % peers) for i in range(peers)])


def other_core(shard):
    peers = lax.axis_size("ctx")
    return lax.ppermute(shard, "ctx", [(i, i ^ 1) for i in range(peers)])


def same_core_groups():
    peers = lax.axis_size("ctx")
    return [list(range(core, peers, 2)) for core in range(2)]


def sum_over_chips(half):
    chips = lax.axis_size("ctx") // 2
    groups = same_core_groups()
    shares = lax.all_to_all(
        half.reshape(chips, -1, half.shape[-1]), "ctx", 0, 0, axis_index_groups=groups, tiled=True
    )
    summed = jnp.sum(shares.astype(F32), axis=0).astype(BF16)
    spread = jnp.broadcast_to(summed[None], shares.shape)
    every = lax.all_to_all(spread, "ctx", 0, 0, axis_index_groups=groups, tiled=True)
    return every.reshape(half.shape)


def pack_kernel(place, verts, keys, values, *rest, devices, heads, nv, per_device):
    sends = rest[:WDEV]
    keep, give, picked, sems, pick_sems = rest[WDEV:]
    slab, me = place[0], place[1]
    core = me % 2
    head_dim = picked.shape[2]
    copies = []
    for distance in range(1, WDEV + 1):
        region = slab - (me + distance >= devices).astype(jnp.int32)
        for kv, source in enumerate((keys, values)):
            copy = pltpu.make_async_copy(
                source.at[region], sends[distance - 1].at[kv], sems.at[distance - 1, kv]
            )
            copy.start()
            copies.append(copy)
    picked[...] = jnp.zeros_like(picked)
    slab_blocks = per_device * devices

    def unit_copy(h, m, kv, source):
        inner = verts[h, m] % slab_blocks
        region = verts[h, m] // slab_blocks
        row = pl.multiple_of((inner % per_device) * BLOCK, BLOCK)
        unit = h * nv + m
        return pltpu.make_async_copy(
            source.at[region, pl.ds(row, BLOCK), pl.ds(h * head_dim, head_dim)],
            picked.at[(kv + core) % 2, pl.ds(unit * BLOCK, BLOCK), :],
            pick_sems.at[kv, unit],
        )

    def owned(h, m):
        return (verts[h, m] % slab_blocks) // per_device == me

    for h in range(heads):
        for m in range(nv):

            @pl.when(owned(h, m))
            def _():
                unit_copy(h, m, 0, keys).start()
                unit_copy(h, m, 1, values).start()

    for h in range(heads):
        for m in range(nv):

            @pl.when(owned(h, m))
            def _():
                unit_copy(h, m, 0, keys).wait()
                unit_copy(h, m, 1, values).wait()

    keep[...] = picked[0]
    give[...] = picked[1]
    for copy in copies:
        copy.wait()


def pack(place, verticals, keys, values, devices):
    regions, rows, features = keys.shape
    heads, nv = verticals.shape
    head_dim = features // heads
    smem = pl.BlockSpec(memory_space=pltpu.SMEM)
    hbm = pl.BlockSpec(memory_space=pl.ANY)
    return pl.pallas_call(
        functools.partial(
            pack_kernel, devices=devices, heads=heads, nv=nv, per_device=rows // BLOCK
        ),
        in_specs=[smem, smem, hbm, hbm],
        out_specs=[hbm] * WDEV + [pl.BlockSpec(memory_space=pltpu.VMEM)] * 2,
        out_shape=[jax.ShapeDtypeStruct((2, rows, features), BF16)] * WDEV
        + [jax.ShapeDtypeStruct((heads * nv * BLOCK, head_dim), BF16)] * 2,
        scratch_shapes=[
            pltpu.VMEM((2, heads * nv * BLOCK, head_dim), BF16),
            pltpu.SemaphoreType.DMA((WDEV, 2)),
            pltpu.SemaphoreType.DMA((2, heads * nv)),
        ],
        compiler_params=pltpu.CompilerParams(vmem_limit_bytes=VMEM_LIMIT),
    )(place, verticals, keys, values)


def attend_kernel(
    place, verts, offs, q, grad, out, keys, values, vert_mine, vert_other, *rest,
    devices, heads, nv, ns, per_device,
):
    recv = rest[:WDEV]
    dq, near, home, vkeep, vgive = rest[WDEV : WDEV + 5]
    (win, vkv, kc, vc, qs, gs, s_ref, dp_ref, w_ref, ds_ref, nacc, vacc, sems) = rest[WDEV + 5 :]
    h, j = pl.program_id(0), pl.program_id(1)
    slab, me = place[0], place[1]
    core = me % 2
    head_dim = kc.shape[1]
    group = q.shape[1] // head_dim
    cand = 1 + nv + ns
    scaling = 1.0 / math.sqrt(head_dim)
    rows = per_device * BLOCK
    block = slab * (per_device * devices) + me * per_device + j
    lanes = pl.ds(pl.multiple_of(h * head_dim, head_dim), head_dim)

    @pl.when((h == 0) & (j == 0))
    def _():
        copies = [
            pltpu.make_async_copy(
                recv[d - 1], win.at[:, pl.ds((WDEV - d) * rows, rows), :], sems.at[d - 1]
            )
            for d in range(1, WDEV + 1)
        ]
        own_rows = pl.ds(WDEV * rows, rows)
        copies.append(pltpu.make_async_copy(keys.at[slab], win.at[0, own_rows, :], sems.at[WDEV]))
        copies.append(
            pltpu.make_async_copy(values.at[slab], win.at[1, own_rows, :], sems.at[WDEV + 1])
        )
        copies.append(pltpu.make_async_copy(vert_mine, vkv.at[core], sems.at[WDEV + 2]))
        copies.append(pltpu.make_async_copy(vert_other, vkv.at[1 - core], sems.at[WDEV + 3]))
        for copy in copies:
            copy.start()
        nacc[...] = jnp.zeros_like(nacc)
        for copy in copies:
            copy.wait()

    own_at = pl.multiple_of((WDEV * per_device + j) * BLOCK, BLOCK)
    slash_at = [
        pl.multiple_of((WDEV * per_device + j - offs[h, s]) * BLOCK, BLOCK) for s in range(ns)
    ]
    vert_at = pl.multiple_of(h * (nv * BLOCK), nv * BLOCK)
    valid = [None]
    for m in range(nv):
        valid.append(verts[h, m] < block)
    for s in range(ns):
        collide = verts[h, 0] == block - offs[h, s]
        for m in range(1, nv):
            collide = collide | (verts[h, m] == block - offs[h, s])
        valid.append((offs[h, s] > 0) & jnp.logical_not(collide))
    for kv, to in enumerate((kc, vc)):
        to[0:BLOCK, :] = win[kv, pl.ds(own_at, BLOCK), lanes]
        to[BLOCK : (1 + nv) * BLOCK, :] = vkv[kv, pl.ds(vert_at, nv * BLOCK), :]
        for s in range(ns):
            to[(1 + nv + s) * BLOCK : (2 + nv + s) * BLOCK, :] = win[
                kv, pl.ds(slash_at[s], BLOCK), lanes
            ]
    products = []
    for g in range(group):
        cols = slice(g * head_dim, (g + 1) * head_dim)
        qs[g * BLOCK : (g + 1) * BLOCK, :] = q[:, cols]
        gs[g * BLOCK : (g + 1) * BLOCK, :] = grad[:, cols]
        products.append(grad[:, cols].astype(F32) * out[:, cols].astype(F32))
    width = group * BLOCK
    delta = jnp.sum(jnp.transpose(jnp.concatenate(products, axis=0)), axis=0, keepdims=True)

    nt = (((1,), (1,)), ((), ()))
    s_ref[...] = lax.dot_general(kc[...], qs[...], nt, preferred_element_type=F32)
    dp_ref[...] = lax.dot_general(vc[...], gs[...], nt, preferred_element_type=F32)

    log2_scale = scaling * math.log2(math.e)
    neg = jnp.float32(-jnp.inf)
    key_at = lax.broadcasted_iota(jnp.int32, (BLOCK, width), 0)
    row_at = lax.broadcasted_iota(jnp.int32, (BLOCK, width), 1) % BLOCK
    s_ref[0:BLOCK, :] = jnp.where(key_at <= row_at, s_ref[0:BLOCK, :], neg)

    def scaled(c):
        t = s_ref[c * BLOCK : (c + 1) * BLOCK, :] * log2_scale
        if c > 0:
            t = t + jnp.where(valid[c], jnp.float32(0), neg)
        return t

    def fold(x, op):
        y = x[0:8, :]
        for r in range(1, BLOCK // 8):
            y = op(y, x[r * 8 : (r + 1) * 8, :])
        return y

    top = fold(scaled(0), jnp.maximum)
    for c in range(1, cand):
        top = jnp.maximum(top, fold(scaled(c), jnp.maximum))
    top = jnp.max(top, axis=0, keepdims=True)
    total = jnp.zeros((8, width), F32)
    for c in range(cand):
        p = jnp.exp2(scaled(c) - top)
        s_ref[c * BLOCK : (c + 1) * BLOCK, :] = p
        total = total + fold(p, jnp.add)
    inverse = 1.0 / jnp.sum(total, axis=0, keepdims=True)
    for c in range(cand):
        span = slice(c * BLOCK, (c + 1) * BLOCK)
        w = s_ref[span, :] * inverse
        w_ref[span, :] = w.astype(BF16)
        ds_ref[span, :] = (w * (dp_ref[span, :] - delta)).astype(BF16)

    dv = jnp.dot(w_ref[...], gs[...], preferred_element_type=F32)
    dk = jnp.dot(ds_ref[...], qs[...], preferred_element_type=F32) * scaling
    dqt = lax.dot_general(
        kc[...], ds_ref[...], (((0,), (0,)), ((), ())), preferred_element_type=F32
    )
    dqr = (jnp.transpose(dqt) * scaling).astype(BF16)
    for g in range(group):
        dq[:, g * head_dim : (g + 1) * head_dim] = dqr[g * BLOCK : (g + 1) * BLOCK, :]

    for kv, part in enumerate((dk, dv)):
        nacc[kv, pl.ds(own_at, BLOCK), lanes] += part[0:BLOCK]
        for s in range(ns):
            nacc[kv, pl.ds(slash_at[s], BLOCK), lanes] += part[
                (1 + nv + s) * BLOCK : (2 + nv + s) * BLOCK
            ]
        verticals_part = part[BLOCK : (1 + nv) * BLOCK]

        @pl.when(j == 0)
        def _():
            vacc[kv] = verticals_part

        @pl.when(j > 0)
        def _():
            vacc[kv] += verticals_part

    @pl.when(j == per_device - 1)
    def _():
        vkeep[pl.ds(vert_at, nv * BLOCK), :] = vacc[core]
        vgive[pl.ds(vert_at, nv * BLOCK), :] = vacc[1 - core].astype(BF16)
        for kv in range(2):
            home[kv, :, lanes] = nacc[kv, WDEV * rows :, lanes]
            for d in range(1, WDEV + 1):
                near[d - 1, kv, :, lanes] = nacc[
                    kv, (WDEV - d) * rows : (WDEV - d + 1) * rows, lanes
                ].astype(BF16)


def attend(place, verticals, offsets, queries, cotangent, output, keys, values, vert_mine,
           vert_other, recv, devices):
    rows, width = queries.shape
    features = keys.shape[2]
    heads, nv = verticals.shape
    ns = offsets.shape[1]
    head_dim = features // heads
    group = width // features
    per_device = rows // BLOCK
    cand = 1 + nv + ns
    smem = pl.BlockSpec(memory_space=pltpu.SMEM)
    hbm = pl.BlockSpec(memory_space=pl.ANY)
    tile = pl.BlockSpec((BLOCK, group * head_dim), lambda h, j: (j, h))

    def whole(shape):
        return pl.BlockSpec(shape, lambda h, j: (0,) * len(shape))

    near_shape = (WDEV, 2, rows, features)
    home_shape = (2, rows, features)
    vert_shape = (heads * nv * BLOCK, head_dim)
    return pl.pallas_call(
        functools.partial(
            attend_kernel, devices=devices, heads=heads, nv=nv, ns=ns, per_device=per_device
        ),
        grid=(heads, per_device),
        in_specs=[smem] * 3 + [tile] * 3 + [hbm] * (4 + WDEV),
        out_specs=[tile, whole(near_shape), whole(home_shape), whole(vert_shape), whole(vert_shape)],
        out_shape=[
            jax.ShapeDtypeStruct((rows, width), BF16),
            jax.ShapeDtypeStruct(near_shape, BF16),
            jax.ShapeDtypeStruct(home_shape, F32),
            jax.ShapeDtypeStruct(vert_shape, F32),
            jax.ShapeDtypeStruct(vert_shape, BF16),
        ],
        scratch_shapes=[
            pltpu.VMEM((2, (WDEV + 1) * rows, features), BF16),
            pltpu.VMEM((2,) + vert_shape, BF16),
            pltpu.VMEM((cand * BLOCK, head_dim), BF16),
            pltpu.VMEM((cand * BLOCK, head_dim), BF16),
            pltpu.VMEM((group * BLOCK, head_dim), BF16),
            pltpu.VMEM((group * BLOCK, head_dim), BF16),
            pltpu.VMEM((cand * BLOCK, group * BLOCK), F32),
            pltpu.VMEM((cand * BLOCK, group * BLOCK), F32),
            pltpu.VMEM((cand * BLOCK, group * BLOCK), BF16),
            pltpu.VMEM((cand * BLOCK, group * BLOCK), BF16),
            pltpu.VMEM((2, (WDEV + 1) * rows, features), F32),
            pltpu.VMEM((2, nv * BLOCK, head_dim), F32),
            pltpu.SemaphoreType.DMA((WDEV + 4,)),
        ],
        compiler_params=pltpu.CompilerParams(vmem_limit_bytes=VMEM_LIMIT),
    )(
        place, verticals, offsets, queries, cotangent, output, keys, values, vert_mine, vert_other,
        *recv,
    )


def assemble_kernel(place, verts, home, *rest, devices, heads, nv, per_device):
    back = rest[:WDEV]
    vert_mine, vert_other, key_out, value_out, vert, acc = rest[WDEV:]
    slab, me = place[0], place[1]
    core = me % 2
    vert[core] = vert_mine[...]
    vert[1 - core] = vert_other[...]
    head_dim = vert.shape[2]
    slab_blocks = per_device * devices
    acc[0] = home[...]
    acc[1] = jnp.zeros_like(home)
    for d in range(1, WDEV + 1):
        slot = (me + d >= devices).astype(jnp.int32)
        acc[slot] += back[d - 1][...].astype(F32)
    key_out[...] = jnp.zeros_like(key_out)
    value_out[...] = jnp.zeros_like(value_out)
    outs = (key_out, value_out)
    for h in range(heads):
        lanes = slice(h * head_dim, (h + 1) * head_dim)
        for m in range(nv):
            inner = verts[h, m] % slab_blocks
            region = verts[h, m] // slab_blocks
            row = pl.multiple_of((inner % per_device) * BLOCK, BLOCK)
            at = (h * nv + m) * BLOCK

            @pl.when(inner // per_device == me)
            def _():
                close = (region == slab) | (region == slab - 1)

                @pl.when(close)
                def _():
                    for kv in range(2):
                        acc[slab - region, kv, pl.ds(row, BLOCK), lanes] += vert[
                            kv, at : at + BLOCK, :
                        ].astype(F32)

                @pl.when(jnp.logical_not(close))
                def _():
                    for kv in range(2):
                        outs[kv][region, pl.ds(row, BLOCK), lanes] = vert[kv, at : at + BLOCK, :]

    for kv in range(2):
        outs[kv][slab] = acc[0, kv].astype(BF16)
        outs[kv][slab - 1] = acc[1, kv].astype(BF16)


def assemble(place, verticals, home, back, vert_mine, vert_other, regions, devices):
    _, rows, features = home.shape
    heads, nv = verticals.shape
    smem = pl.BlockSpec(memory_space=pltpu.SMEM)
    vmem = pl.BlockSpec(memory_space=pltpu.VMEM)
    return pl.pallas_call(
        functools.partial(
            assemble_kernel, devices=devices, heads=heads, nv=nv, per_device=rows // BLOCK
        ),
        in_specs=[smem] * 2 + [vmem] * (3 + WDEV),
        out_specs=[vmem] * 2,
        out_shape=[jax.ShapeDtypeStruct((regions, rows, features), BF16)] * 2,
        scratch_shapes=[
            pltpu.VMEM((2,) + vert_mine.shape, BF16),
            pltpu.VMEM((2, 2, rows, features), F32),
        ],
        compiler_params=pltpu.CompilerParams(vmem_limit_bytes=VMEM_LIMIT),
    )(place, verticals, home, *back, vert_mine, vert_other)


def shards(
    queries,
    context_keys,
    context_values,
    forward_output,
    output_cotangent,
    verticals,
    offsets,
    slab_index,
):
    devices = lax.axis_size("ctx")
    me = lax.axis_index("ctx")
    regions = context_keys.shape[0]
    place = jnp.stack([slab_index[0], me.astype(jnp.int32)])
    *sends, keep, give = pack(place, verticals, context_keys, context_values, devices)
    recv = [from_behind(sends[d - 1], d) for d in range(1, WDEV + 1)]
    vert_mine = sum_over_chips(keep + other_core(give))
    vert_other = other_core(vert_mine)
    query_grad, near, home, vkeep, vgive = attend(
        place, verticals, offsets, queries, output_cotangent, forward_output,
        context_keys, context_values, vert_mine, vert_other, recv, devices,
    )
    back = [from_behind(near[d - 1], -d) for d in range(1, WDEV + 1)]
    half = (vkeep + other_core(vgive).astype(F32)).astype(BF16)
    total_mine = sum_over_chips(half)
    total_other = other_core(total_mine)
    key_gradient, value_gradient = assemble(
        place, verticals, home, back, total_mine, total_other, regions, devices
    )
    return query_grad, key_gradient, value_gradient


def solution(mesh):
    in_specs = (
        P(("groups", "ctx"), None),
        P("groups", "ctx", None),
        P("groups", "ctx", None),
        P(("groups", "ctx"), None),
        P(("groups", "ctx"), None),
        P("groups", None),
        P("groups", None),
        P("groups"),
    )
    out_specs = (P(("groups", "ctx"), None), P("groups", "ctx", None), P("groups", "ctx", None))
    return jax.shard_map(shards, mesh=mesh, in_specs=in_specs, out_specs=out_specs, check_vma=False)
```

```python
import functools
import math

import jax
import jax.numpy as jnp
from jax import lax
from jax.experimental import pallas as pl
from jax.experimental.pallas import tpu as pltpu
from jax.sharding import PartitionSpec as P

BLOCK = 64
WDEV = 5
VMEM_LIMIT = 60 * 1024 * 1024
BF16 = jnp.bfloat16
F32 = jnp.float32


class Lines:
    def __init__(self, devices):
        self.devices = devices
        self.far = devices // 4

    def place(self, me):
        return me // 4, (me // 2) % 2, me % 2

    def core_pairs(self):
        return [(i, i ^ 1) for i in range(self.devices)]

    def near_pairs(self):
        return [(i, i ^ 2) for i in range(self.devices)]

    def far_pairs(self, by):
        return [(i, (i + 4 * by) % self.devices) for i in range(self.devices)]

    def shift_pairs(self, by):
        return [(i, (i + by) % self.devices) for i in range(self.devices)]

    def mixed_pairs(self):
        return [(i, (i + (5 if i % 2 else 1)) % self.devices) for i in range(self.devices)]


def back(pairs):
    return [(b, a) for a, b in pairs]


def move(array, pairs):
    return lax.ppermute(array, "ctx", pairs)


def gather_verticals(lines, own):
    parts = [own] + [move(own, lines.far_pairs(by)) for by in range(1, lines.far)]
    mine = jnp.stack(parts)
    across = move(mine, lines.near_pairs())
    core_mine = move(mine, lines.core_pairs())
    core_across = move(across, lines.core_pairs())
    return mine, across, core_mine, core_across


def sum_verticals(lines, keep, give, wide):
    half = keep.astype(wide) + move(give, lines.core_pairs()).astype(wide)
    quarter = half[0] + move(half[1].astype(BF16), lines.near_pairs()).astype(wide)
    share = quarter[0]
    for by in range(1, lines.far):
        share = share + move(quarter[by].astype(BF16), lines.far_pairs(by)).astype(wide)
    return share.astype(BF16)


def wraps(me, devices):
    return [me + 2 >= devices, me + 4 >= devices, (me % 2 == 1) & (me + 5 >= devices)]


def pack_kernel(place, verts, keys, values, *rest, lines, heads, nv, per_device):
    sends = rest[:3]
    keep, give, picked, sems, pick_sems = rest[3:]
    slab, me = place[0], place[1]
    far, near, core = lines.place(me)
    _, _, chunk, head_dim = keep.shape
    copies = []
    for n, wrapped in enumerate(wraps(me, lines.devices)):
        region = slab - wrapped.astype(jnp.int32)
        for kv, source in enumerate((keys, values)):
            copy = pltpu.make_async_copy(source.at[region], sends[n].at[kv], sems.at[n, kv])
            copy.start()
            copies.append(copy)
    picked[...] = jnp.zeros_like(picked)
    slab_blocks = per_device * lines.devices
    piece = min(BLOCK, chunk)

    def unit_copies(h, m):
        inner = verts[h, m] % slab_blocks
        region = verts[h, m] // slab_blocks
        row = (inner % per_device) * BLOCK
        for p in range(BLOCK // piece):
            at = (h * nv + m) * BLOCK + p * piece
            line, at = at // (lines.far * chunk), at % (lines.far * chunk)
            slot, at = at // chunk, at % chunk
            line = lax.rem(line + near, 2)
            slot = lax.rem(slot - far + lines.far, lines.far)
            for kv, source in enumerate((keys, values)):
                yield pltpu.make_async_copy(
                    source.at[
                        region,
                        pl.ds(pl.multiple_of(row + p * piece, piece), piece),
                        pl.ds(h * head_dim, head_dim),
                    ],
                    picked.at[lax.rem(kv + core, 2), line, slot, pl.ds(at, piece), :],
                    pick_sems.at[kv, (h * nv + m) * (BLOCK // piece) + p],
                )

    def owned(h, m):
        return (verts[h, m] % slab_blocks) // per_device == me

    for h in range(heads):
        for m in range(nv):

            @pl.when(owned(h, m))
            def _():
                for copy in unit_copies(h, m):
                    copy.start()

    for h in range(heads):
        for m in range(nv):

            @pl.when(owned(h, m))
            def _():
                for copy in unit_copies(h, m):
                    copy.wait()

    keep[...] = picked[0]
    give[...] = picked[1]
    for copy in copies:
        copy.wait()


def pack(place, verticals, keys, values, lines):
    regions, rows, features = keys.shape
    heads, nv = verticals.shape
    head_dim = features // heads
    chunk = heads * nv * BLOCK // (2 * lines.far)
    smem = pl.BlockSpec(memory_space=pltpu.SMEM)
    hbm = pl.BlockSpec(memory_space=pl.ANY)
    share = (2, lines.far, chunk, head_dim)
    return pl.pallas_call(
        functools.partial(pack_kernel, lines=lines, heads=heads, nv=nv, per_device=rows // BLOCK),
        in_specs=[smem, smem, hbm, hbm],
        out_specs=[pl.BlockSpec(memory_space=pltpu.VMEM)] * 5,
        out_shape=[jax.ShapeDtypeStruct((2, rows, features), BF16)] * 3
        + [jax.ShapeDtypeStruct(share, BF16)] * 2,
        scratch_shapes=[
            pltpu.VMEM((2,) + share, BF16),
            pltpu.SemaphoreType.DMA((3, 2)),
            pltpu.SemaphoreType.DMA((2, heads * nv * max(1, BLOCK // chunk))),
        ],
        compiler_params=pltpu.CompilerParams(vmem_limit_bytes=VMEM_LIMIT),
    )(place, verticals, keys, values)


def distances(core):
    return [2, 4, 5 - 4 * core, 1 + 2 * core, 3 + 2 * core]


def vertical_copies(lines, me, chunk, gathered, to, sems, first):
    far, near, core = lines.place(me)
    copies = []
    for n, source in enumerate(gathered):
        kv = core if n < 2 else 1 - core
        line = near if n % 2 == 0 else 1 - near
        for s in range(lines.far):
            slot = lax.rem(far - s + lines.far, lines.far)
            row = pl.multiple_of((line * lines.far + slot) * chunk, chunk)
            copies.append(
                pltpu.make_async_copy(
                    source.at[s], to.at[kv, pl.ds(row, chunk), :], sems.at[first + len(copies)]
                )
            )
    return copies


def attend_kernel(
    place, verts, offs, q, grad, out, keys, values, *rest, lines, heads, nv, ns, per_device,
):
    gathered, recv, rest = rest[:4], rest[4 : 4 + WDEV], rest[4 + WDEV :]
    dq, home, near_parts, vkeep, vgive = rest[0], rest[1], rest[2 : 2 + WDEV], rest[-15], rest[-14]
    (win, vkv, kc, vc, qs, gs, s_ref, dp_ref, w_ref, ds_ref, nacc, vacc, sems) = rest[-13:]
    h, j = pl.program_id(0), pl.program_id(1)
    slab, me = place[0], place[1]
    far, near, core = lines.place(me)
    devices = lines.devices
    _, _, chunk, _ = vkeep.shape
    head_dim = kc.shape[1]
    group = q.shape[1] // head_dim
    cand = 1 + nv + ns
    scaling = 1.0 / math.sqrt(head_dim)
    rows = per_device * BLOCK
    block = slab * (per_device * devices) + me * per_device + j
    lanes = pl.ds(pl.multiple_of(h * head_dim, head_dim), head_dim)

    def window_row(d):
        return pl.multiple_of((WDEV - d) * rows, rows)

    @pl.when((h == 0) & (j == 0))
    def _():
        copies = [
            pltpu.make_async_copy(
                recv[n], win.at[:, pl.ds(window_row(d), rows), :], sems.at[n]
            )
            for n, d in enumerate(distances(core))
        ]
        own_rows = pl.ds(WDEV * rows, rows)
        copies.append(pltpu.make_async_copy(keys.at[slab], win.at[0, own_rows, :], sems.at[WDEV]))
        copies.append(
            pltpu.make_async_copy(values.at[slab], win.at[1, own_rows, :], sems.at[WDEV + 1])
        )
        copies += vertical_copies(lines, me, chunk, gathered, vkv, sems, WDEV + 2)
        for copy in copies:
            copy.start()
        nacc[...] = jnp.zeros_like(nacc)
        for copy in copies:
            copy.wait()

    own_at = pl.multiple_of((WDEV * per_device + j) * BLOCK, BLOCK)
    slash_at = [
        pl.multiple_of((WDEV * per_device + j - offs[h, s]) * BLOCK, BLOCK) for s in range(ns)
    ]
    vert_at = pl.multiple_of(h * (nv * BLOCK), nv * BLOCK)
    valid = [None]
    for m in range(nv):
        valid.append(verts[h, m] < block)
    for s in range(ns):
        collide = verts[h, 0] == block - offs[h, s]
        for m in range(1, nv):
            collide = collide | (verts[h, m] == block - offs[h, s])
        valid.append((offs[h, s] > 0) & jnp.logical_not(collide))
    for kv, to in enumerate((kc, vc)):
        to[0:BLOCK, :] = win[kv, pl.ds(own_at, BLOCK), lanes]
        to[BLOCK : (1 + nv) * BLOCK, :] = vkv[kv, pl.ds(vert_at, nv * BLOCK), :]
        for s in range(ns):
            to[(1 + nv + s) * BLOCK : (2 + nv + s) * BLOCK, :] = win[
                kv, pl.ds(slash_at[s], BLOCK), lanes
            ]
    products = []
    for g in range(group):
        cols = slice(g * head_dim, (g + 1) * head_dim)
        qs[g * BLOCK : (g + 1) * BLOCK, :] = q[:, cols]
        gs[g * BLOCK : (g + 1) * BLOCK, :] = grad[:, cols]
        products.append(grad[:, cols].astype(F32) * out[:, cols].astype(F32))
    width = group * BLOCK
    delta = jnp.sum(jnp.transpose(jnp.concatenate(products, axis=0)), axis=0, keepdims=True)

    nt = (((1,), (1,)), ((), ()))
    s_ref[...] = lax.dot_general(kc[...], qs[...], nt, preferred_element_type=F32)
    dp_ref[...] = lax.dot_general(vc[...], gs[...], nt, preferred_element_type=F32)

    log2_scale = scaling * math.log2(math.e)
    neg = jnp.float32(-jnp.inf)
    key_at = lax.broadcasted_iota(jnp.int32, (BLOCK, width), 0)
    row_at = lax.broadcasted_iota(jnp.int32, (BLOCK, width), 1) % BLOCK
    s_ref[0:BLOCK, :] = jnp.where(key_at <= row_at, s_ref[0:BLOCK, :], neg)

    def scaled(c):
        t = s_ref[c * BLOCK : (c + 1) * BLOCK, :] * log2_scale
        if c > 0:
            t = t + jnp.where(valid[c], jnp.float32(0), neg)
        return t

    def fold(x, op):
        y = x[0:8, :]
        for r in range(1, BLOCK // 8):
            y = op(y, x[r * 8 : (r + 1) * 8, :])
        return y

    top = fold(scaled(0), jnp.maximum)
    for c in range(1, cand):
        top = jnp.maximum(top, fold(scaled(c), jnp.maximum))
    top = jnp.max(top, axis=0, keepdims=True)
    total = jnp.zeros((8, width), F32)
    for c in range(cand):
        p = jnp.exp2(scaled(c) - top)
        s_ref[c * BLOCK : (c + 1) * BLOCK, :] = p
        total = total + fold(p, jnp.add)
    inverse = 1.0 / jnp.sum(total, axis=0, keepdims=True)
    for c in range(cand):
        span = slice(c * BLOCK, (c + 1) * BLOCK)
        w = s_ref[span, :] * inverse
        w_ref[span, :] = w.astype(BF16)
        ds_ref[span, :] = (w * (dp_ref[span, :] - delta)).astype(BF16)

    dv = jnp.dot(w_ref[...], gs[...], preferred_element_type=F32)
    dk = jnp.dot(ds_ref[...], qs[...], preferred_element_type=F32) * scaling
    dqt = lax.dot_general(
        kc[...], ds_ref[...], (((0,), (0,)), ((), ())), preferred_element_type=F32
    )
    dqr = (jnp.transpose(dqt) * scaling).astype(BF16)
    for g in range(group):
        dq[:, g * head_dim : (g + 1) * head_dim] = dqr[g * BLOCK : (g + 1) * BLOCK, :]

    for kv, part in enumerate((dk, dv)):
        nacc[kv, pl.ds(own_at, BLOCK), lanes] += part[0:BLOCK]
        for s in range(ns):
            nacc[kv, pl.ds(slash_at[s], BLOCK), lanes] += part[
                (1 + nv + s) * BLOCK : (2 + nv + s) * BLOCK
            ]
        verticals_part = part[BLOCK : (1 + nv) * BLOCK]

        @pl.when(j == 0)
        def _():
            vacc[kv] = verticals_part

        @pl.when(j > 0)
        def _():
            vacc[kv] += verticals_part

    @pl.when(j == per_device - 1)
    def _():
        per_line = heads // 2
        for c in range(nv * BLOCK // chunk):
            line = lax.rem(h // per_line + near, 2)
            slot = (h % per_line) * (nv * BLOCK // chunk) + c
            slot = lax.rem(slot - far + lines.far, lines.far)
            span = slice(c * chunk, (c + 1) * chunk)
            vkeep[line, slot] = vacc[core, span, :]
            vgive[line, slot] = vacc[1 - core, span, :].astype(BF16)
        for kv in range(2):
            home[kv, :, lanes] = nacc[kv, WDEV * rows :, lanes]
            for part, d in zip(near_parts, distances(core)):
                part[kv, :, lanes] = nacc[kv, pl.ds(window_row(d), rows), lanes].astype(part.dtype)


def attend(place, verticals, offsets, queries, cotangent, output, keys, values, gathered, recv, lines):
    rows, width = queries.shape
    features = keys.shape[2]
    heads, nv = verticals.shape
    ns = offsets.shape[1]
    head_dim = features // heads
    group = width // features
    per_device = rows // BLOCK
    cand = 1 + nv + ns
    smem = pl.BlockSpec(memory_space=pltpu.SMEM)
    hbm = pl.BlockSpec(memory_space=pl.ANY)
    tile = pl.BlockSpec((BLOCK, group * head_dim), lambda h, j: (j, h))

    def whole(shape):
        return pl.BlockSpec(shape, lambda h, j: (0,) * len(shape))

    shard = (2, rows, features)
    vert_shape = (2, heads * nv * BLOCK, head_dim)
    share = (2, lines.far, heads * nv * BLOCK // (2 * lines.far), head_dim)
    return pl.pallas_call(
        functools.partial(
            attend_kernel, lines=lines, heads=heads, nv=nv, ns=ns, per_device=per_device
        ),
        grid=(heads, per_device),
        in_specs=[smem] * 3 + [tile] * 3 + [hbm] * (6 + WDEV),
        out_specs=[tile] + [whole(shard)] * (1 + WDEV) + [whole(share)] * 2,
        out_shape=[
            jax.ShapeDtypeStruct((rows, width), BF16),
            jax.ShapeDtypeStruct(shard, F32),
            jax.ShapeDtypeStruct(shard, F32),
            jax.ShapeDtypeStruct(shard, F32),
            jax.ShapeDtypeStruct(shard, BF16),
            jax.ShapeDtypeStruct(shard, BF16),
            jax.ShapeDtypeStruct(shard, BF16),
            jax.ShapeDtypeStruct(share, F32),
            jax.ShapeDtypeStruct(share, BF16),
        ],
        scratch_shapes=[
            pltpu.VMEM((2, (WDEV + 1) * rows, features), BF16),
            pltpu.VMEM(vert_shape, BF16),
            pltpu.VMEM((cand * BLOCK, head_dim), BF16),
            pltpu.VMEM((cand * BLOCK, head_dim), BF16),
            pltpu.VMEM((group * BLOCK, head_dim), BF16),
            pltpu.VMEM((group * BLOCK, head_dim), BF16),
            pltpu.VMEM((cand * BLOCK, group * BLOCK), F32),
            pltpu.VMEM((cand * BLOCK, group * BLOCK), F32),
            pltpu.VMEM((cand * BLOCK, group * BLOCK), BF16),
            pltpu.VMEM((cand * BLOCK, group * BLOCK), BF16),
            pltpu.VMEM((2, (WDEV + 1) * rows, features), F32),
            pltpu.VMEM((2, nv * BLOCK, head_dim), F32),
            pltpu.SemaphoreType.DMA((WDEV + 2 + 4 * lines.far,)),
        ],
        compiler_params=pltpu.CompilerParams(vmem_limit_bytes=VMEM_LIMIT),
    )(
        place, verticals, offsets, queries, cotangent, output, keys, values, *gathered, *recv,
    )


def assemble_kernel(place, verts, home, *rest, lines, heads, nv, per_device):
    arrived, gathered = rest[:3], rest[3:7]
    key_out, value_out, vert, acc, sems = rest[7:]
    slab, me = place[0], place[1]
    devices = lines.devices
    chunk = gathered[0].shape[1]
    copies = vertical_copies(lines, me, chunk, gathered, vert, sems, 0)
    for copy in copies:
        copy.start()
    head_dim = vert.shape[2]
    slab_blocks = per_device * devices
    acc[0] = home[...]
    acc[1] = jnp.zeros_like(home)
    for part, wrapped in zip(arrived, wraps(me, devices)):
        acc[wrapped.astype(jnp.int32)] += part[...].astype(F32)
    key_out[...] = jnp.zeros_like(key_out)
    value_out[...] = jnp.zeros_like(value_out)
    outs = (key_out, value_out)
    for copy in copies:
        copy.wait()
    for h in range(heads):
        lanes = slice(h * head_dim, (h + 1) * head_dim)
        for m in range(nv):
            inner = verts[h, m] % slab_blocks
            region = verts[h, m] // slab_blocks
            row = pl.multiple_of((inner % per_device) * BLOCK, BLOCK)
            at = (h * nv + m) * BLOCK

            @pl.when(inner // per_device == me)
            def _():
                close = (region == slab) | (region == slab - 1)

                @pl.when(close)
                def _():
                    for kv in range(2):
                        acc[slab - region, kv, pl.ds(row, BLOCK), lanes] += vert[
                            kv, at : at + BLOCK, :
                        ].astype(F32)

                @pl.when(jnp.logical_not(close))
                def _():
                    for kv in range(2):
                        outs[kv][region, pl.ds(row, BLOCK), lanes] = vert[kv, at : at + BLOCK, :]

    for kv in range(2):
        outs[kv][slab] = acc[0, kv].astype(BF16)
        outs[kv][slab - 1] = acc[1, kv].astype(BF16)


def assemble(place, verticals, home, arrived, gathered, regions, lines):
    _, rows, features = home.shape
    heads, nv = verticals.shape
    smem = pl.BlockSpec(memory_space=pltpu.SMEM)
    vmem = pl.BlockSpec(memory_space=pltpu.VMEM)
    hbm = pl.BlockSpec(memory_space=pl.ANY)
    return pl.pallas_call(
        functools.partial(
            assemble_kernel, lines=lines, heads=heads, nv=nv, per_device=rows // BLOCK
        ),
        in_specs=[smem] * 2 + [vmem] * 4 + [hbm] * 4,
        out_specs=[vmem] * 2,
        out_shape=[jax.ShapeDtypeStruct((regions, rows, features), BF16)] * 2,
        scratch_shapes=[
            pltpu.VMEM((2, heads * nv * BLOCK, features // heads), BF16),
            pltpu.VMEM((2, 2, rows, features), F32),
            pltpu.SemaphoreType.DMA((4 * lines.far,)),
        ],
        compiler_params=pltpu.CompilerParams(vmem_limit_bytes=VMEM_LIMIT),
    )(place, verticals, home, *arrived, *gathered)


def shards(
    queries,
    context_keys,
    context_values,
    forward_output,
    output_cotangent,
    verticals,
    offsets,
    slab_index,
):
    lines = Lines(lax.axis_size("ctx"))
    me = lax.axis_index("ctx").astype(jnp.int32)
    regions = context_keys.shape[0]
    place = jnp.stack([slab_index[0], me])

    send2, send4, mixed, keep, give = pack(place, verticals, context_keys, context_values, lines)
    recv2 = move(send2, lines.shift_pairs(2))
    recv4 = move(send4, lines.shift_pairs(4))
    recv_mixed = move(mixed, lines.mixed_pairs())
    other2 = move(recv2, lines.core_pairs())
    other4 = move(recv4, lines.core_pairs())
    gathered = gather_verticals(lines, sum_verticals(lines, keep, give, BF16))

    query_grad, home, part2, part4, mixed, give2, give4, vkeep, vgive = attend(
        place, verticals, offsets, queries, output_cotangent, forward_output,
        context_keys, context_values, gathered, [recv2, recv4, recv_mixed, other2, other4], lines,
    )

    sum2 = (part2 + move(give2, lines.core_pairs()).astype(F32)).astype(BF16)
    sum4 = (part4 + move(give4, lines.core_pairs()).astype(F32)).astype(BF16)
    arrived = [
        move(sum2, back(lines.shift_pairs(2))),
        move(sum4, back(lines.shift_pairs(4))),
        move(mixed, back(lines.mixed_pairs())),
    ]
    totals = gather_verticals(lines, sum_verticals(lines, vkeep, vgive, F32))
    key_gradient, value_gradient = assemble(
        place, verticals, home, arrived, totals, regions, lines
    )
    return query_grad, key_gradient, value_gradient


def solution(mesh):
    in_specs = (
        P(("groups", "ctx"), None),
        P("groups", "ctx", None),
        P("groups", "ctx", None),
        P(("groups", "ctx"), None),
        P(("groups", "ctx"), None),
        P("groups", None),
        P("groups", None),
        P("groups"),
    )
    out_specs = (P(("groups", "ctx"), None), P("groups", "ctx", None), P("groups", "ctx", None))
    return jax.shard_map(shards, mesh=mesh, in_specs=in_specs, out_specs=out_specs, check_vma=False)
```

```python
import functools
import math

import jax
import jax.numpy as jnp
from jax import lax
from jax.experimental import pallas as pl
from jax.experimental.pallas import tpu as pltpu
from jax.sharding import PartitionSpec as P

BLOCK = 64
WDEV = 5
VMEM_LIMIT = 60 * 1024 * 1024
BF16 = jnp.bfloat16
F32 = jnp.float32


class Lines:
    def __init__(self, devices):
        self.devices = devices
        self.far = devices // 4

    def place(self, me):
        return lax.div(me, 4), lax.rem(lax.div(me, 2), 2), lax.rem(me, 2)

    def core_pairs(self):
        return [(i, i ^ 1) for i in range(self.devices)]

    def near_pairs(self):
        return [(i, i ^ 2) for i in range(self.devices)]

    def far_pairs(self, by):
        return [(i, (i + 4 * by) % self.devices) for i in range(self.devices)]

    def shift_pairs(self, by):
        return [(i, (i + by) % self.devices) for i in range(self.devices)]

    def mixed_pairs(self):
        return [(i, (i + (5 if i % 2 else 1)) % self.devices) for i in range(self.devices)]


def back(pairs):
    return [(b, a) for a, b in pairs]


def move(array, pairs):
    return lax.ppermute(array, "ctx", pairs)


def gather_verticals(lines, own):
    parts = [own] + [move(own, lines.far_pairs(by)) for by in range(1, lines.far)]
    mine = jnp.stack(parts)
    across = move(mine, lines.near_pairs())
    core_mine = move(mine, lines.core_pairs())
    core_across = move(across, lines.core_pairs())
    return mine, across, core_mine, core_across


def after(array, *others):
    return lax.optimization_barrier((array, *others))[0]


def sum_verticals(lines, keep, give, wide, ahead_of_far, ahead_of_share):
    half = keep.astype(wide) + move(give, lines.core_pairs()).astype(wide)
    quarter = half[0] + move(half[1].astype(BF16), lines.near_pairs()).astype(wide)
    quarter = after(quarter, *ahead_of_far)
    share = quarter[0]
    for by in range(1, lines.far):
        share = share + move(quarter[by].astype(BF16), lines.far_pairs(by)).astype(wide)
    return after(share.astype(BF16), *ahead_of_share)


def wraps(me, devices):
    return [me + 2 >= devices, me + 4 >= devices, (lax.rem(me, 2) == 1) & (me + 5 >= devices)]


def pack_kernel(slab_index, verts, keys, values, *rest, lines, heads, nv, per_device):
    sends = rest[:3]
    keep, give, picked, sems, pick_sems = rest[3:]
    slab, me = slab_index[0], lax.axis_index("ctx")
    far, near, core = lines.place(me)
    _, _, chunk, head_dim = keep.shape
    copies = []
    _, wrapped4, wrapped_mixed = wraps(me, lines.devices)
    for n, region in enumerate(
        (slab, slab - wrapped4.astype(jnp.int32), slab - wrapped_mixed.astype(jnp.int32))
    ):
        for kv, source in enumerate((keys, values)):
            copy = pltpu.make_async_copy(source.at[region], sends[n].at[kv], sems.at[n, kv])
            copy.start()
            copies.append(copy)
    picked[...] = jnp.zeros_like(picked)
    slab_blocks = per_device * lines.devices
    piece = min(BLOCK, chunk)

    def unit_copies(h, m):
        inner = lax.rem(verts[h, m], slab_blocks)
        region = lax.div(verts[h, m], slab_blocks)
        row = lax.rem(inner, per_device) * BLOCK
        for p in range(BLOCK // piece):
            at = (h * nv + m) * BLOCK + p * piece
            line, at = at // (lines.far * chunk), at % (lines.far * chunk)
            slot, at = at // chunk, at % chunk
            line = lax.rem(line + near, 2)
            slot = lax.rem(slot - far + lines.far, lines.far)
            for kv, source in enumerate((keys, values)):
                yield pltpu.make_async_copy(
                    source.at[
                        region,
                        pl.ds(pl.multiple_of(row + p * piece, piece), piece),
                        pl.ds(h * head_dim, head_dim),
                    ],
                    picked.at[lax.rem(kv + core, 2), line, slot, pl.ds(at, piece), :],
                    pick_sems.at[kv, (h * nv + m) * (BLOCK // piece) + p],
                )

    def owned(h, m):
        return lax.div(lax.rem(verts[h, m], slab_blocks), per_device) == me

    for h in range(heads):
        for m in range(nv):

            @pl.when(owned(h, m))
            def _():
                for copy in unit_copies(h, m):
                    copy.start()

    for h in range(heads):
        for m in range(nv):

            @pl.when(owned(h, m))
            def _():
                for copy in unit_copies(h, m):
                    copy.wait()

    keep[...] = picked[0]
    give[...] = picked[1]
    for copy in copies:
        copy.wait()


def pack(slab_index, verticals, keys, values, lines):
    regions, rows, features = keys.shape
    heads, nv = verticals.shape
    head_dim = features // heads
    chunk = heads * nv * BLOCK // (2 * lines.far)
    smem = pl.BlockSpec(memory_space=pltpu.SMEM)
    hbm = pl.BlockSpec(memory_space=pl.ANY)
    share = (2, lines.far, chunk, head_dim)
    return pl.pallas_call(
        functools.partial(pack_kernel, lines=lines, heads=heads, nv=nv, per_device=rows // BLOCK),
        in_specs=[smem, smem, hbm, hbm],
        out_specs=[pl.BlockSpec(memory_space=pltpu.VMEM)] * 5,
        out_shape=[jax.ShapeDtypeStruct((2, rows, features), BF16)] * 3
        + [jax.ShapeDtypeStruct(share, BF16)] * 2,
        scratch_shapes=[
            pltpu.VMEM((2,) + share, BF16),
            pltpu.SemaphoreType.DMA((3, 2)),
            pltpu.SemaphoreType.DMA((2, heads * nv * max(1, BLOCK // chunk))),
        ],
        compiler_params=pltpu.CompilerParams(vmem_limit_bytes=VMEM_LIMIT),
    )(slab_index, verticals, keys, values)


def distances(core):
    return [2, 4, 5 - 4 * core, 1 + 2 * core, 3 + 2 * core]


def vertical_copies(lines, me, chunk, gathered, to, sems, first):
    far, near, core = lines.place(me)
    copies = []
    for n, source in enumerate(gathered):
        kv = core if n < 2 else 1 - core
        line = near if n % 2 == 0 else 1 - near
        for s in range(lines.far):
            slot = lax.rem(far - s + lines.far, lines.far)
            row = pl.multiple_of((line * lines.far + slot) * chunk, chunk)
            copies.append(
                pltpu.make_async_copy(
                    source.at[s], to.at[kv, pl.ds(row, chunk), :], sems.at[first + len(copies)]
                )
            )
    return copies


def attend_kernel(
    slab_index, verts, offs, q, grad, out, keys, values, *rest, lines, heads, nv, ns, per_device,
):
    gathered, recv, rest = rest[:4], rest[4 : 4 + WDEV], rest[4 + WDEV :]
    dq, home, near_parts, vkeep, vgive = rest[0], rest[1], rest[2 : 2 + WDEV], rest[7], rest[8]
    (win, vkv, kc, vc, qs, gs, s_ref, dp_ref, w_ref, ds_ref, nacc, sems) = rest[9:]
    h = pl.program_id(0)
    slab, me = slab_index[0], lax.axis_index("ctx")
    far, near, core = lines.place(me)
    _, _, chunk, head_dim = vkeep.shape
    group = q.shape[1] // head_dim
    cand = 1 + nv + ns
    scaling = 1.0 / math.sqrt(head_dim)
    rows = per_device * BLOCK
    width = group * BLOCK
    first_block = slab * (per_device * lines.devices) + me * per_device
    lanes = pl.ds(pl.multiple_of(h * head_dim, head_dim), head_dim)

    def window_row(d):
        return pl.multiple_of((WDEV - d) * rows, rows)

    @pl.when(h == 0)
    def _():
        own_rows = pl.ds(WDEV * rows, rows)
        copies = [
            pltpu.make_async_copy(
                recv[n], win.at[:, pl.ds(window_row(d), rows), :], sems.at[n]
            )
            for n, d in enumerate(distances(core))
        ]
        copies.append(pltpu.make_async_copy(keys.at[slab], win.at[0, own_rows, :], sems.at[WDEV]))
        copies.append(
            pltpu.make_async_copy(values.at[slab], win.at[1, own_rows, :], sems.at[WDEV + 1])
        )
        copies += vertical_copies(lines, me, chunk, gathered, vkv, sems, WDEV + 2)
        for copy in copies:
            copy.start()
        nacc[...] = jnp.zeros_like(nacc)
        for copy in copies:
            copy.wait()

    vert_rows = pl.ds(pl.multiple_of(h * (nv * BLOCK), nv * BLOCK), nv * BLOCK)
    neg, posinf = jnp.float32(-jnp.inf), jnp.float32(jnp.inf)
    log2_scale = scaling * math.log2(math.e)
    key_at = lax.broadcasted_iota(jnp.int32, (BLOCK, width), 0)
    row_at = lax.broadcasted_iota(jnp.int32, (BLOCK, width), 1) % BLOCK
    nt = (((1,), (1,)), ((), ()))

    def fold(x, op):
        y = x[0:8, :]
        for r in range(1, BLOCK // 8):
            y = op(y, x[r * 8 : (r + 1) * 8, :])
        return y

    vertical_sum = [None, None]
    for j in range(per_device):
        block = first_block + j
        own_at = (WDEV * per_device + j) * BLOCK
        slash_at = [
            pl.multiple_of((WDEV * per_device + j - offs[h, s]) * BLOCK, BLOCK) for s in range(ns)
        ]
        valid = [None]
        for m in range(nv):
            valid.append(verts[h, m] < block)
        for s in range(ns):
            collide = verts[h, 0] == block - offs[h, s]
            for m in range(1, nv):
                collide = collide | (verts[h, m] == block - offs[h, s])
            valid.append((offs[h, s] > 0) & jnp.logical_not(collide))
        for kv, to in enumerate((kc, vc)):
            to[j, 0:BLOCK, :] = win[kv, own_at : own_at + BLOCK, lanes]
            to[j, BLOCK : (1 + nv) * BLOCK, :] = vkv[kv, vert_rows, :]
            for s in range(ns):
                to[j, (1 + nv + s) * BLOCK : (2 + nv + s) * BLOCK, :] = win[
                    kv, pl.ds(slash_at[s], BLOCK), lanes
                ]
        products = []
        block_rows = slice(j * BLOCK, (j + 1) * BLOCK)
        for g in range(group):
            cols = slice(g * head_dim, (g + 1) * head_dim)
            qs[j, g * BLOCK : (g + 1) * BLOCK, :] = q[block_rows, cols]
            gs[j, g * BLOCK : (g + 1) * BLOCK, :] = grad[block_rows, cols]
            products.append(grad[block_rows, cols].astype(F32) * out[block_rows, cols].astype(F32))
        delta = jnp.sum(jnp.transpose(jnp.concatenate(products, axis=0)), axis=0, keepdims=True)

        s_ref[j] = lax.dot_general(kc[j], qs[j], nt, preferred_element_type=F32)
        dp_ref[j] = lax.dot_general(vc[j], gs[j], nt, preferred_element_type=F32)

        own = jnp.where(key_at <= row_at, s_ref[j, 0:BLOCK, :], neg)
        s_ref[j, 0:BLOCK, :] = own
        top = fold(own, jnp.maximum)
        for c in range(1, cand):
            best = fold(s_ref[j, c * BLOCK : (c + 1) * BLOCK, :], jnp.maximum)
            top = jnp.maximum(top, best + jnp.where(valid[c], jnp.float32(0), neg))
        top = jnp.max(top, axis=0, keepdims=True) * log2_scale
        total = jnp.zeros((8, width), F32)
        for c in range(cand):
            span = slice(c * BLOCK, (c + 1) * BLOCK)
            less = top if c == 0 else top + jnp.where(valid[c], jnp.float32(0), posinf)
            p = jnp.exp2(s_ref[j, span, :] * log2_scale - less)
            s_ref[j, span, :] = p
            total = total + fold(p, jnp.add)
        inverse = 1.0 / jnp.sum(total, axis=0, keepdims=True)
        for c in range(cand):
            span = slice(c * BLOCK, (c + 1) * BLOCK)
            w = s_ref[j, span, :] * inverse
            w_ref[j, span, :] = w.astype(BF16)
            ds_ref[j, span, :] = (w * (dp_ref[j, span, :] - delta)).astype(BF16)

        dv = jnp.dot(w_ref[j], gs[j], preferred_element_type=F32)
        dk = jnp.dot(ds_ref[j], qs[j], preferred_element_type=F32) * scaling
        dqt = lax.dot_general(
            kc[j], ds_ref[j], (((0,), (0,)), ((), ())), preferred_element_type=F32
        )
        dqr = (jnp.transpose(dqt) * scaling).astype(BF16)
        for g in range(group):
            dq[block_rows, g * head_dim : (g + 1) * head_dim] = dqr[g * BLOCK : (g + 1) * BLOCK, :]

        for kv, part in enumerate((dk, dv)):
            nacc[kv, own_at : own_at + BLOCK, lanes] += part[0:BLOCK]
            for s in range(ns):
                nacc[kv, pl.ds(slash_at[s], BLOCK), lanes] += part[
                    (1 + nv + s) * BLOCK : (2 + nv + s) * BLOCK
                ]
            of_verticals = part[BLOCK : (1 + nv) * BLOCK]
            vertical_sum[kv] = of_verticals if j == 0 else vertical_sum[kv] + of_verticals

    first = core == 0
    keep = jnp.where(first, vertical_sum[0], vertical_sum[1])
    give = jnp.where(first, vertical_sum[1], vertical_sum[0]).astype(BF16)
    per_line = heads // 2
    for c in range(nv * BLOCK // chunk):
        line = lax.rem(lax.div(h, per_line) + near, 2)
        slot = lax.rem(h, per_line) * (nv * BLOCK // chunk) + c
        slot = lax.rem(slot - far + lines.far, lines.far)
        span = slice(c * chunk, (c + 1) * chunk)
        vkeep[line, slot] = keep[span, :]
        vgive[line, slot] = give[span, :]
    for kv in range(2):
        home[kv, :, lanes] = nacc[kv, WDEV * rows :, lanes]
        for part, d in zip(near_parts, distances(core)):
            part[kv, :, lanes] = nacc[kv, pl.ds(window_row(d), rows), lanes].astype(part.dtype)


def attend(
    slab_index, verticals, offsets, queries, cotangent, output, keys, values, gathered, recv, lines
):
    rows, width = queries.shape
    features = keys.shape[2]
    heads, nv = verticals.shape
    ns = offsets.shape[1]
    head_dim = features // heads
    group = width // features
    per_device = rows // BLOCK
    cand = 1 + nv + ns
    smem = pl.BlockSpec(memory_space=pltpu.SMEM)
    hbm = pl.BlockSpec(memory_space=pl.ANY)
    tile = pl.BlockSpec((rows, group * head_dim), lambda h: (0, h))

    def whole(shape):
        return pl.BlockSpec(shape, lambda h: (0,) * len(shape))

    shard = (2, rows, features)
    vert_shape = (2, heads * nv * BLOCK, head_dim)
    share = (2, lines.far, heads * nv * BLOCK // (2 * lines.far), head_dim)
    return pl.pallas_call(
        functools.partial(
            attend_kernel, lines=lines, heads=heads, nv=nv, ns=ns, per_device=per_device
        ),
        grid=(heads,),
        in_specs=[smem] * 3 + [tile] * 3 + [hbm] * (6 + WDEV),
        out_specs=[tile] + [whole(shard)] * (1 + WDEV) + [whole(share)] * 2,
        out_shape=[
            jax.ShapeDtypeStruct((rows, width), BF16),
            jax.ShapeDtypeStruct(shard, F32),
            jax.ShapeDtypeStruct(shard, F32),
            jax.ShapeDtypeStruct(shard, F32),
            jax.ShapeDtypeStruct(shard, BF16),
            jax.ShapeDtypeStruct(shard, BF16),
            jax.ShapeDtypeStruct(shard, BF16),
            jax.ShapeDtypeStruct(share, F32),
            jax.ShapeDtypeStruct(share, BF16),
        ],
        scratch_shapes=[
            pltpu.VMEM((2, (WDEV + 1) * rows, features), BF16),
            pltpu.VMEM(vert_shape, BF16),
            pltpu.VMEM((per_device, cand * BLOCK, head_dim), BF16),
            pltpu.VMEM((per_device, cand * BLOCK, head_dim), BF16),
            pltpu.VMEM((per_device, group * BLOCK, head_dim), BF16),
            pltpu.VMEM((per_device, group * BLOCK, head_dim), BF16),
            pltpu.VMEM((per_device, cand * BLOCK, group * BLOCK), F32),
            pltpu.VMEM((per_device, cand * BLOCK, group * BLOCK), F32),
            pltpu.VMEM((per_device, cand * BLOCK, group * BLOCK), BF16),
            pltpu.VMEM((per_device, cand * BLOCK, group * BLOCK), BF16),
            pltpu.VMEM((2, (WDEV + 1) * rows, features), F32),
            pltpu.SemaphoreType.DMA((WDEV + 2 + 4 * lines.far,)),
        ],
        compiler_params=pltpu.CompilerParams(vmem_limit_bytes=VMEM_LIMIT),
    )(
        slab_index, verticals, offsets, queries, cotangent, output, keys, values, *gathered, *recv,
    )


def assemble_kernel(slab_index, verts, home, *rest, lines, heads, nv, per_device):
    arrived, gathered = rest[:3], rest[3:7]
    key_out, value_out, vert, acc, sems = rest[7:]
    slab, me = slab_index[0], lax.axis_index("ctx")
    devices = lines.devices
    chunk = gathered[0].shape[1]
    copies = vertical_copies(lines, me, chunk, gathered, vert, sems, 0)
    for copy in copies:
        copy.start()
    head_dim = vert.shape[2]
    slab_blocks = per_device * devices
    acc[0] = home[...]
    acc[1] = jnp.zeros_like(home)
    for part, wrapped in zip(arrived, wraps(me, devices)):
        acc[wrapped.astype(jnp.int32)] += part[...].astype(F32)
    key_out[...] = jnp.zeros_like(key_out)
    value_out[...] = jnp.zeros_like(value_out)
    outs = (key_out, value_out)
    for copy in copies:
        copy.wait()
    for h in range(heads):
        lanes = slice(h * head_dim, (h + 1) * head_dim)
        for m in range(nv):
            inner = lax.rem(verts[h, m], slab_blocks)
            region = lax.div(verts[h, m], slab_blocks)
            row = pl.multiple_of(lax.rem(inner, per_device) * BLOCK, BLOCK)
            at = (h * nv + m) * BLOCK

            @pl.when(lax.div(inner, per_device) == me)
            def _():
                close = (region == slab) | (region == slab - 1)

                @pl.when(close)
                def _():
                    for kv in range(2):
                        acc[slab - region, kv, pl.ds(row, BLOCK), lanes] += vert[
                            kv, at : at + BLOCK, :
                        ].astype(F32)

                @pl.when(jnp.logical_not(close))
                def _():
                    for kv in range(2):
                        outs[kv][region, pl.ds(row, BLOCK), lanes] = vert[kv, at : at + BLOCK, :]

    for kv in range(2):
        outs[kv][slab] = acc[0, kv].astype(BF16)
        outs[kv][slab - 1] = acc[1, kv].astype(BF16)


def assemble(slab_index, verticals, home, arrived, gathered, regions, lines):
    _, rows, features = home.shape
    heads, nv = verticals.shape
    smem = pl.BlockSpec(memory_space=pltpu.SMEM)
    vmem = pl.BlockSpec(memory_space=pltpu.VMEM)
    hbm = pl.BlockSpec(memory_space=pl.ANY)
    return pl.pallas_call(
        functools.partial(
            assemble_kernel, lines=lines, heads=heads, nv=nv, per_device=rows // BLOCK
        ),
        in_specs=[smem] * 2 + [vmem] * 4 + [hbm] * 4,
        out_specs=[vmem] * 2,
        out_shape=[jax.ShapeDtypeStruct((regions, rows, features), BF16)] * 2,
        scratch_shapes=[
            pltpu.VMEM((2, heads * nv * BLOCK, features // heads), BF16),
            pltpu.VMEM((2, 2, rows, features), F32),
            pltpu.SemaphoreType.DMA((4 * lines.far,)),
        ],
        compiler_params=pltpu.CompilerParams(vmem_limit_bytes=VMEM_LIMIT),
    )(slab_index, verticals, home, *arrived, *gathered)


def shards(
    queries,
    context_keys,
    context_values,
    forward_output,
    output_cotangent,
    verticals,
    offsets,
    slab_index,
):
    lines = Lines(lax.axis_size("ctx"))
    regions = context_keys.shape[0]
    _, near, _ = lines.place(lax.axis_index("ctx"))

    own, send4, mixed, keep, give = pack(
        slab_index, verticals, context_keys, context_values, lines
    )
    recv4 = move(send4, lines.shift_pairs(4))
    recv_mixed = move(mixed, lines.mixed_pairs())
    recv2 = move(jnp.where(near == 1, recv4, own), lines.near_pairs())
    other2 = move(recv2, lines.core_pairs())
    other4 = move(recv4, lines.core_pairs())
    share = sum_verticals(lines, keep, give, BF16, (recv4, recv_mixed), ())
    gathered = gather_verticals(lines, share)

    query_grad, home, part2, part4, mixed, give2, give4, vkeep, vgive = attend(
        slab_index, verticals, offsets, queries, output_cotangent, forward_output,
        context_keys, context_values, gathered, [recv2, recv4, recv_mixed, other2, other4], lines,
    )

    sum2 = (part2 + move(give2, lines.core_pairs()).astype(F32)).astype(BF16)
    sum4 = (part4 + move(give4, lines.core_pairs()).astype(F32)).astype(BF16)
    arrived2 = move(sum2, back(lines.shift_pairs(2)))
    arrived4 = move(sum4, back(lines.shift_pairs(4)))
    arrived_mixed = move(mixed, back(lines.mixed_pairs()))
    share = sum_verticals(lines, vkeep, vgive, F32, (arrived4, arrived_mixed), (arrived2,))
    totals = gather_verticals(lines, share)
    key_gradient, value_gradient = assemble(
        slab_index, verticals, home, (arrived2, arrived4, arrived_mixed), totals, regions, lines
    )
    return query_grad, key_gradient, value_gradient


def solution(mesh):
    in_specs = (
        P(("groups", "ctx"), None),
        P("groups", "ctx", None),
        P("groups", "ctx", None),
        P(("groups", "ctx"), None),
        P(("groups", "ctx"), None),
        P("groups", None),
        P("groups", None),
        P("groups"),
    )
    out_specs = (P(("groups", "ctx"), None), P("groups", "ctx", None), P("groups", "ctx", None))
    return jax.shard_map(shards, mesh=mesh, in_specs=in_specs, out_specs=out_specs, check_vma=False)
```

```python
import functools
import math

import jax
import jax.numpy as jnp
from jax import lax
from jax.experimental import pallas as pl
from jax.experimental.pallas import tpu as pltpu
from jax.sharding import PartitionSpec as P

BLOCK = 64
WDEV = 5
VMEM_LIMIT = 60 * 1024 * 1024
BF16 = jnp.bfloat16
F32 = jnp.float32


class Lines:
    def __init__(self, devices):
        self.devices = devices
        self.far = devices // 4

    def place(self, me):
        return lax.div(me, 4), lax.rem(lax.div(me, 2), 2), lax.rem(me, 2)

    def core_pairs(self):
        return [(i, i ^ 1) for i in range(self.devices)]

    def near_pairs(self):
        return [(i, i ^ 2) for i in range(self.devices)]

    def both_pairs(self):
        return [(i, i ^ 3) for i in range(self.devices)]

    def far_pairs(self, by):
        return [(i, (i + 4 * by) % self.devices) for i in range(self.devices)]

    def shift_pairs(self, by):
        return [(i, (i + by) % self.devices) for i in range(self.devices)]

    def mixed_pairs(self):
        return [(i, (i + (5 if i % 2 else 1)) % self.devices) for i in range(self.devices)]


def back(pairs):
    return [(b, a) for a, b in pairs]


def move(array, pairs):
    return lax.ppermute(array, "ctx", pairs)


def gather_verticals(lines, own):
    parts = [own] + [move(own, lines.far_pairs(by)) for by in range(1, lines.far)]
    mine = jnp.stack(parts)
    across = move(mine, lines.near_pairs())
    core_mine = move(mine, lines.core_pairs())
    core_across = move(across, lines.core_pairs())
    return mine, across, core_mine, core_across


def after(array, *others):
    return lax.optimization_barrier((array, *others))[0]


def sum_verticals(lines, mine, to_core, to_near, to_both, ahead_of_far, ahead_of_share):
    quarter = (
        mine.astype(F32)
        + move(to_core, lines.core_pairs()).astype(F32)
        + move(to_near, lines.near_pairs()).astype(F32)
        + move(to_both, lines.both_pairs()).astype(F32)
    )
    quarter = after(quarter, *ahead_of_far)
    share = quarter[0]
    for by in range(1, lines.far):
        share = share + move(quarter[by].astype(BF16), lines.far_pairs(by)).astype(F32)
    return after(share.astype(BF16), *ahead_of_share)


def wraps(me, devices):
    return [me + 2 >= devices, me + 4 >= devices, (lax.rem(me, 2) == 1) & (me + 5 >= devices)]


def pack_kernel(slab_index, verts, keys, values, *rest, lines, heads, nv, per_device):
    sends = rest[:3]
    shares = rest[3:7]
    picked, sems, pick_sems = rest[7:]
    slab, me = slab_index[0], lax.axis_index("ctx")
    far, near, core = lines.place(me)
    _, chunk, head_dim = shares[0].shape
    copies = []
    _, wrapped4, wrapped_mixed = wraps(me, lines.devices)
    for n, region in enumerate(
        (slab, slab - wrapped4.astype(jnp.int32), slab - wrapped_mixed.astype(jnp.int32))
    ):
        for kv, source in enumerate((keys, values)):
            copy = pltpu.make_async_copy(source.at[region], sends[n].at[kv], sems.at[n, kv])
            copy.start()
            copies.append(copy)
    picked[...] = jnp.zeros_like(picked)
    slab_blocks = per_device * lines.devices
    piece = min(BLOCK, chunk)

    def unit_copies(h, m):
        inner = lax.rem(verts[h, m], slab_blocks)
        region = lax.div(verts[h, m], slab_blocks)
        row = lax.rem(inner, per_device) * BLOCK
        for p in range(BLOCK // piece):
            at = (h * nv + m) * BLOCK + p * piece
            line, at = at // (lines.far * chunk), at % (lines.far * chunk)
            slot, at = at // chunk, at % chunk
            line = lax.rem(line + near, 2)
            slot = lax.rem(slot - far + lines.far, lines.far)
            for kv, source in enumerate((keys, values)):
                yield pltpu.make_async_copy(
                    source.at[
                        region,
                        pl.ds(pl.multiple_of(row + p * piece, piece), piece),
                        pl.ds(h * head_dim, head_dim),
                    ],
                    picked.at[lax.rem(kv + core, 2), line, slot, pl.ds(at, piece), :],
                    pick_sems.at[kv, (h * nv + m) * (BLOCK // piece) + p],
                )

    def owned(h, m):
        return lax.div(lax.rem(verts[h, m], slab_blocks), per_device) == me

    for h in range(heads):
        for m in range(nv):

            @pl.when(owned(h, m))
            def _():
                for copy in unit_copies(h, m):
                    copy.start()

    for h in range(heads):
        for m in range(nv):

            @pl.when(owned(h, m))
            def _():
                for copy in unit_copies(h, m):
                    copy.wait()

    for n, share in enumerate(shares):
        share[...] = picked[n // 2, n % 2]
    for copy in copies:
        copy.wait()


def pack(slab_index, verticals, keys, values, lines):
    regions, rows, features = keys.shape
    heads, nv = verticals.shape
    head_dim = features // heads
    chunk = heads * nv * BLOCK // (2 * lines.far)
    smem = pl.BlockSpec(memory_space=pltpu.SMEM)
    hbm = pl.BlockSpec(memory_space=pl.ANY)
    share = (lines.far, chunk, head_dim)
    return pl.pallas_call(
        functools.partial(pack_kernel, lines=lines, heads=heads, nv=nv, per_device=rows // BLOCK),
        in_specs=[smem, smem, hbm, hbm],
        out_specs=[pl.BlockSpec(memory_space=pltpu.VMEM)] * 7,
        out_shape=[jax.ShapeDtypeStruct((2, rows, features), BF16)] * 3
        + [jax.ShapeDtypeStruct(share, BF16)] * 4,
        scratch_shapes=[
            pltpu.VMEM((2, 2) + share, BF16),
            pltpu.SemaphoreType.DMA((3, 2)),
            pltpu.SemaphoreType.DMA((2, heads * nv * max(1, BLOCK // chunk))),
        ],
        compiler_params=pltpu.CompilerParams(vmem_limit_bytes=VMEM_LIMIT),
    )(slab_index, verticals, keys, values)


def distances(core):
    return [2, 4, 5 - 4 * core, 1 + 2 * core, 3 + 2 * core]


def vertical_copies(lines, me, chunk, gathered, to, sems, first):
    far, near, core = lines.place(me)
    copies = []
    for n, source in enumerate(gathered):
        kv = core if n < 2 else 1 - core
        line = near if n % 2 == 0 else 1 - near
        for s in range(lines.far):
            slot = lax.rem(far - s + lines.far, lines.far)
            row = pl.multiple_of((line * lines.far + slot) * chunk, chunk)
            copies.append(
                pltpu.make_async_copy(
                    source.at[s], to.at[kv, pl.ds(row, chunk), :], sems.at[first + len(copies)]
                )
            )
    return copies


def attend_kernel(
    slab_index, verts, offs, q, grad, out, keys, values, *rest, lines, heads, nv, ns, per_device,
):
    gathered, recv, rest = rest[:4], rest[4 : 4 + WDEV], rest[4 + WDEV :]
    dq, home, near_parts, shares = rest[0], rest[1], rest[2 : 2 + WDEV], rest[7:11]
    (win, vkv, kc, vc, qs, gs, s_ref, dp_ref, w_ref, ds_ref, nacc, sems) = rest[11:]
    h = pl.program_id(0)
    slab, me = slab_index[0], lax.axis_index("ctx")
    far, near, core = lines.place(me)
    _, chunk, head_dim = shares[0].shape
    group = q.shape[1] // head_dim
    cand = 1 + nv + ns
    scaling = 1.0 / math.sqrt(head_dim)
    rows = per_device * BLOCK
    width = group * BLOCK
    first_block = slab * (per_device * lines.devices) + me * per_device
    lanes = pl.ds(pl.multiple_of(h * head_dim, head_dim), head_dim)

    def window_row(d):
        return pl.multiple_of((WDEV - d) * rows, rows)

    @pl.when(h == 0)
    def _():
        own_rows = pl.ds(WDEV * rows, rows)
        copies = [
            pltpu.make_async_copy(
                recv[n], win.at[:, pl.ds(window_row(d), rows), :], sems.at[n]
            )
            for n, d in enumerate(distances(core))
        ]
        copies.append(pltpu.make_async_copy(keys.at[slab], win.at[0, own_rows, :], sems.at[WDEV]))
        copies.append(
            pltpu.make_async_copy(values.at[slab], win.at[1, own_rows, :], sems.at[WDEV + 1])
        )
        copies += vertical_copies(lines, me, chunk, gathered, vkv, sems, WDEV + 2)
        for copy in copies:
            copy.start()
        nacc[...] = jnp.zeros_like(nacc)
        for copy in copies:
            copy.wait()

    vert_rows = pl.ds(pl.multiple_of(h * (nv * BLOCK), nv * BLOCK), nv * BLOCK)
    neg, posinf = jnp.float32(-jnp.inf), jnp.float32(jnp.inf)
    log2_scale = scaling * math.log2(math.e)
    key_at = lax.broadcasted_iota(jnp.int32, (BLOCK, width), 0)
    row_at = lax.broadcasted_iota(jnp.int32, (BLOCK, width), 1) % BLOCK
    nt = (((1,), (1,)), ((), ()))

    def fold(x, op):
        y = x[0:8, :]
        for r in range(1, BLOCK // 8):
            y = op(y, x[r * 8 : (r + 1) * 8, :])
        return y

    vertical_sum = [None, None]
    for j in range(per_device):
        block = first_block + j
        own_at = (WDEV * per_device + j) * BLOCK
        slash_at = [
            pl.multiple_of((WDEV * per_device + j - offs[h, s]) * BLOCK, BLOCK) for s in range(ns)
        ]
        valid = [None]
        for m in range(nv):
            valid.append(verts[h, m] < block)
        for s in range(ns):
            collide = verts[h, 0] == block - offs[h, s]
            for m in range(1, nv):
                collide = collide | (verts[h, m] == block - offs[h, s])
            valid.append((offs[h, s] > 0) & jnp.logical_not(collide))
        for kv, to in enumerate((kc, vc)):
            to[j, 0:BLOCK, :] = win[kv, own_at : own_at + BLOCK, lanes]
            to[j, BLOCK : (1 + nv) * BLOCK, :] = vkv[kv, vert_rows, :]
            for s in range(ns):
                to[j, (1 + nv + s) * BLOCK : (2 + nv + s) * BLOCK, :] = win[
                    kv, pl.ds(slash_at[s], BLOCK), lanes
                ]
        products = []
        block_rows = slice(j * BLOCK, (j + 1) * BLOCK)
        for g in range(group):
            cols = slice(g * head_dim, (g + 1) * head_dim)
            qs[j, g * BLOCK : (g + 1) * BLOCK, :] = q[block_rows, cols]
            gs[j, g * BLOCK : (g + 1) * BLOCK, :] = grad[block_rows, cols]
            products.append(grad[block_rows, cols].astype(F32) * out[block_rows, cols].astype(F32))
        delta = jnp.sum(jnp.transpose(jnp.concatenate(products, axis=0)), axis=0, keepdims=True)

        s_ref[j] = lax.dot_general(kc[j], qs[j], nt, preferred_element_type=F32)
        dp_ref[j] = lax.dot_general(vc[j], gs[j], nt, preferred_element_type=F32)

        own = jnp.where(key_at <= row_at, s_ref[j, 0:BLOCK, :], neg)
        s_ref[j, 0:BLOCK, :] = own
        top = fold(own, jnp.maximum)
        for c in range(1, cand):
            best = fold(s_ref[j, c * BLOCK : (c + 1) * BLOCK, :], jnp.maximum)
            top = jnp.maximum(top, best + jnp.where(valid[c], jnp.float32(0), neg))
        top = jnp.max(top, axis=0, keepdims=True) * log2_scale
        total = jnp.zeros((8, width), F32)
        for c in range(cand):
            span = slice(c * BLOCK, (c + 1) * BLOCK)
            less = top if c == 0 else top + jnp.where(valid[c], jnp.float32(0), posinf)
            p = jnp.exp2(s_ref[j, span, :] * log2_scale - less)
            s_ref[j, span, :] = p
            total = total + fold(p, jnp.add)
        inverse = 1.0 / jnp.sum(total, axis=0, keepdims=True)
        for c in range(cand):
            span = slice(c * BLOCK, (c + 1) * BLOCK)
            w = s_ref[j, span, :] * inverse
            w_ref[j, span, :] = w.astype(BF16)
            ds_ref[j, span, :] = (w * (dp_ref[j, span, :] - delta)).astype(BF16)

        dv = jnp.dot(w_ref[j], gs[j], preferred_element_type=F32)
        dk = jnp.dot(ds_ref[j], qs[j], preferred_element_type=F32) * scaling
        dqt = lax.dot_general(
            kc[j], ds_ref[j], (((0,), (0,)), ((), ())), preferred_element_type=F32
        )
        dqr = (jnp.transpose(dqt) * scaling).astype(BF16)
        for g in range(group):
            dq[block_rows, g * head_dim : (g + 1) * head_dim] = dqr[g * BLOCK : (g + 1) * BLOCK, :]

        for kv, part in enumerate((dk, dv)):
            nacc[kv, own_at : own_at + BLOCK, lanes] += part[0:BLOCK]
            for s in range(ns):
                nacc[kv, pl.ds(slash_at[s], BLOCK), lanes] += part[
                    (1 + nv + s) * BLOCK : (2 + nv + s) * BLOCK
                ]
            of_verticals = part[BLOCK : (1 + nv) * BLOCK]
            vertical_sum[kv] = of_verticals if j == 0 else vertical_sum[kv] + of_verticals

    first = core == 0
    keep = jnp.where(first, vertical_sum[0], vertical_sum[1])
    give = jnp.where(first, vertical_sum[1], vertical_sum[0])
    per_line = heads // 2
    for line in range(2):

        @pl.when(lax.rem(lax.div(h, per_line) + near, 2) == line)
        def _():
            for c in range(nv * BLOCK // chunk):
                slot = lax.rem(h, per_line) * (nv * BLOCK // chunk) + c
                slot = lax.rem(slot - far + lines.far, lines.far)
                span = slice(c * chunk, (c + 1) * chunk)
                shares[line][slot] = keep[span, :].astype(shares[line].dtype)
                shares[2 + line][slot] = give[span, :].astype(BF16)

    for kv in range(2):
        home[kv, :, lanes] = nacc[kv, WDEV * rows :, lanes]
        for part, d in zip(near_parts, distances(core)):
            part[kv, :, lanes] = nacc[kv, pl.ds(window_row(d), rows), lanes].astype(part.dtype)


def attend(
    slab_index, verticals, offsets, queries, cotangent, output, keys, values, gathered, recv, lines
):
    rows, width = queries.shape
    features = keys.shape[2]
    heads, nv = verticals.shape
    ns = offsets.shape[1]
    head_dim = features // heads
    group = width // features
    per_device = rows // BLOCK
    cand = 1 + nv + ns
    smem = pl.BlockSpec(memory_space=pltpu.SMEM)
    hbm = pl.BlockSpec(memory_space=pl.ANY)
    tile = pl.BlockSpec((rows, group * head_dim), lambda h: (0, h))

    def whole(shape):
        return pl.BlockSpec(shape, lambda h: (0,) * len(shape))

    shard = (2, rows, features)
    vert_shape = (2, heads * nv * BLOCK, head_dim)
    share = (lines.far, heads * nv * BLOCK // (2 * lines.far), head_dim)
    return pl.pallas_call(
        functools.partial(
            attend_kernel, lines=lines, heads=heads, nv=nv, ns=ns, per_device=per_device
        ),
        grid=(heads,),
        in_specs=[smem] * 3 + [tile] * 3 + [hbm] * (6 + WDEV),
        out_specs=[tile] + [whole(shard)] * (1 + WDEV) + [whole(share)] * 4,
        out_shape=[
            jax.ShapeDtypeStruct((rows, width), BF16),
            jax.ShapeDtypeStruct(shard, F32),
            jax.ShapeDtypeStruct(shard, F32),
            jax.ShapeDtypeStruct(shard, F32),
            jax.ShapeDtypeStruct(shard, BF16),
            jax.ShapeDtypeStruct(shard, BF16),
            jax.ShapeDtypeStruct(shard, BF16),
            jax.ShapeDtypeStruct(share, F32),
            jax.ShapeDtypeStruct(share, BF16),
            jax.ShapeDtypeStruct(share, BF16),
            jax.ShapeDtypeStruct(share, BF16),
        ],
        scratch_shapes=[
            pltpu.VMEM((2, (WDEV + 1) * rows, features), BF16),
            pltpu.VMEM(vert_shape, BF16),
            pltpu.VMEM((per_device, cand * BLOCK, head_dim), BF16),
            pltpu.VMEM((per_device, cand * BLOCK, head_dim), BF16),
            pltpu.VMEM((per_device, group * BLOCK, head_dim), BF16),
            pltpu.VMEM((per_device, group * BLOCK, head_dim), BF16),
            pltpu.VMEM((per_device, cand * BLOCK, group * BLOCK), F32),
            pltpu.VMEM((per_device, cand * BLOCK, group * BLOCK), F32),
            pltpu.VMEM((per_device, cand * BLOCK, group * BLOCK), BF16),
            pltpu.VMEM((per_device, cand * BLOCK, group * BLOCK), BF16),
            pltpu.VMEM((2, (WDEV + 1) * rows, features), F32),
            pltpu.SemaphoreType.DMA((WDEV + 2 + 4 * lines.far,)),
        ],
        compiler_params=pltpu.CompilerParams(vmem_limit_bytes=VMEM_LIMIT),
    )(
        slab_index, verticals, offsets, queries, cotangent, output, keys, values, *gathered, *recv,
    )


def assemble_kernel(slab_index, verts, home, *rest, lines, heads, nv, per_device):
    arrived, gathered = rest[:3], rest[3:7]
    key_out, value_out, vert, acc, sems = rest[7:]
    slab, me = slab_index[0], lax.axis_index("ctx")
    devices = lines.devices
    chunk = gathered[0].shape[1]
    copies = vertical_copies(lines, me, chunk, gathered, vert, sems, 0)
    for copy in copies:
        copy.start()
    head_dim = vert.shape[2]
    slab_blocks = per_device * devices
    acc[0] = home[...]
    acc[1] = jnp.zeros_like(home)
    for part, wrapped in zip(arrived, wraps(me, devices)):
        acc[wrapped.astype(jnp.int32)] += part[...].astype(F32)
    key_out[...] = jnp.zeros_like(key_out)
    value_out[...] = jnp.zeros_like(value_out)
    outs = (key_out, value_out)
    for copy in copies:
        copy.wait()
    for h in range(heads):
        lanes = slice(h * head_dim, (h + 1) * head_dim)
        for m in range(nv):
            inner = lax.rem(verts[h, m], slab_blocks)
            region = lax.div(verts[h, m], slab_blocks)
            row = pl.multiple_of(lax.rem(inner, per_device) * BLOCK, BLOCK)
            at = (h * nv + m) * BLOCK

            @pl.when(lax.div(inner, per_device) == me)
            def _():
                close = (region == slab) | (region == slab - 1)

                @pl.when(close)
                def _():
                    for kv in range(2):
                        acc[slab - region, kv, pl.ds(row, BLOCK), lanes] += vert[
                            kv, at : at + BLOCK, :
                        ].astype(F32)

                @pl.when(jnp.logical_not(close))
                def _():
                    for kv in range(2):
                        outs[kv][region, pl.ds(row, BLOCK), lanes] = vert[kv, at : at + BLOCK, :]

    for kv in range(2):
        outs[kv][slab] = acc[0, kv].astype(BF16)
        outs[kv][slab - 1] = acc[1, kv].astype(BF16)


def assemble(slab_index, verticals, home, arrived, gathered, regions, lines):
    _, rows, features = home.shape
    heads, nv = verticals.shape
    smem = pl.BlockSpec(memory_space=pltpu.SMEM)
    vmem = pl.BlockSpec(memory_space=pltpu.VMEM)
    hbm = pl.BlockSpec(memory_space=pl.ANY)
    return pl.pallas_call(
        functools.partial(
            assemble_kernel, lines=lines, heads=heads, nv=nv, per_device=rows // BLOCK
        ),
        in_specs=[smem] * 2 + [vmem] * 4 + [hbm] * 4,
        out_specs=[vmem] * 2,
        out_shape=[jax.ShapeDtypeStruct((regions, rows, features), BF16)] * 2,
        scratch_shapes=[
            pltpu.VMEM((2, heads * nv * BLOCK, features // heads), BF16),
            pltpu.VMEM((2, 2, rows, features), F32),
            pltpu.SemaphoreType.DMA((4 * lines.far,)),
        ],
        compiler_params=pltpu.CompilerParams(vmem_limit_bytes=VMEM_LIMIT),
    )(slab_index, verticals, home, *arrived, *gathered)


def shards(
    queries,
    context_keys,
    context_values,
    forward_output,
    output_cotangent,
    verticals,
    offsets,
    slab_index,
):
    lines = Lines(lax.axis_size("ctx"))
    regions = context_keys.shape[0]
    _, near, _ = lines.place(lax.axis_index("ctx"))

    own, send4, mixed, mine, to_near, to_core, to_both = pack(
        slab_index, verticals, context_keys, context_values, lines
    )
    recv4 = move(send4, lines.shift_pairs(4))
    recv_mixed = move(mixed, lines.mixed_pairs())
    recv2 = move(jnp.where(near == 1, recv4, own), lines.near_pairs())
    other2 = move(recv2, lines.core_pairs())
    other4 = move(recv4, lines.core_pairs())
    share = sum_verticals(
        lines, mine, to_core, to_near, to_both, (recv4, recv_mixed), ()
    )
    gathered = gather_verticals(lines, share)

    query_grad, home, part2, part4, mixed, give2, give4, *shares = attend(
        slab_index, verticals, offsets, queries, output_cotangent, forward_output,
        context_keys, context_values, gathered, [recv2, recv4, recv_mixed, other2, other4], lines,
    )

    sum2 = (part2 + move(give2, lines.core_pairs()).astype(F32)).astype(BF16)
    sum4 = (part4 + move(give4, lines.core_pairs()).astype(F32)).astype(BF16)
    arrived2 = move(sum2, back(lines.shift_pairs(2)))
    arrived4 = move(sum4, back(lines.shift_pairs(4)))
    arrived_mixed = move(mixed, back(lines.mixed_pairs()))
    mine, to_near, to_core, to_both = shares
    share = sum_verticals(
        lines, mine, to_core, to_near, to_both, (arrived4, arrived_mixed), (arrived2,)
    )
    totals = gather_verticals(lines, share)
    key_gradient, value_gradient = assemble(
        slab_index, verticals, home, (arrived2, arrived4, arrived_mixed), totals, regions, lines
    )
    return query_grad, key_gradient, value_gradient


def solution(mesh):
    in_specs = (
        P(("groups", "ctx"), None),
        P("groups", "ctx", None),
        P("groups", "ctx", None),
        P(("groups", "ctx"), None),
        P(("groups", "ctx"), None),
        P("groups", None),
        P("groups", None),
        P("groups"),
    )
    out_specs = (P(("groups", "ctx"), None), P("groups", "ctx", None), P("groups", "ctx", None))
    return jax.shard_map(shards, mesh=mesh, in_specs=in_specs, out_specs=out_specs, check_vma=False)
```

```python
import functools
import math

import jax
import jax.numpy as jnp
from jax import lax
from jax.experimental import pallas as pl
from jax.experimental.pallas import tpu as pltpu
from jax.sharding import PartitionSpec as P

BLOCK = 64
WDEV = 5
VMEM_LIMIT = 60 * 1024 * 1024
BF16 = jnp.bfloat16
F32 = jnp.float32


class Lines:
    def __init__(self, devices):
        self.devices = devices
        self.far = devices // 4

    def place(self, me):
        return lax.div(me, 4), lax.rem(lax.div(me, 2), 2), lax.rem(me, 2)

    def core_pairs(self):
        return [(i, i ^ 1) for i in range(self.devices)]

    def near_pairs(self):
        return [(i, i ^ 2) for i in range(self.devices)]

    def both_pairs(self):
        return [(i, i ^ 3) for i in range(self.devices)]

    def far_pairs(self, by):
        return [(i, (i + 4 * by) % self.devices) for i in range(self.devices)]

    def shift_pairs(self, by):
        return [(i, (i + by) % self.devices) for i in range(self.devices)]

    def mixed_pairs(self):
        return [(i, (i + (5 if i % 2 else 1)) % self.devices) for i in range(self.devices)]


def back(pairs):
    return [(b, a) for a, b in pairs]


def move(array, pairs):
    return lax.ppermute(array, "ctx", pairs)


def after(array, *others):
    return lax.optimization_barrier((array, *others))[0]


def plane_sum(lines, mine, to_near, to_core, to_both):
    to_near = (to_near.astype(F32) + move(to_both, lines.core_pairs()).astype(F32)).astype(BF16)
    from_near = move(to_near, lines.near_pairs())
    from_core = move(to_core, lines.core_pairs())
    return mine.astype(F32) + from_core.astype(F32) + from_near.astype(F32)


def far_sum(lines, quarter):
    share = quarter[0]
    for by in range(1, lines.far):
        share = share + move(quarter[by].astype(BF16), lines.far_pairs(by)).astype(F32)
    share = share.astype(BF16)
    parts = [share] + [move(share, lines.far_pairs(by)) for by in range(1, lines.far)]
    return jnp.stack(parts)


def plane_gather(lines, mine):
    across = move(mine, lines.near_pairs())
    core_mine = move(mine, lines.core_pairs())
    core_across = move(across, lines.core_pairs())
    return mine, across, core_mine, core_across


def wraps(me, devices):
    return [me + 4 >= devices, (lax.rem(me, 2) == 1) & (me + 5 >= devices)]


def pack_kernel(slab_index, verts, keys, values, *rest, lines, heads, nv, per_device):
    sends = rest[:3]
    shares = rest[3:7]
    picked, sems, pick_sems = rest[7:]
    slab, me = slab_index[0], lax.axis_index("ctx")
    far, near, core = lines.place(me)
    _, chunk, head_dim = shares[0].shape
    copies = []
    wrapped4, wrapped_mixed = wraps(me, lines.devices)
    for n, region in enumerate(
        (slab, slab - wrapped4.astype(jnp.int32), slab - wrapped_mixed.astype(jnp.int32))
    ):
        for kv, source in enumerate((keys, values)):
            copy = pltpu.make_async_copy(source.at[region], sends[n].at[kv], sems.at[n, kv])
            copy.start()
            copies.append(copy)
    picked[...] = jnp.zeros_like(picked)
    slab_blocks = per_device * lines.devices
    piece = min(BLOCK, chunk)

    def unit_copies(h, m):
        inner = lax.rem(verts[h, m], slab_blocks)
        region = lax.div(verts[h, m], slab_blocks)
        row = lax.rem(inner, per_device) * BLOCK
        for p in range(BLOCK // piece):
            at = (h * nv + m) * BLOCK + p * piece
            line, at = at // (lines.far * chunk), at % (lines.far * chunk)
            slot, at = at // chunk, at % chunk
            line = lax.rem(line + near, 2)
            slot = lax.rem(slot - far + lines.far, lines.far)
            for kv, source in enumerate((keys, values)):
                yield pltpu.make_async_copy(
                    source.at[
                        region,
                        pl.ds(pl.multiple_of(row + p * piece, piece), piece),
                        pl.ds(h * head_dim, head_dim),
                    ],
                    picked.at[lax.rem(kv + core, 2), line, slot, pl.ds(at, piece), :],
                    pick_sems.at[kv, (h * nv + m) * (BLOCK // piece) + p],
                )

    def owned(h, m):
        return lax.div(lax.rem(verts[h, m], slab_blocks), per_device) == me

    for h in range(heads):
        for m in range(nv):

            @pl.when(owned(h, m))
            def _():
                for copy in unit_copies(h, m):
                    copy.start()

    for h in range(heads):
        for m in range(nv):

            @pl.when(owned(h, m))
            def _():
                for copy in unit_copies(h, m):
                    copy.wait()

    for n, share in enumerate(shares):
        share[...] = picked[n // 2, n % 2]
    for copy in copies:
        copy.wait()


def pack(slab_index, verticals, keys, values, lines):
    regions, rows, features = keys.shape
    heads, nv = verticals.shape
    head_dim = features // heads
    chunk = heads * nv * BLOCK // (2 * lines.far)
    smem = pl.BlockSpec(memory_space=pltpu.SMEM)
    hbm = pl.BlockSpec(memory_space=pl.ANY)
    share = (lines.far, chunk, head_dim)
    return pl.pallas_call(
        functools.partial(pack_kernel, lines=lines, heads=heads, nv=nv, per_device=rows // BLOCK),
        in_specs=[smem, smem, hbm, hbm],
        out_specs=[pl.BlockSpec(memory_space=pltpu.VMEM)] * 7,
        out_shape=[jax.ShapeDtypeStruct((2, rows, features), BF16)] * 3
        + [jax.ShapeDtypeStruct(share, BF16)] * 4,
        scratch_shapes=[
            pltpu.VMEM((2, 2) + share, BF16),
            pltpu.SemaphoreType.DMA((3, 2)),
            pltpu.SemaphoreType.DMA((2, heads * nv * max(1, BLOCK // chunk))),
        ],
        compiler_params=pltpu.CompilerParams(vmem_limit_bytes=VMEM_LIMIT),
    )(slab_index, verticals, keys, values)


def distances(core):
    return [2, 4, 5 - 4 * core, 1 + 2 * core, 3 + 2 * core]


def vertical_copies(lines, me, chunk, gathered, to, sems, first):
    far, near, core = lines.place(me)
    copies = []
    for n, source in enumerate(gathered):
        kv = core if n < 2 else 1 - core
        line = near if n % 2 == 0 else 1 - near
        for s in range(lines.far):
            slot = lax.rem(far - s + lines.far, lines.far)
            row = pl.multiple_of((line * lines.far + slot) * chunk, chunk)
            copies.append(
                pltpu.make_async_copy(
                    source.at[s], to.at[kv, pl.ds(row, chunk), :], sems.at[first + len(copies)]
                )
            )
    return copies


def attend_kernel(
    slab_index, verts, offs, q, grad, out, keys, values, *rest, lines, heads, nv, ns, per_device,
):
    gathered, recv, rest = rest[:4], rest[4 : 4 + WDEV], rest[4 + WDEV :]
    dq, home, near_parts, shares = rest[0], rest[1], rest[2 : 2 + WDEV], rest[7:11]
    (win, vkv, kc, vc, qs, gs, s_ref, dp_ref, w_ref, ds_ref, nacc, sems) = rest[11:]
    h = pl.program_id(0)
    slab, me = slab_index[0], lax.axis_index("ctx")
    far, near, core = lines.place(me)
    _, chunk, head_dim = shares[0].shape
    group = q.shape[1] // head_dim
    cand = 1 + nv + ns
    scaling = 1.0 / math.sqrt(head_dim)
    rows = per_device * BLOCK
    width = group * BLOCK
    first_block = slab * (per_device * lines.devices) + me * per_device
    lanes = pl.ds(pl.multiple_of(h * head_dim, head_dim), head_dim)

    def window_row(d):
        return pl.multiple_of((WDEV - d) * rows, rows)

    @pl.when(h == 0)
    def _():
        own_rows = pl.ds(WDEV * rows, rows)
        copies = [
            pltpu.make_async_copy(
                recv[n], win.at[:, pl.ds(window_row(d), rows), :], sems.at[n]
            )
            for n, d in enumerate(distances(core))
        ]
        copies.append(pltpu.make_async_copy(keys.at[slab], win.at[0, own_rows, :], sems.at[WDEV]))
        copies.append(
            pltpu.make_async_copy(values.at[slab], win.at[1, own_rows, :], sems.at[WDEV + 1])
        )
        copies += vertical_copies(lines, me, chunk, gathered, vkv, sems, WDEV + 2)
        for copy in copies:
            copy.start()
        nacc[...] = jnp.zeros_like(nacc)
        for copy in copies:
            copy.wait()

    vert_rows = pl.ds(pl.multiple_of(h * (nv * BLOCK), nv * BLOCK), nv * BLOCK)
    neg, posinf = jnp.float32(-jnp.inf), jnp.float32(jnp.inf)
    log2_scale = scaling * math.log2(math.e)
    key_at = lax.broadcasted_iota(jnp.int32, (BLOCK, width), 0)
    row_at = lax.broadcasted_iota(jnp.int32, (BLOCK, width), 1) % BLOCK
    nt = (((1,), (1,)), ((), ()))

    def fold(x, op):
        y = x[0:8, :]
        for r in range(1, BLOCK // 8):
            y = op(y, x[r * 8 : (r + 1) * 8, :])
        return y

    vertical_sum = [None, None]
    for j in range(per_device):
        block = first_block + j
        own_at = (WDEV * per_device + j) * BLOCK
        slash_at = [
            pl.multiple_of((WDEV * per_device + j - offs[h, s]) * BLOCK, BLOCK) for s in range(ns)
        ]
        valid = [None]
        for m in range(nv):
            valid.append(verts[h, m] < block)
        for s in range(ns):
            collide = verts[h, 0] == block - offs[h, s]
            for m in range(1, nv):
                collide = collide | (verts[h, m] == block - offs[h, s])
            valid.append((offs[h, s] > 0) & jnp.logical_not(collide))
        for kv, to in enumerate((kc, vc)):
            to[j, 0:BLOCK, :] = win[kv, own_at : own_at + BLOCK, lanes]
            to[j, BLOCK : (1 + nv) * BLOCK, :] = vkv[kv, vert_rows, :]
            for s in range(ns):
                to[j, (1 + nv + s) * BLOCK : (2 + nv + s) * BLOCK, :] = win[
                    kv, pl.ds(slash_at[s], BLOCK), lanes
                ]
        products = []
        block_rows = slice(j * BLOCK, (j + 1) * BLOCK)
        for g in range(group):
            cols = slice(g * head_dim, (g + 1) * head_dim)
            qs[j, g * BLOCK : (g + 1) * BLOCK, :] = q[block_rows, cols]
            gs[j, g * BLOCK : (g + 1) * BLOCK, :] = grad[block_rows, cols]
            products.append(grad[block_rows, cols].astype(F32) * out[block_rows, cols].astype(F32))
        delta = jnp.sum(jnp.transpose(jnp.concatenate(products, axis=0)), axis=0, keepdims=True)

        s_ref[j] = lax.dot_general(kc[j], qs[j], nt, preferred_element_type=F32)
        dp_ref[j] = lax.dot_general(vc[j], gs[j], nt, preferred_element_type=F32)

        own = jnp.where(key_at <= row_at, s_ref[j, 0:BLOCK, :], neg)
        s_ref[j, 0:BLOCK, :] = own
        top = fold(own, jnp.maximum)
        for c in range(1, cand):
            best = fold(s_ref[j, c * BLOCK : (c + 1) * BLOCK, :], jnp.maximum)
            top = jnp.maximum(top, best + jnp.where(valid[c], jnp.float32(0), neg))
        top = jnp.max(top, axis=0, keepdims=True) * log2_scale
        total = jnp.zeros((8, width), F32)
        for c in range(cand):
            span = slice(c * BLOCK, (c + 1) * BLOCK)
            less = top if c == 0 else top + jnp.where(valid[c], jnp.float32(0), posinf)
            p = jnp.exp2(s_ref[j, span, :] * log2_scale - less)
            s_ref[j, span, :] = p
            total = total + fold(p, jnp.add)
        inverse = 1.0 / jnp.sum(total, axis=0, keepdims=True)
        for c in range(cand):
            span = slice(c * BLOCK, (c + 1) * BLOCK)
            w = s_ref[j, span, :] * inverse
            w_ref[j, span, :] = w.astype(BF16)
            ds_ref[j, span, :] = (w * (dp_ref[j, span, :] - delta)).astype(BF16)

        dv = jnp.dot(w_ref[j], gs[j], preferred_element_type=F32)
        dk = jnp.dot(ds_ref[j], qs[j], preferred_element_type=F32) * scaling
        dqt = lax.dot_general(
            kc[j], ds_ref[j], (((0,), (0,)), ((), ())), preferred_element_type=F32
        )
        dqr = (jnp.transpose(dqt) * scaling).astype(BF16)
        for g in range(group):
            dq[block_rows, g * head_dim : (g + 1) * head_dim] = dqr[g * BLOCK : (g + 1) * BLOCK, :]

        for kv, part in enumerate((dk, dv)):
            nacc[kv, own_at : own_at + BLOCK, lanes] += part[0:BLOCK]
            for s in range(ns):
                nacc[kv, pl.ds(slash_at[s], BLOCK), lanes] += part[
                    (1 + nv + s) * BLOCK : (2 + nv + s) * BLOCK
                ]
            of_verticals = part[BLOCK : (1 + nv) * BLOCK]
            vertical_sum[kv] = of_verticals if j == 0 else vertical_sum[kv] + of_verticals

    first = core == 0
    keep = jnp.where(first, vertical_sum[0], vertical_sum[1])
    give = jnp.where(first, vertical_sum[1], vertical_sum[0])
    per_line = heads // 2
    for line in range(2):

        @pl.when(lax.rem(lax.div(h, per_line) + near, 2) == line)
        def _():
            for c in range(nv * BLOCK // chunk):
                slot = lax.rem(h, per_line) * (nv * BLOCK // chunk) + c
                slot = lax.rem(slot - far + lines.far, lines.far)
                span = slice(c * chunk, (c + 1) * chunk)
                shares[line][slot] = keep[span, :].astype(shares[line].dtype)
                shares[2 + line][slot] = give[span, :].astype(BF16)

    for kv in range(2):
        home[kv, :, lanes] = nacc[kv, WDEV * rows :, lanes]
        for part, d in zip(near_parts, distances(core)):
            part[kv, :, lanes] = nacc[kv, pl.ds(window_row(d), rows), lanes].astype(part.dtype)


def attend(
    slab_index, verticals, offsets, queries, cotangent, output, keys, values, gathered, recv, lines
):
    rows, width = queries.shape
    features = keys.shape[2]
    heads, nv = verticals.shape
    ns = offsets.shape[1]
    head_dim = features // heads
    group = width // features
    per_device = rows // BLOCK
    cand = 1 + nv + ns
    smem = pl.BlockSpec(memory_space=pltpu.SMEM)
    hbm = pl.BlockSpec(memory_space=pl.ANY)
    tile = pl.BlockSpec((rows, group * head_dim), lambda h: (0, h))

    def whole(shape):
        return pl.BlockSpec(shape, lambda h: (0,) * len(shape))

    shard = (2, rows, features)
    vert_shape = (2, heads * nv * BLOCK, head_dim)
    share = (lines.far, heads * nv * BLOCK // (2 * lines.far), head_dim)
    return pl.pallas_call(
        functools.partial(
            attend_kernel, lines=lines, heads=heads, nv=nv, ns=ns, per_device=per_device
        ),
        grid=(heads,),
        in_specs=[smem] * 3 + [tile] * 3 + [hbm] * (6 + WDEV),
        out_specs=[tile] + [whole(shard)] * (1 + WDEV) + [whole(share)] * 4,
        out_shape=[
            jax.ShapeDtypeStruct((rows, width), BF16),
            jax.ShapeDtypeStruct(shard, F32),
            jax.ShapeDtypeStruct(shard, F32),
            jax.ShapeDtypeStruct(shard, F32),
            jax.ShapeDtypeStruct(shard, BF16),
            jax.ShapeDtypeStruct(shard, BF16),
            jax.ShapeDtypeStruct(shard, BF16),
            jax.ShapeDtypeStruct(share, F32),
            jax.ShapeDtypeStruct(share, BF16),
            jax.ShapeDtypeStruct(share, BF16),
            jax.ShapeDtypeStruct(share, BF16),
        ],
        scratch_shapes=[
            pltpu.VMEM((2, (WDEV + 1) * rows, features), BF16),
            pltpu.VMEM(vert_shape, BF16),
            pltpu.VMEM((per_device, cand * BLOCK, head_dim), BF16),
            pltpu.VMEM((per_device, cand * BLOCK, head_dim), BF16),
            pltpu.VMEM((per_device, group * BLOCK, head_dim), BF16),
            pltpu.VMEM((per_device, group * BLOCK, head_dim), BF16),
            pltpu.VMEM((per_device, cand * BLOCK, group * BLOCK), F32),
            pltpu.VMEM((per_device, cand * BLOCK, group * BLOCK), F32),
            pltpu.VMEM((per_device, cand * BLOCK, group * BLOCK), BF16),
            pltpu.VMEM((per_device, cand * BLOCK, group * BLOCK), BF16),
            pltpu.VMEM((2, (WDEV + 1) * rows, features), F32),
            pltpu.SemaphoreType.DMA((WDEV + 2 + 4 * lines.far,)),
        ],
        compiler_params=pltpu.CompilerParams(vmem_limit_bytes=VMEM_LIMIT),
    )(
        slab_index, verticals, offsets, queries, cotangent, output, keys, values, *gathered, *recv,
    )


def assemble_kernel(slab_index, verts, home, *rest, lines, heads, nv, per_device):
    from_near, arrived, gathered = rest[0], rest[1:3], rest[3:7]
    key_out, value_out, vert, acc, sems = rest[7:]
    slab, me = slab_index[0], lax.axis_index("ctx")
    devices = lines.devices
    chunk = gathered[0].shape[1]
    copies = vertical_copies(lines, me, chunk, gathered, vert, sems, 0)
    for copy in copies:
        copy.start()
    head_dim = vert.shape[2]
    slab_blocks = per_device * devices
    acc[0] = home[...]
    acc[1] = jnp.zeros_like(home)
    _, near, _ = lines.place(me)

    @pl.when(near == 0)
    def _():
        acc[0] += from_near[...].astype(F32)

    for part, wrapped in zip(arrived, wraps(me, devices)):
        acc[wrapped.astype(jnp.int32)] += part[...].astype(F32)
    key_out[...] = jnp.zeros_like(key_out)
    value_out[...] = jnp.zeros_like(value_out)
    outs = (key_out, value_out)
    for copy in copies:
        copy.wait()
    for h in range(heads):
        lanes = slice(h * head_dim, (h + 1) * head_dim)
        for m in range(nv):
            inner = lax.rem(verts[h, m], slab_blocks)
            region = lax.div(verts[h, m], slab_blocks)
            row = pl.multiple_of(lax.rem(inner, per_device) * BLOCK, BLOCK)
            at = (h * nv + m) * BLOCK

            @pl.when(lax.div(inner, per_device) == me)
            def _():
                close = (region == slab) | (region == slab - 1)

                @pl.when(close)
                def _():
                    for kv in range(2):
                        acc[slab - region, kv, pl.ds(row, BLOCK), lanes] += vert[
                            kv, at : at + BLOCK, :
                        ].astype(F32)

                @pl.when(jnp.logical_not(close))
                def _():
                    for kv in range(2):
                        outs[kv][region, pl.ds(row, BLOCK), lanes] = vert[kv, at : at + BLOCK, :]

    for kv in range(2):
        outs[kv][slab] = acc[0, kv].astype(BF16)
        outs[kv][slab - 1] = acc[1, kv].astype(BF16)


def assemble(slab_index, verticals, home, from_near, arrived, gathered, regions, lines):
    _, rows, features = home.shape
    heads, nv = verticals.shape
    smem = pl.BlockSpec(memory_space=pltpu.SMEM)
    vmem = pl.BlockSpec(memory_space=pltpu.VMEM)
    hbm = pl.BlockSpec(memory_space=pl.ANY)
    return pl.pallas_call(
        functools.partial(
            assemble_kernel, lines=lines, heads=heads, nv=nv, per_device=rows // BLOCK
        ),
        in_specs=[smem] * 2 + [vmem] * 4 + [hbm] * 4,
        out_specs=[vmem] * 2,
        out_shape=[jax.ShapeDtypeStruct((regions, rows, features), BF16)] * 2,
        scratch_shapes=[
            pltpu.VMEM((2, heads * nv * BLOCK, features // heads), BF16),
            pltpu.VMEM((2, 2, rows, features), F32),
            pltpu.SemaphoreType.DMA((4 * lines.far,)),
        ],
        compiler_params=pltpu.CompilerParams(vmem_limit_bytes=VMEM_LIMIT),
    )(slab_index, verticals, home, from_near, *arrived, *gathered)


def shards(
    queries,
    context_keys,
    context_values,
    forward_output,
    output_cotangent,
    verticals,
    offsets,
    slab_index,
):
    lines = Lines(lax.axis_size("ctx"))
    regions = context_keys.shape[0]
    _, near, _ = lines.place(lax.axis_index("ctx"))

    own, send4, mixed, mine, to_near, to_core, to_both = pack(
        slab_index, verticals, context_keys, context_values, lines
    )
    recv4 = move(send4, lines.shift_pairs(4))
    quarter = plane_sum(lines, mine, to_near, to_core, to_both)
    recv2 = move(jnp.where(near == 1, recv4, own), lines.near_pairs())
    gathered = after(far_sum(lines, after(quarter, recv4)), recv2)
    recv_mixed = move(after(mixed, gathered), lines.mixed_pairs())
    gathered = plane_gather(lines, gathered)
    other2 = move(recv2, lines.core_pairs())
    other4 = move(recv4, lines.core_pairs())

    query_grad, home, part2, part4, mixed, give2, give4, *shares = attend(
        slab_index, verticals, offsets, queries, output_cotangent, forward_output,
        context_keys, context_values, gathered, [recv2, recv4, recv_mixed, other2, other4], lines,
    )

    arrived_mixed = move(mixed, back(lines.mixed_pairs()))
    sum2 = (part2 + move(give2, lines.core_pairs()).astype(F32)).astype(BF16)
    sum4 = part4 + move(give4, lines.core_pairs()).astype(F32)
    mine, to_near, to_core, to_both = shares
    quarter = plane_sum(lines, mine, to_near, to_core, to_both)
    from_near = move(after(sum2, quarter), lines.near_pairs())
    totals = after(far_sum(lines, after(quarter, arrived_mixed)), from_near)
    sum4 = (sum4 + jnp.where(near == 1, from_near.astype(F32), 0.0)).astype(BF16)
    arrived4 = move(after(sum4, totals), back(lines.shift_pairs(4)))
    totals = plane_gather(lines, totals)
    key_gradient, value_gradient = assemble(
        slab_index, verticals, home, from_near, (arrived4, arrived_mixed), totals, regions, lines
    )
    return query_grad, key_gradient, value_gradient


def solution(mesh):
    in_specs = (
        P(("groups", "ctx"), None),
        P("groups", "ctx", None),
        P("groups", "ctx", None),
        P(("groups", "ctx"), None),
        P(("groups", "ctx"), None),
        P("groups", None),
        P("groups", None),
        P("groups"),
    )
    out_specs = (P(("groups", "ctx"), None), P("groups", "ctx", None), P("groups", "ctx", None))
    return jax.shard_map(shards, mesh=mesh, in_specs=in_specs, out_specs=out_specs, check_vma=False)
```

```python
import functools
import math

import jax
import jax.numpy as jnp
from jax import lax
from jax.experimental import pallas as pl
from jax.experimental.pallas import tpu as pltpu
from jax.sharding import PartitionSpec as P

BLOCK = 64
WDEV = 5
JOIN = 4
FULL_VMEM = 60 * 1024 * 1024
PART_VMEM = 32 * 1024 * 1024
BF16 = jnp.bfloat16
F32 = jnp.float32


class Lines:
    def __init__(self, devices):
        self.devices = devices
        self.far = devices // 4

    def place(self, me):
        return lax.div(me, 4), lax.rem(lax.div(me, 2), 2), lax.rem(me, 2)

    def core_pairs(self):
        return [(i, i ^ 1) for i in range(self.devices)]

    def near_pairs(self):
        return [(i, i ^ 2) for i in range(self.devices)]

    def both_pairs(self):
        return [(i, i ^ 3) for i in range(self.devices)]

    def far_pairs(self, by):
        return [(i, (i + 4 * by) % self.devices) for i in range(self.devices)]

    def shift_pairs(self, by):
        return [(i, (i + by) % self.devices) for i in range(self.devices)]

    def mixed_pairs(self):
        return [(i, (i + (5 if i % 2 else 1)) % self.devices) for i in range(self.devices)]


def back(pairs):
    return [(b, a) for a, b in pairs]


def move(array, pairs):
    return lax.ppermute(array, "ctx", pairs)


def after(array, *others):
    return lax.optimization_barrier((array, *others))[0]


def plane_sum(lines, mine, to_near, to_core, to_both):
    to_near = (to_near.astype(F32) + move(to_both, lines.core_pairs()).astype(F32)).astype(BF16)
    from_near = move(to_near, lines.near_pairs())
    from_core = move(to_core, lines.core_pairs())
    return mine.astype(F32) + from_core.astype(F32) + from_near.astype(F32)


def far_sum(lines, quarter):
    share = quarter[0]
    for by in range(1, lines.far):
        share = share + move(quarter[by].astype(BF16), lines.far_pairs(by)).astype(F32)
    share = share.astype(BF16)
    parts = [share] + [move(share, lines.far_pairs(by)) for by in range(1, lines.far)]
    return jnp.stack(parts)


def plane_gather(lines, mine):
    across = move(mine, lines.near_pairs())
    core_mine = move(mine, lines.core_pairs())
    core_across = move(across, lines.core_pairs())
    return mine, across, core_mine, core_across


def wraps(me, devices):
    return [me + 4 >= devices, (lax.rem(me, 2) == 1) & (me + 5 >= devices)]


def pack_window_kernel(slab_index, keys, values, *rest, lines):
    key4, value4, mixed, own, sems = rest
    slab, me = slab_index[0], lax.axis_index("ctx")
    copies = []
    wrapped4, wrapped_mixed = wraps(me, lines.devices)
    for n, (region, to) in enumerate(
        (
            (slab - wrapped4.astype(jnp.int32), (key4, value4)),
            (slab - wrapped_mixed.astype(jnp.int32), (mixed.at[0], mixed.at[1])),
            (slab, (own.at[0], own.at[1])),
        )
    ):
        for kv, source in enumerate((keys, values)):
            copy = pltpu.make_async_copy(source.at[region], to[kv], sems.at[n, kv])
            copy.start()
            copies.append(copy)
    for copy in copies:
        copy.wait()


def pack_window(slab_index, keys, values, lines):
    _, rows, features = keys.shape
    hbm = pl.BlockSpec(memory_space=pl.ANY)
    return pl.pallas_call(
        functools.partial(pack_window_kernel, lines=lines),
        in_specs=[pl.BlockSpec(memory_space=pltpu.SMEM), hbm, hbm],
        out_specs=[pl.BlockSpec(memory_space=pltpu.VMEM)] * 4,
        out_shape=[jax.ShapeDtypeStruct((rows, features), BF16)] * 2
        + [jax.ShapeDtypeStruct((2, rows, features), BF16)] * 2,
        scratch_shapes=[pltpu.SemaphoreType.DMA((3, 2))],
        compiler_params=pltpu.CompilerParams(vmem_limit_bytes=FULL_VMEM),
    )(slab_index, keys, values)


def pack_verticals_kernel(verts, keys, values, _, *rest, lines, heads, nv, per_device):
    shares = rest[:4]
    picked, pick_sems = rest[4:]
    me = lax.axis_index("ctx")
    far, near, core = lines.place(me)
    _, chunk, head_dim = shares[0].shape
    slab_blocks = per_device * lines.devices
    piece = min(BLOCK, chunk)

    def unit_copies(h, m):
        inner = lax.rem(verts[h, m], slab_blocks)
        region = lax.div(verts[h, m], slab_blocks)
        row = lax.rem(inner, per_device) * BLOCK
        for p in range(BLOCK // piece):
            at = (h * nv + m) * BLOCK + p * piece
            line, at = at // (lines.far * chunk), at % (lines.far * chunk)
            slot, at = at // chunk, at % chunk
            line = lax.rem(line + near, 2)
            slot = lax.rem(slot - far + lines.far, lines.far)
            for kv, source in enumerate((keys, values)):
                yield pltpu.make_async_copy(
                    source.at[
                        region,
                        pl.ds(pl.multiple_of(row + p * piece, piece), piece),
                        pl.ds(h * head_dim, head_dim),
                    ],
                    picked.at[lax.rem(kv + core, 2), line, slot, pl.ds(at, piece), :],
                    pick_sems.at[kv, (h * nv + m) * (BLOCK // piece) + p],
                )

    def owned(h, m):
        return lax.div(lax.rem(verts[h, m], slab_blocks), per_device) == me

    picked[...] = jnp.zeros_like(picked)
    for h in range(heads):
        for m in range(nv):

            @pl.when(owned(h, m))
            def _():
                for copy in unit_copies(h, m):
                    copy.start()

    for h in range(heads):
        for m in range(nv):

            @pl.when(owned(h, m))
            def _():
                for copy in unit_copies(h, m):
                    copy.wait()

    for n, share in enumerate(shares):
        share[...] = picked[n // 2, n % 2]


def pack_verticals(verticals, keys, values, ahead, lines):
    heads, nv = verticals.shape
    rows, features = keys.shape[1:]
    head_dim = features // heads
    chunk = heads * nv * BLOCK // (2 * lines.far)
    hbm = pl.BlockSpec(memory_space=pl.ANY)
    share = (lines.far, chunk, head_dim)
    return pl.pallas_call(
        functools.partial(
            pack_verticals_kernel, lines=lines, heads=heads, nv=nv, per_device=rows // BLOCK
        ),
        in_specs=[pl.BlockSpec(memory_space=pltpu.SMEM), hbm, hbm, hbm],
        out_specs=[pl.BlockSpec(memory_space=pltpu.VMEM)] * 4,
        out_shape=[jax.ShapeDtypeStruct(share, BF16)] * 4,
        scratch_shapes=[
            pltpu.VMEM((2, 2) + share, BF16),
            pltpu.SemaphoreType.DMA((2, heads * nv * max(1, BLOCK // chunk))),
        ],
        compiler_params=pltpu.CompilerParams(vmem_limit_bytes=FULL_VMEM),
    )(verticals, keys, values, ahead)


def distances(core):
    return [2, 4, 5 - 4 * core, 1 + 2 * core, 3 + 2 * core]


def vertical_copies(lines, me, chunk, gathered, to, sems, first):
    far, near, core = lines.place(me)
    copies = []
    for n, source in enumerate(gathered):
        kv = core if n < 2 else 1 - core
        line = near if n % 2 == 0 else 1 - near
        for s in range(lines.far):
            slot = lax.rem(far - s + lines.far, lines.far)
            row = pl.multiple_of((line * lines.far + slot) * chunk, chunk)
            copies.append(
                pltpu.make_async_copy(
                    source.at[s], to.at[kv, pl.ds(row, chunk), :], sems.at[first + len(copies)]
                )
            )
    return copies


def attend_kernel(
    slab_index, verts, offs, q, grad, out, keys, values, *rest, lines, heads, nv, ns, per_device,
):
    gathered, recv, rest = rest[:4], rest[4 : 4 + WDEV], rest[4 + WDEV :]
    dq, home, near_parts, shares = rest[0], rest[1], rest[2 : 2 + WDEV], rest[7:11]
    (win, vkv, kc, vc, qs, gs, split, s_ref, w_ref, ds_ref, nacc, sems) = rest[11:]
    h = pl.program_id(0)
    slab, me = slab_index[0], lax.axis_index("ctx")
    far, near, core = lines.place(me)
    _, chunk, head_dim = shares[0].shape
    group = q.shape[1] // head_dim
    cand = 1 + nv + ns
    scaling = 1.0 / math.sqrt(head_dim)
    rows = per_device * BLOCK
    width = group * BLOCK
    first_block = slab * (per_device * lines.devices) + me * per_device
    lanes = pl.ds(pl.multiple_of(h * head_dim, head_dim), head_dim)

    def window_row(d):
        return pl.multiple_of((WDEV - d) * rows, rows)

    @pl.when(h == 0)
    def _():
        own_rows = pl.ds(WDEV * rows, rows)
        copies = [
            pltpu.make_async_copy(
                recv[n], win.at[:, pl.ds(window_row(d), rows), :], sems.at[n]
            )
            for n, d in enumerate(distances(core))
        ]
        copies.append(pltpu.make_async_copy(keys.at[slab], win.at[0, own_rows, :], sems.at[WDEV]))
        copies.append(
            pltpu.make_async_copy(values.at[slab], win.at[1, own_rows, :], sems.at[WDEV + 1])
        )
        copies += vertical_copies(lines, me, chunk, gathered, vkv, sems, WDEV + 2)
        for copy in copies:
            copy.start()
        nacc[...] = jnp.zeros_like(nacc)
        for copy in copies:
            copy.wait()

    vert_rows = pl.ds(pl.multiple_of(h * (nv * BLOCK), nv * BLOCK), nv * BLOCK)
    neg, posinf = jnp.float32(-jnp.inf), jnp.float32(jnp.inf)
    log2_scale = scaling * math.log2(math.e)
    key_at = lax.broadcasted_iota(jnp.int32, (BLOCK, width), 0)
    row_at = lax.broadcasted_iota(jnp.int32, (BLOCK, width), 1) % BLOCK
    nt = (((1,), (1,)), ((), ()))

    def fold(x, op):
        y = x[0:8, :]
        for r in range(1, BLOCK // 8):
            y = op(y, x[r * 8 : (r + 1) * 8, :])
        return y

    vertical_sum = [None, None]
    for j in range(per_device):
        block = first_block + j
        own_at = (WDEV * per_device + j) * BLOCK
        slash_at = [
            pl.multiple_of((WDEV * per_device + j - offs[h, s]) * BLOCK, BLOCK) for s in range(ns)
        ]
        valid = [None]
        for m in range(nv):
            valid.append(verts[h, m] < block)
        for s in range(ns):
            collide = verts[h, 0] == block - offs[h, s]
            for m in range(1, nv):
                collide = collide | (verts[h, m] == block - offs[h, s])
            valid.append((offs[h, s] > 0) & jnp.logical_not(collide))
        for kv, to in enumerate((kc, vc)):
            to[j, 0:BLOCK, :] = win[kv, own_at : own_at + BLOCK, lanes]
            to[j, BLOCK : (1 + nv) * BLOCK, :] = vkv[kv, vert_rows, :]
            for s in range(ns):
                to[j, (1 + nv + s) * BLOCK : (2 + nv + s) * BLOCK, :] = win[
                    kv, pl.ds(slash_at[s], BLOCK), lanes
                ]
        block_rows = slice(j * BLOCK, (j + 1) * BLOCK)
        for g in range(group):
            cols = slice(g * head_dim, (g + 1) * head_dim)
            here = slice(g * BLOCK, (g + 1) * BLOCK)
            qs[j, here, :] = q[block_rows, cols]
            gs[j, here, :] = grad[block_rows, cols]
            product = grad[block_rows, cols].astype(F32) * out[block_rows, cols].astype(F32)
            upper = product.astype(BF16)
            split[j, here, 0:head_dim] = upper
            split[j, here, head_dim:] = (product - upper.astype(F32)).astype(BF16)
        ones = jnp.ones((8, 2 * head_dim), BF16)
        delta = lax.dot_general(ones, split[j], nt, preferred_element_type=F32)[0:1, :]

        top = None
        for n in range(cand // JOIN):
            rows_n = slice(n * JOIN * BLOCK, (n + 1) * JOIN * BLOCK)
            s = lax.dot_general(kc[j, rows_n, :], qs[j], nt, preferred_element_type=F32)
            for i in range(JOIN):
                c = n * JOIN + i
                part = s[i * BLOCK : (i + 1) * BLOCK, :]
                if c == 0:
                    part = jnp.where(key_at <= row_at, part, neg)
                s_ref[j, c * BLOCK : (c + 1) * BLOCK, :] = part
                best = fold(part, jnp.maximum)
                if c == 0:
                    top = best
                else:
                    top = jnp.maximum(top, best + jnp.where(valid[c], jnp.float32(0), neg))
        top = jnp.max(top, axis=0, keepdims=True) * log2_scale
        total = jnp.zeros((8, width), F32)
        for c in range(cand):
            span = slice(c * BLOCK, (c + 1) * BLOCK)
            less = top if c == 0 else top + jnp.where(valid[c], jnp.float32(0), posinf)
            p = jnp.exp2(s_ref[j, span, :] * log2_scale - less)
            s_ref[j, span, :] = p
            total = total + fold(p, jnp.add)
        inverse = 1.0 / jnp.sum(total, axis=0, keepdims=True)
        for n in range(cand // JOIN):
            span = slice(n * JOIN * BLOCK, (n + 1) * JOIN * BLOCK)
            dp = lax.dot_general(vc[j, span, :], gs[j], nt, preferred_element_type=F32)
            w = s_ref[j, span, :] * inverse
            w_ref[j, span, :] = w.astype(BF16)
            ds_ref[j, span, :] = (w * (dp - delta)).astype(BF16)

        dv = jnp.dot(w_ref[j], gs[j], preferred_element_type=F32)
        dk = jnp.dot(ds_ref[j], qs[j], preferred_element_type=F32) * scaling
        dqt = lax.dot_general(
            kc[j], ds_ref[j], (((0,), (0,)), ((), ())), preferred_element_type=F32
        )
        dqr = (jnp.transpose(dqt) * scaling).astype(BF16)
        for g in range(group):
            dq[block_rows, g * head_dim : (g + 1) * head_dim] = dqr[g * BLOCK : (g + 1) * BLOCK, :]

        for kv, part in enumerate((dk, dv)):
            nacc[kv, own_at : own_at + BLOCK, lanes] += part[0:BLOCK]
            for s in range(ns):
                nacc[kv, pl.ds(slash_at[s], BLOCK), lanes] += part[
                    (1 + nv + s) * BLOCK : (2 + nv + s) * BLOCK
                ]
            of_verticals = part[BLOCK : (1 + nv) * BLOCK]
            vertical_sum[kv] = of_verticals if j == 0 else vertical_sum[kv] + of_verticals

    first = core == 0
    keep = jnp.where(first, vertical_sum[0], vertical_sum[1])
    give = jnp.where(first, vertical_sum[1], vertical_sum[0])
    per_line = heads // 2
    for line in range(2):

        @pl.when(lax.rem(lax.div(h, per_line) + near, 2) == line)
        def _():
            for c in range(nv * BLOCK // chunk):
                slot = lax.rem(h, per_line) * (nv * BLOCK // chunk) + c
                slot = lax.rem(slot - far + lines.far, lines.far)
                span = slice(c * chunk, (c + 1) * chunk)
                shares[line][slot] = keep[span, :].astype(shares[line].dtype)
                shares[2 + line][slot] = give[span, :].astype(BF16)

    for kv in range(2):
        home[kv, :, lanes] = nacc[kv, WDEV * rows :, lanes]
        for part, d in zip(near_parts, distances(core)):
            part[kv, :, lanes] = nacc[kv, pl.ds(window_row(d), rows), lanes].astype(part.dtype)


def attend(
    slab_index, verticals, offsets, queries, cotangent, output, keys, values, gathered, recv, lines
):
    rows, width = queries.shape
    features = keys.shape[2]
    heads, nv = verticals.shape
    ns = offsets.shape[1]
    head_dim = features // heads
    group = width // features
    per_device = rows // BLOCK
    cand = 1 + nv + ns
    smem = pl.BlockSpec(memory_space=pltpu.SMEM)
    hbm = pl.BlockSpec(memory_space=pl.ANY)
    tile = pl.BlockSpec((rows, group * head_dim), lambda h: (0, h))

    def whole(shape):
        return pl.BlockSpec(shape, lambda h: (0,) * len(shape))

    shard = (2, rows, features)
    vert_shape = (2, heads * nv * BLOCK, head_dim)
    share = (lines.far, heads * nv * BLOCK // (2 * lines.far), head_dim)
    return pl.pallas_call(
        functools.partial(
            attend_kernel, lines=lines, heads=heads, nv=nv, ns=ns, per_device=per_device
        ),
        grid=(heads,),
        in_specs=[smem] * 3 + [tile] * 3 + [hbm] * (6 + WDEV),
        out_specs=[tile] + [whole(shard)] * (1 + WDEV) + [whole(share)] * 4,
        out_shape=[
            jax.ShapeDtypeStruct((rows, width), BF16),
            jax.ShapeDtypeStruct(shard, F32),
            jax.ShapeDtypeStruct(shard, F32),
            jax.ShapeDtypeStruct(shard, F32),
            jax.ShapeDtypeStruct(shard, BF16),
            jax.ShapeDtypeStruct(shard, BF16),
            jax.ShapeDtypeStruct(shard, BF16),
            jax.ShapeDtypeStruct(share, F32),
            jax.ShapeDtypeStruct(share, BF16),
            jax.ShapeDtypeStruct(share, BF16),
            jax.ShapeDtypeStruct(share, BF16),
        ],
        scratch_shapes=[
            pltpu.VMEM((2, (WDEV + 1) * rows, features), BF16),
            pltpu.VMEM(vert_shape, BF16),
            pltpu.VMEM((per_device, cand * BLOCK, head_dim), BF16),
            pltpu.VMEM((per_device, cand * BLOCK, head_dim), BF16),
            pltpu.VMEM((per_device, group * BLOCK, head_dim), BF16),
            pltpu.VMEM((per_device, group * BLOCK, head_dim), BF16),
            pltpu.VMEM((per_device, group * BLOCK, 2 * head_dim), BF16),
            pltpu.VMEM((per_device, cand * BLOCK, group * BLOCK), F32),
            pltpu.VMEM((per_device, cand * BLOCK, group * BLOCK), BF16),
            pltpu.VMEM((per_device, cand * BLOCK, group * BLOCK), BF16),
            pltpu.VMEM((2, (WDEV + 1) * rows, features), F32),
            pltpu.SemaphoreType.DMA((WDEV + 2 + 4 * lines.far,)),
        ],
        compiler_params=pltpu.CompilerParams(vmem_limit_bytes=PART_VMEM),
    )(
        slab_index, verticals, offsets, queries, cotangent, output, keys, values, *gathered, *recv,
    )


def assemble_kernel(slab_index, verts, home, *rest, lines, heads, nv, per_device):
    from_near, arrived, gathered = rest[0], rest[1:3], rest[3:7]
    key_out, value_out, vert, acc, sems = rest[7:]
    slab, me = slab_index[0], lax.axis_index("ctx")
    devices = lines.devices
    chunk = gathered[0].shape[1]
    copies = vertical_copies(lines, me, chunk, gathered, vert, sems, 0)
    for copy in copies:
        copy.start()
    head_dim = vert.shape[2]
    slab_blocks = per_device * devices
    acc[0] = home[...]
    acc[1] = jnp.zeros_like(home)
    _, near, _ = lines.place(me)

    @pl.when(near == 0)
    def _():
        acc[0] += from_near[...].astype(F32)

    for part, wrapped in zip(arrived, wraps(me, devices)):
        acc[wrapped.astype(jnp.int32)] += part[...].astype(F32)
    key_out[...] = jnp.zeros_like(key_out)
    value_out[...] = jnp.zeros_like(value_out)
    outs = (key_out, value_out)
    for copy in copies:
        copy.wait()
    for h in range(heads):
        lanes = slice(h * head_dim, (h + 1) * head_dim)
        for m in range(nv):
            inner = lax.rem(verts[h, m], slab_blocks)
            region = lax.div(verts[h, m], slab_blocks)
            row = pl.multiple_of(lax.rem(inner, per_device) * BLOCK, BLOCK)
            at = (h * nv + m) * BLOCK

            @pl.when(lax.div(inner, per_device) == me)
            def _():
                close = (region == slab) | (region == slab - 1)

                @pl.when(close)
                def _():
                    for kv in range(2):
                        acc[slab - region, kv, pl.ds(row, BLOCK), lanes] += vert[
                            kv, at : at + BLOCK, :
                        ].astype(F32)

                @pl.when(jnp.logical_not(close))
                def _():
                    for kv in range(2):
                        outs[kv][region, pl.ds(row, BLOCK), lanes] = vert[kv, at : at + BLOCK, :]

    for kv in range(2):
        outs[kv][slab] = acc[0, kv].astype(BF16)
        outs[kv][slab - 1] = acc[1, kv].astype(BF16)


def assemble(slab_index, verticals, home, from_near, arrived, gathered, regions, lines):
    _, rows, features = home.shape
    heads, nv = verticals.shape
    smem = pl.BlockSpec(memory_space=pltpu.SMEM)
    vmem = pl.BlockSpec(memory_space=pltpu.VMEM)
    hbm = pl.BlockSpec(memory_space=pl.ANY)
    return pl.pallas_call(
        functools.partial(
            assemble_kernel, lines=lines, heads=heads, nv=nv, per_device=rows // BLOCK
        ),
        in_specs=[smem] * 2 + [vmem] * 4 + [hbm] * 4,
        out_specs=[vmem] * 2,
        out_shape=[jax.ShapeDtypeStruct((regions, rows, features), BF16)] * 2,
        scratch_shapes=[
            pltpu.VMEM((2, heads * nv * BLOCK, features // heads), BF16),
            pltpu.VMEM((2, 2, rows, features), F32),
            pltpu.SemaphoreType.DMA((4 * lines.far,)),
        ],
        compiler_params=pltpu.CompilerParams(vmem_limit_bytes=PART_VMEM),
    )(slab_index, verticals, home, from_near, *arrived, *gathered)


def shards(
    queries,
    context_keys,
    context_values,
    forward_output,
    output_cotangent,
    verticals,
    offsets,
    slab_index,
):
    lines = Lines(lax.axis_size("ctx"))
    regions = context_keys.shape[0]
    _, near, _ = lines.place(lax.axis_index("ctx"))

    key4, value4, mixed, own = pack_window(slab_index, context_keys, context_values, lines)
    key4 = move(key4, lines.shift_pairs(4))
    value4 = move(value4, lines.shift_pairs(4))
    recv4 = jnp.stack([key4, value4])
    recv_mixed = move(mixed, lines.mixed_pairs())
    mine, to_near, to_core, to_both = pack_verticals(
        verticals, context_keys, context_values, own, lines
    )
    to_both, to_core = after(to_both, key4), after(to_core, key4)
    quarter = plane_sum(lines, mine, to_near, to_core, to_both)
    recv2 = move(jnp.where(near == 1, recv4, own), lines.near_pairs())
    gathered = after(far_sum(lines, after(quarter, recv4, recv_mixed)), recv2)
    gathered = plane_gather(lines, gathered)
    other2 = move(recv2, lines.core_pairs())
    other4 = move(recv4, lines.core_pairs())

    query_grad, home, part2, part4, mixed, give2, give4, *shares = attend(
        slab_index, verticals, offsets, queries, output_cotangent, forward_output,
        context_keys, context_values, gathered, [recv2, recv4, recv_mixed, other2, other4], lines,
    )

    arrived_mixed = move(mixed, back(lines.mixed_pairs()))
    sum2 = (part2 + move(give2, lines.core_pairs()).astype(F32)).astype(BF16)
    sum4 = part4 + move(give4, lines.core_pairs()).astype(F32)
    mine, to_near, to_core, to_both = shares
    quarter = plane_sum(lines, mine, to_near, to_core, to_both)
    from_near = move(after(sum2, quarter), lines.near_pairs())
    totals = after(far_sum(lines, after(quarter, arrived_mixed)), from_near)
    sum4 = (sum4 + jnp.where(near == 1, from_near.astype(F32), 0.0)).astype(BF16)
    arrived4 = move(after(sum4, totals), back(lines.shift_pairs(4)))
    totals = plane_gather(lines, totals)
    key_gradient, value_gradient = assemble(
        slab_index, verticals, home, from_near, (arrived4, arrived_mixed), totals, regions, lines
    )
    return query_grad, key_gradient, value_gradient


def solution(mesh):
    in_specs = (
        P(("groups", "ctx"), None),
        P("groups", "ctx", None),
        P("groups", "ctx", None),
        P(("groups", "ctx"), None),
        P(("groups", "ctx"), None),
        P("groups", None),
        P("groups", None),
        P("groups"),
    )
    out_specs = (P(("groups", "ctx"), None), P("groups", "ctx", None), P("groups", "ctx", None))
    return jax.shard_map(shards, mesh=mesh, in_specs=in_specs, out_specs=out_specs, check_vma=False)
```

```python
import functools
import math

import jax
import jax.numpy as jnp
from jax import lax
from jax.experimental import pallas as pl
from jax.experimental.pallas import tpu as pltpu
from jax.sharding import PartitionSpec as P

BLOCK = 64
WDEV = 5
VMEM_LIMIT = 32 * 1024 * 1024
MOST_VMEM = 60 * 1024 * 1024
JOIN = 4
BF16 = jnp.bfloat16
F32 = jnp.float32


class Lines:
    def __init__(self, devices):
        self.devices = devices
        self.far = devices // 4

    def place(self, me):
        return lax.div(me, 4), lax.rem(lax.div(me, 2), 2), lax.rem(me, 2)

    def core_pairs(self):
        return [(i, i ^ 1) for i in range(self.devices)]

    def near_pairs(self):
        return [(i, i ^ 2) for i in range(self.devices)]

    def both_pairs(self):
        return [(i, i ^ 3) for i in range(self.devices)]

    def far_pairs(self, by):
        return [(i, (i + 4 * by) % self.devices) for i in range(self.devices)]

    def shift_pairs(self, by):
        return [(i, (i + by) % self.devices) for i in range(self.devices)]

    def mixed_pairs(self):
        return [(i, (i + (5 if i % 2 else 1)) % self.devices) for i in range(self.devices)]


def back(pairs):
    return [(b, a) for a, b in pairs]


def move(array, pairs):
    return lax.ppermute(array, "ctx", pairs)


def after(array, *others):
    return lax.optimization_barrier((array, *others))[0]


def core_sum(lines, to_near, to_both):
    return (to_near.astype(F32) + move(to_both, lines.core_pairs()).astype(F32)).astype(BF16)


def near_sum(lines, mine, to_near, to_core):
    from_near = move(to_near, lines.near_pairs())
    from_core = move(to_core, lines.core_pairs())
    return mine.astype(F32) + from_core.astype(F32) + from_near.astype(F32)


def far_sum(lines, quarter):
    share = quarter[0]
    for by in range(1, lines.far):
        share = share + move(quarter[by].astype(BF16), lines.far_pairs(by)).astype(F32)
    return share.astype(BF16)


def far_gather(lines, share):
    parts = [share] + [move(share, lines.far_pairs(by)) for by in range(1, lines.far)]
    return jnp.stack(parts)


def plane_gather(lines, mine):
    across = move(mine, lines.near_pairs())
    core_mine = move(mine, lines.core_pairs())
    core_across = move(across, lines.core_pairs())
    return mine, across, core_mine, core_across


def wraps(me, devices):
    return [me + 4 >= devices, (lax.rem(me, 2) == 1) & (me + 5 >= devices)]


def pack_kernel(slab_index, verts, keys, values, *rest, lines, heads, nv, per_device):
    sends = rest[:3]
    shares = rest[3:7]
    picked, sems, pick_sems = rest[7:]
    slab, me = slab_index[0], lax.axis_index("ctx")
    far, near, core = lines.place(me)
    _, chunk, head_dim = shares[0].shape
    copies = []
    wrapped4, wrapped_mixed = wraps(me, lines.devices)
    for n, region in enumerate(
        (slab, slab - wrapped4.astype(jnp.int32), slab - wrapped_mixed.astype(jnp.int32))
    ):
        for kv, source in enumerate((keys, values)):
            copy = pltpu.make_async_copy(source.at[region], sends[n].at[kv], sems.at[n, kv])
            copy.start()
            copies.append(copy)
    picked[...] = jnp.zeros_like(picked)
    slab_blocks = per_device * lines.devices
    piece = min(BLOCK, chunk)

    def unit_copies(h, m):
        inner = lax.rem(verts[h, m], slab_blocks)
        region = lax.div(verts[h, m], slab_blocks)
        row = lax.rem(inner, per_device) * BLOCK
        for p in range(BLOCK // piece):
            at = (h * nv + m) * BLOCK + p * piece
            line, at = at // (lines.far * chunk), at % (lines.far * chunk)
            slot, at = at // chunk, at % chunk
            line = lax.rem(line + near, 2)
            slot = lax.rem(slot - far + lines.far, lines.far)
            for kv, source in enumerate((keys, values)):
                yield pltpu.make_async_copy(
                    source.at[
                        region,
                        pl.ds(pl.multiple_of(row + p * piece, piece), piece),
                        pl.ds(h * head_dim, head_dim),
                    ],
                    picked.at[lax.rem(kv + core, 2), line, slot, pl.ds(at, piece), :],
                    pick_sems.at[kv, (h * nv + m) * (BLOCK // piece) + p],
                )

    def owned(h, m):
        return lax.div(lax.rem(verts[h, m], slab_blocks), per_device) == me

    for h in range(heads):
        for m in range(nv):

            @pl.when(owned(h, m))
            def _():
                for copy in unit_copies(h, m):
                    copy.start()

    for h in range(heads):
        for m in range(nv):

            @pl.when(owned(h, m))
            def _():
                for copy in unit_copies(h, m):
                    copy.wait()

    for n, share in enumerate(shares):
        share[...] = picked[n // 2, n % 2]
    for copy in copies:
        copy.wait()


def pack(slab_index, verticals, keys, values, lines):
    regions, rows, features = keys.shape
    heads, nv = verticals.shape
    head_dim = features // heads
    chunk = heads * nv * BLOCK // (2 * lines.far)
    smem = pl.BlockSpec(memory_space=pltpu.SMEM)
    hbm = pl.BlockSpec(memory_space=pltpu.HBM)
    share = (lines.far, chunk, head_dim)
    return pl.pallas_call(
        functools.partial(pack_kernel, lines=lines, heads=heads, nv=nv, per_device=rows // BLOCK),
        in_specs=[smem, smem, hbm, hbm],
        out_specs=[pl.BlockSpec(memory_space=pltpu.VMEM)] * 7,
        out_shape=[jax.ShapeDtypeStruct((2, rows, features), BF16)] * 3
        + [jax.ShapeDtypeStruct(share, BF16)] * 4,
        scratch_shapes=[
            pltpu.VMEM((2, 2) + share, BF16),
            pltpu.SemaphoreType.DMA((3, 2)),
            pltpu.SemaphoreType.DMA((2, heads * nv * max(1, BLOCK // chunk))),
        ],
        compiler_params=pltpu.CompilerParams(vmem_limit_bytes=MOST_VMEM),
    )(slab_index, verticals, keys, values)


def distances(core):
    return [2, 4, 5 - 4 * core, 1 + 2 * core, 3 + 2 * core]


def vertical_copies(lines, me, chunk, gathered, to, sems, first):
    far, near, core = lines.place(me)
    copies = []
    for n, source in enumerate(gathered):
        kv = core if n < 2 else 1 - core
        line = near if n % 2 == 0 else 1 - near
        for s in range(lines.far):
            slot = lax.rem(far - s + lines.far, lines.far)
            row = pl.multiple_of((line * lines.far + slot) * chunk, chunk)
            copies.append(
                pltpu.make_async_copy(
                    source.at[s], to.at[kv, pl.ds(row, chunk), :], sems.at[first + len(copies)]
                )
            )
    return copies


NT = (((1,), (1,)), ((), ()))


def prepare_kernel(q, grad, out, qs, gs, qt, gt, delta, *, head_dim):
    per_device = qs.shape[1]
    group = q.shape[1] // head_dim
    ones = jnp.ones((8, 2 * head_dim), BF16)
    for j in range(per_device):
        rows = slice(j * BLOCK, (j + 1) * BLOCK)
        split = []
        for g in range(group):
            cols = slice(g * head_dim, (g + 1) * head_dim)
            here = slice(g * BLOCK, (g + 1) * BLOCK)
            qs[0, j, here, :] = q[rows, cols]
            gs[0, j, here, :] = grad[rows, cols]
            product = grad[rows, cols].astype(F32) * out[rows, cols].astype(F32)
            upper = product.astype(BF16)
            lower = (product - upper.astype(F32)).astype(BF16)
            split.append(jnp.concatenate([upper, lower], axis=1))
        qt[0, j] = jnp.transpose(qs[0, j])
        gt[0, j] = jnp.transpose(gs[0, j])
        delta[0, j] = lax.dot_general(
            ones, jnp.concatenate(split, axis=0), NT, preferred_element_type=F32
        )


def prepare(queries, cotangent, output, heads, head_dim):
    rows, width = queries.shape
    per_device = rows // BLOCK
    deep = width // heads // head_dim * BLOCK
    tile = pl.BlockSpec((rows, width // heads), lambda h: (0, h))

    def by_head(*shape):
        return pl.BlockSpec((1,) + shape, lambda h: (h,) + (0,) * len(shape))

    stacked = (per_device, deep, head_dim)
    turned = (per_device, head_dim, deep)
    sums = (per_device, 8, deep)
    return pl.pallas_call(
        functools.partial(prepare_kernel, head_dim=head_dim),
        grid=(heads,),
        in_specs=[tile] * 3,
        out_specs=[by_head(*stacked)] * 2 + [by_head(*turned)] * 2 + [by_head(*sums)],
        out_shape=[jax.ShapeDtypeStruct((heads,) + stacked, BF16)] * 2
        + [jax.ShapeDtypeStruct((heads,) + turned, BF16)] * 2
        + [jax.ShapeDtypeStruct((heads,) + sums, F32)],
        compiler_params=pltpu.CompilerParams(vmem_limit_bytes=VMEM_LIMIT),
        cost_estimate=pl.CostEstimate(flops=0, bytes_accessed=7 << 20, transcendentals=0),
    )(queries, cotangent, output)


def slash_rows(offs, h, j, s, per_device):
    return pl.multiple_of((WDEV * per_device + j - offs[h, s]) * BLOCK, BLOCK)


def attend_kernel(
    slab_index, verts, offs, qs, gs, qt, gt, delta, keys, values, *rest,
    lines, heads, nv, ns, per_device,
):
    gathered, recv, rest = rest[:4], rest[4 : 4 + WDEV], rest[4 + WDEV :]
    shares, low_w, low_ds, cand_keys = rest[:4], rest[4], rest[5], rest[6]
    win, vkv, vc, s_ref, vert_w, sems = rest[7:]
    h = pl.program_id(0)
    slab, me = slab_index[0], lax.axis_index("ctx")
    far, near, core = lines.place(me)
    _, chunk, head_dim = shares[0].shape
    cand = nv + 1 + ns
    scaling = 1.0 / math.sqrt(head_dim)
    rows = per_device * BLOCK
    width = qs.shape[2]
    first_block = slab * (per_device * lines.devices) + me * per_device
    lanes = pl.ds(pl.multiple_of(h * head_dim, head_dim), head_dim)

    def window_row(d):
        return pl.multiple_of((WDEV - d) * rows, rows)

    @pl.when(h == 0)
    def _():
        own_rows = pl.ds(WDEV * rows, rows)
        copies = [
            pltpu.make_async_copy(
                recv[n], win.at[:, pl.ds(window_row(d), rows), :], sems.at[n]
            )
            for n, d in enumerate(distances(core))
        ]
        copies.append(pltpu.make_async_copy(keys.at[slab], win.at[0, own_rows, :], sems.at[WDEV]))
        copies.append(
            pltpu.make_async_copy(values.at[slab], win.at[1, own_rows, :], sems.at[WDEV + 1])
        )
        copies += vertical_copies(lines, me, chunk, gathered, vkv, sems, WDEV + 2)
        for copy in copies:
            copy.start()
        for copy in copies:
            copy.wait()

    vert_rows = pl.ds(pl.multiple_of(h * (nv * BLOCK), nv * BLOCK), nv * BLOCK)
    neg, posinf = jnp.float32(-jnp.inf), jnp.float32(jnp.inf)
    log2_scale = scaling * math.log2(math.e)
    key_at = lax.broadcasted_iota(jnp.int32, (BLOCK, width), 0)
    row_at = lax.broadcasted_iota(jnp.int32, (BLOCK, width), 1) % BLOCK

    def fold(x, op):
        y = x[0:8, :]
        for r in range(1, BLOCK // 8):
            y = op(y, x[r * 8 : (r + 1) * 8, :])
        return y

    vertical_sum = [None, None]
    for j in range(per_device):
        block = first_block + j
        own_at = (WDEV * per_device + j) * BLOCK
        valid = [verts[h, m] < block for m in range(nv)] + [None]
        for s in range(ns):
            collide = verts[h, 0] == block - offs[h, s]
            for m in range(1, nv):
                collide = collide | (verts[h, m] == block - offs[h, s])
            valid.append((offs[h, s] > 0) & jnp.logical_not(collide))
        for kv, to in enumerate((cand_keys.at[0], vc)):
            to[j, 0 : nv * BLOCK, :] = vkv[kv, vert_rows, :]
            to[j, nv * BLOCK : (nv + 1) * BLOCK, :] = win[kv, own_at : own_at + BLOCK, lanes]
            for s in range(ns):
                to[j, (nv + 1 + s) * BLOCK : (nv + 2 + s) * BLOCK, :] = win[
                    kv, pl.ds(slash_rows(offs, h, j, s, per_device), BLOCK), lanes
                ]

        top = None
        for n in range(cand // JOIN):
            span = slice(n * JOIN * BLOCK, (n + 1) * JOIN * BLOCK)
            scores = jnp.dot(cand_keys[0, j, span, :], qt[0, j], preferred_element_type=F32)
            for i in range(JOIN):
                c = n * JOIN + i
                part = scores[i * BLOCK : (i + 1) * BLOCK, :]
                if c == nv:
                    part = jnp.where(key_at <= row_at, part, neg)
                s_ref[j, c * BLOCK : (c + 1) * BLOCK, :] = part
                best = fold(part, jnp.maximum)
                if c != nv:
                    best = best + jnp.where(valid[c], jnp.float32(0), neg)
                top = best if top is None else jnp.maximum(top, best)
        top = jnp.max(top, axis=0, keepdims=True) * log2_scale
        total = jnp.zeros((8, width), F32)
        for c in range(cand):
            span = slice(c * BLOCK, (c + 1) * BLOCK)
            less = top if c == nv else top + jnp.where(valid[c], jnp.float32(0), posinf)
            p = jnp.exp2(s_ref[j, span, :] * log2_scale - less)
            s_ref[j, span, :] = p
            total = total + fold(p, jnp.add)
        inverse = 1.0 / jnp.sum(total, axis=0, keepdims=True)
        row_delta = delta[0, j, 0:1, :]
        for n in range(cand // JOIN):
            span = slice(n * JOIN * BLOCK, (n + 1) * JOIN * BLOCK)
            weight_grad = jnp.dot(vc[j, span, :], gt[0, j], preferred_element_type=F32)
            w = s_ref[j, span, :] * inverse
            if n * JOIN < nv:
                vert_w[j, span, :] = w.astype(BF16)
            else:
                low_w[0, j] = w.astype(BF16)
            low_ds[0, j, span, :] = (w * (weight_grad - row_delta)).astype(BF16)

        here = slice(0, nv * BLOCK)
        dv = jnp.dot(vert_w[j], gs[0, j], preferred_element_type=F32)
        dk = jnp.dot(low_ds[0, j, here, :], qs[0, j], preferred_element_type=F32) * scaling
        for kv, part in enumerate((dk, dv)):
            vertical_sum[kv] = part if j == 0 else vertical_sum[kv] + part

    first = core == 0
    keep = jnp.where(first, vertical_sum[0], vertical_sum[1])
    give = jnp.where(first, vertical_sum[1], vertical_sum[0])
    per_line = heads // 2
    for line in range(2):

        @pl.when(lax.rem(lax.div(h, per_line) + near, 2) == line)
        def _():
            for c in range(nv * BLOCK // chunk):
                slot = lax.rem(h, per_line) * (nv * BLOCK // chunk) + c
                slot = lax.rem(slot - far + lines.far, lines.far)
                span = slice(c * chunk, (c + 1) * chunk)
                shares[line][slot] = keep[span, :].astype(shares[line].dtype)
                shares[2 + line][slot] = give[span, :].astype(BF16)


def attend(slab_index, verticals, offsets, prepared, keys, values, gathered, recv, lines):
    heads, per_device, deep, head_dim = prepared[0].shape
    _, rows, features = keys.shape
    nv, ns = verticals.shape[1], offsets.shape[1]
    cand = nv + 1 + ns
    smem = pl.BlockSpec(memory_space=pltpu.SMEM)
    hbm = pl.BlockSpec(memory_space=pltpu.HBM)
    anywhere = pl.BlockSpec(memory_space=pl.ANY)

    def by_head(shape):
        return pl.BlockSpec((1,) + shape[1:], lambda h: (h,) + (0,) * (len(shape) - 1))

    def whole(shape):
        return pl.BlockSpec(shape, lambda h: (0,) * len(shape))

    share = (lines.far, heads * nv * BLOCK // (2 * lines.far), head_dim)
    low = (heads, per_device, cand * BLOCK, deep)
    low_tail = (heads, per_device, (1 + ns) * BLOCK, deep)
    cand_keys = (heads, per_device, cand * BLOCK, head_dim)
    return pl.pallas_call(
        functools.partial(
            attend_kernel, lines=lines, heads=heads, nv=nv, ns=ns, per_device=per_device
        ),
        grid=(heads,),
        in_specs=[smem] * 3
        + [by_head(array.shape) for array in prepared]
        + [hbm] * 2
        + [anywhere] * (4 + WDEV),
        out_specs=[whole(share)] * 4 + [by_head(low_tail), by_head(low), by_head(cand_keys)],
        out_shape=[
            jax.ShapeDtypeStruct(share, F32),
            jax.ShapeDtypeStruct(share, BF16),
            jax.ShapeDtypeStruct(share, BF16),
            jax.ShapeDtypeStruct(share, BF16),
            jax.ShapeDtypeStruct(low_tail, BF16),
            jax.ShapeDtypeStruct(low, BF16),
            jax.ShapeDtypeStruct(cand_keys, BF16),
        ],
        scratch_shapes=[
            pltpu.VMEM((2, (WDEV + 1) * rows, features), BF16),
            pltpu.VMEM((2, heads * nv * BLOCK, head_dim), BF16),
            pltpu.VMEM((per_device, cand * BLOCK, head_dim), BF16),
            pltpu.VMEM((per_device, cand * BLOCK, deep), F32),
            pltpu.VMEM((per_device, nv * BLOCK, deep), BF16),
            pltpu.SemaphoreType.DMA((WDEV + 2 + 4 * lines.far,)),
        ],
        compiler_params=pltpu.CompilerParams(vmem_limit_bytes=VMEM_LIMIT),
    )(slab_index, verticals, offsets, *prepared, keys, values, *gathered, *recv)


def window_kernel(offs, qs, gs, low_w, low_ds, home, *rest, lines, ns, per_device):
    parts, total = rest[:WDEV], rest[WDEV]
    h = pl.program_id(0)
    _, _, core = lines.place(lax.axis_index("ctx"))
    head_dim = qs.shape[3]
    rows = per_device * BLOCK
    scaling = 1.0 / math.sqrt(head_dim)
    lanes = pl.ds(pl.multiple_of(h * head_dim, head_dim), head_dim)
    total[...] = jnp.zeros_like(total)
    for j in range(per_device):
        dv = jnp.dot(low_w[0, j], gs[0, j], preferred_element_type=F32)
        dk = jnp.dot(low_ds[0, j], qs[0, j], preferred_element_type=F32) * scaling
        own_at = (WDEV * per_device + j) * BLOCK
        for kv, part in enumerate((dk, dv)):
            total[kv, own_at : own_at + BLOCK, :] += part[0:BLOCK]
            for s in range(ns):
                total[kv, pl.ds(slash_rows(offs, h, j, s, per_device), BLOCK), :] += part[
                    (1 + s) * BLOCK : (2 + s) * BLOCK
                ]
    for kv in range(2):
        home[kv, :, lanes] = total[kv, WDEV * rows :, :]
        for part, d in zip(parts, distances(core)):
            at = pl.multiple_of((WDEV - d) * rows, rows)
            part[kv, :, lanes] = total[kv, pl.ds(at, rows), :].astype(part.dtype)


def window_gradients(offsets, qs, gs, low_w, low_ds, lines, nv):
    heads, per_device, deep, head_dim = qs.shape
    ns = offsets.shape[1]
    rows, features = per_device * BLOCK, heads * head_dim
    shard = (2, rows, features)
    whole = pl.BlockSpec(shard, lambda h: (0, 0, 0))
    stacked = pl.BlockSpec((1,) + qs.shape[1:], lambda h: (h, 0, 0, 0))
    tail = (1 + ns) * BLOCK
    low_tail = pl.BlockSpec((1, per_device, tail, deep), lambda h: (h, 0, 0, 0))
    low = pl.BlockSpec(
        (1, per_device, tail, deep), lambda h: (h, 0, nv * BLOCK // tail, 0)
    )
    return pl.pallas_call(
        functools.partial(window_kernel, lines=lines, ns=ns, per_device=per_device),
        grid=(heads,),
        in_specs=[pl.BlockSpec(memory_space=pltpu.SMEM), stacked, stacked, low_tail, low],
        out_specs=[whole] * (1 + WDEV),
        out_shape=[jax.ShapeDtypeStruct(shard, F32)] * 3 + [jax.ShapeDtypeStruct(shard, BF16)] * 3,
        scratch_shapes=[pltpu.VMEM((2, (WDEV + 1) * rows, head_dim), F32)],
        compiler_params=pltpu.CompilerParams(vmem_limit_bytes=VMEM_LIMIT),
        cost_estimate=pl.CostEstimate(flops=0, bytes_accessed=9 << 20, transcendentals=0),
    )(offsets, qs, gs, low_w, low_ds)


def query_kernel(cand_keys, low_ds, dq):
    per_device, _, head_dim = cand_keys.shape[1:]
    scaling = 1.0 / math.sqrt(head_dim)
    for j in range(per_device):
        turned = lax.dot_general(
            cand_keys[0, j], low_ds[0, j], (((0,), (0,)), ((), ())), preferred_element_type=F32
        )
        stacked = (jnp.transpose(turned) * scaling).astype(BF16)
        for g in range(dq.shape[1] // head_dim):
            dq[j * BLOCK : (j + 1) * BLOCK, g * head_dim : (g + 1) * head_dim] = stacked[
                g * BLOCK : (g + 1) * BLOCK, :
            ]


def query_gradients(cand_keys, low_ds):
    heads, per_device, keys, head_dim = cand_keys.shape
    deep = low_ds.shape[3]
    rows, width = per_device * BLOCK, deep // BLOCK * head_dim

    def by_head(shape):
        return pl.BlockSpec((1,) + shape[1:], lambda h: (h, 0, 0, 0))

    return pl.pallas_call(
        query_kernel,
        grid=(heads,),
        in_specs=[by_head(cand_keys.shape), by_head(low_ds.shape)],
        out_specs=pl.BlockSpec((rows, width), lambda h: (0, h)),
        out_shape=jax.ShapeDtypeStruct((rows, heads * width), BF16),
        compiler_params=pltpu.CompilerParams(vmem_limit_bytes=VMEM_LIMIT),
        cost_estimate=pl.CostEstimate(flops=0, bytes_accessed=10 << 20, transcendentals=0),
    )(cand_keys, low_ds)


def zeros_kernel(_, key_out, value_out, blank, sems):
    blank[...] = jnp.zeros_like(blank)
    copies = [
        pltpu.make_async_copy(blank, out.at[r], sems.at[n, r])
        for n, out in enumerate((key_out, value_out))
        for r in range(out.shape[0])
    ]
    for copy in copies:
        copy.start()
    for copy in copies:
        copy.wait()


def zeros(ahead, shape):
    hbm = pl.BlockSpec(memory_space=pltpu.HBM)
    return pl.pallas_call(
        zeros_kernel,
        in_specs=[pl.BlockSpec(memory_space=pl.ANY)],
        out_specs=[hbm] * 2,
        out_shape=[jax.ShapeDtypeStruct(shape, BF16)] * 2,
        scratch_shapes=[pltpu.VMEM(shape[1:], BF16), pltpu.SemaphoreType.DMA((2, shape[0]))],
        compiler_params=pltpu.CompilerParams(vmem_limit_bytes=VMEM_LIMIT),
        cost_estimate=pl.CostEstimate(flops=0, bytes_accessed=5 << 20, transcendentals=0),
    )(ahead)


def assemble_kernel(slab_index, verts, home, *rest, lines, heads, nv, per_device):
    from_near, arrived, gathered = rest[0], rest[1:3], rest[3:7]
    outs, vert, acc, low, sems, out_sems, unit_sems = rest[9:11], *rest[11:]
    slab, me = slab_index[0], lax.axis_index("ctx")
    _, near, _ = lines.place(me)
    devices = lines.devices
    chunk, head_dim = gathered[0].shape[1:]
    slab_blocks = per_device * devices
    copies = vertical_copies(lines, me, chunk, gathered, vert, sems, 0)
    for copy in copies:
        copy.start()
    acc[0] = home[...]
    acc[1] = jnp.zeros_like(home)

    @pl.when(near == 0)
    def _():
        acc[0] += from_near[...].astype(F32)

    for part, wrapped in zip(arrived, wraps(me, devices)):
        acc[wrapped.astype(jnp.int32)] += part[...].astype(F32)
    for copy in copies:
        copy.wait()

    def unit(h, m):
        inner = lax.rem(verts[h, m], slab_blocks)
        region = lax.div(verts[h, m], slab_blocks)
        row = pl.multiple_of(lax.rem(inner, per_device) * BLOCK, BLOCK)
        close = (region == slab) | (region == slab - 1)
        return lax.div(inner, per_device) == me, close, region, row

    def unit_copies(h, m, region, row):
        at = (h * nv + m) * BLOCK
        for kv in range(2):
            yield pltpu.make_async_copy(
                vert.at[kv, pl.ds(at, BLOCK), :],
                outs[kv].at[region, pl.ds(row, BLOCK), pl.ds(h * head_dim, head_dim)],
                unit_sems.at[kv, h * nv + m],
            )

    for h in range(heads):
        lanes = slice(h * head_dim, (h + 1) * head_dim)
        for m in range(nv):
            mine, close, region, row = unit(h, m)
            at = (h * nv + m) * BLOCK

            @pl.when(mine & close)
            def _():
                for kv in range(2):
                    acc[slab - region, kv, pl.ds(row, BLOCK), lanes] += vert[
                        kv, at : at + BLOCK, :
                    ].astype(F32)

            @pl.when(mine & jnp.logical_not(close))
            def _():
                for copy in unit_copies(h, m, region, row):
                    copy.start()

    low[...] = acc[...].astype(BF16)
    copies = [
        pltpu.make_async_copy(low.at[n, kv], outs[kv].at[slab - n], out_sems.at[n, kv])
        for n in range(2)
        for kv in range(2)
    ]
    for copy in copies:
        copy.start()
    for h in range(heads):
        for m in range(nv):
            mine, close, region, row = unit(h, m)

            @pl.when(mine & jnp.logical_not(close))
            def _():
                for copy in unit_copies(h, m, region, row):
                    copy.wait()

    for copy in copies:
        copy.wait()


def assemble(slab_index, verticals, home, from_near, arrived, gathered, blank, lines):
    _, rows, features = home.shape
    heads, nv = verticals.shape
    smem = pl.BlockSpec(memory_space=pltpu.SMEM)
    vmem = pl.BlockSpec(memory_space=pltpu.VMEM)
    anywhere = pl.BlockSpec(memory_space=pl.ANY)
    hbm = pl.BlockSpec(memory_space=pltpu.HBM)
    return pl.pallas_call(
        functools.partial(
            assemble_kernel, lines=lines, heads=heads, nv=nv, per_device=rows // BLOCK
        ),
        in_specs=[smem] * 2 + [vmem] * 4 + [anywhere] * 4 + [hbm] * 2,
        out_specs=[hbm] * 2,
        out_shape=[jax.ShapeDtypeStruct(blank[0].shape, BF16)] * 2,
        input_output_aliases={10: 0, 11: 1},
        scratch_shapes=[
            pltpu.VMEM((2, heads * nv * BLOCK, features // heads), BF16),
            pltpu.VMEM((2, 2, rows, features), F32),
            pltpu.VMEM((2, 2, rows, features), BF16),
            pltpu.SemaphoreType.DMA((4 * lines.far,)),
            pltpu.SemaphoreType.DMA((2, 2)),
            pltpu.SemaphoreType.DMA((2, heads * nv)),
        ],
        compiler_params=pltpu.CompilerParams(vmem_limit_bytes=VMEM_LIMIT),
    )(slab_index, verticals, home, from_near, *arrived, *gathered, *blank)


def shards(
    queries,
    context_keys,
    context_values,
    forward_output,
    output_cotangent,
    verticals,
    offsets,
    slab_index,
):
    lines = Lines(lax.axis_size("ctx"))
    heads, nv = verticals.shape
    head_dim = context_keys.shape[2] // heads
    _, near, _ = lines.place(lax.axis_index("ctx"))

    own, send4, mixed, mine, to_near, to_core, to_both = pack(
        slab_index, verticals, context_keys, context_values, lines
    )
    recv4 = move(send4, lines.shift_pairs(4))
    to_near = core_sum(lines, to_near, to_both)
    quarter = near_sum(lines, mine, to_near, to_core)
    prepared = prepare(after(queries, to_near), output_cotangent, forward_output, heads, head_dim)
    quarter = after(quarter, recv4, *prepared)
    share = far_sum(lines, quarter)
    recv2 = move(jnp.where(near == 1, recv4, own), lines.near_pairs())
    other4 = move(recv4, lines.core_pairs())
    blank = zeros(share, context_keys.shape)
    gathered = far_gather(lines, after(share, other4))
    other2 = move(recv2, lines.core_pairs())
    gathered = after(gathered, other2, *blank)
    recv_mixed = move(after(mixed, gathered), lines.mixed_pairs())
    gathered = plane_gather(lines, gathered)

    *shares, low_w, low_ds, cand_keys = attend(
        slab_index, verticals, offsets, prepared, context_keys, context_values, gathered,
        [recv2, recv4, recv_mixed, other2, other4], lines,
    )

    mine, to_near, to_core, to_both = shares
    to_near = core_sum(lines, to_near, to_both)
    home, part2, part4, mixed, give2, give4 = window_gradients(
        after(offsets, to_near), prepared[0], prepared[1], low_w, low_ds, lines, nv
    )
    arrived_mixed = move(mixed, back(lines.mixed_pairs()))
    quarter = near_sum(lines, mine, to_near, to_core)
    quarter = after(quarter, home)
    sum2 = (part2 + move(give2, lines.core_pairs()).astype(F32)).astype(BF16)
    sum4 = part4 + move(give4, lines.core_pairs()).astype(F32)
    from_near = move(after(sum2, quarter), lines.near_pairs())
    share = far_sum(lines, quarter)
    totals = after(far_gather(lines, share), from_near, arrived_mixed)
    sum4 = (sum4 + jnp.where(near == 1, from_near.astype(F32), 0.0)).astype(BF16)
    arrived4 = move(after(sum4, totals), back(lines.shift_pairs(4)))
    query_grad = query_gradients(after(cand_keys, totals), low_ds)
    totals = plane_gather(lines, totals)
    key_gradient, value_gradient = assemble(
        slab_index, verticals, after(home, query_grad), from_near, (arrived4, arrived_mixed),
        totals, blank, lines,
    )
    return query_grad, key_gradient, value_gradient


def solution(mesh):
    in_specs = (
        P(("groups", "ctx"), None),
        P("groups", "ctx", None),
        P("groups", "ctx", None),
        P(("groups", "ctx"), None),
        P(("groups", "ctx"), None),
        P("groups", None),
        P("groups", None),
        P("groups"),
    )
    out_specs = (P(("groups", "ctx"), None), P("groups", "ctx", None), P("groups", "ctx", None))
    return jax.shard_map(shards, mesh=mesh, in_specs=in_specs, out_specs=out_specs, check_vma=False)
```

```python
import functools
import math

import jax
import jax.numpy as jnp
from jax import lax
from jax.experimental import pallas as pl
from jax.experimental.pallas import tpu as pltpu
from jax.sharding import PartitionSpec as P

BLOCK = 64
WDEV = 5
VMEM_LIMIT = 32 * 1024 * 1024
PACK_VMEM = 52 * 1024 * 1024
JOIN = 4
BF16 = jnp.bfloat16
F32 = jnp.float32


class Lines:
    def __init__(self, devices):
        self.devices = devices
        self.far = devices // 4

    def place(self, me):
        return lax.div(me, 4), lax.rem(lax.div(me, 2), 2), lax.rem(me, 2)

    def core_pairs(self):
        return [(i, i ^ 1) for i in range(self.devices)]

    def near_pairs(self):
        return [(i, i ^ 2) for i in range(self.devices)]

    def both_pairs(self):
        return [(i, i ^ 3) for i in range(self.devices)]

    def far_pairs(self, by):
        return [(i, (i + 4 * by) % self.devices) for i in range(self.devices)]

    def shift_pairs(self, by):
        return [(i, (i + by) % self.devices) for i in range(self.devices)]

    def mixed_pairs(self):
        return [(i, (i + (5 if i % 2 else 1)) % self.devices) for i in range(self.devices)]


def back(pairs):
    return [(b, a) for a, b in pairs]


def move(array, pairs):
    return lax.ppermute(array, "ctx", pairs)


def after(array, *others):
    return lax.optimization_barrier((array, *others))[0]


def core_sum(lines, to_near, to_both):
    return (to_near.astype(F32) + move(to_both, lines.core_pairs()).astype(F32)).astype(BF16)


def near_sum(lines, mine, from_near, to_core):
    from_core = move(to_core, lines.core_pairs())
    return mine.astype(F32) + from_core.astype(F32) + from_near.astype(F32)


def far_sum(lines, quarter):
    parts = [
        move(quarter[by].astype(BF16), lines.far_pairs(by)) for by in range(1, lines.far)
    ]
    share = quarter[0]
    for part in parts:
        share = share + part.astype(F32)
    return share.astype(BF16)


def far_gather(lines, share):
    parts = [share] + [move(share, lines.far_pairs(by)) for by in range(1, lines.far)]
    return jnp.stack(parts)


def plane_gather(lines, mine):
    across = move(mine, lines.near_pairs())
    core_mine = move(mine, lines.core_pairs())
    core_across = move(across, lines.core_pairs())
    return mine, across, core_mine, core_across


def wraps(me, devices):
    return [me + 4 >= devices, (lax.rem(me, 2) == 1) & (me + 5 >= devices)]


def pack_kernel(slab_index, verts, keys, values, *rest, lines, heads, nv, per_device):
    sends = rest[:3]
    shares = rest[3:7]
    picked, sems, pick_sems = rest[7:]
    slab, me = slab_index[0], lax.axis_index("ctx")
    far, near, core = lines.place(me)
    _, chunk, head_dim = shares[0].shape
    copies = []
    wrapped4, wrapped_mixed = wraps(me, lines.devices)
    for n, region in enumerate(
        (slab, slab - wrapped4.astype(jnp.int32), slab - wrapped_mixed.astype(jnp.int32))
    ):
        for kv, source in enumerate((keys, values)):
            copy = pltpu.make_async_copy(source.at[region], sends[n].at[kv], sems.at[n, kv])
            copy.start()
            copies.append(copy)
    picked[...] = jnp.zeros_like(picked)
    slab_blocks = per_device * lines.devices
    piece = min(BLOCK, chunk)

    def unit_copies(h, m):
        inner = lax.rem(verts[h, m], slab_blocks)
        region = lax.div(verts[h, m], slab_blocks)
        row = lax.rem(inner, per_device) * BLOCK
        for p in range(BLOCK // piece):
            at = (h * nv + m) * BLOCK + p * piece
            line, at = at // (lines.far * chunk), at % (lines.far * chunk)
            slot, at = at // chunk, at % chunk
            line = lax.rem(line + near, 2)
            slot = lax.rem(slot - far + lines.far, lines.far)
            for kv, source in enumerate((keys, values)):
                yield pltpu.make_async_copy(
                    source.at[
                        region,
                        pl.ds(pl.multiple_of(row + p * piece, piece), piece),
                        pl.ds(h * head_dim, head_dim),
                    ],
                    picked.at[lax.rem(kv + core, 2), line, slot, pl.ds(at, piece), :],
                    pick_sems.at[kv, (h * nv + m) * (BLOCK // piece) + p],
                )

    def owned(h, m):
        return lax.div(lax.rem(verts[h, m], slab_blocks), per_device) == me

    for h in range(heads):
        for m in range(nv):

            @pl.when(owned(h, m))
            def _():
                for copy in unit_copies(h, m):
                    copy.start()

    for h in range(heads):
        for m in range(nv):

            @pl.when(owned(h, m))
            def _():
                for copy in unit_copies(h, m):
                    copy.wait()

    for n, share in enumerate(shares):
        share[...] = picked[n // 2, n % 2]
    for copy in copies:
        copy.wait()


def pack(slab_index, verticals, keys, values, lines):
    regions, rows, features = keys.shape
    heads, nv = verticals.shape
    head_dim = features // heads
    chunk = heads * nv * BLOCK // (2 * lines.far)
    smem = pl.BlockSpec(memory_space=pltpu.SMEM)
    hbm = pl.BlockSpec(memory_space=pltpu.HBM)
    share = (lines.far, chunk, head_dim)
    return pl.pallas_call(
        functools.partial(pack_kernel, lines=lines, heads=heads, nv=nv, per_device=rows // BLOCK),
        in_specs=[smem, smem, hbm, hbm],
        out_specs=[pl.BlockSpec(memory_space=pltpu.VMEM)] * 7,
        out_shape=[jax.ShapeDtypeStruct((2, rows, features), BF16)] * 3
        + [jax.ShapeDtypeStruct(share, BF16)] * 4,
        scratch_shapes=[
            pltpu.VMEM((2, 2) + share, BF16),
            pltpu.SemaphoreType.DMA((3, 2)),
            pltpu.SemaphoreType.DMA((2, heads * nv * max(1, BLOCK // chunk))),
        ],
        compiler_params=pltpu.CompilerParams(vmem_limit_bytes=PACK_VMEM),
    )(slab_index, verticals, keys, values)


def distances(core):
    return [2, 4, 5 - 4 * core, 1 + 2 * core, 3 + 2 * core]


def vertical_copies(lines, me, line, chunk, gathered, to, sems, first):
    far, _, core = lines.place(me)
    copies = []
    for kv, source in zip((core, 1 - core), gathered):
        for s in range(lines.far):
            slot = lax.rem(far - s + lines.far, lines.far)
            row = pl.multiple_of((line * lines.far + slot) * chunk, chunk)
            copies.append(
                pltpu.make_async_copy(
                    source.at[s], to.at[kv, pl.ds(row, chunk), :], sems.at[first + len(copies)]
                )
            )
    return copies


NT = (((1,), (1,)), ((), ()))


def prepare_kernel(q, grad, out, qs, gs, qt, gt, delta, *, head_dim):
    per_device = qs.shape[1]
    group = q.shape[1] // head_dim
    ones = jnp.ones((8, 2 * head_dim), BF16)
    for j in range(per_device):
        rows = slice(j * BLOCK, (j + 1) * BLOCK)
        split = []
        for g in range(group):
            cols = slice(g * head_dim, (g + 1) * head_dim)
            here = slice(g * BLOCK, (g + 1) * BLOCK)
            qs[0, j, here, :] = q[rows, cols]
            gs[0, j, here, :] = grad[rows, cols]
            product = grad[rows, cols].astype(F32) * out[rows, cols].astype(F32)
            upper = product.astype(BF16)
            lower = (product - upper.astype(F32)).astype(BF16)
            split.append(jnp.concatenate([upper, lower], axis=1))
        qt[0, j] = jnp.transpose(qs[0, j])
        gt[0, j] = jnp.transpose(gs[0, j])
        delta[0, j] = lax.dot_general(
            ones, jnp.concatenate(split, axis=0), NT, preferred_element_type=F32
        )


def prepare(queries, cotangent, output, heads, head_dim):
    rows, width = queries.shape
    per_device = rows // BLOCK
    deep = width // heads // head_dim * BLOCK
    tile = pl.BlockSpec((rows, width // heads), lambda h: (0, h))

    def by_head(*shape):
        return pl.BlockSpec((1,) + shape, lambda h: (h,) + (0,) * len(shape))

    stacked = (per_device, deep, head_dim)
    turned = (per_device, head_dim, deep)
    sums = (per_device, 8, deep)
    return pl.pallas_call(
        functools.partial(prepare_kernel, head_dim=head_dim),
        grid=(heads,),
        in_specs=[tile] * 3,
        out_specs=[by_head(*stacked)] * 2 + [by_head(*turned)] * 2 + [by_head(*sums)],
        out_shape=[jax.ShapeDtypeStruct((heads,) + stacked, BF16)] * 2
        + [jax.ShapeDtypeStruct((heads,) + turned, BF16)] * 2
        + [jax.ShapeDtypeStruct((heads,) + sums, F32)],
        compiler_params=pltpu.CompilerParams(vmem_limit_bytes=VMEM_LIMIT),
        cost_estimate=pl.CostEstimate(flops=0, bytes_accessed=7 << 20, transcendentals=0),
    )(queries, cotangent, output)


def slash_rows(offs, h, j, s, per_device):
    return pl.multiple_of((WDEV * per_device + j - offs[h, s]) * BLOCK, BLOCK)


def attend_kernel(
    base, slab_index, verts, offs, qs, gs, qt, gt, delta, keys, values, *rest,
    lines, nv, ns, per_device, continued,
):
    gathered, recv, rest = rest[:2], rest[2 : 2 + WDEV], rest[2 + WDEV :]
    rest = rest[3:] if continued else rest
    (share, give, low_w, low_ds, cand_keys), scratch = rest[:5], rest[5:]
    win, vkv, vc, s_ref, vert_w, hold, sems = scratch
    i = pl.program_id(0)
    h = base[0] + i
    slab, me = slab_index[0], lax.axis_index("ctx")
    far, near, core = lines.place(me)
    _, chunk, head_dim = share.shape
    cand = nv + 1 + ns
    scaling = 1.0 / math.sqrt(head_dim)
    rows = per_device * BLOCK
    width = qs.shape[2]
    first_block = slab * (per_device * lines.devices) + me * per_device
    lanes = pl.ds(pl.multiple_of(i * head_dim, head_dim), head_dim)

    def window_row(d):
        return pl.multiple_of((WDEV - d) * rows, rows)

    @pl.when(i == 0)
    def _():
        half = win.shape[2]
        own_rows = pl.ds(WDEV * rows, rows)
        side = pl.ds(pl.multiple_of(base[0] * head_dim, half), half)
        copies = [
            pltpu.make_async_copy(
                recv[n].at[:, :, side], win.at[:, pl.ds(window_row(d), rows), :], sems.at[n]
            )
            for n, d in enumerate(distances(core))
        ]
        for kv, source in enumerate((keys, values)):
            copies.append(
                pltpu.make_async_copy(
                    source.at[slab, :, side], win.at[kv, own_rows, :], sems.at[WDEV + kv]
                )
            )
        copies += vertical_copies(lines, me, 0, chunk, gathered, vkv, sems, WDEV + 2)
        for copy in copies:
            copy.start()
        for copy in copies:
            copy.wait()

    vert_rows = pl.ds(pl.multiple_of(i * (nv * BLOCK), nv * BLOCK), nv * BLOCK)
    neg, posinf = jnp.float32(-jnp.inf), jnp.float32(jnp.inf)
    log2_scale = scaling * math.log2(math.e)
    key_at = lax.broadcasted_iota(jnp.int32, (BLOCK, width), 0)
    row_at = lax.broadcasted_iota(jnp.int32, (BLOCK, width), 1) % BLOCK

    def fold(x, op):
        y = x[0:8, :]
        for r in range(1, BLOCK // 8):
            y = op(y, x[r * 8 : (r + 1) * 8, :])
        return y

    vertical_sum = [None, None]
    for j in range(per_device):
        block = first_block + j
        own_at = (WDEV * per_device + j) * BLOCK
        valid = [verts[h, m] < block for m in range(nv)] + [None]
        for s in range(ns):
            collide = verts[h, 0] == block - offs[h, s]
            for m in range(1, nv):
                collide = collide | (verts[h, m] == block - offs[h, s])
            valid.append((offs[h, s] > 0) & jnp.logical_not(collide))
        for kv, to in enumerate((cand_keys.at[0], vc)):
            to[j, 0 : nv * BLOCK, :] = vkv[kv, vert_rows, :]
            to[j, nv * BLOCK : (nv + 1) * BLOCK, :] = win[kv, own_at : own_at + BLOCK, lanes]
            for s in range(ns):
                to[j, (nv + 1 + s) * BLOCK : (nv + 2 + s) * BLOCK, :] = win[
                    kv, pl.ds(slash_rows(offs, h, j, s, per_device), BLOCK), lanes
                ]

        top = None
        for n in range(cand // JOIN):
            span = slice(n * JOIN * BLOCK, (n + 1) * JOIN * BLOCK)
            scores = jnp.dot(cand_keys[0, j, span, :], qt[0, j], preferred_element_type=F32)
            for k in range(JOIN):
                c = n * JOIN + k
                part = scores[k * BLOCK : (k + 1) * BLOCK, :]
                if c == nv:
                    part = jnp.where(key_at <= row_at, part, neg)
                s_ref[j, c * BLOCK : (c + 1) * BLOCK, :] = part
                best = fold(part, jnp.maximum)
                if c != nv:
                    best = best + jnp.where(valid[c], jnp.float32(0), neg)
                top = best if top is None else jnp.maximum(top, best)
        top = jnp.max(top, axis=0, keepdims=True) * log2_scale
        total = jnp.zeros((8, width), F32)
        for c in range(cand):
            span = slice(c * BLOCK, (c + 1) * BLOCK)
            less = top if c == nv else top + jnp.where(valid[c], jnp.float32(0), posinf)
            p = jnp.exp2(s_ref[j, span, :] * log2_scale - less)
            s_ref[j, span, :] = p
            total = total + fold(p, jnp.add)
        inverse = 1.0 / jnp.sum(total, axis=0, keepdims=True)
        row_delta = delta[0, j, 0:1, :]
        for n in range(cand // JOIN):
            span = slice(n * JOIN * BLOCK, (n + 1) * JOIN * BLOCK)
            weight_grad = jnp.dot(vc[j, span, :], gt[0, j], preferred_element_type=F32)
            w = s_ref[j, span, :] * inverse
            if n * JOIN < nv:
                vert_w[j, span, :] = w.astype(BF16)
            else:
                low_w[0, j] = w.astype(BF16)
            low_ds[0, j, span, :] = (w * (weight_grad - row_delta)).astype(BF16)

        here = slice(0, nv * BLOCK)
        dv = jnp.dot(vert_w[j], gs[0, j], preferred_element_type=F32)
        dk = jnp.dot(low_ds[0, j, here, :], qs[0, j], preferred_element_type=F32) * scaling
        for kv, part in enumerate((dk, dv)):
            vertical_sum[kv] = part if j == 0 else vertical_sum[kv] + part

    first = core == 0
    parts = (
        jnp.where(first, vertical_sum[0], vertical_sum[1]),
        jnp.where(first, vertical_sum[1], vertical_sum[0]),
    )
    for c in range(nv * BLOCK // chunk):
        slot = lax.rem(i * (nv * BLOCK // chunk) + c - far + lines.far, lines.far)
        for n, part in enumerate(parts):
            hold[n, slot] = part[c * chunk : (c + 1) * chunk, :]

    @pl.when(i == pl.num_programs(0) - 1)
    def _():
        share[...] = hold[0].astype(share.dtype)
        give[...] = hold[1].astype(give.dtype)


def attend(base, slab_index, verticals, offsets, prepared, keys, values, gathered, recv, lines, lows):
    heads, per_device, deep, head_dim = prepared[0].shape
    _, rows, features = keys.shape
    nv, ns = verticals.shape[1], offsets.shape[1]
    cand = nv + 1 + ns
    half = heads // 2
    hbm = pl.BlockSpec(memory_space=pltpu.HBM)
    anywhere = pl.BlockSpec(memory_space=pl.ANY)

    def by_head(shape):
        return pl.BlockSpec(
            (1,) + shape[1:], lambda i, base, *_: (base[0] + i,) + (0,) * (len(shape) - 1)
        )

    share = (lines.far, half * nv * BLOCK // lines.far, head_dim)
    shares = pl.BlockSpec(share, lambda i, *_: (0, 0, 0))
    low_shapes = [
        (heads, per_device, (1 + ns) * BLOCK, deep),
        (heads, per_device, cand * BLOCK, deep),
        (heads, per_device, cand * BLOCK, head_dim),
    ]
    before = 4 + len(prepared) + 2 + 2 + WDEV
    return pl.pallas_call(
        functools.partial(
            attend_kernel, lines=lines, nv=nv, ns=ns, per_device=per_device, continued=bool(lows)
        ),
        grid_spec=pltpu.PrefetchScalarGridSpec(
            num_scalar_prefetch=4,
            grid=(half,),
            in_specs=[by_head(array.shape) for array in prepared]
            + [hbm] * 2
            + [anywhere] * (2 + WDEV + len(lows)),
            out_specs=[shares] * 2 + [by_head(shape) for shape in low_shapes],
            scratch_shapes=[
                pltpu.VMEM((2, (WDEV + 1) * rows, features // 2), BF16),
                pltpu.VMEM((2, half * nv * BLOCK, head_dim), BF16),
                pltpu.VMEM((per_device, cand * BLOCK, head_dim), BF16),
                pltpu.VMEM((per_device, cand * BLOCK, deep), F32),
                pltpu.VMEM((per_device, nv * BLOCK, deep), BF16),
                pltpu.VMEM((2,) + share, F32),
                pltpu.SemaphoreType.DMA((WDEV + 2 + 2 * lines.far,)),
            ],
        ),
        out_shape=[
            jax.ShapeDtypeStruct(share, F32 if lows else BF16),
            jax.ShapeDtypeStruct(share, BF16),
        ]
        + [jax.ShapeDtypeStruct(shape, BF16) for shape in low_shapes],
        input_output_aliases={before + n: 2 + n for n in range(len(lows))},
        compiler_params=pltpu.CompilerParams(vmem_limit_bytes=VMEM_LIMIT),
        cost_estimate=pl.CostEstimate(
            flops=2 * 5 * half * per_device * cand * BLOCK * deep * head_dim,
            bytes_accessed=12 << 20,
            transcendentals=half * per_device * cand * BLOCK * deep,
        ),
    )(base, slab_index, verticals, offsets, *prepared, keys, values, *gathered, *recv, *lows)


def window_kernel(offs, qs, gs, low_w, low_ds, home, *rest, lines, ns, per_device):
    parts, total = rest[:WDEV], rest[WDEV]
    h = pl.program_id(0)
    _, _, core = lines.place(lax.axis_index("ctx"))
    head_dim = qs.shape[3]
    rows = per_device * BLOCK
    scaling = 1.0 / math.sqrt(head_dim)
    lanes = pl.ds(pl.multiple_of(h * head_dim, head_dim), head_dim)
    total[...] = jnp.zeros_like(total)
    for j in range(per_device):
        dv = jnp.dot(low_w[0, j], gs[0, j], preferred_element_type=F32)
        dk = jnp.dot(low_ds[0, j], qs[0, j], preferred_element_type=F32) * scaling
        own_at = (WDEV * per_device + j) * BLOCK
        for kv, part in enumerate((dk, dv)):
            total[kv, own_at : own_at + BLOCK, :] += part[0:BLOCK]
            for s in range(ns):
                total[kv, pl.ds(slash_rows(offs, h, j, s, per_device), BLOCK), :] += part[
                    (1 + s) * BLOCK : (2 + s) * BLOCK
                ]
    for kv in range(2):
        home[kv, :, lanes] = total[kv, WDEV * rows :, :]
        for part, d in zip(parts, distances(core)):
            at = pl.multiple_of((WDEV - d) * rows, rows)
            part[kv, :, lanes] = total[kv, pl.ds(at, rows), :].astype(part.dtype)


def window_gradients(offsets, qs, gs, low_w, low_ds, lines, nv):
    heads, per_device, deep, head_dim = qs.shape
    ns = offsets.shape[1]
    rows, features = per_device * BLOCK, heads * head_dim
    shard = (2, rows, features)
    whole = pl.BlockSpec(shard, lambda h: (0, 0, 0))
    stacked = pl.BlockSpec((1,) + qs.shape[1:], lambda h: (h, 0, 0, 0))
    tail = (1 + ns) * BLOCK
    low_tail = pl.BlockSpec((1, per_device, tail, deep), lambda h: (h, 0, 0, 0))
    low = pl.BlockSpec(
        (1, per_device, tail, deep), lambda h: (h, 0, nv * BLOCK // tail, 0)
    )
    return pl.pallas_call(
        functools.partial(window_kernel, lines=lines, ns=ns, per_device=per_device),
        grid=(heads,),
        in_specs=[pl.BlockSpec(memory_space=pltpu.SMEM), stacked, stacked, low_tail, low],
        out_specs=[whole] * (1 + WDEV),
        out_shape=[jax.ShapeDtypeStruct(shard, F32)] * 3 + [jax.ShapeDtypeStruct(shard, BF16)] * 3,
        scratch_shapes=[pltpu.VMEM((2, (WDEV + 1) * rows, head_dim), F32)],
        compiler_params=pltpu.CompilerParams(vmem_limit_bytes=VMEM_LIMIT),
        cost_estimate=pl.CostEstimate(flops=0, bytes_accessed=9 << 20, transcendentals=0),
    )(offsets, qs, gs, low_w, low_ds)


def query_kernel(cand_keys, low_ds, dq):
    per_device, _, head_dim = cand_keys.shape[1:]
    scaling = 1.0 / math.sqrt(head_dim)
    for j in range(per_device):
        turned = lax.dot_general(
            cand_keys[0, j], low_ds[0, j], (((0,), (0,)), ((), ())), preferred_element_type=F32
        )
        stacked = (jnp.transpose(turned) * scaling).astype(BF16)
        for g in range(dq.shape[1] // head_dim):
            dq[j * BLOCK : (j + 1) * BLOCK, g * head_dim : (g + 1) * head_dim] = stacked[
                g * BLOCK : (g + 1) * BLOCK, :
            ]


def query_gradients(cand_keys, low_ds):
    heads, per_device, keys, head_dim = cand_keys.shape
    deep = low_ds.shape[3]
    rows, width = per_device * BLOCK, deep // BLOCK * head_dim

    def by_head(shape):
        return pl.BlockSpec((1,) + shape[1:], lambda h: (h, 0, 0, 0))

    return pl.pallas_call(
        query_kernel,
        grid=(heads,),
        in_specs=[by_head(cand_keys.shape), by_head(low_ds.shape)],
        out_specs=pl.BlockSpec((rows, width), lambda h: (0, h)),
        out_shape=jax.ShapeDtypeStruct((rows, heads * width), BF16),
        compiler_params=pltpu.CompilerParams(vmem_limit_bytes=VMEM_LIMIT),
        cost_estimate=pl.CostEstimate(flops=0, bytes_accessed=10 << 20, transcendentals=0),
    )(cand_keys, low_ds)


def zeros_kernel(_, key_out, value_out, blank, sems):
    blank[...] = jnp.zeros_like(blank)
    copies = [
        pltpu.make_async_copy(blank, out.at[r], sems.at[n, r])
        for n, out in enumerate((key_out, value_out))
        for r in range(out.shape[0])
    ]
    for copy in copies:
        copy.start()
    for copy in copies:
        copy.wait()


def zeros(ahead, shape):
    hbm = pl.BlockSpec(memory_space=pltpu.HBM)
    return pl.pallas_call(
        zeros_kernel,
        in_specs=[pl.BlockSpec(memory_space=pl.ANY)],
        out_specs=[hbm] * 2,
        out_shape=[jax.ShapeDtypeStruct(shape, BF16)] * 2,
        scratch_shapes=[pltpu.VMEM(shape[1:], BF16), pltpu.SemaphoreType.DMA((2, shape[0]))],
        compiler_params=pltpu.CompilerParams(vmem_limit_bytes=VMEM_LIMIT),
        cost_estimate=pl.CostEstimate(flops=0, bytes_accessed=5 << 20, transcendentals=0),
    )(ahead)


def assemble_kernel(slab_index, verts, home, *rest, lines, heads, nv, per_device):
    from_near, arrived, gathered = rest[0], rest[1:3], rest[3:7]
    outs, vert, acc, low, sems, out_sems, unit_sems = rest[9:11], *rest[11:]
    slab, me = slab_index[0], lax.axis_index("ctx")
    _, near, _ = lines.place(me)
    devices = lines.devices
    chunk, head_dim = gathered[0].shape[1:]
    slab_blocks = per_device * devices
    copies = vertical_copies(lines, me, 1 - near, chunk, gathered[0::2], vert, sems, 0)
    copies += vertical_copies(lines, me, near, chunk, gathered[1::2], vert, sems, 2 * lines.far)
    for copy in copies:
        copy.start()
    acc[0] = home[...]
    acc[1] = jnp.zeros_like(home)

    @pl.when(near == 0)
    def _():
        acc[0] += from_near[...].astype(F32)

    for part, wrapped in zip(arrived, wraps(me, devices)):
        acc[wrapped.astype(jnp.int32)] += part[...].astype(F32)
    for copy in copies:
        copy.wait()

    def unit(h, m):
        inner = lax.rem(verts[h, m], slab_blocks)
        region = lax.div(verts[h, m], slab_blocks)
        row = pl.multiple_of(lax.rem(inner, per_device) * BLOCK, BLOCK)
        close = (region == slab) | (region == slab - 1)
        return lax.div(inner, per_device) == me, close, region, row

    def unit_copies(h, m, region, row):
        at = (h * nv + m) * BLOCK
        for kv in range(2):
            yield pltpu.make_async_copy(
                vert.at[kv, pl.ds(at, BLOCK), :],
                outs[kv].at[region, pl.ds(row, BLOCK), pl.ds(h * head_dim, head_dim)],
                unit_sems.at[kv, h * nv + m],
            )

    for h in range(heads):
        lanes = slice(h * head_dim, (h + 1) * head_dim)
        for m in range(nv):
            mine, close, region, row = unit(h, m)
            at = (h * nv + m) * BLOCK

            @pl.when(mine & close)
            def _():
                for kv in range(2):
                    acc[slab - region, kv, pl.ds(row, BLOCK), lanes] += vert[
                        kv, at : at + BLOCK, :
                    ].astype(F32)

            @pl.when(mine & jnp.logical_not(close))
            def _():
                for copy in unit_copies(h, m, region, row):
                    copy.start()

    low[...] = acc[...].astype(BF16)
    copies = [
        pltpu.make_async_copy(low.at[n, kv], outs[kv].at[slab - n], out_sems.at[n, kv])
        for n in range(2)
        for kv in range(2)
    ]
    for copy in copies:
        copy.start()
    for h in range(heads):
        for m in range(nv):
            mine, close, region, row = unit(h, m)

            @pl.when(mine & jnp.logical_not(close))
            def _():
                for copy in unit_copies(h, m, region, row):
                    copy.wait()

    for copy in copies:
        copy.wait()


def assemble(slab_index, verticals, home, from_near, arrived, gathered, blank, lines):
    _, rows, features = home.shape
    heads, nv = verticals.shape
    smem = pl.BlockSpec(memory_space=pltpu.SMEM)
    vmem = pl.BlockSpec(memory_space=pltpu.VMEM)
    anywhere = pl.BlockSpec(memory_space=pl.ANY)
    hbm = pl.BlockSpec(memory_space=pltpu.HBM)
    return pl.pallas_call(
        functools.partial(
            assemble_kernel, lines=lines, heads=heads, nv=nv, per_device=rows // BLOCK
        ),
        in_specs=[smem] * 2 + [vmem] * 4 + [anywhere] * 4 + [hbm] * 2,
        out_specs=[hbm] * 2,
        out_shape=[jax.ShapeDtypeStruct(blank[0].shape, BF16)] * 2,
        input_output_aliases={10: 0, 11: 1},
        scratch_shapes=[
            pltpu.VMEM((2, heads * nv * BLOCK, features // heads), BF16),
            pltpu.VMEM((2, 2, rows, features), F32),
            pltpu.VMEM((2, 2, rows, features), BF16),
            pltpu.SemaphoreType.DMA((4 * lines.far,)),
            pltpu.SemaphoreType.DMA((2, 2)),
            pltpu.SemaphoreType.DMA((2, heads * nv)),
        ],
        compiler_params=pltpu.CompilerParams(vmem_limit_bytes=VMEM_LIMIT),
    )(slab_index, verticals, home, from_near, *arrived, *gathered, *blank)


def shards(
    queries,
    context_keys,
    context_values,
    forward_output,
    output_cotangent,
    verticals,
    offsets,
    slab_index,
):
    lines = Lines(lax.axis_size("ctx"))
    heads, nv = verticals.shape
    head_dim = context_keys.shape[2] // heads
    _, near, _ = lines.place(lax.axis_index("ctx"))

    own, send4, mixed, mine, to_near, to_core, to_both = pack(
        slab_index, verticals, context_keys, context_values, lines
    )
    recv4 = move(send4, lines.shift_pairs(4))
    to_near = core_sum(lines, to_near, to_both)
    quarter = near_sum(lines, mine, move(to_near, lines.near_pairs()), to_core)
    prepared = prepare(after(queries, to_near), output_cotangent, forward_output, heads, head_dim)
    quarter = after(quarter, recv4, *prepared)
    share = far_sum(lines, quarter)
    recv_mixed = move(after(mixed, quarter), lines.mixed_pairs())
    recv2 = move(jnp.where(near == 1, recv4, own), lines.near_pairs())
    other4 = move(recv4, lines.core_pairs())
    blank = zeros(share, context_keys.shape)
    gathered = far_gather(lines, after(share, other4))
    other2 = move(recv2, lines.core_pairs())
    gathered = after(gathered, other2, recv_mixed, *blank)
    gathered = plane_gather(lines, gathered)
    recv = [recv2, recv4, recv_mixed, other2, other4]

    def attend_line(line, gathered, lows):
        base = (line * (heads // 2)).astype(jnp.int32).reshape(1)
        return attend(
            base, slab_index, verticals, offsets, prepared, context_keys, context_values,
            gathered, recv, lines, lows,
        )

    to_near, to_both, *lows = attend_line(near, gathered[0::2], ())
    to_near = core_sum(lines, to_near, to_both)
    from_near = move(to_near, lines.near_pairs())
    mine, to_core, low_w, low_ds, cand_keys = attend_line(1 - near, gathered[1::2], lows)

    home, part2, part4, mixed, give2, give4 = window_gradients(
        after(offsets, from_near), prepared[0], prepared[1], low_w, low_ds, lines, nv
    )
    quarter = after(near_sum(lines, mine, from_near, to_core), home)
    share = far_sum(lines, quarter)
    arrived_mixed = move(mixed, back(lines.mixed_pairs()))
    sum2 = (part2 + move(give2, lines.core_pairs()).astype(F32)).astype(BF16)
    sum4 = part4 + move(give4, lines.core_pairs()).astype(F32)
    from_near = move(sum2, lines.near_pairs())
    totals = after(far_gather(lines, share), from_near, arrived_mixed)
    sum4 = (sum4 + jnp.where(near == 1, from_near.astype(F32), 0.0)).astype(BF16)
    arrived4 = move(after(sum4, totals), back(lines.shift_pairs(4)))
    query_grad = query_gradients(after(cand_keys, totals), low_ds)
    totals = plane_gather(lines, totals)
    key_gradient, value_gradient = assemble(
        slab_index, verticals, after(home, query_grad), from_near, (arrived4, arrived_mixed),
        totals, blank, lines,
    )
    return query_grad, key_gradient, value_gradient


def solution(mesh):
    in_specs = (
        P(("groups", "ctx"), None),
        P("groups", "ctx", None),
        P("groups", "ctx", None),
        P(("groups", "ctx"), None),
        P(("groups", "ctx"), None),
        P("groups", None),
        P("groups", None),
        P("groups"),
    )
    out_specs = (P(("groups", "ctx"), None), P("groups", "ctx", None), P("groups", "ctx", None))
    return jax.shard_map(shards, mesh=mesh, in_specs=in_specs, out_specs=out_specs, check_vma=False)
```

```python
import functools
import math

import jax
import jax.numpy as jnp
from jax import lax
from jax.experimental import pallas as pl
from jax.experimental.pallas import tpu as pltpu
from jax.sharding import PartitionSpec as P

BLOCK = 64
WDEV = 5
VMEM_LIMIT = 20 * 1024 * 1024
PACK_VMEM = 60 * 1024 * 1024
JOIN = 4
BF16 = jnp.bfloat16
F32 = jnp.float32


class Lines:
    def __init__(self, devices):
        self.devices = devices
        self.far = devices // 4

    def place(self, me):
        return lax.div(me, 4), lax.rem(lax.div(me, 2), 2), lax.rem(me, 2)

    def core_pairs(self):
        return [(i, i ^ 1) for i in range(self.devices)]

    def near_pairs(self):
        return [(i, i ^ 2) for i in range(self.devices)]

    def both_pairs(self):
        return [(i, i ^ 3) for i in range(self.devices)]

    def far_pairs(self, by):
        return [(i, (i + 4 * by) % self.devices) for i in range(self.devices)]

    def shift_pairs(self, by):
        return [(i, (i + by) % self.devices) for i in range(self.devices)]

    def mixed_pairs(self):
        return [(i, (i + (5 if i % 2 else 1)) % self.devices) for i in range(self.devices)]


def back(pairs):
    return [(b, a) for a, b in pairs]


def move(array, pairs):
    return lax.ppermute(array, "ctx", pairs)


def after(array, *others):
    return lax.optimization_barrier((array, *others))[0]


def core_sum(lines, to_near, to_both):
    return (to_near.astype(F32) + move(to_both, lines.core_pairs()).astype(F32)).astype(BF16)


def near_sum(lines, mine, from_near, to_core):
    from_core = move(to_core, lines.core_pairs())
    return mine.astype(F32) + from_core.astype(F32) + from_near.astype(F32)


def far_sum(lines, quarter):
    parts = [
        move(quarter[by].astype(BF16), lines.far_pairs(by)) for by in range(1, lines.far)
    ]
    share = quarter[0]
    for part in parts:
        share = share + part.astype(F32)
    return share.astype(BF16)


def far_gather(lines, share):
    parts = [share] + [move(share, lines.far_pairs(by)) for by in range(1, lines.far)]
    return jnp.stack(parts)


def plane_gather(lines, mine):
    across = move(mine, lines.near_pairs())
    core_mine = move(mine, lines.core_pairs())
    core_across = move(across, lines.core_pairs())
    return mine, across, core_mine, core_across


def wraps(me, devices):
    return [me + 4 >= devices, (lax.rem(me, 2) == 1) & (me + 5 >= devices)]


def pack_kernel(slab_index, verts, keys, values, *rest, lines, heads, nv, per_device):
    sends = rest[:3]
    shares = rest[3:7]
    picked, sems, pick_sems = rest[7:]
    slab, me = slab_index[0], lax.axis_index("ctx")
    far, near, core = lines.place(me)
    _, chunk, head_dim = shares[0].shape
    copies = []
    wrapped4, wrapped_mixed = wraps(me, lines.devices)
    for n, region in enumerate(
        (slab, slab - wrapped4.astype(jnp.int32), slab - wrapped_mixed.astype(jnp.int32))
    ):
        for kv, source in enumerate((keys, values)):
            copy = pltpu.make_async_copy(source.at[region], sends[n].at[kv], sems.at[n, kv])
            copy.start()
            copies.append(copy)
    picked[...] = jnp.zeros_like(picked)
    slab_blocks = per_device * lines.devices
    piece = min(BLOCK, chunk)

    def unit_copies(h, m):
        inner = lax.rem(verts[h, m], slab_blocks)
        region = lax.div(verts[h, m], slab_blocks)
        row = lax.rem(inner, per_device) * BLOCK
        for p in range(BLOCK // piece):
            at = (h * nv + m) * BLOCK + p * piece
            line, at = at // (lines.far * chunk), at % (lines.far * chunk)
            slot, at = at // chunk, at % chunk
            line = lax.rem(line + near, 2)
            slot = lax.rem(slot - far + lines.far, lines.far)
            for kv, source in enumerate((keys, values)):
                yield pltpu.make_async_copy(
                    source.at[
                        region,
                        pl.ds(pl.multiple_of(row + p * piece, piece), piece),
                        pl.ds(h * head_dim, head_dim),
                    ],
                    picked.at[lax.rem(kv + core, 2), line, slot, pl.ds(at, piece), :],
                    pick_sems.at[kv, (h * nv + m) * (BLOCK // piece) + p],
                )

    def owned(h, m):
        return lax.div(lax.rem(verts[h, m], slab_blocks), per_device) == me

    for h in range(heads):
        for m in range(nv):

            @pl.when(owned(h, m))
            def _():
                for copy in unit_copies(h, m):
                    copy.start()

    for h in range(heads):
        for m in range(nv):

            @pl.when(owned(h, m))
            def _():
                for copy in unit_copies(h, m):
                    copy.wait()

    for n, share in enumerate(shares):
        share[...] = picked[n // 2, n % 2]
    for copy in copies:
        copy.wait()


def pack(slab_index, verticals, keys, values, lines):
    regions, rows, features = keys.shape
    heads, nv = verticals.shape
    head_dim = features // heads
    chunk = heads * nv * BLOCK // (2 * lines.far)
    smem = pl.BlockSpec(memory_space=pltpu.SMEM)
    hbm = pl.BlockSpec(memory_space=pltpu.HBM)
    share = (lines.far, chunk, head_dim)
    return pl.pallas_call(
        functools.partial(pack_kernel, lines=lines, heads=heads, nv=nv, per_device=rows // BLOCK),
        in_specs=[smem, smem, hbm, hbm],
        out_specs=[pl.BlockSpec(memory_space=pltpu.VMEM)] * 7,
        out_shape=[jax.ShapeDtypeStruct((2, rows, features), BF16)] * 3
        + [jax.ShapeDtypeStruct(share, BF16)] * 4,
        scratch_shapes=[
            pltpu.VMEM((2, 2) + share, BF16),
            pltpu.SemaphoreType.DMA((3, 2)),
            pltpu.SemaphoreType.DMA((2, heads * nv * max(1, BLOCK // chunk))),
        ],
        compiler_params=pltpu.CompilerParams(vmem_limit_bytes=PACK_VMEM),
    )(slab_index, verticals, keys, values)


def distances(core):
    return [2, 4, 5 - 4 * core, 1 + 2 * core, 3 + 2 * core]


def vertical_copies(lines, me, line, chunk, gathered, to, sems, first):
    far, _, core = lines.place(me)
    copies = []
    for kv, source in zip((core, 1 - core), gathered):
        for s in range(lines.far):
            slot = lax.rem(far - s + lines.far, lines.far)
            row = pl.multiple_of((line * lines.far + slot) * chunk, chunk)
            copies.append(
                pltpu.make_async_copy(
                    source.at[s], to.at[kv, pl.ds(row, chunk), :], sems.at[first + len(copies)]
                )
            )
    return copies


NT = (((1,), (1,)), ((), ()))


def prepare_kernel(q, grad, out, qs, gs, qt, gt, delta, *, head_dim):
    per_device = qs.shape[1]
    group = q.shape[1] // head_dim
    ones = jnp.ones((8, 2 * head_dim), BF16)
    for j in range(per_device):
        rows = slice(j * BLOCK, (j + 1) * BLOCK)
        split = []
        for g in range(group):
            cols = slice(g * head_dim, (g + 1) * head_dim)
            here = slice(g * BLOCK, (g + 1) * BLOCK)
            qs[0, j, here, :] = q[rows, cols]
            gs[0, j, here, :] = grad[rows, cols]
            product = grad[rows, cols].astype(F32) * out[rows, cols].astype(F32)
            upper = product.astype(BF16)
            lower = (product - upper.astype(F32)).astype(BF16)
            split.append(jnp.concatenate([upper, lower], axis=1))
        qt[0, j] = jnp.transpose(qs[0, j])
        gt[0, j] = jnp.transpose(gs[0, j])
        delta[0, j] = lax.dot_general(
            ones, jnp.concatenate(split, axis=0), NT, preferred_element_type=F32
        )


def prepare(queries, cotangent, output, heads, head_dim):
    rows, width = queries.shape
    per_device = rows // BLOCK
    deep = width // heads // head_dim * BLOCK
    tile = pl.BlockSpec((rows, width // heads), lambda h: (0, h))

    def by_head(*shape):
        return pl.BlockSpec((1,) + shape, lambda h: (h,) + (0,) * len(shape))

    stacked = (per_device, deep, head_dim)
    turned = (per_device, head_dim, deep)
    sums = (per_device, 8, deep)
    return pl.pallas_call(
        functools.partial(prepare_kernel, head_dim=head_dim),
        grid=(heads,),
        in_specs=[tile] * 3,
        out_specs=[by_head(*stacked)] * 2 + [by_head(*turned)] * 2 + [by_head(*sums)],
        out_shape=[jax.ShapeDtypeStruct((heads,) + stacked, BF16)] * 2
        + [jax.ShapeDtypeStruct((heads,) + turned, BF16)] * 2
        + [jax.ShapeDtypeStruct((heads,) + sums, F32)],
        compiler_params=pltpu.CompilerParams(vmem_limit_bytes=VMEM_LIMIT),
        cost_estimate=pl.CostEstimate(flops=0, bytes_accessed=7 << 20, transcendentals=0),
    )(queries, cotangent, output)


def slash_rows(offs, h, j, s, per_device):
    return pl.multiple_of((WDEV * per_device + j - offs[h, s]) * BLOCK, BLOCK)


def attend_kernel(
    base, slab_index, verts, offs, qs, gs, qt, gt, delta, own, *rest,
    lines, nv, ns, per_device, continued,
):
    gathered, recv, rest = rest[:2], rest[2 : 2 + WDEV], rest[2 + WDEV :]
    rest = rest[3:] if continued else rest
    (share, give, low_w, low_ds, cand_keys), scratch = rest[:5], rest[5:]
    win, vkv, vc, s_ref, vert_w, hold, sems = scratch
    i = pl.program_id(0)
    h = base[0] + i
    slab, me = slab_index[0], lax.axis_index("ctx")
    far, near, core = lines.place(me)
    _, chunk, head_dim = share.shape
    cand = nv + 1 + ns
    scaling = 1.0 / math.sqrt(head_dim)
    rows = per_device * BLOCK
    width = qs.shape[2]
    first_block = slab * (per_device * lines.devices) + me * per_device
    lanes = pl.ds(pl.multiple_of(i * head_dim, head_dim), head_dim)

    def window_row(d):
        return pl.multiple_of((WDEV - d) * rows, rows)

    @pl.when(i == 0)
    def _():
        half = win.shape[2]
        own_rows = pl.ds(WDEV * rows, rows)
        side = pl.ds(pl.multiple_of(base[0] * head_dim, half), half)
        copies = [
            pltpu.make_async_copy(
                recv[n].at[:, :, side], win.at[:, pl.ds(window_row(d), rows), :], sems.at[n]
            )
            for n, d in enumerate(distances(core))
        ]
        copies.append(
            pltpu.make_async_copy(own.at[:, :, side], win.at[:, own_rows, :], sems.at[WDEV])
        )
        copies += vertical_copies(lines, me, 0, chunk, gathered, vkv, sems, WDEV + 1)
        for copy in copies:
            copy.start()
        for copy in copies:
            copy.wait()

    vert_rows = pl.ds(pl.multiple_of(i * (nv * BLOCK), nv * BLOCK), nv * BLOCK)
    neg, posinf = jnp.float32(-jnp.inf), jnp.float32(jnp.inf)
    log2_scale = scaling * math.log2(math.e)
    key_at = lax.broadcasted_iota(jnp.int32, (BLOCK, width), 0)
    row_at = lax.broadcasted_iota(jnp.int32, (BLOCK, width), 1) % BLOCK

    def fold(x, op):
        y = x[0:8, :]
        for r in range(1, BLOCK // 8):
            y = op(y, x[r * 8 : (r + 1) * 8, :])
        return y

    vertical_sum = [None, None]
    for j in range(per_device):
        block = first_block + j
        own_at = (WDEV * per_device + j) * BLOCK
        valid = [verts[h, m] < block for m in range(nv)] + [None]
        for s in range(ns):
            collide = verts[h, 0] == block - offs[h, s]
            for m in range(1, nv):
                collide = collide | (verts[h, m] == block - offs[h, s])
            valid.append((offs[h, s] > 0) & jnp.logical_not(collide))
        for kv, to in enumerate((cand_keys.at[0], vc)):
            to[j, 0 : nv * BLOCK, :] = vkv[kv, vert_rows, :]
            to[j, nv * BLOCK : (nv + 1) * BLOCK, :] = win[kv, own_at : own_at + BLOCK, lanes]
            for s in range(ns):
                to[j, (nv + 1 + s) * BLOCK : (nv + 2 + s) * BLOCK, :] = win[
                    kv, pl.ds(slash_rows(offs, h, j, s, per_device), BLOCK), lanes
                ]

        top = None
        for n in range(cand // JOIN):
            span = slice(n * JOIN * BLOCK, (n + 1) * JOIN * BLOCK)
            scores = jnp.dot(cand_keys[0, j, span, :], qt[0, j], preferred_element_type=F32)
            for k in range(JOIN):
                c = n * JOIN + k
                part = scores[k * BLOCK : (k + 1) * BLOCK, :]
                if c == nv:
                    part = jnp.where(key_at <= row_at, part, neg)
                s_ref[j, c * BLOCK : (c + 1) * BLOCK, :] = part
                best = fold(part, jnp.maximum)
                if c != nv:
                    best = best + jnp.where(valid[c], jnp.float32(0), neg)
                top = best if top is None else jnp.maximum(top, best)
        top = jnp.max(top, axis=0, keepdims=True) * log2_scale
        total = jnp.zeros((8, width), F32)
        for c in range(cand):
            span = slice(c * BLOCK, (c + 1) * BLOCK)
            less = top if c == nv else top + jnp.where(valid[c], jnp.float32(0), posinf)
            p = jnp.exp2(s_ref[j, span, :] * log2_scale - less)
            s_ref[j, span, :] = p
            total = total + fold(p, jnp.add)
        inverse = 1.0 / jnp.sum(total, axis=0, keepdims=True)
        row_delta = delta[0, j, 0:1, :]
        for n in range(cand // JOIN):
            span = slice(n * JOIN * BLOCK, (n + 1) * JOIN * BLOCK)
            weight_grad = jnp.dot(vc[j, span, :], gt[0, j], preferred_element_type=F32)
            w = s_ref[j, span, :] * inverse
            if n * JOIN < nv:
                vert_w[j, span, :] = w.astype(BF16)
            else:
                low_w[0, j] = w.astype(BF16)
            low_ds[0, j, span, :] = (w * (weight_grad - row_delta)).astype(BF16)

        here = slice(0, nv * BLOCK)
        dv = jnp.dot(vert_w[j], gs[0, j], preferred_element_type=F32)
        dk = jnp.dot(low_ds[0, j, here, :], qs[0, j], preferred_element_type=F32) * scaling
        for kv, part in enumerate((dk, dv)):
            vertical_sum[kv] = part if j == 0 else vertical_sum[kv] + part

    first = core == 0
    parts = (
        jnp.where(first, vertical_sum[0], vertical_sum[1]),
        jnp.where(first, vertical_sum[1], vertical_sum[0]),
    )
    for c in range(nv * BLOCK // chunk):
        slot = lax.rem(i * (nv * BLOCK // chunk) + c - far + lines.far, lines.far)
        for n, part in enumerate(parts):
            hold[n, slot] = part[c * chunk : (c + 1) * chunk, :]

    @pl.when(i == pl.num_programs(0) - 1)
    def _():
        share[...] = hold[0].astype(share.dtype)
        give[...] = hold[1].astype(give.dtype)


def attend(base, slab_index, verticals, offsets, prepared, own, gathered, recv, lines, lows):
    heads, per_device, deep, head_dim = prepared[0].shape
    _, rows, features = own.shape
    nv, ns = verticals.shape[1], offsets.shape[1]
    cand = nv + 1 + ns
    half = heads // 2
    anywhere = pl.BlockSpec(memory_space=pl.ANY)

    def by_head(shape):
        return pl.BlockSpec(
            (1,) + shape[1:], lambda i, base, *_: (base[0] + i,) + (0,) * (len(shape) - 1)
        )

    share = (lines.far, half * nv * BLOCK // lines.far, head_dim)
    shares = pl.BlockSpec(share, lambda i, *_: (0, 0, 0))
    low_shapes = [
        (heads, per_device, (1 + ns) * BLOCK, deep),
        (heads, per_device, cand * BLOCK, deep),
        (heads, per_device, cand * BLOCK, head_dim),
    ]
    before = 4 + len(prepared) + 1 + 2 + WDEV
    return pl.pallas_call(
        functools.partial(
            attend_kernel, lines=lines, nv=nv, ns=ns, per_device=per_device, continued=bool(lows)
        ),
        grid_spec=pltpu.PrefetchScalarGridSpec(
            num_scalar_prefetch=4,
            grid=(half,),
            in_specs=[by_head(array.shape) for array in prepared]
            + [anywhere] * (3 + WDEV + len(lows)),
            out_specs=[shares] * 2 + [by_head(shape) for shape in low_shapes],
            scratch_shapes=[
                pltpu.VMEM((2, (WDEV + 1) * rows, features // 2), BF16),
                pltpu.VMEM((2, half * nv * BLOCK, head_dim), BF16),
                pltpu.VMEM((per_device, cand * BLOCK, head_dim), BF16),
                pltpu.VMEM((per_device, cand * BLOCK, deep), F32),
                pltpu.VMEM((per_device, nv * BLOCK, deep), BF16),
                pltpu.VMEM((2,) + share, F32),
                pltpu.SemaphoreType.DMA((WDEV + 1 + 2 * lines.far,)),
            ],
        ),
        out_shape=[
            jax.ShapeDtypeStruct(share, F32 if lows else BF16),
            jax.ShapeDtypeStruct(share, BF16),
        ]
        + [jax.ShapeDtypeStruct(shape, BF16) for shape in low_shapes],
        input_output_aliases={before + n: 2 + n for n in range(len(lows))},
        compiler_params=pltpu.CompilerParams(vmem_limit_bytes=VMEM_LIMIT),
        cost_estimate=pl.CostEstimate(
            flops=2 * 5 * half * per_device * cand * BLOCK * deep * head_dim,
            bytes_accessed=12 << 20,
            transcendentals=half * per_device * cand * BLOCK * deep,
        ),
    )(base, slab_index, verticals, offsets, *prepared, own, *gathered, *recv, *lows)


def window_kernel(offs, qs, gs, low_w, low_ds, home, *rest, lines, ns, per_device):
    parts, total = rest[:WDEV], rest[WDEV]
    h = pl.program_id(0)
    _, _, core = lines.place(lax.axis_index("ctx"))
    head_dim = qs.shape[3]
    rows = per_device * BLOCK
    scaling = 1.0 / math.sqrt(head_dim)
    lanes = pl.ds(pl.multiple_of(h * head_dim, head_dim), head_dim)
    total[...] = jnp.zeros_like(total)
    for j in range(per_device):
        dv = jnp.dot(low_w[0, j], gs[0, j], preferred_element_type=F32)
        dk = jnp.dot(low_ds[0, j], qs[0, j], preferred_element_type=F32) * scaling
        own_at = (WDEV * per_device + j) * BLOCK
        for kv, part in enumerate((dk, dv)):
            total[kv, own_at : own_at + BLOCK, :] += part[0:BLOCK]
            for s in range(ns):
                total[kv, pl.ds(slash_rows(offs, h, j, s, per_device), BLOCK), :] += part[
                    (1 + s) * BLOCK : (2 + s) * BLOCK
                ]
    for kv in range(2):
        home[kv, :, lanes] = total[kv, WDEV * rows :, :]
        for part, d in zip(parts, distances(core)):
            at = pl.multiple_of((WDEV - d) * rows, rows)
            part[kv, :, lanes] = total[kv, pl.ds(at, rows), :].astype(part.dtype)


def window_gradients(offsets, qs, gs, low_w, low_ds, lines, nv):
    heads, per_device, deep, head_dim = qs.shape
    ns = offsets.shape[1]
    rows, features = per_device * BLOCK, heads * head_dim
    shard = (2, rows, features)
    whole = pl.BlockSpec(shard, lambda h: (0, 0, 0))
    stacked = pl.BlockSpec((1,) + qs.shape[1:], lambda h: (h, 0, 0, 0))
    tail = (1 + ns) * BLOCK
    low_tail = pl.BlockSpec((1, per_device, tail, deep), lambda h: (h, 0, 0, 0))
    low = pl.BlockSpec(
        (1, per_device, tail, deep), lambda h: (h, 0, nv * BLOCK // tail, 0)
    )
    return pl.pallas_call(
        functools.partial(window_kernel, lines=lines, ns=ns, per_device=per_device),
        grid=(heads,),
        in_specs=[pl.BlockSpec(memory_space=pltpu.SMEM), stacked, stacked, low_tail, low],
        out_specs=[whole] * (1 + WDEV),
        out_shape=[jax.ShapeDtypeStruct(shard, F32)] * 3 + [jax.ShapeDtypeStruct(shard, BF16)] * 3,
        scratch_shapes=[pltpu.VMEM((2, (WDEV + 1) * rows, head_dim), F32)],
        compiler_params=pltpu.CompilerParams(vmem_limit_bytes=VMEM_LIMIT),
        cost_estimate=pl.CostEstimate(flops=0, bytes_accessed=9 << 20, transcendentals=0),
    )(offsets, qs, gs, low_w, low_ds)


def query_kernel(cand_keys, low_ds, dq):
    per_device, _, head_dim = cand_keys.shape[1:]
    scaling = 1.0 / math.sqrt(head_dim)
    for j in range(per_device):
        turned = lax.dot_general(
            cand_keys[0, j], low_ds[0, j], (((0,), (0,)), ((), ())), preferred_element_type=F32
        )
        stacked = (jnp.transpose(turned) * scaling).astype(BF16)
        for g in range(dq.shape[1] // head_dim):
            dq[j * BLOCK : (j + 1) * BLOCK, g * head_dim : (g + 1) * head_dim] = stacked[
                g * BLOCK : (g + 1) * BLOCK, :
            ]


def query_gradients(cand_keys, low_ds):
    heads, per_device, keys, head_dim = cand_keys.shape
    deep = low_ds.shape[3]
    rows, width = per_device * BLOCK, deep // BLOCK * head_dim

    def by_head(shape):
        return pl.BlockSpec((1,) + shape[1:], lambda h: (h, 0, 0, 0))

    return pl.pallas_call(
        query_kernel,
        grid=(heads,),
        in_specs=[by_head(cand_keys.shape), by_head(low_ds.shape)],
        out_specs=pl.BlockSpec((rows, width), lambda h: (0, h)),
        out_shape=jax.ShapeDtypeStruct((rows, heads * width), BF16),
        compiler_params=pltpu.CompilerParams(vmem_limit_bytes=VMEM_LIMIT),
        cost_estimate=pl.CostEstimate(flops=0, bytes_accessed=10 << 20, transcendentals=0),
    )(cand_keys, low_ds)


def zeros_kernel(_, key_out, value_out, blank, sems):
    blank[...] = jnp.zeros_like(blank)
    copies = [
        pltpu.make_async_copy(blank, out.at[r], sems.at[n, r])
        for n, out in enumerate((key_out, value_out))
        for r in range(out.shape[0])
    ]
    for copy in copies:
        copy.start()
    for copy in copies:
        copy.wait()


def zeros(ahead, shape):
    hbm = pl.BlockSpec(memory_space=pltpu.HBM)
    return pl.pallas_call(
        zeros_kernel,
        in_specs=[pl.BlockSpec(memory_space=pl.ANY)],
        out_specs=[hbm] * 2,
        out_shape=[jax.ShapeDtypeStruct(shape, BF16)] * 2,
        scratch_shapes=[pltpu.VMEM(shape[1:], BF16), pltpu.SemaphoreType.DMA((2, shape[0]))],
        compiler_params=pltpu.CompilerParams(vmem_limit_bytes=VMEM_LIMIT),
        cost_estimate=pl.CostEstimate(flops=0, bytes_accessed=5 << 20, transcendentals=0),
    )(ahead)


def assemble_kernel(slab_index, verts, home, *rest, lines, heads, nv, per_device):
    from_near, arrived, gathered = rest[0], rest[1:3], rest[3:7]
    outs, vert, acc, low, sems, out_sems, unit_sems = rest[9:11], *rest[11:]
    slab, me = slab_index[0], lax.axis_index("ctx")
    _, near, _ = lines.place(me)
    devices = lines.devices
    chunk, head_dim = gathered[0].shape[1:]
    slab_blocks = per_device * devices
    copies = vertical_copies(lines, me, 1 - near, chunk, gathered[0::2], vert, sems, 0)
    copies += vertical_copies(lines, me, near, chunk, gathered[1::2], vert, sems, 2 * lines.far)
    for copy in copies:
        copy.start()
    acc[0] = home[...]
    acc[1] = jnp.zeros_like(home)

    @pl.when(near == 0)
    def _():
        acc[0] += from_near[...].astype(F32)

    for part, wrapped in zip(arrived, wraps(me, devices)):
        acc[wrapped.astype(jnp.int32)] += part[...].astype(F32)
    for copy in copies:
        copy.wait()

    def unit(h, m):
        inner = lax.rem(verts[h, m], slab_blocks)
        region = lax.div(verts[h, m], slab_blocks)
        row = pl.multiple_of(lax.rem(inner, per_device) * BLOCK, BLOCK)
        close = (region == slab) | (region == slab - 1)
        return lax.div(inner, per_device) == me, close, region, row

    def unit_copies(h, m, region, row):
        at = (h * nv + m) * BLOCK
        for kv in range(2):
            yield pltpu.make_async_copy(
                vert.at[kv, pl.ds(at, BLOCK), :],
                outs[kv].at[region, pl.ds(row, BLOCK), pl.ds(h * head_dim, head_dim)],
                unit_sems.at[kv, h * nv + m],
            )

    for h in range(heads):
        lanes = slice(h * head_dim, (h + 1) * head_dim)
        for m in range(nv):
            mine, close, region, row = unit(h, m)
            at = (h * nv + m) * BLOCK

            @pl.when(mine & close)
            def _():
                for kv in range(2):
                    acc[slab - region, kv, pl.ds(row, BLOCK), lanes] += vert[
                        kv, at : at + BLOCK, :
                    ].astype(F32)

            @pl.when(mine & jnp.logical_not(close))
            def _():
                for copy in unit_copies(h, m, region, row):
                    copy.start()

    low[...] = acc[...].astype(BF16)
    copies = [
        pltpu.make_async_copy(low.at[n, kv], outs[kv].at[slab - n], out_sems.at[n, kv])
        for n in range(2)
        for kv in range(2)
    ]
    for copy in copies:
        copy.start()
    for h in range(heads):
        for m in range(nv):
            mine, close, region, row = unit(h, m)

            @pl.when(mine & jnp.logical_not(close))
            def _():
                for copy in unit_copies(h, m, region, row):
                    copy.wait()

    for copy in copies:
        copy.wait()


def assemble(slab_index, verticals, home, from_near, arrived, gathered, blank, lines):
    _, rows, features = home.shape
    heads, nv = verticals.shape
    smem = pl.BlockSpec(memory_space=pltpu.SMEM)
    vmem = pl.BlockSpec(memory_space=pltpu.VMEM)
    anywhere = pl.BlockSpec(memory_space=pl.ANY)
    hbm = pl.BlockSpec(memory_space=pltpu.HBM)
    return pl.pallas_call(
        functools.partial(
            assemble_kernel, lines=lines, heads=heads, nv=nv, per_device=rows // BLOCK
        ),
        in_specs=[smem] * 2 + [vmem] * 4 + [anywhere] * 4 + [hbm] * 2,
        out_specs=[hbm] * 2,
        out_shape=[jax.ShapeDtypeStruct(blank[0].shape, BF16)] * 2,
        input_output_aliases={10: 0, 11: 1},
        scratch_shapes=[
            pltpu.VMEM((2, heads * nv * BLOCK, features // heads), BF16),
            pltpu.VMEM((2, 2, rows, features), F32),
            pltpu.VMEM((2, 2, rows, features), BF16),
            pltpu.SemaphoreType.DMA((4 * lines.far,)),
            pltpu.SemaphoreType.DMA((2, 2)),
            pltpu.SemaphoreType.DMA((2, heads * nv)),
        ],
        compiler_params=pltpu.CompilerParams(vmem_limit_bytes=VMEM_LIMIT),
    )(slab_index, verticals, home, from_near, *arrived, *gathered, *blank)


def shards(
    queries,
    context_keys,
    context_values,
    forward_output,
    output_cotangent,
    verticals,
    offsets,
    slab_index,
):
    lines = Lines(lax.axis_size("ctx"))
    heads, nv = verticals.shape
    head_dim = context_keys.shape[2] // heads
    _, near, _ = lines.place(lax.axis_index("ctx"))

    own, send4, mixed, mine, to_near, to_core, to_both = pack(
        slab_index, verticals, context_keys, context_values, lines
    )
    recv4 = move(send4, lines.shift_pairs(4))
    to_near = core_sum(lines, to_near, to_both)
    quarter = near_sum(lines, mine, move(to_near, lines.near_pairs()), to_core)
    prepared = prepare(after(queries, to_near), output_cotangent, forward_output, heads, head_dim)
    quarter = after(quarter, recv4, *prepared)
    share = far_sum(lines, quarter)
    recv_mixed = move(after(mixed, quarter), lines.mixed_pairs())
    recv2 = move(jnp.where(near == 1, recv4, own), lines.near_pairs())
    other4 = move(recv4, lines.core_pairs())
    blank = zeros(share, context_keys.shape)
    gathered = far_gather(lines, after(share, other4))
    other2 = move(recv2, lines.core_pairs())
    gathered = after(gathered, other2, recv_mixed, *blank)
    gathered = plane_gather(lines, gathered)
    recv = [recv2, recv4, recv_mixed, other2, other4]

    def attend_line(line, gathered, lows):
        base = (line * (heads // 2)).astype(jnp.int32).reshape(1)
        return attend(
            base, slab_index, verticals, offsets, prepared, own, gathered, recv, lines, lows
        )

    to_near, to_both, *lows = attend_line(near, gathered[0::2], ())
    to_near = core_sum(lines, to_near, to_both)
    from_near = move(to_near, lines.near_pairs())
    mine, to_core, low_w, low_ds, cand_keys = attend_line(1 - near, gathered[1::2], lows)

    home, part2, part4, mixed, give2, give4 = window_gradients(
        after(offsets, from_near), prepared[0], prepared[1], low_w, low_ds, lines, nv
    )
    quarter = after(near_sum(lines, mine, from_near, to_core), home)
    share = far_sum(lines, quarter)
    arrived_mixed = move(mixed, back(lines.mixed_pairs()))
    sum2 = (part2 + move(give2, lines.core_pairs()).astype(F32)).astype(BF16)
    sum4 = part4 + move(give4, lines.core_pairs()).astype(F32)
    from_near = move(sum2, lines.near_pairs())
    totals = after(far_gather(lines, share), from_near, arrived_mixed)
    sum4 = (sum4 + jnp.where(near == 1, from_near.astype(F32), 0.0)).astype(BF16)
    arrived4 = move(after(sum4, totals), back(lines.shift_pairs(4)))
    query_grad = query_gradients(after(cand_keys, totals), low_ds)
    totals = plane_gather(lines, totals)
    key_gradient, value_gradient = assemble(
        slab_index, verticals, after(home, query_grad), from_near, (arrived4, arrived_mixed),
        totals, blank, lines,
    )
    return query_grad, key_gradient, value_gradient


def solution(mesh):
    in_specs = (
        P(("groups", "ctx"), None),
        P("groups", "ctx", None),
        P("groups", "ctx", None),
        P(("groups", "ctx"), None),
        P(("groups", "ctx"), None),
        P("groups", None),
        P("groups", None),
        P("groups"),
    )
    out_specs = (P(("groups", "ctx"), None), P("groups", "ctx", None), P("groups", "ctx", None))
    return jax.shard_map(shards, mesh=mesh, in_specs=in_specs, out_specs=out_specs, check_vma=False)
```

```python
import functools
import math

import jax
import jax.numpy as jnp
from jax import lax
from jax.experimental import pallas as pl
from jax.experimental.pallas import tpu as pltpu
from jax.sharding import PartitionSpec as P

BLOCK = 64
WDEV = 5
VMEM_LIMIT = 60 * 1024 * 1024
PACK_VMEM = 60 * 1024 * 1024
JOIN = 4
BF16 = jnp.bfloat16
F32 = jnp.float32


class Lines:
    def __init__(self, devices):
        self.devices = devices
        self.far = devices // 4

    def place(self, me):
        return lax.div(me, 4), lax.rem(lax.div(me, 2), 2), lax.rem(me, 2)

    def core_pairs(self):
        return [(i, i ^ 1) for i in range(self.devices)]

    def near_pairs(self):
        return [(i, i ^ 2) for i in range(self.devices)]

    def both_pairs(self):
        return [(i, i ^ 3) for i in range(self.devices)]

    def far_pairs(self, by):
        return [(i, (i + 4 * by) % self.devices) for i in range(self.devices)]

    def shift_pairs(self, by):
        return [(i, (i + by) % self.devices) for i in range(self.devices)]

    def mixed_pairs(self):
        return [(i, (i + (5 if i % 2 else 1)) % self.devices) for i in range(self.devices)]


def back(pairs):
    return [(b, a) for a, b in pairs]


def move(array, pairs):
    return lax.ppermute(array, "ctx", pairs)


def after(array, *others):
    return lax.optimization_barrier((array, *others))[0]


def core_sum(lines, to_near, to_both):
    return (to_near.astype(F32) + move(to_both, lines.core_pairs()).astype(F32)).astype(BF16)


def near_sum(lines, mine, from_near, to_core):
    from_core = move(to_core, lines.core_pairs())
    return mine.astype(F32) + from_core.astype(F32) + from_near.astype(F32)


def far_sum(lines, quarter):
    parts = [
        move(quarter[by].astype(BF16), lines.far_pairs(by)) for by in range(1, lines.far)
    ]
    share = quarter[0]
    for part in parts:
        share = share + part.astype(F32)
    return share.astype(BF16)


def far_gather(lines, share):
    parts = [share] + [move(share, lines.far_pairs(by)) for by in range(1, lines.far)]
    return jnp.stack(parts)


def plane_gather(lines, mine):
    across = move(mine, lines.near_pairs())
    core_mine = move(mine, lines.core_pairs())
    core_across = move(across, lines.core_pairs())
    return mine, across, core_mine, core_across


def wraps(me, devices):
    return [me + 4 >= devices, (lax.rem(me, 2) == 1) & (me + 5 >= devices)]


def pack_kernel(slab_index, verts, keys, values, *rest, lines, heads, nv, per_device):
    sends = rest[:3]
    shares = rest[3:7]
    picked, sems, pick_sems = rest[7:]
    slab, me = slab_index[0], lax.axis_index("ctx")
    far, near, core = lines.place(me)
    _, chunk, head_dim = shares[0].shape
    copies = []
    wrapped4, wrapped_mixed = wraps(me, lines.devices)
    for n, region in enumerate(
        (slab, slab - wrapped4.astype(jnp.int32), slab - wrapped_mixed.astype(jnp.int32))
    ):
        for kv, source in enumerate((keys, values)):
            copy = pltpu.make_async_copy(source.at[region], sends[n].at[kv], sems.at[n, kv])
            copy.start()
            copies.append(copy)
    picked[...] = jnp.zeros_like(picked)
    slab_blocks = per_device * lines.devices
    piece = min(BLOCK, chunk)

    def unit_copies(h, m):
        inner = lax.rem(verts[h, m], slab_blocks)
        region = lax.div(verts[h, m], slab_blocks)
        row = lax.rem(inner, per_device) * BLOCK
        for p in range(BLOCK // piece):
            at = (h * nv + m) * BLOCK + p * piece
            line, at = at // (lines.far * chunk), at % (lines.far * chunk)
            slot, at = at // chunk, at % chunk
            line = lax.rem(line + near, 2)
            slot = lax.rem(slot - far + lines.far, lines.far)
            for kv, source in enumerate((keys, values)):
                yield pltpu.make_async_copy(
                    source.at[
                        region,
                        pl.ds(pl.multiple_of(row + p * piece, piece), piece),
                        pl.ds(h * head_dim, head_dim),
                    ],
                    picked.at[lax.rem(kv + core, 2), line, slot, pl.ds(at, piece), :],
                    pick_sems.at[kv, (h * nv + m) * (BLOCK // piece) + p],
                )

    def owned(h, m):
        return lax.div(lax.rem(verts[h, m], slab_blocks), per_device) == me

    for h in range(heads):
        for m in range(nv):

            @pl.when(owned(h, m))
            def _():
                for copy in unit_copies(h, m):
                    copy.start()

    for h in range(heads):
        for m in range(nv):

            @pl.when(owned(h, m))
            def _():
                for copy in unit_copies(h, m):
                    copy.wait()

    for n, share in enumerate(shares):
        share[...] = picked[n // 2, n % 2]
    for copy in copies:
        copy.wait()


def pack(slab_index, verticals, keys, values, lines):
    regions, rows, features = keys.shape
    heads, nv = verticals.shape
    head_dim = features // heads
    chunk = heads * nv * BLOCK // (2 * lines.far)
    smem = pl.BlockSpec(memory_space=pltpu.SMEM)
    hbm = pl.BlockSpec(memory_space=pltpu.HBM)
    share = (lines.far, chunk, head_dim)
    return pl.pallas_call(
        functools.partial(pack_kernel, lines=lines, heads=heads, nv=nv, per_device=rows // BLOCK),
        in_specs=[smem, smem, hbm, hbm],
        out_specs=[pl.BlockSpec(memory_space=pltpu.VMEM)] * 7,
        out_shape=[jax.ShapeDtypeStruct((2, rows, features), BF16)] * 3
        + [jax.ShapeDtypeStruct(share, BF16)] * 4,
        scratch_shapes=[
            pltpu.VMEM((2, 2) + share, BF16),
            pltpu.SemaphoreType.DMA((3, 2)),
            pltpu.SemaphoreType.DMA((2, heads * nv * max(1, BLOCK // chunk))),
        ],
        compiler_params=pltpu.CompilerParams(vmem_limit_bytes=PACK_VMEM),
    )(slab_index, verticals, keys, values)


def distances(core):
    return [2, 4, 5 - 4 * core, 1 + 2 * core, 3 + 2 * core]


def vertical_copies(lines, me, line, chunk, gathered, to, sems, first):
    far, _, core = lines.place(me)
    copies = []
    for kv, source in zip((core, 1 - core), gathered):
        for s in range(lines.far):
            slot = lax.rem(far - s + lines.far, lines.far)
            row = pl.multiple_of((line * lines.far + slot) * chunk, chunk)
            copies.append(
                pltpu.make_async_copy(
                    source.at[s], to.at[kv, pl.ds(row, chunk), :], sems.at[first + len(copies)]
                )
            )
    return copies


NT = (((1,), (1,)), ((), ()))


def prepare_kernel(q, grad, out, qs, gs, qt, gt, delta, *, head_dim):
    per_device = qs.shape[1]
    group = q.shape[1] // head_dim
    ones = jnp.ones((8, 2 * head_dim), BF16)
    for j in range(per_device):
        rows = slice(j * BLOCK, (j + 1) * BLOCK)
        split = []
        for g in range(group):
            cols = slice(g * head_dim, (g + 1) * head_dim)
            here = slice(g * BLOCK, (g + 1) * BLOCK)
            qs[0, j, here, :] = q[rows, cols]
            gs[0, j, here, :] = grad[rows, cols]
            product = grad[rows, cols].astype(F32) * out[rows, cols].astype(F32)
            upper = product.astype(BF16)
            lower = (product - upper.astype(F32)).astype(BF16)
            split.append(jnp.concatenate([upper, lower], axis=1))
        qt[0, j] = jnp.transpose(qs[0, j])
        gt[0, j] = jnp.transpose(gs[0, j])
        delta[0, j] = lax.dot_general(
            ones, jnp.concatenate(split, axis=0), NT, preferred_element_type=F32
        )


def prepare(queries, cotangent, output, heads, head_dim):
    rows, width = queries.shape
    per_device = rows // BLOCK
    deep = width // heads // head_dim * BLOCK
    tile = pl.BlockSpec((rows, width // heads), lambda h: (0, h))

    def by_head(*shape):
        return pl.BlockSpec((1,) + shape, lambda h: (h,) + (0,) * len(shape))

    stacked = (per_device, deep, head_dim)
    turned = (per_device, head_dim, deep)
    sums = (per_device, 8, deep)
    return pl.pallas_call(
        functools.partial(prepare_kernel, head_dim=head_dim),
        grid=(heads,),
        in_specs=[tile] * 3,
        out_specs=[by_head(*stacked)] * 2 + [by_head(*turned)] * 2 + [by_head(*sums)],
        out_shape=[jax.ShapeDtypeStruct((heads,) + stacked, BF16)] * 2
        + [jax.ShapeDtypeStruct((heads,) + turned, BF16)] * 2
        + [jax.ShapeDtypeStruct((heads,) + sums, F32)],
        compiler_params=pltpu.CompilerParams(vmem_limit_bytes=VMEM_LIMIT),
        cost_estimate=pl.CostEstimate(flops=0, bytes_accessed=7 << 20, transcendentals=0),
    )(queries, cotangent, output)


def slash_rows(offs, h, j, s, per_device):
    return pl.multiple_of((WDEV * per_device + j - offs[h, s]) * BLOCK, BLOCK)


def attend_kernel(
    base, slab_index, verts, offs, qs, gs, qt, gt, delta, own, *rest,
    lines, nv, ns, per_device, continued,
):
    gathered, recv, rest = rest[:2], rest[2 : 2 + WDEV], rest[2 + WDEV :]
    rest = rest[3:] if continued else rest
    (share, give, low_w, low_ds, cand_keys), scratch = rest[:5], rest[5:]
    win, vkv, vc, s_ref, vert_w, hold, sems = scratch
    i = pl.program_id(0)
    h = base[0] + i
    slab, me = slab_index[0], lax.axis_index("ctx")
    far, near, core = lines.place(me)
    _, chunk, head_dim = share.shape
    cand = nv + 1 + ns
    scaling = 1.0 / math.sqrt(head_dim)
    rows = per_device * BLOCK
    width = qs.shape[2]
    first_block = slab * (per_device * lines.devices) + me * per_device
    lanes = pl.ds(pl.multiple_of(i * head_dim, head_dim), head_dim)

    def window_row(d):
        return pl.multiple_of((WDEV - d) * rows, rows)

    @pl.when(i == 0)
    def _():
        half = win.shape[2]
        own_rows = pl.ds(WDEV * rows, rows)
        side = pl.ds(pl.multiple_of(base[0] * head_dim, half), half)
        copies = [
            pltpu.make_async_copy(
                recv[n].at[:, :, side], win.at[:, pl.ds(window_row(d), rows), :], sems.at[n]
            )
            for n, d in enumerate(distances(core))
        ]
        copies.append(
            pltpu.make_async_copy(own.at[:, :, side], win.at[:, own_rows, :], sems.at[WDEV])
        )
        copies += vertical_copies(lines, me, 0, chunk, gathered, vkv, sems, WDEV + 1)
        for copy in copies:
            copy.start()
        for copy in copies:
            copy.wait()

    vert_rows = pl.ds(pl.multiple_of(i * (nv * BLOCK), nv * BLOCK), nv * BLOCK)
    neg, posinf = jnp.float32(-jnp.inf), jnp.float32(jnp.inf)
    log2_scale = scaling * math.log2(math.e)
    key_at = lax.broadcasted_iota(jnp.int32, (BLOCK, width), 0)
    row_at = lax.broadcasted_iota(jnp.int32, (BLOCK, width), 1) % BLOCK

    def fold(x, op):
        y = x[0:8, :]
        for r in range(1, BLOCK // 8):
            y = op(y, x[r * 8 : (r + 1) * 8, :])
        return y

    vertical_sum = [None, None]
    for j in range(per_device):
        block = first_block + j
        own_at = (WDEV * per_device + j) * BLOCK
        valid = [verts[h, m] < block for m in range(nv)] + [None]
        for s in range(ns):
            collide = verts[h, 0] == block - offs[h, s]
            for m in range(1, nv):
                collide = collide | (verts[h, m] == block - offs[h, s])
            valid.append((offs[h, s] > 0) & jnp.logical_not(collide))
        for kv, to in enumerate((cand_keys.at[0], vc)):
            to[j, 0 : nv * BLOCK, :] = vkv[kv, vert_rows, :]
            to[j, nv * BLOCK : (nv + 1) * BLOCK, :] = win[kv, own_at : own_at + BLOCK, lanes]
            for s in range(ns):
                to[j, (nv + 1 + s) * BLOCK : (nv + 2 + s) * BLOCK, :] = win[
                    kv, pl.ds(slash_rows(offs, h, j, s, per_device), BLOCK), lanes
                ]

        top = None
        for n in range(cand // JOIN):
            span = slice(n * JOIN * BLOCK, (n + 1) * JOIN * BLOCK)
            scores = jnp.dot(cand_keys[0, j, span, :], qt[0, j], preferred_element_type=F32)
            for k in range(JOIN):
                c = n * JOIN + k
                part = scores[k * BLOCK : (k + 1) * BLOCK, :]
                if c == nv:
                    part = jnp.where(key_at <= row_at, part, neg)
                s_ref[j, c * BLOCK : (c + 1) * BLOCK, :] = part
                best = fold(part, jnp.maximum)
                if c != nv:
                    best = best + jnp.where(valid[c], jnp.float32(0), neg)
                top = best if top is None else jnp.maximum(top, best)
        top = jnp.max(top, axis=0, keepdims=True) * log2_scale
        total = jnp.zeros((8, width), F32)
        for c in range(cand):
            span = slice(c * BLOCK, (c + 1) * BLOCK)
            less = top if c == nv else top + jnp.where(valid[c], jnp.float32(0), posinf)
            p = jnp.exp2(s_ref[j, span, :] * log2_scale - less)
            s_ref[j, span, :] = p
            total = total + fold(p, jnp.add)
        inverse = 1.0 / jnp.sum(total, axis=0, keepdims=True)
        row_delta = delta[0, j, 0:1, :]
        for n in range(cand // JOIN):
            span = slice(n * JOIN * BLOCK, (n + 1) * JOIN * BLOCK)
            weight_grad = jnp.dot(vc[j, span, :], gt[0, j], preferred_element_type=F32)
            w = s_ref[j, span, :] * inverse
            if n * JOIN < nv:
                vert_w[j, span, :] = w.astype(BF16)
            else:
                low_w[0, j] = w.astype(BF16)
            low_ds[0, j, span, :] = (w * (weight_grad - row_delta)).astype(BF16)

        here = slice(0, nv * BLOCK)
        dv = jnp.dot(vert_w[j], gs[0, j], preferred_element_type=F32)
        dk = jnp.dot(low_ds[0, j, here, :], qs[0, j], preferred_element_type=F32) * scaling
        for kv, part in enumerate((dk, dv)):
            vertical_sum[kv] = part if j == 0 else vertical_sum[kv] + part

    first = core == 0
    parts = (
        jnp.where(first, vertical_sum[0], vertical_sum[1]),
        jnp.where(first, vertical_sum[1], vertical_sum[0]),
    )
    for c in range(nv * BLOCK // chunk):
        slot = lax.rem(i * (nv * BLOCK // chunk) + c - far + lines.far, lines.far)
        for n, part in enumerate(parts):
            hold[n, slot] = part[c * chunk : (c + 1) * chunk, :]

    @pl.when(i == pl.num_programs(0) - 1)
    def _():
        share[...] = hold[0].astype(share.dtype)
        give[...] = hold[1].astype(give.dtype)


def attend(base, slab_index, verticals, offsets, prepared, own, gathered, recv, lines, lows):
    heads, per_device, deep, head_dim = prepared[0].shape
    _, rows, features = own.shape
    nv, ns = verticals.shape[1], offsets.shape[1]
    cand = nv + 1 + ns
    half = heads // 2
    anywhere = pl.BlockSpec(memory_space=pl.ANY)

    def by_head(shape):
        return pl.BlockSpec(
            (1,) + shape[1:], lambda i, base, *_: (base[0] + i,) + (0,) * (len(shape) - 1)
        )

    share = (lines.far, half * nv * BLOCK // lines.far, head_dim)
    shares = pl.BlockSpec(share, lambda i, *_: (0, 0, 0))
    low_shapes = [
        (heads, per_device, (1 + ns) * BLOCK, deep),
        (heads, per_device, cand * BLOCK, deep),
        (heads, per_device, cand * BLOCK, head_dim),
    ]
    before = 4 + len(prepared) + 1 + 2 + WDEV
    return pl.pallas_call(
        functools.partial(
            attend_kernel, lines=lines, nv=nv, ns=ns, per_device=per_device, continued=bool(lows)
        ),
        grid_spec=pltpu.PrefetchScalarGridSpec(
            num_scalar_prefetch=4,
            grid=(half,),
            in_specs=[by_head(array.shape) for array in prepared]
            + [anywhere] * (3 + WDEV + len(lows)),
            out_specs=[shares] * 2 + [by_head(shape) for shape in low_shapes],
            scratch_shapes=[
                pltpu.VMEM((2, (WDEV + 1) * rows, features // 2), BF16),
                pltpu.VMEM((2, half * nv * BLOCK, head_dim), BF16),
                pltpu.VMEM((per_device, cand * BLOCK, head_dim), BF16),
                pltpu.VMEM((per_device, cand * BLOCK, deep), F32),
                pltpu.VMEM((per_device, nv * BLOCK, deep), BF16),
                pltpu.VMEM((2,) + share, F32),
                pltpu.SemaphoreType.DMA((WDEV + 1 + 2 * lines.far,)),
            ],
        ),
        out_shape=[
            jax.ShapeDtypeStruct(share, F32 if lows else BF16),
            jax.ShapeDtypeStruct(share, BF16),
        ]
        + [jax.ShapeDtypeStruct(shape, BF16) for shape in low_shapes],
        input_output_aliases={before + n: 2 + n for n in range(len(lows))},
        compiler_params=pltpu.CompilerParams(vmem_limit_bytes=VMEM_LIMIT),
        cost_estimate=pl.CostEstimate(
            flops=2 * 5 * half * per_device * cand * BLOCK * deep * head_dim,
            bytes_accessed=12 << 20,
            transcendentals=half * per_device * cand * BLOCK * deep,
        ),
    )(base, slab_index, verticals, offsets, *prepared, own, *gathered, *recv, *lows)


def window_kernel(offs, qs, gs, low_w, low_ds, home, *rest, lines, ns, per_device):
    parts, total = rest[:WDEV], rest[WDEV]
    h = pl.program_id(0)
    _, _, core = lines.place(lax.axis_index("ctx"))
    head_dim = qs.shape[3]
    rows = per_device * BLOCK
    scaling = 1.0 / math.sqrt(head_dim)
    lanes = pl.ds(pl.multiple_of(h * head_dim, head_dim), head_dim)
    total[...] = jnp.zeros_like(total)
    for j in range(per_device):
        dv = jnp.dot(low_w[0, j], gs[0, j], preferred_element_type=F32)
        dk = jnp.dot(low_ds[0, j], qs[0, j], preferred_element_type=F32) * scaling
        own_at = (WDEV * per_device + j) * BLOCK
        for kv, part in enumerate((dk, dv)):
            total[kv, own_at : own_at + BLOCK, :] += part[0:BLOCK]
            for s in range(ns):
                total[kv, pl.ds(slash_rows(offs, h, j, s, per_device), BLOCK), :] += part[
                    (1 + s) * BLOCK : (2 + s) * BLOCK
                ]
    for kv in range(2):
        home[kv, :, lanes] = total[kv, WDEV * rows :, :]
        for part, d in zip(parts, distances(core)):
            at = pl.multiple_of((WDEV - d) * rows, rows)
            part[kv, :, lanes] = total[kv, pl.ds(at, rows), :].astype(part.dtype)


def window_gradients(offsets, qs, gs, low_w, low_ds, lines, nv):
    heads, per_device, deep, head_dim = qs.shape
    ns = offsets.shape[1]
    rows, features = per_device * BLOCK, heads * head_dim
    shard = (2, rows, features)
    whole = pl.BlockSpec(shard, lambda h: (0, 0, 0))
    stacked = pl.BlockSpec((1,) + qs.shape[1:], lambda h: (h, 0, 0, 0))
    tail = (1 + ns) * BLOCK
    low_tail = pl.BlockSpec((1, per_device, tail, deep), lambda h: (h, 0, 0, 0))
    low = pl.BlockSpec(
        (1, per_device, tail, deep), lambda h: (h, 0, nv * BLOCK // tail, 0)
    )
    return pl.pallas_call(
        functools.partial(window_kernel, lines=lines, ns=ns, per_device=per_device),
        grid=(heads,),
        in_specs=[pl.BlockSpec(memory_space=pltpu.SMEM), stacked, stacked, low_tail, low],
        out_specs=[whole] * (1 + WDEV),
        out_shape=[jax.ShapeDtypeStruct(shard, F32)] * 3 + [jax.ShapeDtypeStruct(shard, BF16)] * 3,
        scratch_shapes=[pltpu.VMEM((2, (WDEV + 1) * rows, head_dim), F32)],
        compiler_params=pltpu.CompilerParams(vmem_limit_bytes=VMEM_LIMIT),
        cost_estimate=pl.CostEstimate(flops=0, bytes_accessed=9 << 20, transcendentals=0),
    )(offsets, qs, gs, low_w, low_ds)


def query_kernel(cand_keys, low_ds, dq):
    per_device, _, head_dim = cand_keys.shape[1:]
    scaling = 1.0 / math.sqrt(head_dim)
    for j in range(per_device):
        turned = lax.dot_general(
            cand_keys[0, j], low_ds[0, j], (((0,), (0,)), ((), ())), preferred_element_type=F32
        )
        stacked = (jnp.transpose(turned) * scaling).astype(BF16)
        for g in range(dq.shape[1] // head_dim):
            dq[j * BLOCK : (j + 1) * BLOCK, g * head_dim : (g + 1) * head_dim] = stacked[
                g * BLOCK : (g + 1) * BLOCK, :
            ]


def query_gradients(cand_keys, low_ds):
    heads, per_device, keys, head_dim = cand_keys.shape
    deep = low_ds.shape[3]
    rows, width = per_device * BLOCK, deep // BLOCK * head_dim

    def by_head(shape):
        return pl.BlockSpec((1,) + shape[1:], lambda h: (h, 0, 0, 0))

    return pl.pallas_call(
        query_kernel,
        grid=(heads,),
        in_specs=[by_head(cand_keys.shape), by_head(low_ds.shape)],
        out_specs=pl.BlockSpec((rows, width), lambda h: (0, h)),
        out_shape=jax.ShapeDtypeStruct((rows, heads * width), BF16),
        compiler_params=pltpu.CompilerParams(vmem_limit_bytes=VMEM_LIMIT),
        cost_estimate=pl.CostEstimate(flops=0, bytes_accessed=10 << 20, transcendentals=0),
    )(cand_keys, low_ds)


def zeros_kernel(_, key_out, value_out, blank, sems):
    blank[...] = jnp.zeros_like(blank)
    copies = [
        pltpu.make_async_copy(blank, out.at[r], sems.at[n, r])
        for n, out in enumerate((key_out, value_out))
        for r in range(out.shape[0])
    ]
    for copy in copies:
        copy.start()
    for copy in copies:
        copy.wait()


def zeros(ahead, shape):
    hbm = pl.BlockSpec(memory_space=pltpu.HBM)
    return pl.pallas_call(
        zeros_kernel,
        in_specs=[pl.BlockSpec(memory_space=pl.ANY)],
        out_specs=[hbm] * 2,
        out_shape=[jax.ShapeDtypeStruct(shape, BF16)] * 2,
        scratch_shapes=[pltpu.VMEM(shape[1:], BF16), pltpu.SemaphoreType.DMA((2, shape[0]))],
        compiler_params=pltpu.CompilerParams(vmem_limit_bytes=VMEM_LIMIT),
        cost_estimate=pl.CostEstimate(flops=0, bytes_accessed=5 << 20, transcendentals=0),
    )(ahead)


def assemble_kernel(slab_index, verts, home, *rest, lines, heads, nv, per_device):
    from_near, arrived, gathered = rest[0], rest[1:3], rest[3:7]
    outs, vert, acc, low, sems, out_sems, unit_sems = rest[9:11], *rest[11:]
    slab, me = slab_index[0], lax.axis_index("ctx")
    _, near, _ = lines.place(me)
    devices = lines.devices
    chunk, head_dim = gathered[0].shape[1:]
    slab_blocks = per_device * devices
    copies = vertical_copies(lines, me, 1 - near, chunk, gathered[0::2], vert, sems, 0)
    copies += vertical_copies(lines, me, near, chunk, gathered[1::2], vert, sems, 2 * lines.far)
    for copy in copies:
        copy.start()
    acc[0] = home[...]
    acc[1] = jnp.zeros_like(home)

    @pl.when(near == 0)
    def _():
        acc[0] += from_near[...].astype(F32)

    for part, wrapped in zip(arrived, wraps(me, devices)):
        acc[wrapped.astype(jnp.int32)] += part[...].astype(F32)
    for copy in copies:
        copy.wait()

    def unit(h, m):
        inner = lax.rem(verts[h, m], slab_blocks)
        region = lax.div(verts[h, m], slab_blocks)
        row = pl.multiple_of(lax.rem(inner, per_device) * BLOCK, BLOCK)
        close = (region == slab) | (region == slab - 1)
        return lax.div(inner, per_device) == me, close, region, row

    def unit_copies(h, m, region, row):
        at = (h * nv + m) * BLOCK
        for kv in range(2):
            yield pltpu.make_async_copy(
                vert.at[kv, pl.ds(at, BLOCK), :],
                outs[kv].at[region, pl.ds(row, BLOCK), pl.ds(h * head_dim, head_dim)],
                unit_sems.at[kv, h * nv + m],
            )

    for h in range(heads):
        lanes = slice(h * head_dim, (h + 1) * head_dim)
        for m in range(nv):
            mine, close, region, row = unit(h, m)
            at = (h * nv + m) * BLOCK

            @pl.when(mine & close)
            def _():
                for kv in range(2):
                    acc[slab - region, kv, pl.ds(row, BLOCK), lanes] += vert[
                        kv, at : at + BLOCK, :
                    ].astype(F32)

            @pl.when(mine & jnp.logical_not(close))
            def _():
                for copy in unit_copies(h, m, region, row):
                    copy.start()

    low[...] = acc[...].astype(BF16)
    copies = [
        pltpu.make_async_copy(low.at[n, kv], outs[kv].at[slab - n], out_sems.at[n, kv])
        for n in range(2)
        for kv in range(2)
    ]
    for copy in copies:
        copy.start()
    for h in range(heads):
        for m in range(nv):
            mine, close, region, row = unit(h, m)

            @pl.when(mine & jnp.logical_not(close))
            def _():
                for copy in unit_copies(h, m, region, row):
                    copy.wait()

    for copy in copies:
        copy.wait()


def assemble(slab_index, verticals, home, from_near, arrived, gathered, blank, lines):
    _, rows, features = home.shape
    heads, nv = verticals.shape
    smem = pl.BlockSpec(memory_space=pltpu.SMEM)
    vmem = pl.BlockSpec(memory_space=pltpu.VMEM)
    anywhere = pl.BlockSpec(memory_space=pl.ANY)
    hbm = pl.BlockSpec(memory_space=pltpu.HBM)
    return pl.pallas_call(
        functools.partial(
            assemble_kernel, lines=lines, heads=heads, nv=nv, per_device=rows // BLOCK
        ),
        in_specs=[smem] * 2 + [vmem] * 4 + [anywhere] * 4 + [hbm] * 2,
        out_specs=[hbm] * 2,
        out_shape=[jax.ShapeDtypeStruct(blank[0].shape, BF16)] * 2,
        input_output_aliases={10: 0, 11: 1},
        scratch_shapes=[
            pltpu.VMEM((2, heads * nv * BLOCK, features // heads), BF16),
            pltpu.VMEM((2, 2, rows, features), F32),
            pltpu.VMEM((2, 2, rows, features), BF16),
            pltpu.SemaphoreType.DMA((4 * lines.far,)),
            pltpu.SemaphoreType.DMA((2, 2)),
            pltpu.SemaphoreType.DMA((2, heads * nv)),
        ],
        compiler_params=pltpu.CompilerParams(vmem_limit_bytes=VMEM_LIMIT),
    )(slab_index, verticals, home, from_near, *arrived, *gathered, *blank)


def shards(
    queries,
    context_keys,
    context_values,
    forward_output,
    output_cotangent,
    verticals,
    offsets,
    slab_index,
):
    lines = Lines(lax.axis_size("ctx"))
    heads, nv = verticals.shape
    head_dim = context_keys.shape[2] // heads
    _, near, _ = lines.place(lax.axis_index("ctx"))

    own, send4, mixed, mine, to_near, to_core, to_both = pack(
        slab_index, verticals, context_keys, context_values, lines
    )
    recv4 = move(send4, lines.shift_pairs(4))
    to_near = core_sum(lines, to_near, to_both)
    quarter = near_sum(lines, mine, move(to_near, lines.near_pairs()), to_core)
    prepared = prepare(after(queries, to_near), output_cotangent, forward_output, heads, head_dim)
    quarter = after(quarter, recv4, *prepared)
    share = far_sum(lines, quarter)
    recv_mixed = move(after(mixed, quarter), lines.mixed_pairs())
    recv2 = move(jnp.where(near == 1, recv4, own), lines.near_pairs())
    other4 = move(recv4, lines.core_pairs())
    blank = zeros(share, context_keys.shape)
    gathered = far_gather(lines, after(share, other4))
    other2 = move(recv2, lines.core_pairs())
    gathered = after(gathered, other2, recv_mixed, *blank)
    gathered = plane_gather(lines, gathered)
    recv = [recv2, recv4, recv_mixed, other2, other4]

    def attend_line(line, gathered, lows):
        base = (line * (heads // 2)).astype(jnp.int32).reshape(1)
        return attend(
            base, slab_index, verticals, offsets, prepared, own, gathered, recv, lines, lows
        )

    to_near, to_both, *lows = attend_line(near, gathered[0::2], ())
    to_near = core_sum(lines, to_near, to_both)
    from_near = move(to_near, lines.near_pairs())
    mine, to_core, low_w, low_ds, cand_keys = attend_line(1 - near, gathered[1::2], lows)

    home, part2, part4, mixed, give2, give4 = window_gradients(
        after(offsets, from_near), prepared[0], prepared[1], low_w, low_ds, lines, nv
    )
    quarter = after(near_sum(lines, mine, from_near, to_core), home)
    share = far_sum(lines, quarter)
    arrived_mixed = move(mixed, back(lines.mixed_pairs()))
    sum2 = (part2 + move(give2, lines.core_pairs()).astype(F32)).astype(BF16)
    sum4 = part4 + move(give4, lines.core_pairs()).astype(F32)
    from_near = move(sum2, lines.near_pairs())
    totals = after(far_gather(lines, share), from_near, arrived_mixed)
    sum4 = (sum4 + jnp.where(near == 1, from_near.astype(F32), 0.0)).astype(BF16)
    arrived4 = move(after(sum4, totals), back(lines.shift_pairs(4)))
    query_grad = query_gradients(after(cand_keys, totals), low_ds)
    totals = plane_gather(lines, totals)
    key_gradient, value_gradient = assemble(
        slab_index, verticals, after(home, query_grad), from_near, (arrived4, arrived_mixed),
        totals, blank, lines,
    )
    return query_grad, key_gradient, value_gradient


def solution(mesh):
    in_specs = (
        P(("groups", "ctx"), None),
        P("groups", "ctx", None),
        P("groups", "ctx", None),
        P(("groups", "ctx"), None),
        P(("groups", "ctx"), None),
        P("groups", None),
        P("groups", None),
        P("groups"),
    )
    out_specs = (P(("groups", "ctx"), None), P("groups", "ctx", None), P("groups", "ctx", None))
    return jax.shard_map(shards, mesh=mesh, in_specs=in_specs, out_specs=out_specs, check_vma=False)
```

```python
import functools
import math

import jax
import jax.numpy as jnp
from jax import lax
from jax.experimental import pallas as pl
from jax.experimental.pallas import tpu as pltpu
from jax.sharding import PartitionSpec as P

BLOCK = 64
WDEV = 5
VMEM_LIMIT = 24 * 1024 * 1024
PACK_VMEM = 60 * 1024 * 1024
JOIN = 4
BF16 = jnp.bfloat16
F32 = jnp.float32


class Lines:
    def __init__(self, devices):
        self.devices = devices
        self.far = devices // 4

    def place(self, me):
        return lax.div(me, 4), lax.rem(lax.div(me, 2), 2), lax.rem(me, 2)

    def core_pairs(self):
        return [(i, i ^ 1) for i in range(self.devices)]

    def near_pairs(self):
        return [(i, i ^ 2) for i in range(self.devices)]

    def both_pairs(self):
        return [(i, i ^ 3) for i in range(self.devices)]

    def far_pairs(self, by):
        return [(i, (i + 4 * by) % self.devices) for i in range(self.devices)]

    def shift_pairs(self, by):
        return [(i, (i + by) % self.devices) for i in range(self.devices)]

    def mixed_pairs(self):
        return [(i, (i + (5 if i % 2 else 1)) % self.devices) for i in range(self.devices)]


def back(pairs):
    return [(b, a) for a, b in pairs]


def move(array, pairs):
    return lax.ppermute(array, "ctx", pairs)


def after(array, *others):
    return lax.optimization_barrier((array, *others))[0]


def core_sum(lines, to_near, to_both):
    return (to_near.astype(F32) + move(to_both, lines.core_pairs()).astype(F32)).astype(BF16)


def near_sum(lines, mine, from_near, to_core):
    from_core = move(to_core, lines.core_pairs())
    return mine.astype(F32) + from_core.astype(F32) + from_near.astype(F32)


def far_sum(lines, quarter):
    parts = [
        move(quarter[by].astype(BF16), lines.far_pairs(by)) for by in range(1, lines.far)
    ]
    share = quarter[0]
    for part in parts:
        share = share + part.astype(F32)
    return share.astype(BF16)


def far_gather(lines, share):
    parts = [share] + [move(share, lines.far_pairs(by)) for by in range(1, lines.far)]
    return jnp.stack(parts)


def plane_gather(lines, mine):
    across = move(mine, lines.near_pairs())
    core_mine = move(mine, lines.core_pairs())
    core_across = move(across, lines.core_pairs())
    return mine, across, core_mine, core_across


def wraps(me, devices):
    return [me + 4 >= devices, (lax.rem(me, 2) == 1) & (me + 5 >= devices)]


def pack_kernel(slab_index, verts, keys, values, *rest, lines, heads, nv, per_device):
    sends = rest[:3]
    shares = rest[3:7]
    picked, sems, pick_sems = rest[7:]
    slab, me = slab_index[0], lax.axis_index("ctx")
    far, near, core = lines.place(me)
    _, chunk, head_dim = shares[0].shape
    copies = []
    wrapped4, wrapped_mixed = wraps(me, lines.devices)
    for n, region in enumerate(
        (slab, slab - wrapped4.astype(jnp.int32), slab - wrapped_mixed.astype(jnp.int32))
    ):
        for kv, source in enumerate((keys, values)):
            copy = pltpu.make_async_copy(source.at[region], sends[n].at[kv], sems.at[n, kv])
            copy.start()
            copies.append(copy)
    picked[...] = jnp.zeros_like(picked)
    slab_blocks = per_device * lines.devices
    piece = min(BLOCK, chunk)

    def unit_copies(h, m):
        inner = lax.rem(verts[h, m], slab_blocks)
        region = lax.div(verts[h, m], slab_blocks)
        row = lax.rem(inner, per_device) * BLOCK
        for p in range(BLOCK // piece):
            at = (h * nv + m) * BLOCK + p * piece
            line, at = at // (lines.far * chunk), at % (lines.far * chunk)
            slot, at = at // chunk, at % chunk
            line = lax.rem(line + near, 2)
            slot = lax.rem(slot - far + lines.far, lines.far)
            for kv, source in enumerate((keys, values)):
                yield pltpu.make_async_copy(
                    source.at[
                        region,
                        pl.ds(pl.multiple_of(row + p * piece, piece), piece),
                        pl.ds(h * head_dim, head_dim),
                    ],
                    picked.at[lax.rem(kv + core, 2), line, slot, pl.ds(at, piece), :],
                    pick_sems.at[kv, (h * nv + m) * (BLOCK // piece) + p],
                )

    def owned(h, m):
        return lax.div(lax.rem(verts[h, m], slab_blocks), per_device) == me

    for h in range(heads):
        for m in range(nv):

            @pl.when(owned(h, m))
            def _():
                for copy in unit_copies(h, m):
                    copy.start()

    for h in range(heads):
        for m in range(nv):

            @pl.when(owned(h, m))
            def _():
                for copy in unit_copies(h, m):
                    copy.wait()

    for n, share in enumerate(shares):
        share[...] = picked[n // 2, n % 2]
    for copy in copies:
        copy.wait()


def pack(slab_index, verticals, keys, values, lines):
    regions, rows, features = keys.shape
    heads, nv = verticals.shape
    head_dim = features // heads
    chunk = heads * nv * BLOCK // (2 * lines.far)
    smem = pl.BlockSpec(memory_space=pltpu.SMEM)
    hbm = pl.BlockSpec(memory_space=pltpu.HBM)
    share = (lines.far, chunk, head_dim)
    return pl.pallas_call(
        functools.partial(pack_kernel, lines=lines, heads=heads, nv=nv, per_device=rows // BLOCK),
        in_specs=[smem, smem, hbm, hbm],
        out_specs=[pl.BlockSpec(memory_space=pltpu.VMEM)] * 7,
        out_shape=[jax.ShapeDtypeStruct((2, rows, features), BF16)] * 3
        + [jax.ShapeDtypeStruct(share, BF16)] * 4,
        scratch_shapes=[
            pltpu.VMEM((2, 2) + share, BF16),
            pltpu.SemaphoreType.DMA((3, 2)),
            pltpu.SemaphoreType.DMA((2, heads * nv * max(1, BLOCK // chunk))),
        ],
        compiler_params=pltpu.CompilerParams(vmem_limit_bytes=PACK_VMEM),
    )(slab_index, verticals, keys, values)


def distances(core):
    return [2, 4, 5 - 4 * core, 1 + 2 * core, 3 + 2 * core]


def vertical_copies(lines, me, line, chunk, gathered, to, sems, first):
    far, _, core = lines.place(me)
    copies = []
    for kv, source in zip((core, 1 - core), gathered):
        for s in range(lines.far):
            slot = lax.rem(far - s + lines.far, lines.far)
            row = pl.multiple_of((line * lines.far + slot) * chunk, chunk)
            copies.append(
                pltpu.make_async_copy(
                    source.at[s], to.at[kv, pl.ds(row, chunk), :], sems.at[first + len(copies)]
                )
            )
    return copies


NT = (((1,), (1,)), ((), ()))


def prepare_kernel(q, grad, out, qs, gs, qt, gt, delta, *, head_dim):
    per_device = qs.shape[1]
    group = q.shape[1] // head_dim
    ones = jnp.ones((8, 2 * head_dim), BF16)
    for j in range(per_device):
        rows = slice(j * BLOCK, (j + 1) * BLOCK)
        split = []
        for g in range(group):
            cols = slice(g * head_dim, (g + 1) * head_dim)
            here = slice(g * BLOCK, (g + 1) * BLOCK)
            qs[0, j, here, :] = q[rows, cols]
            gs[0, j, here, :] = grad[rows, cols]
            product = grad[rows, cols].astype(F32) * out[rows, cols].astype(F32)
            upper = product.astype(BF16)
            lower = (product - upper.astype(F32)).astype(BF16)
            split.append(jnp.concatenate([upper, lower], axis=1))
        qt[0, j] = jnp.transpose(qs[0, j])
        gt[0, j] = jnp.transpose(gs[0, j])
        delta[0, j] = lax.dot_general(
            ones, jnp.concatenate(split, axis=0), NT, preferred_element_type=F32
        )


def prepare(queries, cotangent, output, heads, head_dim):
    rows, width = queries.shape
    per_device = rows // BLOCK
    deep = width // heads // head_dim * BLOCK
    tile = pl.BlockSpec((rows, width // heads), lambda h: (0, h))

    def by_head(*shape):
        return pl.BlockSpec((1,) + shape, lambda h: (h,) + (0,) * len(shape))

    stacked = (per_device, deep, head_dim)
    turned = (per_device, head_dim, deep)
    sums = (per_device, 8, deep)
    return pl.pallas_call(
        functools.partial(prepare_kernel, head_dim=head_dim),
        grid=(heads,),
        in_specs=[tile] * 3,
        out_specs=[by_head(*stacked)] * 2 + [by_head(*turned)] * 2 + [by_head(*sums)],
        out_shape=[jax.ShapeDtypeStruct((heads,) + stacked, BF16)] * 2
        + [jax.ShapeDtypeStruct((heads,) + turned, BF16)] * 2
        + [jax.ShapeDtypeStruct((heads,) + sums, F32)],
        compiler_params=pltpu.CompilerParams(vmem_limit_bytes=VMEM_LIMIT),
        cost_estimate=pl.CostEstimate(flops=0, bytes_accessed=7 << 20, transcendentals=0),
    )(queries, cotangent, output)


def slash_rows(offs, h, j, s, per_device):
    return pl.multiple_of((WDEV * per_device + j - offs[h, s]) * BLOCK, BLOCK)


def attend_kernel(
    base, slab_index, verts, offs, qs, gs, qt, gt, delta, own, *rest,
    lines, nv, ns, per_device,
):
    gathered, recv, rest = rest[:2], rest[2 : 2 + WDEV], rest[2 + WDEV :]
    (share, give, low_w, low_ds, cand_keys), scratch = rest[:5], rest[5:]
    win, vkv, vc, s_ref, vert_w, hold, sems = scratch
    i = pl.program_id(0)
    h = base[0] + i
    slab, me = slab_index[0], lax.axis_index("ctx")
    far, near, core = lines.place(me)
    _, chunk, head_dim = share.shape
    cand = nv + 1 + ns
    scaling = 1.0 / math.sqrt(head_dim)
    rows = per_device * BLOCK
    width = qs.shape[2]
    first_block = slab * (per_device * lines.devices) + me * per_device
    lanes = pl.ds(pl.multiple_of(i * head_dim, head_dim), head_dim)

    def window_row(d):
        return pl.multiple_of((WDEV - d) * rows, rows)

    @pl.when(i == 0)
    def _():
        half = win.shape[2]
        own_rows = pl.ds(WDEV * rows, rows)
        side = pl.ds(pl.multiple_of(base[0] * head_dim, half), half)
        copies = [
            pltpu.make_async_copy(
                recv[n].at[:, :, side], win.at[:, pl.ds(window_row(d), rows), :], sems.at[n]
            )
            for n, d in enumerate(distances(core))
        ]
        copies.append(
            pltpu.make_async_copy(own.at[:, :, side], win.at[:, own_rows, :], sems.at[WDEV])
        )
        copies += vertical_copies(lines, me, 0, chunk, gathered, vkv, sems, WDEV + 1)
        for copy in copies:
            copy.start()
        for copy in copies:
            copy.wait()

    vert_rows = pl.ds(pl.multiple_of(i * (nv * BLOCK), nv * BLOCK), nv * BLOCK)
    neg, posinf = jnp.float32(-jnp.inf), jnp.float32(jnp.inf)
    log2_scale = scaling * math.log2(math.e)
    key_at = lax.broadcasted_iota(jnp.int32, (BLOCK, width), 0)
    row_at = lax.broadcasted_iota(jnp.int32, (BLOCK, width), 1) % BLOCK

    def fold(x, op):
        y = x[0:8, :]
        for r in range(1, BLOCK // 8):
            y = op(y, x[r * 8 : (r + 1) * 8, :])
        return y

    vertical_sum = [None, None]
    for j in range(per_device):
        block = first_block + j
        own_at = (WDEV * per_device + j) * BLOCK
        valid = [verts[h, m] < block for m in range(nv)] + [None]
        for s in range(ns):
            collide = verts[h, 0] == block - offs[h, s]
            for m in range(1, nv):
                collide = collide | (verts[h, m] == block - offs[h, s])
            valid.append((offs[h, s] > 0) & jnp.logical_not(collide))
        for kv, to in enumerate((cand_keys.at[0], vc)):
            to[j, 0 : nv * BLOCK, :] = vkv[kv, vert_rows, :]
            to[j, nv * BLOCK : (nv + 1) * BLOCK, :] = win[kv, own_at : own_at + BLOCK, lanes]
            for s in range(ns):
                to[j, (nv + 1 + s) * BLOCK : (nv + 2 + s) * BLOCK, :] = win[
                    kv, pl.ds(slash_rows(offs, h, j, s, per_device), BLOCK), lanes
                ]

        top = None
        for n in range(cand // JOIN):
            span = slice(n * JOIN * BLOCK, (n + 1) * JOIN * BLOCK)
            scores = jnp.dot(cand_keys[0, j, span, :], qt[0, j], preferred_element_type=F32)
            for k in range(JOIN):
                c = n * JOIN + k
                part = scores[k * BLOCK : (k + 1) * BLOCK, :]
                if c == nv:
                    part = jnp.where(key_at <= row_at, part, neg)
                s_ref[j, c * BLOCK : (c + 1) * BLOCK, :] = part
                best = fold(part, jnp.maximum)
                if c != nv:
                    best = best + jnp.where(valid[c], jnp.float32(0), neg)
                top = best if top is None else jnp.maximum(top, best)
        top = jnp.max(top, axis=0, keepdims=True) * log2_scale
        total = jnp.zeros((8, width), F32)
        for c in range(cand):
            span = slice(c * BLOCK, (c + 1) * BLOCK)
            less = top if c == nv else top + jnp.where(valid[c], jnp.float32(0), posinf)
            p = jnp.exp2(s_ref[j, span, :] * log2_scale - less)
            s_ref[j, span, :] = p
            total = total + fold(p, jnp.add)
        inverse = 1.0 / jnp.sum(total, axis=0, keepdims=True)
        row_delta = delta[0, j, 0:1, :]
        for n in range(cand // JOIN):
            span = slice(n * JOIN * BLOCK, (n + 1) * JOIN * BLOCK)
            weight_grad = jnp.dot(vc[j, span, :], gt[0, j], preferred_element_type=F32)
            w = s_ref[j, span, :] * inverse
            if n * JOIN < nv:
                vert_w[j, span, :] = w.astype(BF16)
            else:
                low_w[0, j] = w.astype(BF16)
            low_ds[0, j, span, :] = (w * (weight_grad - row_delta)).astype(BF16)

        here = slice(0, nv * BLOCK)
        dv = jnp.dot(vert_w[j], gs[0, j], preferred_element_type=F32)
        dk = jnp.dot(low_ds[0, j, here, :], qs[0, j], preferred_element_type=F32) * scaling
        for kv, part in enumerate((dk, dv)):
            vertical_sum[kv] = part if j == 0 else vertical_sum[kv] + part

    first = core == 0
    parts = (
        jnp.where(first, vertical_sum[0], vertical_sum[1]),
        jnp.where(first, vertical_sum[1], vertical_sum[0]),
    )
    for c in range(nv * BLOCK // chunk):
        slot = lax.rem(i * (nv * BLOCK // chunk) + c - far + lines.far, lines.far)
        for n, part in enumerate(parts):
            hold[n, slot] = part[c * chunk : (c + 1) * chunk, :]

    @pl.when(i == pl.num_programs(0) - 1)
    def _():
        share[...] = hold[0].astype(share.dtype)
        give[...] = hold[1].astype(give.dtype)


def attend(base, slab_index, verticals, offsets, prepared, own, gathered, recv, lines, kept_as):
    heads, per_device, deep, head_dim = prepared[0].shape
    _, rows, features = own.shape
    nv, ns = verticals.shape[1], offsets.shape[1]
    cand = nv + 1 + ns
    half = heads // 2
    anywhere = pl.BlockSpec(memory_space=pl.ANY)

    def by_head(shape):
        return pl.BlockSpec(
            (1,) + shape[1:], lambda i, base, *_: (base[0] + i,) + (0,) * (len(shape) - 1)
        )

    def by_turn(shape):
        return pl.BlockSpec((1,) + shape[1:], lambda i, *_: (i,) + (0,) * (len(shape) - 1))

    share = (lines.far, half * nv * BLOCK // lines.far, head_dim)
    shares = pl.BlockSpec(share, lambda i, *_: (0, 0, 0))
    low_shapes = [
        (half, per_device, (1 + ns) * BLOCK, deep),
        (half, per_device, cand * BLOCK, deep),
        (half, per_device, cand * BLOCK, head_dim),
    ]
    return pl.pallas_call(
        functools.partial(
            attend_kernel, lines=lines, nv=nv, ns=ns, per_device=per_device
        ),
        grid_spec=pltpu.PrefetchScalarGridSpec(
            num_scalar_prefetch=4,
            grid=(half,),
            in_specs=[by_head(array.shape) for array in prepared]
            + [anywhere] * (3 + WDEV),
            out_specs=[shares] * 2 + [by_turn(shape) for shape in low_shapes],
            scratch_shapes=[
                pltpu.VMEM((2, (WDEV + 1) * rows, features // 2), BF16),
                pltpu.VMEM((2, half * nv * BLOCK, head_dim), BF16),
                pltpu.VMEM((per_device, cand * BLOCK, head_dim), BF16),
                pltpu.VMEM((per_device, cand * BLOCK, deep), F32),
                pltpu.VMEM((per_device, nv * BLOCK, deep), BF16),
                pltpu.VMEM((2,) + share, F32),
                pltpu.SemaphoreType.DMA((WDEV + 1 + 2 * lines.far,)),
            ],
        ),
        out_shape=[
            jax.ShapeDtypeStruct(share, kept_as),
            jax.ShapeDtypeStruct(share, BF16),
        ]
        + [jax.ShapeDtypeStruct(shape, BF16) for shape in low_shapes],
        compiler_params=pltpu.CompilerParams(vmem_limit_bytes=VMEM_LIMIT),
        cost_estimate=pl.CostEstimate(
            flops=2 * 5 * half * per_device * cand * BLOCK * deep * head_dim,
            bytes_accessed=12 << 20,
            transcendentals=half * per_device * cand * BLOCK * deep,
        ),
    )(base, slab_index, verticals, offsets, *prepared, own, *gathered, *recv)


def turn_to_head(t, bases, half):
    return bases[lax.div(t, half)] + lax.rem(t, half)


def of_call(call, half, shape, block=0):
    def index(t, *_):
        turn = jnp.minimum(t, half - 1) if call == 0 else jnp.maximum(t - half, 0)
        return (turn, 0, block, 0)

    return pl.BlockSpec((1,) + tuple(shape), index)


def window_kernel(bases, offs, qs, gs, *rest, lines, half, ns, per_device):
    lows, home, parts, total = (rest[0:2], rest[2:4]), rest[4], rest[5 : 5 + WDEV], rest[5 + WDEV]
    t = pl.program_id(0)
    h = turn_to_head(t, bases, half)
    _, _, core = lines.place(lax.axis_index("ctx"))
    head_dim = qs.shape[3]
    rows = per_device * BLOCK
    scaling = 1.0 / math.sqrt(head_dim)
    lanes = pl.ds(pl.multiple_of(h * head_dim, head_dim), head_dim)
    total[...] = jnp.zeros_like(total)
    for call, (low_w, low_ds) in enumerate(lows):

        @pl.when(lax.div(t, half) == call)
        def _():
            for j in range(per_device):
                dv = jnp.dot(low_w[0, j], gs[0, j], preferred_element_type=F32)
                dk = jnp.dot(low_ds[0, j], qs[0, j], preferred_element_type=F32) * scaling
                own_at = (WDEV * per_device + j) * BLOCK
                for kv, part in enumerate((dk, dv)):
                    total[kv, own_at : own_at + BLOCK, :] += part[0:BLOCK]
                    for s in range(ns):
                        at = slash_rows(offs, h, j, s, per_device)
                        total[kv, pl.ds(at, BLOCK), :] += part[(1 + s) * BLOCK : (2 + s) * BLOCK]

    for kv in range(2):
        home[kv, :, lanes] = total[kv, WDEV * rows :, :]
        for part, d in zip(parts, distances(core)):
            at = pl.multiple_of((WDEV - d) * rows, rows)
            part[kv, :, lanes] = total[kv, pl.ds(at, rows), :].astype(part.dtype)


def window_gradients(bases, offsets, qs, gs, lows, lines, nv):
    heads, per_device, deep, head_dim = qs.shape
    ns = offsets.shape[1]
    half = heads // 2
    rows, features = per_device * BLOCK, heads * head_dim
    shard = (2, rows, features)
    whole = pl.BlockSpec(shard, lambda t, *_: (0, 0, 0))
    stacked = pl.BlockSpec(
        (1,) + qs.shape[1:], lambda t, bases, _: (turn_to_head(t, bases, half), 0, 0, 0)
    )
    tail = (1 + ns) * BLOCK
    block = (per_device, tail, deep)
    specs = []
    for call in range(2):
        specs += [of_call(call, half, block), of_call(call, half, block, nv * BLOCK // tail)]
    return pl.pallas_call(
        functools.partial(window_kernel, lines=lines, half=half, ns=ns, per_device=per_device),
        grid_spec=pltpu.PrefetchScalarGridSpec(
            num_scalar_prefetch=2,
            grid=(heads,),
            in_specs=[stacked] * 2 + specs,
            out_specs=[whole] * (1 + WDEV),
            scratch_shapes=[pltpu.VMEM((2, (WDEV + 1) * rows, head_dim), F32)],
        ),
        out_shape=[jax.ShapeDtypeStruct(shard, F32)] * 3 + [jax.ShapeDtypeStruct(shard, BF16)] * 3,
        compiler_params=pltpu.CompilerParams(vmem_limit_bytes=VMEM_LIMIT),
        cost_estimate=pl.CostEstimate(flops=0, bytes_accessed=9 << 20, transcendentals=0),
    )(bases, offsets, qs, gs, *lows[0][:2], *lows[1][:2])


def query_kernel(bases, *rest):
    calls, dq = (rest[0:2], rest[2:4]), rest[4]
    t = pl.program_id(0)
    per_device, _, head_dim = rest[0].shape[1:]
    scaling = 1.0 / math.sqrt(head_dim)
    half = pl.num_programs(0) // 2
    for call, (cand_keys, low_ds) in enumerate(calls):

        @pl.when(lax.div(t, half) == call)
        def _():
            for j in range(per_device):
                turned = lax.dot_general(
                    cand_keys[0, j],
                    low_ds[0, j],
                    (((0,), (0,)), ((), ())),
                    preferred_element_type=F32,
                )
                stacked = (jnp.transpose(turned) * scaling).astype(BF16)
                for g in range(dq.shape[1] // head_dim):
                    dq[j * BLOCK : (j + 1) * BLOCK, g * head_dim : (g + 1) * head_dim] = stacked[
                        g * BLOCK : (g + 1) * BLOCK, :
                    ]


def query_gradients(bases, lows):
    half, per_device, _, head_dim = lows[0][2].shape
    deep = lows[0][1].shape[3]
    rows, width = per_device * BLOCK, deep // BLOCK * head_dim
    specs = []
    for call in range(2):
        specs += [of_call(call, half, lows[0][n].shape[1:]) for n in (2, 1)]
    return pl.pallas_call(
        query_kernel,
        grid_spec=pltpu.PrefetchScalarGridSpec(
            num_scalar_prefetch=1,
            grid=(2 * half,),
            in_specs=specs,
            out_specs=pl.BlockSpec(
                (rows, width), lambda t, bases: (0, turn_to_head(t, bases, half))
            ),
        ),
        out_shape=jax.ShapeDtypeStruct((rows, 2 * half * width), BF16),
        compiler_params=pltpu.CompilerParams(vmem_limit_bytes=VMEM_LIMIT),
        cost_estimate=pl.CostEstimate(flops=0, bytes_accessed=10 << 20, transcendentals=0),
    )(bases, lows[0][2], lows[0][1], lows[1][2], lows[1][1])


def zeros_kernel(_, key_out, value_out, blank, sems):
    blank[...] = jnp.zeros_like(blank)
    copies = [
        pltpu.make_async_copy(blank, out.at[r], sems.at[n, r])
        for n, out in enumerate((key_out, value_out))
        for r in range(out.shape[0])
    ]
    for copy in copies:
        copy.start()
    for copy in copies:
        copy.wait()


def zeros(ahead, shape):
    hbm = pl.BlockSpec(memory_space=pltpu.HBM)
    return pl.pallas_call(
        zeros_kernel,
        in_specs=[pl.BlockSpec(memory_space=pl.ANY)],
        out_specs=[hbm] * 2,
        out_shape=[jax.ShapeDtypeStruct(shape, BF16)] * 2,
        scratch_shapes=[pltpu.VMEM(shape[1:], BF16), pltpu.SemaphoreType.DMA((2, shape[0]))],
        compiler_params=pltpu.CompilerParams(vmem_limit_bytes=VMEM_LIMIT),
        cost_estimate=pl.CostEstimate(flops=0, bytes_accessed=5 << 20, transcendentals=0),
    )(ahead)


def assemble_kernel(slab_index, verts, home, *rest, lines, heads, nv, per_device):
    from_near, arrived, gathered = rest[0], rest[1:3], rest[3:7]
    outs, vert, acc, low, sems, out_sems, unit_sems = rest[9:11], *rest[11:]
    slab, me = slab_index[0], lax.axis_index("ctx")
    _, near, _ = lines.place(me)
    devices = lines.devices
    chunk, head_dim = gathered[0].shape[1:]
    slab_blocks = per_device * devices
    copies = vertical_copies(lines, me, 1 - near, chunk, gathered[0::2], vert, sems, 0)
    copies += vertical_copies(lines, me, near, chunk, gathered[1::2], vert, sems, 2 * lines.far)
    for copy in copies:
        copy.start()
    acc[0] = home[...]
    acc[1] = jnp.zeros_like(home)

    @pl.when(near == 0)
    def _():
        acc[0] += from_near[...].astype(F32)

    for part, wrapped in zip(arrived, wraps(me, devices)):
        acc[wrapped.astype(jnp.int32)] += part[...].astype(F32)
    for copy in copies:
        copy.wait()

    def unit(h, m):
        inner = lax.rem(verts[h, m], slab_blocks)
        region = lax.div(verts[h, m], slab_blocks)
        row = pl.multiple_of(lax.rem(inner, per_device) * BLOCK, BLOCK)
        close = (region == slab) | (region == slab - 1)
        return lax.div(inner, per_device) == me, close, region, row

    def unit_copies(h, m, region, row):
        at = (h * nv + m) * BLOCK
        for kv in range(2):
            yield pltpu.make_async_copy(
                vert.at[kv, pl.ds(at, BLOCK), :],
                outs[kv].at[region, pl.ds(row, BLOCK), pl.ds(h * head_dim, head_dim)],
                unit_sems.at[kv, h * nv + m],
            )

    for h in range(heads):
        lanes = slice(h * head_dim, (h + 1) * head_dim)
        for m in range(nv):
            mine, close, region, row = unit(h, m)
            at = (h * nv + m) * BLOCK

            @pl.when(mine & close)
            def _():
                for kv in range(2):
                    acc[slab - region, kv, pl.ds(row, BLOCK), lanes] += vert[
                        kv, at : at + BLOCK, :
                    ].astype(F32)

            @pl.when(mine & jnp.logical_not(close))
            def _():
                for copy in unit_copies(h, m, region, row):
                    copy.start()

    low[...] = acc[...].astype(BF16)
    copies = [
        pltpu.make_async_copy(low.at[n, kv], outs[kv].at[slab - n], out_sems.at[n, kv])
        for n in range(2)
        for kv in range(2)
    ]
    for copy in copies:
        copy.start()
    for h in range(heads):
        for m in range(nv):
            mine, close, region, row = unit(h, m)

            @pl.when(mine & jnp.logical_not(close))
            def _():
                for copy in unit_copies(h, m, region, row):
                    copy.wait()

    for copy in copies:
        copy.wait()


def assemble(slab_index, verticals, home, from_near, arrived, gathered, blank, lines):
    _, rows, features = home.shape
    heads, nv = verticals.shape
    smem = pl.BlockSpec(memory_space=pltpu.SMEM)
    vmem = pl.BlockSpec(memory_space=pltpu.VMEM)
    anywhere = pl.BlockSpec(memory_space=pl.ANY)
    hbm = pl.BlockSpec(memory_space=pltpu.HBM)
    return pl.pallas_call(
        functools.partial(
            assemble_kernel, lines=lines, heads=heads, nv=nv, per_device=rows // BLOCK
        ),
        in_specs=[smem] * 2 + [vmem] * 4 + [anywhere] * 4 + [hbm] * 2,
        out_specs=[hbm] * 2,
        out_shape=[jax.ShapeDtypeStruct(blank[0].shape, BF16)] * 2,
        input_output_aliases={10: 0, 11: 1},
        scratch_shapes=[
            pltpu.VMEM((2, heads * nv * BLOCK, features // heads), BF16),
            pltpu.VMEM((2, 2, rows, features), F32),
            pltpu.VMEM((2, 2, rows, features), BF16),
            pltpu.SemaphoreType.DMA((4 * lines.far,)),
            pltpu.SemaphoreType.DMA((2, 2)),
            pltpu.SemaphoreType.DMA((2, heads * nv)),
        ],
        compiler_params=pltpu.CompilerParams(vmem_limit_bytes=VMEM_LIMIT),
    )(slab_index, verticals, home, from_near, *arrived, *gathered, *blank)


def shards(
    queries,
    context_keys,
    context_values,
    forward_output,
    output_cotangent,
    verticals,
    offsets,
    slab_index,
):
    lines = Lines(lax.axis_size("ctx"))
    heads, nv = verticals.shape
    head_dim = context_keys.shape[2] // heads
    _, near, _ = lines.place(lax.axis_index("ctx"))

    own, send4, mixed, mine, to_near, to_core, to_both = pack(
        slab_index, verticals, context_keys, context_values, lines
    )
    recv4 = move(send4, lines.shift_pairs(4))
    to_near = core_sum(lines, to_near, to_both)
    quarter = near_sum(lines, mine, move(to_near, lines.near_pairs()), to_core)
    prepared = prepare(after(queries, to_near), output_cotangent, forward_output, heads, head_dim)
    quarter = after(quarter, recv4, *prepared)
    share = far_sum(lines, quarter)
    recv_mixed = move(after(mixed, quarter), lines.mixed_pairs())
    recv2 = move(jnp.where(near == 1, recv4, own), lines.near_pairs())
    other4 = move(recv4, lines.core_pairs())
    blank = zeros(share, context_keys.shape)
    gathered = far_gather(lines, after(share, other4))
    other2 = move(recv2, lines.core_pairs())
    gathered = after(gathered, other2, recv_mixed, *blank)
    gathered = plane_gather(lines, gathered)
    recv = [recv2, recv4, recv_mixed, other2, other4]

    bases = (jnp.stack([near, 1 - near]) * (heads // 2)).astype(jnp.int32)

    def attend_line(call, gathered, kept_as):
        return attend(
            bases[call : call + 1], slab_index, verticals, offsets, prepared, own, gathered, recv,
            lines, kept_as,
        )

    to_near, to_both, *first_lows = attend_line(0, gathered[0::2], BF16)
    to_near = core_sum(lines, to_near, to_both)
    from_near = move(to_near, lines.near_pairs())
    mine, to_core, *second_lows = attend_line(1, gathered[1::2], F32)
    lows = (first_lows, second_lows)

    home, part2, part4, mixed, give2, give4 = window_gradients(
        bases, after(offsets, from_near), prepared[0], prepared[1], lows, lines, nv
    )
    quarter = after(near_sum(lines, mine, from_near, to_core), home)
    share = far_sum(lines, quarter)
    arrived_mixed = move(mixed, back(lines.mixed_pairs()))
    sum2 = (part2 + move(give2, lines.core_pairs()).astype(F32)).astype(BF16)
    sum4 = part4 + move(give4, lines.core_pairs()).astype(F32)
    from_near = move(sum2, lines.near_pairs())
    totals = after(far_gather(lines, share), from_near, arrived_mixed)
    sum4 = (sum4 + jnp.where(near == 1, from_near.astype(F32), 0.0)).astype(BF16)
    arrived4 = move(after(sum4, totals), back(lines.shift_pairs(4)))
    query_grad = query_gradients(after(bases, totals), lows)
    totals = plane_gather(lines, totals)
    key_gradient, value_gradient = assemble(
        slab_index, verticals, after(home, query_grad), from_near, (arrived4, arrived_mixed),
        totals, blank, lines,
    )
    return query_grad, key_gradient, value_gradient


def solution(mesh):
    in_specs = (
        P(("groups", "ctx"), None),
        P("groups", "ctx", None),
        P("groups", "ctx", None),
        P(("groups", "ctx"), None),
        P(("groups", "ctx"), None),
        P("groups", None),
        P("groups", None),
        P("groups"),
    )
    out_specs = (P(("groups", "ctx"), None), P("groups", "ctx", None), P("groups", "ctx", None))
    return jax.shard_map(shards, mesh=mesh, in_specs=in_specs, out_specs=out_specs, check_vma=False)
```

```python
import functools
import math

import jax
import jax.numpy as jnp
from jax import lax
from jax.experimental import pallas as pl
from jax.experimental.pallas import tpu as pltpu
from jax.sharding import PartitionSpec as P

BLOCK = 64
WDEV = 5
MIB = 1024 * 1024
PACK_VMEM = 60 * MIB
JOIN = 4
BF16 = jnp.bfloat16
F32 = jnp.float32


class Lines:
    def __init__(self, devices):
        self.devices = devices
        self.far = devices // 4

    def place(self, me):
        return lax.div(me, 4), lax.rem(lax.div(me, 2), 2), lax.rem(me, 2)

    def core_pairs(self):
        return [(i, i ^ 1) for i in range(self.devices)]

    def near_pairs(self):
        return [(i, i ^ 2) for i in range(self.devices)]

    def both_pairs(self):
        return [(i, i ^ 3) for i in range(self.devices)]

    def far_pairs(self, by):
        return [(i, (i + 4 * by) % self.devices) for i in range(self.devices)]

    def shift_pairs(self, by):
        return [(i, (i + by) % self.devices) for i in range(self.devices)]

    def mixed_pairs(self):
        return [(i, (i + (5 if i % 2 else 1)) % self.devices) for i in range(self.devices)]


def back(pairs):
    return [(b, a) for a, b in pairs]


def move(array, pairs):
    return lax.ppermute(array, "ctx", pairs)


def after(array, *others):
    return lax.optimization_barrier((array, *others))[0]


def core_sum(lines, to_near, to_both):
    return (to_near.astype(F32) + move(to_both, lines.core_pairs()).astype(F32)).astype(BF16)


def near_sum(lines, mine, from_near, to_core):
    from_core = move(to_core, lines.core_pairs())
    return mine.astype(F32) + from_core.astype(F32) + from_near.astype(F32)


def far_sum(lines, quarter):
    parts = [
        move(quarter[by].astype(BF16), lines.far_pairs(by)) for by in range(1, lines.far)
    ]
    share = quarter[0]
    for part in parts:
        share = share + part.astype(F32)
    return share.astype(BF16)


def far_gather(lines, share):
    parts = [share] + [move(share, lines.far_pairs(by)) for by in range(1, lines.far)]
    return jnp.stack(parts)


def plane_gather(lines, mine):
    across = move(mine, lines.near_pairs())
    core_mine = move(mine, lines.core_pairs())
    core_across = move(across, lines.core_pairs())
    return mine, across, core_mine, core_across


def wraps(me, devices):
    return [me + 4 >= devices, (lax.rem(me, 2) == 1) & (me + 5 >= devices)]


def pack_kernel(slab_index, verts, keys, values, *rest, lines, heads, nv, per_device):
    sends = rest[:3]
    shares = rest[3:7]
    picked, sems, pick_sems = rest[7:]
    slab, me = slab_index[0], lax.axis_index("ctx")
    far, near, core = lines.place(me)
    _, chunk, head_dim = shares[0].shape
    copies = []
    wrapped4, wrapped_mixed = wraps(me, lines.devices)
    for n, region in enumerate(
        (slab, slab - wrapped4.astype(jnp.int32), slab - wrapped_mixed.astype(jnp.int32))
    ):
        for kv, source in enumerate((keys, values)):
            copy = pltpu.make_async_copy(source.at[region], sends[n].at[kv], sems.at[n, kv])
            copy.start()
            copies.append(copy)
    picked[...] = jnp.zeros_like(picked)
    slab_blocks = per_device * lines.devices
    piece = min(BLOCK, chunk)

    def unit_copies(h, m):
        inner = lax.rem(verts[h, m], slab_blocks)
        region = lax.div(verts[h, m], slab_blocks)
        row = lax.rem(inner, per_device) * BLOCK
        for p in range(BLOCK // piece):
            at = (h * nv + m) * BLOCK + p * piece
            line, at = at // (lines.far * chunk), at % (lines.far * chunk)
            slot, at = at // chunk, at % chunk
            line = lax.rem(line + near, 2)
            slot = lax.rem(slot - far + lines.far, lines.far)
            for kv, source in enumerate((keys, values)):
                yield pltpu.make_async_copy(
                    source.at[
                        region,
                        pl.ds(pl.multiple_of(row + p * piece, piece), piece),
                        pl.ds(h * head_dim, head_dim),
                    ],
                    picked.at[lax.rem(kv + core, 2), line, slot, pl.ds(at, piece), :],
                    pick_sems.at[kv, (h * nv + m) * (BLOCK // piece) + p],
                )

    def owned(h, m):
        return lax.div(lax.rem(verts[h, m], slab_blocks), per_device) == me

    for h in range(heads):
        for m in range(nv):

            @pl.when(owned(h, m))
            def _():
                for copy in unit_copies(h, m):
                    copy.start()

    for h in range(heads):
        for m in range(nv):

            @pl.when(owned(h, m))
            def _():
                for copy in unit_copies(h, m):
                    copy.wait()

    for n, share in enumerate(shares):
        share[...] = picked[n // 2, n % 2]
    for copy in copies:
        copy.wait()


def pack(slab_index, verticals, keys, values, lines):
    regions, rows, features = keys.shape
    heads, nv = verticals.shape
    head_dim = features // heads
    chunk = heads * nv * BLOCK // (2 * lines.far)
    smem = pl.BlockSpec(memory_space=pltpu.SMEM)
    hbm = pl.BlockSpec(memory_space=pltpu.HBM)
    share = (lines.far, chunk, head_dim)
    return pl.pallas_call(
        functools.partial(pack_kernel, lines=lines, heads=heads, nv=nv, per_device=rows // BLOCK),
        in_specs=[smem, smem, hbm, hbm],
        out_specs=[pl.BlockSpec(memory_space=pltpu.VMEM)] * 7,
        out_shape=[jax.ShapeDtypeStruct((2, rows, features), BF16)] * 3
        + [jax.ShapeDtypeStruct(share, BF16)] * 4,
        scratch_shapes=[
            pltpu.VMEM((2, 2) + share, BF16),
            pltpu.SemaphoreType.DMA((3, 2)),
            pltpu.SemaphoreType.DMA((2, heads * nv * max(1, BLOCK // chunk))),
        ],
        compiler_params=pltpu.CompilerParams(vmem_limit_bytes=PACK_VMEM),
    )(slab_index, verticals, keys, values)


def distances(core):
    return [2, 4, 5 - 4 * core, 1 + 2 * core, 3 + 2 * core]


def vertical_copies(lines, me, line, chunk, gathered, to, sems, first):
    far, _, core = lines.place(me)
    copies = []
    for kv, source in zip((core, 1 - core), gathered):
        for s in range(lines.far):
            slot = lax.rem(far - s + lines.far, lines.far)
            row = pl.multiple_of((line * lines.far + slot) * chunk, chunk)
            copies.append(
                pltpu.make_async_copy(
                    source.at[s], to.at[kv, pl.ds(row, chunk), :], sems.at[first + len(copies)]
                )
            )
    return copies


NT = (((1,), (1,)), ((), ()))


def prepare_kernel(q, grad, out, qs, gs, qt, gt, delta, *, head_dim):
    per_device = qs.shape[1]
    group = q.shape[1] // head_dim
    ones = jnp.ones((8, 2 * head_dim), BF16)
    for j in range(per_device):
        rows = slice(j * BLOCK, (j + 1) * BLOCK)
        split = []
        for g in range(group):
            cols = slice(g * head_dim, (g + 1) * head_dim)
            here = slice(g * BLOCK, (g + 1) * BLOCK)
            qs[0, j, here, :] = q[rows, cols]
            gs[0, j, here, :] = grad[rows, cols]
            product = grad[rows, cols].astype(F32) * out[rows, cols].astype(F32)
            upper = product.astype(BF16)
            lower = (product - upper.astype(F32)).astype(BF16)
            split.append(jnp.concatenate([upper, lower], axis=1))
        qt[0, j] = jnp.transpose(qs[0, j])
        gt[0, j] = jnp.transpose(gs[0, j])
        delta[0, j] = lax.dot_general(
            ones, jnp.concatenate(split, axis=0), NT, preferred_element_type=F32
        )


def prepare(queries, cotangent, output, heads, head_dim):
    rows, width = queries.shape
    per_device = rows // BLOCK
    deep = width // heads // head_dim * BLOCK
    tile = pl.BlockSpec((rows, width // heads), lambda h: (0, h))

    def by_head(*shape):
        return pl.BlockSpec((1,) + shape, lambda h: (h,) + (0,) * len(shape))

    stacked = (per_device, deep, head_dim)
    turned = (per_device, head_dim, deep)
    sums = (per_device, 8, deep)
    return pl.pallas_call(
        functools.partial(prepare_kernel, head_dim=head_dim),
        grid=(heads,),
        in_specs=[tile] * 3,
        out_specs=[by_head(*stacked)] * 2 + [by_head(*turned)] * 2 + [by_head(*sums)],
        out_shape=[jax.ShapeDtypeStruct((heads,) + stacked, BF16)] * 2
        + [jax.ShapeDtypeStruct((heads,) + turned, BF16)] * 2
        + [jax.ShapeDtypeStruct((heads,) + sums, F32)],
        compiler_params=pltpu.CompilerParams(vmem_limit_bytes=16 * MIB),
        cost_estimate=pl.CostEstimate(flops=0, bytes_accessed=7 << 20, transcendentals=0),
    )(queries, cotangent, output)


def slash_rows(offs, h, j, s, per_device):
    return pl.multiple_of((WDEV * per_device + j - offs[h, s]) * BLOCK, BLOCK)


def attend_kernel(
    bases, slab_index, verts, offs, qs, gs, qt, gt, delta, own, *rest,
    lines, nv, ns, per_device, call,
):
    gathered, recv, rest = rest[:2], rest[2 : 2 + WDEV], rest[2 + WDEV :]
    (share, give, low_w, low_ds, cand_keys), scratch = rest[:5], rest[5:]
    win, vkv, vc, s_ref, vert_w, hold, sems = scratch
    i = pl.program_id(0)
    base = bases[call]
    h = base + i
    slab, me = slab_index[0], lax.axis_index("ctx")
    far, near, core = lines.place(me)
    _, chunk, head_dim = share.shape
    cand = nv + 1 + ns
    scaling = 1.0 / math.sqrt(head_dim)
    rows = per_device * BLOCK
    width = qs.shape[2]
    first_block = slab * (per_device * lines.devices) + me * per_device
    lanes = pl.ds(pl.multiple_of(i * head_dim, head_dim), head_dim)

    def window_row(d):
        return pl.multiple_of((WDEV - d) * rows, rows)

    @pl.when(i == 0)
    def _():
        half = win.shape[2]
        own_rows = pl.ds(WDEV * rows, rows)
        side = pl.ds(pl.multiple_of(base * head_dim, half), half)
        copies = [
            pltpu.make_async_copy(
                recv[n].at[:, :, side], win.at[:, pl.ds(window_row(d), rows), :], sems.at[n]
            )
            for n, d in enumerate(distances(core))
        ]
        copies.append(
            pltpu.make_async_copy(own.at[:, :, side], win.at[:, own_rows, :], sems.at[WDEV])
        )
        copies += vertical_copies(lines, me, 0, chunk, gathered, vkv, sems, WDEV + 1)
        for copy in copies:
            copy.start()
        for copy in copies:
            copy.wait()

    vert_rows = pl.ds(pl.multiple_of(i * (nv * BLOCK), nv * BLOCK), nv * BLOCK)
    neg, posinf = jnp.float32(-jnp.inf), jnp.float32(jnp.inf)
    log2_scale = scaling * math.log2(math.e)
    key_at = lax.broadcasted_iota(jnp.int32, (BLOCK, width), 0)
    row_at = lax.broadcasted_iota(jnp.int32, (BLOCK, width), 1) % BLOCK

    def fold(x, op):
        y = x[0:8, :]
        for r in range(1, BLOCK // 8):
            y = op(y, x[r * 8 : (r + 1) * 8, :])
        return y

    vertical_sum = [None, None]
    for j in range(per_device):
        block = first_block + j
        own_at = (WDEV * per_device + j) * BLOCK
        valid = [verts[h, m] < block for m in range(nv)] + [None]
        for s in range(ns):
            collide = verts[h, 0] == block - offs[h, s]
            for m in range(1, nv):
                collide = collide | (verts[h, m] == block - offs[h, s])
            valid.append((offs[h, s] > 0) & jnp.logical_not(collide))
        for kv, to in enumerate((cand_keys.at[0], vc)):
            to[j, 0 : nv * BLOCK, :] = vkv[kv, vert_rows, :]
            to[j, nv * BLOCK : (nv + 1) * BLOCK, :] = win[kv, own_at : own_at + BLOCK, lanes]
            for s in range(ns):
                to[j, (nv + 1 + s) * BLOCK : (nv + 2 + s) * BLOCK, :] = win[
                    kv, pl.ds(slash_rows(offs, h, j, s, per_device), BLOCK), lanes
                ]

        top = None
        for n in range(cand // JOIN):
            span = slice(n * JOIN * BLOCK, (n + 1) * JOIN * BLOCK)
            scores = jnp.dot(cand_keys[0, j, span, :], qt[0, j], preferred_element_type=F32)
            for k in range(JOIN):
                c = n * JOIN + k
                part = scores[k * BLOCK : (k + 1) * BLOCK, :]
                if c == nv:
                    part = jnp.where(key_at <= row_at, part, neg)
                s_ref[j, c * BLOCK : (c + 1) * BLOCK, :] = part
                best = fold(part, jnp.maximum)
                if c != nv:
                    best = best + jnp.where(valid[c], jnp.float32(0), neg)
                top = best if top is None else jnp.maximum(top, best)
        top = jnp.max(top, axis=0, keepdims=True) * log2_scale
        total = jnp.zeros((8, width), F32)
        for c in range(cand):
            span = slice(c * BLOCK, (c + 1) * BLOCK)
            less = top if c == nv else top + jnp.where(valid[c], jnp.float32(0), posinf)
            p = jnp.exp2(s_ref[j, span, :] * log2_scale - less)
            s_ref[j, span, :] = p
            total = total + fold(p, jnp.add)
        inverse = 1.0 / jnp.sum(total, axis=0, keepdims=True)
        row_delta = delta[0, j, 0:1, :]
        for n in range(cand // JOIN):
            span = slice(n * JOIN * BLOCK, (n + 1) * JOIN * BLOCK)
            weight_grad = jnp.dot(vc[j, span, :], gt[0, j], preferred_element_type=F32)
            w = s_ref[j, span, :] * inverse
            if n * JOIN < nv:
                vert_w[j, span, :] = w.astype(BF16)
            else:
                low_w[0, j] = w.astype(BF16)
            low_ds[0, j, span, :] = (w * (weight_grad - row_delta)).astype(BF16)

        here = slice(0, nv * BLOCK)
        dv = jnp.dot(vert_w[j], gs[0, j], preferred_element_type=F32)
        dk = jnp.dot(low_ds[0, j, here, :], qs[0, j], preferred_element_type=F32) * scaling
        for kv, part in enumerate((dk, dv)):
            vertical_sum[kv] = part if j == 0 else vertical_sum[kv] + part

    first = core == 0
    parts = (
        jnp.where(first, vertical_sum[0], vertical_sum[1]),
        jnp.where(first, vertical_sum[1], vertical_sum[0]),
    )
    for c in range(nv * BLOCK // chunk):
        slot = lax.rem(i * (nv * BLOCK // chunk) + c - far + lines.far, lines.far)
        for n, part in enumerate(parts):
            hold[n, slot] = part[c * chunk : (c + 1) * chunk, :]

    @pl.when(i == pl.num_programs(0) - 1)
    def _():
        share[...] = hold[0].astype(share.dtype)
        give[...] = hold[1].astype(give.dtype)


def attend(
    call, bases, slab_index, verticals, offsets, prepared, own, gathered, recv, lines, kept_as
):
    heads, per_device, deep, head_dim = prepared[0].shape
    _, rows, features = own.shape
    nv, ns = verticals.shape[1], offsets.shape[1]
    cand = nv + 1 + ns
    half = heads // 2
    anywhere = pl.BlockSpec(memory_space=pl.ANY)

    def by_head(shape):
        return pl.BlockSpec(
            (1,) + shape[1:], lambda i, bases, *_: (bases[call] + i,) + (0,) * (len(shape) - 1)
        )

    def by_turn(shape):
        return pl.BlockSpec((1,) + shape[1:], lambda i, *_: (i,) + (0,) * (len(shape) - 1))

    share = (lines.far, half * nv * BLOCK // lines.far, head_dim)
    shares = pl.BlockSpec(share, lambda i, *_: (0, 0, 0))
    low_shapes = [
        (half, per_device, (1 + ns) * BLOCK, deep),
        (half, per_device, cand * BLOCK, deep),
        (half, per_device, cand * BLOCK, head_dim),
    ]
    return pl.pallas_call(
        functools.partial(
            attend_kernel, lines=lines, nv=nv, ns=ns, per_device=per_device, call=call
        ),
        grid_spec=pltpu.PrefetchScalarGridSpec(
            num_scalar_prefetch=4,
            grid=(half,),
            in_specs=[by_head(array.shape) for array in prepared]
            + [anywhere] * (3 + WDEV),
            out_specs=[shares] * 2 + [by_turn(shape) for shape in low_shapes],
            scratch_shapes=[
                pltpu.VMEM((2, (WDEV + 1) * rows, features // 2), BF16),
                pltpu.VMEM((2, half * nv * BLOCK, head_dim), BF16),
                pltpu.VMEM((per_device, cand * BLOCK, head_dim), BF16),
                pltpu.VMEM((per_device, cand * BLOCK, deep), F32),
                pltpu.VMEM((per_device, nv * BLOCK, deep), BF16),
                pltpu.VMEM((2,) + share, F32),
                pltpu.SemaphoreType.DMA((WDEV + 1 + 2 * lines.far,)),
            ],
        ),
        out_shape=[
            jax.ShapeDtypeStruct(share, kept_as),
            jax.ShapeDtypeStruct(share, BF16),
        ]
        + [jax.ShapeDtypeStruct(shape, BF16) for shape in low_shapes],
        compiler_params=pltpu.CompilerParams(vmem_limit_bytes=18 * MIB),
        cost_estimate=pl.CostEstimate(
            flops=2 * 5 * half * per_device * cand * BLOCK * deep * head_dim,
            bytes_accessed=12 << 20,
            transcendentals=half * per_device * cand * BLOCK * deep,
        ),
    )(bases, slab_index, verticals, offsets, *prepared, own, *gathered, *recv)


def turn_to_head(t, bases, half):
    return bases[lax.div(t, half)] + lax.rem(t, half)


def of_call(call, half, shape, block=0):
    def index(t, *_):
        turn = jnp.minimum(t, half - 1) if call == 0 else jnp.maximum(t - half, 0)
        return (turn, 0, block, 0)

    return pl.BlockSpec((1,) + tuple(shape), index)


def window_kernel(bases, offs, qs, gs, *rest, lines, half, ns, per_device):
    lows, home, parts, total = (rest[0:2], rest[2:4]), rest[4], rest[5 : 5 + WDEV], rest[5 + WDEV]
    t = pl.program_id(0)
    h = turn_to_head(t, bases, half)
    _, _, core = lines.place(lax.axis_index("ctx"))
    head_dim = qs.shape[3]
    rows = per_device * BLOCK
    scaling = 1.0 / math.sqrt(head_dim)
    lanes = pl.ds(pl.multiple_of(h * head_dim, head_dim), head_dim)
    total[...] = jnp.zeros_like(total)
    for call, (low_w, low_ds) in enumerate(lows):

        @pl.when(lax.div(t, half) == call)
        def _():
            for j in range(per_device):
                dv = jnp.dot(low_w[0, j], gs[0, j], preferred_element_type=F32)
                dk = jnp.dot(low_ds[0, j], qs[0, j], preferred_element_type=F32) * scaling
                own_at = (WDEV * per_device + j) * BLOCK
                for kv, part in enumerate((dk, dv)):
                    total[kv, own_at : own_at + BLOCK, :] += part[0:BLOCK]
                    for s in range(ns):
                        at = slash_rows(offs, h, j, s, per_device)
                        total[kv, pl.ds(at, BLOCK), :] += part[(1 + s) * BLOCK : (2 + s) * BLOCK]

    for kv in range(2):
        home[kv, :, lanes] = total[kv, WDEV * rows :, :]
        for part, d in zip(parts, distances(core)):
            at = pl.multiple_of((WDEV - d) * rows, rows)
            part[kv, :, lanes] = total[kv, pl.ds(at, rows), :].astype(part.dtype)


def window_gradients(bases, offsets, qs, gs, lows, lines, nv):
    heads, per_device, deep, head_dim = qs.shape
    ns = offsets.shape[1]
    half = heads // 2
    rows, features = per_device * BLOCK, heads * head_dim
    shard = (2, rows, features)
    whole = pl.BlockSpec(shard, lambda t, *_: (0, 0, 0))
    stacked = pl.BlockSpec(
        (1,) + qs.shape[1:], lambda t, bases, _: (turn_to_head(t, bases, half), 0, 0, 0)
    )
    tail = (1 + ns) * BLOCK
    block = (per_device, tail, deep)
    specs = []
    for call in range(2):
        specs += [of_call(call, half, block), of_call(call, half, block, nv * BLOCK // tail)]
    return pl.pallas_call(
        functools.partial(window_kernel, lines=lines, half=half, ns=ns, per_device=per_device),
        grid_spec=pltpu.PrefetchScalarGridSpec(
            num_scalar_prefetch=2,
            grid=(heads,),
            in_specs=[stacked] * 2 + specs,
            out_specs=[whole] * (1 + WDEV),
            scratch_shapes=[pltpu.VMEM((2, (WDEV + 1) * rows, head_dim), F32)],
        ),
        out_shape=[jax.ShapeDtypeStruct(shard, F32)] * 3 + [jax.ShapeDtypeStruct(shard, BF16)] * 3,
        compiler_params=pltpu.CompilerParams(vmem_limit_bytes=16 * MIB),
        cost_estimate=pl.CostEstimate(flops=0, bytes_accessed=9 << 20, transcendentals=0),
    )(bases, offsets, qs, gs, *lows[0][:2], *lows[1][:2])


def query_kernel(bases, *rest):
    calls, dq = (rest[0:2], rest[2:4]), rest[4]
    t = pl.program_id(0)
    per_device, _, head_dim = rest[0].shape[1:]
    scaling = 1.0 / math.sqrt(head_dim)
    half = pl.num_programs(0) // 2
    for call, (cand_keys, low_ds) in enumerate(calls):

        @pl.when(lax.div(t, half) == call)
        def _():
            for j in range(per_device):
                turned = lax.dot_general(
                    cand_keys[0, j],
                    low_ds[0, j],
                    (((0,), (0,)), ((), ())),
                    preferred_element_type=F32,
                )
                stacked = (jnp.transpose(turned) * scaling).astype(BF16)
                for g in range(dq.shape[1] // head_dim):
                    dq[j * BLOCK : (j + 1) * BLOCK, g * head_dim : (g + 1) * head_dim] = stacked[
                        g * BLOCK : (g + 1) * BLOCK, :
                    ]


def query_gradients(bases, lows):
    half, per_device, _, head_dim = lows[0][2].shape
    deep = lows[0][1].shape[3]
    rows, width = per_device * BLOCK, deep // BLOCK * head_dim
    specs = []
    for call in range(2):
        specs += [of_call(call, half, lows[0][n].shape[1:]) for n in (2, 1)]
    return pl.pallas_call(
        query_kernel,
        grid_spec=pltpu.PrefetchScalarGridSpec(
            num_scalar_prefetch=1,
            grid=(2 * half,),
            in_specs=specs,
            out_specs=pl.BlockSpec(
                (rows, width), lambda t, bases: (0, turn_to_head(t, bases, half))
            ),
        ),
        out_shape=jax.ShapeDtypeStruct((rows, 2 * half * width), BF16),
        compiler_params=pltpu.CompilerParams(vmem_limit_bytes=16 * MIB),
        cost_estimate=pl.CostEstimate(flops=0, bytes_accessed=10 << 20, transcendentals=0),
    )(bases, lows[0][2], lows[0][1], lows[1][2], lows[1][1])


def zeros_kernel(_, key_out, value_out, blank, sems):
    blank[...] = jnp.zeros_like(blank)
    copies = [
        pltpu.make_async_copy(blank, out.at[r], sems.at[n, r])
        for n, out in enumerate((key_out, value_out))
        for r in range(out.shape[0])
    ]
    for copy in copies:
        copy.start()
    for copy in copies:
        copy.wait()


def zeros(ahead, shape):
    hbm = pl.BlockSpec(memory_space=pltpu.HBM)
    return pl.pallas_call(
        zeros_kernel,
        in_specs=[pl.BlockSpec(memory_space=pl.ANY)],
        out_specs=[hbm] * 2,
        out_shape=[jax.ShapeDtypeStruct(shape, BF16)] * 2,
        scratch_shapes=[pltpu.VMEM(shape[1:], BF16), pltpu.SemaphoreType.DMA((2, shape[0]))],
        compiler_params=pltpu.CompilerParams(vmem_limit_bytes=2 * MIB),
        cost_estimate=pl.CostEstimate(flops=0, bytes_accessed=5 << 20, transcendentals=0),
    )(ahead)


def assemble_kernel(slab_index, verts, home, *rest, lines, heads, nv, per_device):
    from_near, arrived, gathered = rest[0], rest[1:3], rest[3:7]
    outs, vert, acc, low, sems, out_sems, unit_sems = rest[9:11], *rest[11:]
    slab, me = slab_index[0], lax.axis_index("ctx")
    _, near, _ = lines.place(me)
    devices = lines.devices
    chunk, head_dim = gathered[0].shape[1:]
    slab_blocks = per_device * devices
    copies = vertical_copies(lines, me, 1 - near, chunk, gathered[0::2], vert, sems, 0)
    copies += vertical_copies(lines, me, near, chunk, gathered[1::2], vert, sems, 2 * lines.far)
    for copy in copies:
        copy.start()
    acc[0] = home[...]
    acc[1] = jnp.zeros_like(home)

    @pl.when(near == 0)
    def _():
        acc[0] += from_near[...].astype(F32)

    for part, wrapped in zip(arrived, wraps(me, devices)):
        acc[wrapped.astype(jnp.int32)] += part[...].astype(F32)
    for copy in copies:
        copy.wait()

    def unit(h, m):
        inner = lax.rem(verts[h, m], slab_blocks)
        region = lax.div(verts[h, m], slab_blocks)
        row = pl.multiple_of(lax.rem(inner, per_device) * BLOCK, BLOCK)
        close = (region == slab) | (region == slab - 1)
        return lax.div(inner, per_device) == me, close, region, row

    def unit_copies(h, m, region, row):
        at = (h * nv + m) * BLOCK
        for kv in range(2):
            yield pltpu.make_async_copy(
                vert.at[kv, pl.ds(at, BLOCK), :],
                outs[kv].at[region, pl.ds(row, BLOCK), pl.ds(h * head_dim, head_dim)],
                unit_sems.at[kv, h * nv + m],
            )

    for h in range(heads):
        lanes = slice(h * head_dim, (h + 1) * head_dim)
        for m in range(nv):
            mine, close, region, row = unit(h, m)
            at = (h * nv + m) * BLOCK

            @pl.when(mine & close)
            def _():
                for kv in range(2):
                    acc[slab - region, kv, pl.ds(row, BLOCK), lanes] += vert[
                        kv, at : at + BLOCK, :
                    ].astype(F32)

            @pl.when(mine & jnp.logical_not(close))
            def _():
                for copy in unit_copies(h, m, region, row):
                    copy.start()

    low[...] = acc[...].astype(BF16)
    copies = [
        pltpu.make_async_copy(low.at[n, kv], outs[kv].at[slab - n], out_sems.at[n, kv])
        for n in range(2)
        for kv in range(2)
    ]
    for copy in copies:
        copy.start()
    for h in range(heads):
        for m in range(nv):
            mine, close, region, row = unit(h, m)

            @pl.when(mine & jnp.logical_not(close))
            def _():
                for copy in unit_copies(h, m, region, row):
                    copy.wait()

    for copy in copies:
        copy.wait()


def assemble(slab_index, verticals, home, from_near, arrived, gathered, blank, lines):
    _, rows, features = home.shape
    heads, nv = verticals.shape
    smem = pl.BlockSpec(memory_space=pltpu.SMEM)
    vmem = pl.BlockSpec(memory_space=pltpu.VMEM)
    anywhere = pl.BlockSpec(memory_space=pl.ANY)
    hbm = pl.BlockSpec(memory_space=pltpu.HBM)
    return pl.pallas_call(
        functools.partial(
            assemble_kernel, lines=lines, heads=heads, nv=nv, per_device=rows // BLOCK
        ),
        in_specs=[smem] * 2 + [vmem] * 4 + [anywhere] * 4 + [hbm] * 2,
        out_specs=[hbm] * 2,
        out_shape=[jax.ShapeDtypeStruct(blank[0].shape, BF16)] * 2,
        input_output_aliases={10: 0, 11: 1},
        scratch_shapes=[
            pltpu.VMEM((2, heads * nv * BLOCK, features // heads), BF16),
            pltpu.VMEM((2, 2, rows, features), F32),
            pltpu.VMEM((2, 2, rows, features), BF16),
            pltpu.SemaphoreType.DMA((4 * lines.far,)),
            pltpu.SemaphoreType.DMA((2, 2)),
            pltpu.SemaphoreType.DMA((2, heads * nv)),
        ],
        compiler_params=pltpu.CompilerParams(vmem_limit_bytes=12 * MIB),
    )(slab_index, verticals, home, from_near, *arrived, *gathered, *blank)


def shards(
    queries,
    context_keys,
    context_values,
    forward_output,
    output_cotangent,
    verticals,
    offsets,
    slab_index,
):
    lines = Lines(lax.axis_size("ctx"))
    heads, nv = verticals.shape
    head_dim = context_keys.shape[2] // heads
    _, near, _ = lines.place(lax.axis_index("ctx"))

    own, send4, mixed, mine, to_near, to_core, to_both = pack(
        slab_index, verticals, context_keys, context_values, lines
    )
    recv4 = move(send4, lines.shift_pairs(4))
    to_near = core_sum(lines, to_near, to_both)
    quarter = near_sum(lines, mine, move(to_near, lines.near_pairs()), to_core)
    prepared = prepare(after(queries, to_near), output_cotangent, forward_output, heads, head_dim)
    quarter = after(quarter, recv4, *prepared)
    share = far_sum(lines, quarter)
    recv_mixed = move(after(mixed, quarter), lines.mixed_pairs())
    recv2 = move(jnp.where(near == 1, recv4, own), lines.near_pairs())
    other4 = move(recv4, lines.core_pairs())
    blank = zeros(share, context_keys.shape)
    gathered = far_gather(lines, after(share, other4))
    other2 = move(recv2, lines.core_pairs())
    gathered = after(gathered, other2, recv_mixed, *blank)
    gathered = plane_gather(lines, gathered)
    recv = [recv2, recv4, recv_mixed, other2, other4]

    bases = (jnp.stack([near, 1 - near]) * (heads // 2)).astype(jnp.int32)

    def attend_line(call, gathered, kept_as):
        return attend(
            call, bases, slab_index, verticals, offsets, prepared, own, gathered, recv, lines,
            kept_as,
        )

    to_near, to_both, *first_lows = attend_line(0, gathered[0::2], BF16)
    to_near = core_sum(lines, to_near, to_both)
    from_near = move(to_near, lines.near_pairs())
    mine, to_core, *second_lows = attend_line(1, gathered[1::2], F32)
    lows = (first_lows, second_lows)

    home, part2, part4, mixed, give2, give4 = window_gradients(
        bases, after(offsets, from_near), prepared[0], prepared[1], lows, lines, nv
    )
    quarter = after(near_sum(lines, mine, from_near, to_core), home)
    share = far_sum(lines, quarter)
    arrived_mixed = move(mixed, back(lines.mixed_pairs()))
    sum2 = (part2 + move(give2, lines.core_pairs()).astype(F32)).astype(BF16)
    sum4 = part4 + move(give4, lines.core_pairs()).astype(F32)
    from_near = move(sum2, lines.near_pairs())
    totals = after(far_gather(lines, share), from_near, arrived_mixed)
    sum4 = (sum4 + jnp.where(near == 1, from_near.astype(F32), 0.0)).astype(BF16)
    arrived4 = move(after(sum4, totals), back(lines.shift_pairs(4)))
    query_grad = query_gradients(after(bases, totals), lows)
    totals = plane_gather(lines, totals)
    key_gradient, value_gradient = assemble(
        slab_index, verticals, after(home, query_grad), from_near, (arrived4, arrived_mixed),
        totals, blank, lines,
    )
    return query_grad, key_gradient, value_gradient


def solution(mesh):
    in_specs = (
        P(("groups", "ctx"), None),
        P("groups", "ctx", None),
        P("groups", "ctx", None),
        P(("groups", "ctx"), None),
        P(("groups", "ctx"), None),
        P("groups", None),
        P("groups", None),
        P("groups"),
    )
    out_specs = (P(("groups", "ctx"), None), P("groups", "ctx", None), P("groups", "ctx", None))
    return jax.shard_map(shards, mesh=mesh, in_specs=in_specs, out_specs=out_specs, check_vma=False)
```

```python
import functools
import math

import jax
import jax.numpy as jnp
from jax import lax
from jax.experimental import pallas as pl
from jax.experimental.pallas import tpu as pltpu
from jax.sharding import PartitionSpec as P

BLOCK = 64
WDEV = 5
MIB = 1024 * 1024
PACK_VMEM = 60 * MIB
JOIN = 4
BF16 = jnp.bfloat16
F32 = jnp.float32


class Lines:
    def __init__(self, devices):
        self.devices = devices
        self.far = devices // 4

    def place(self, me):
        return lax.div(me, 4), lax.rem(lax.div(me, 2), 2), lax.rem(me, 2)

    def core_pairs(self):
        return [(i, i ^ 1) for i in range(self.devices)]

    def near_pairs(self):
        return [(i, i ^ 2) for i in range(self.devices)]

    def both_pairs(self):
        return [(i, i ^ 3) for i in range(self.devices)]

    def far_pairs(self, by):
        return [(i, (i + 4 * by) % self.devices) for i in range(self.devices)]

    def shift_pairs(self, by):
        return [(i, (i + by) % self.devices) for i in range(self.devices)]

    def mixed_pairs(self):
        return [(i, (i + (5 if i % 2 else 1)) % self.devices) for i in range(self.devices)]


def back(pairs):
    return [(b, a) for a, b in pairs]


def move(array, pairs):
    return lax.ppermute(array, "ctx", pairs)


def after(array, *others):
    return lax.optimization_barrier((array, *others))[0]


def core_sum(lines, to_near, to_both):
    return (to_near.astype(F32) + move(to_both, lines.core_pairs()).astype(F32)).astype(BF16)


def near_sum(lines, mine, from_near, to_core):
    from_core = move(to_core, lines.core_pairs())
    return mine.astype(F32) + from_core.astype(F32) + from_near.astype(F32)


def far_sum(lines, quarter):
    parts = [
        move(quarter[by].astype(BF16), lines.far_pairs(by)) for by in range(1, lines.far)
    ]
    share = quarter[0]
    for part in parts:
        share = share + part.astype(F32)
    return share.astype(BF16)


def far_gather(lines, share):
    parts = [share] + [move(share, lines.far_pairs(by)) for by in range(1, lines.far)]
    return jnp.stack(parts)


def plane_gather(lines, mine):
    across = move(mine, lines.near_pairs())
    core_mine = move(mine, lines.core_pairs())
    core_across = move(across, lines.core_pairs())
    return mine, across, core_mine, core_across


def wraps(me, devices):
    return [me + 4 >= devices, (lax.rem(me, 2) == 1) & (me + 5 >= devices)]


def pack_kernel(slab_index, verts, keys, values, *rest, lines, heads, nv, per_device):
    sends = rest[:3]
    shares = rest[3:7]
    picked, sems, pick_sems = rest[7:]
    slab, me = slab_index[0], lax.axis_index("ctx")
    far, near, core = lines.place(me)
    _, chunk, head_dim = shares[0].shape
    copies = []
    wrapped4, wrapped_mixed = wraps(me, lines.devices)
    for n, region in enumerate(
        (slab, slab - wrapped4.astype(jnp.int32), slab - wrapped_mixed.astype(jnp.int32))
    ):
        for kv, source in enumerate((keys, values)):
            copy = pltpu.make_async_copy(source.at[region], sends[n].at[kv], sems.at[n, kv])
            copy.start()
            copies.append(copy)
    picked[...] = jnp.zeros_like(picked)
    slab_blocks = per_device * lines.devices
    piece = min(BLOCK, chunk)

    def unit_copies(h, m):
        inner = lax.rem(verts[h, m], slab_blocks)
        region = lax.div(verts[h, m], slab_blocks)
        row = lax.rem(inner, per_device) * BLOCK
        for p in range(BLOCK // piece):
            at = (h * nv + m) * BLOCK + p * piece
            line, at = at // (lines.far * chunk), at % (lines.far * chunk)
            slot, at = at // chunk, at % chunk
            line = lax.rem(line + near, 2)
            slot = lax.rem(slot - far + lines.far, lines.far)
            for kv, source in enumerate((keys, values)):
                yield pltpu.make_async_copy(
                    source.at[
                        region,
                        pl.ds(pl.multiple_of(row + p * piece, piece), piece),
                        pl.ds(h * head_dim, head_dim),
                    ],
                    picked.at[lax.rem(kv + core, 2), line, slot, pl.ds(at, piece), :],
                    pick_sems.at[kv, (h * nv + m) * (BLOCK // piece) + p],
                )

    def owned(h, m):
        return lax.div(lax.rem(verts[h, m], slab_blocks), per_device) == me

    for h in range(heads):
        for m in range(nv):

            @pl.when(owned(h, m))
            def _():
                for copy in unit_copies(h, m):
                    copy.start()

    for h in range(heads):
        for m in range(nv):

            @pl.when(owned(h, m))
            def _():
                for copy in unit_copies(h, m):
                    copy.wait()

    for n, share in enumerate(shares):
        share[...] = picked[n // 2, n % 2]
    for copy in copies:
        copy.wait()


def pack(slab_index, verticals, keys, values, lines):
    regions, rows, features = keys.shape
    heads, nv = verticals.shape
    head_dim = features // heads
    chunk = heads * nv * BLOCK // (2 * lines.far)
    smem = pl.BlockSpec(memory_space=pltpu.SMEM)
    hbm = pl.BlockSpec(memory_space=pltpu.HBM)
    share = (lines.far, chunk, head_dim)
    return pl.pallas_call(
        functools.partial(pack_kernel, lines=lines, heads=heads, nv=nv, per_device=rows // BLOCK),
        in_specs=[smem, smem, hbm, hbm],
        out_specs=[pl.BlockSpec(memory_space=pltpu.VMEM)] * 7,
        out_shape=[jax.ShapeDtypeStruct((2, rows, features), BF16)] * 3
        + [jax.ShapeDtypeStruct(share, BF16)] * 4,
        scratch_shapes=[
            pltpu.VMEM((2, 2) + share, BF16),
            pltpu.SemaphoreType.DMA((3, 2)),
            pltpu.SemaphoreType.DMA((2, heads * nv * max(1, BLOCK // chunk))),
        ],
        compiler_params=pltpu.CompilerParams(vmem_limit_bytes=PACK_VMEM),
    )(slab_index, verticals, keys, values)


def distances(core):
    return [2, 4, 5 - 4 * core, 1 + 2 * core, 3 + 2 * core]


def vertical_copies(lines, me, line, chunk, gathered, to, sems, first):
    far, _, core = lines.place(me)
    copies = []
    for kv, source in zip((core, 1 - core), gathered):
        for s in range(lines.far):
            slot = lax.rem(far - s + lines.far, lines.far)
            row = pl.multiple_of((line * lines.far + slot) * chunk, chunk)
            copies.append(
                pltpu.make_async_copy(
                    source.at[s], to.at[kv, pl.ds(row, chunk), :], sems.at[first + len(copies)]
                )
            )
    return copies


NT = (((1,), (1,)), ((), ()))


def turn_to_head(t, bases, half):
    return bases[lax.div(t, half)] + lax.rem(t, half)


def of_call(call, half, shape, block=0):
    def index(t, *_):
        turn = jnp.minimum(t, half - 1) if call == 0 else jnp.maximum(t - half, 0)
        return (turn, 0, block, 0)

    return pl.BlockSpec((1,) + tuple(shape), index)


def prepare_kernel(bases, q, grad, out, *sets, head_dim):
    t = pl.program_id(0)
    half = pl.num_programs(0) // 2
    for call in range(2):

        @pl.when(lax.div(t, half) == call)
        def _():
            prepare_head(q, grad, out, *sets[5 * call : 5 * call + 5], head_dim=head_dim)


def prepare_head(q, grad, out, qs, gs, qt, gt, delta, *, head_dim):
    per_device = qs.shape[1]
    group = q.shape[1] // head_dim
    ones = jnp.ones((8, 2 * head_dim), BF16)
    for j in range(per_device):
        rows = slice(j * BLOCK, (j + 1) * BLOCK)
        split = []
        for g in range(group):
            cols = slice(g * head_dim, (g + 1) * head_dim)
            here = slice(g * BLOCK, (g + 1) * BLOCK)
            qs[0, j, here, :] = q[rows, cols]
            gs[0, j, here, :] = grad[rows, cols]
            product = grad[rows, cols].astype(F32) * out[rows, cols].astype(F32)
            upper = product.astype(BF16)
            lower = (product - upper.astype(F32)).astype(BF16)
            split.append(jnp.concatenate([upper, lower], axis=1))
        qt[0, j] = jnp.transpose(qs[0, j])
        gt[0, j] = jnp.transpose(gs[0, j])
        delta[0, j] = lax.dot_general(
            ones, jnp.concatenate(split, axis=0), NT, preferred_element_type=F32
        )


def prepare(bases, queries, cotangent, output, heads, head_dim):
    rows, width = queries.shape
    per_device = rows // BLOCK
    deep = width // heads // head_dim * BLOCK
    half = heads // 2
    tile = pl.BlockSpec(
        (rows, width // heads), lambda t, bases: (0, turn_to_head(t, bases, half))
    )
    stacked = (per_device, deep, head_dim)
    turned = (per_device, head_dim, deep)
    shapes = [stacked, stacked, turned, turned, (per_device, 8, deep)]
    types = [BF16] * 4 + [F32]
    arrays = pl.pallas_call(
        functools.partial(prepare_kernel, head_dim=head_dim),
        grid_spec=pltpu.PrefetchScalarGridSpec(
            num_scalar_prefetch=1,
            grid=(heads,),
            in_specs=[tile] * 3,
            out_specs=[of_call(call, half, shape) for call in range(2) for shape in shapes],
        ),
        out_shape=[
            jax.ShapeDtypeStruct((half,) + shape, kind) for shape, kind in zip(shapes, types)
        ]
        * 2,
        compiler_params=pltpu.CompilerParams(vmem_limit_bytes=16 * MIB),
        cost_estimate=pl.CostEstimate(flops=0, bytes_accessed=7 << 20, transcendentals=0),
    )(bases, queries, cotangent, output)
    return arrays[:5], arrays[5:]


def slash_rows(offs, h, j, s, per_device):
    return pl.multiple_of((WDEV * per_device + j - offs[h, s]) * BLOCK, BLOCK)


def attend_kernel(
    bases, slab_index, verts, offs, qs, gs, qt, gt, delta, *rest,
    lines, nv, ns, per_device, call,
):
    sources = 1 if call else 1 + WDEV
    gathered, recv, rest = rest[:2], rest[2 : 2 + sources], rest[2 + sources :]
    (share, give, low_w, low_ds, cand_keys), rest = rest[:5], rest[5:]
    scratch = rest if call else rest[1:]
    win, vkv, vc, s_ref, vert_w, hold, sems = scratch
    i = pl.program_id(0)
    base = bases[call]
    h = base + i
    slab, me = slab_index[0], lax.axis_index("ctx")
    far, near, core = lines.place(me)
    _, chunk, head_dim = share.shape
    cand = nv + 1 + ns
    scaling = 1.0 / math.sqrt(head_dim)
    rows = per_device * BLOCK
    width = qs.shape[2]
    first_block = slab * (per_device * lines.devices) + me * per_device
    lanes = pl.ds(pl.multiple_of(i * head_dim, head_dim), head_dim)

    def window_row(d):
        return pl.multiple_of((WDEV - d) * rows, rows)

    @pl.when(i == 0)
    def _():
        half = win.shape[2]
        copies = []
        if call:
            copies.append(pltpu.make_async_copy(recv[0], win, sems.at[0]))
        else:
            for m, to in enumerate((win, rest[0])):
                side = pl.ds(pl.multiple_of(bases[m] * head_dim, half), half)
                for n, d in enumerate([0] + distances(core)):
                    copies.append(
                        pltpu.make_async_copy(
                            recv[n].at[:, :, side],
                            to.at[:, pl.ds(window_row(d), rows), :],
                            sems.at[m * (1 + WDEV) + n],
                        )
                    )
        copies += vertical_copies(lines, me, 0, chunk, gathered, vkv, sems, 2 + 2 * WDEV)
        for copy in copies:
            copy.start()
        for copy in copies:
            copy.wait()

    vert_rows = pl.ds(pl.multiple_of(i * (nv * BLOCK), nv * BLOCK), nv * BLOCK)
    neg, posinf = jnp.float32(-jnp.inf), jnp.float32(jnp.inf)
    log2_scale = scaling * math.log2(math.e)
    key_at = lax.broadcasted_iota(jnp.int32, (BLOCK, width), 0)
    row_at = lax.broadcasted_iota(jnp.int32, (BLOCK, width), 1) % BLOCK

    def fold(x, op):
        y = x[0:8, :]
        for r in range(1, BLOCK // 8):
            y = op(y, x[r * 8 : (r + 1) * 8, :])
        return y

    vertical_sum = [None, None]
    for j in range(per_device):
        block = first_block + j
        own_at = (WDEV * per_device + j) * BLOCK
        valid = [verts[h, m] < block for m in range(nv)] + [None]
        for s in range(ns):
            collide = verts[h, 0] == block - offs[h, s]
            for m in range(1, nv):
                collide = collide | (verts[h, m] == block - offs[h, s])
            valid.append((offs[h, s] > 0) & jnp.logical_not(collide))
        for kv, to in enumerate((cand_keys.at[0], vc)):
            to[j, 0 : nv * BLOCK, :] = vkv[kv, vert_rows, :]
            to[j, nv * BLOCK : (nv + 1) * BLOCK, :] = win[kv, own_at : own_at + BLOCK, lanes]
            for s in range(ns):
                to[j, (nv + 1 + s) * BLOCK : (nv + 2 + s) * BLOCK, :] = win[
                    kv, pl.ds(slash_rows(offs, h, j, s, per_device), BLOCK), lanes
                ]

        top = None
        for n in range(cand // JOIN):
            span = slice(n * JOIN * BLOCK, (n + 1) * JOIN * BLOCK)
            scores = jnp.dot(cand_keys[0, j, span, :], qt[0, j], preferred_element_type=F32)
            for k in range(JOIN):
                c = n * JOIN + k
                part = scores[k * BLOCK : (k + 1) * BLOCK, :]
                if c == nv:
                    part = jnp.where(key_at <= row_at, part, neg)
                s_ref[j, c * BLOCK : (c + 1) * BLOCK, :] = part
                best = fold(part, jnp.maximum)
                if c != nv:
                    best = best + jnp.where(valid[c], jnp.float32(0), neg)
                top = best if top is None else jnp.maximum(top, best)
        top = jnp.max(top, axis=0, keepdims=True) * log2_scale
        total = jnp.zeros((8, width), F32)
        for c in range(cand):
            span = slice(c * BLOCK, (c + 1) * BLOCK)
            less = top if c == nv else top + jnp.where(valid[c], jnp.float32(0), posinf)
            p = jnp.exp2(s_ref[j, span, :] * log2_scale - less)
            s_ref[j, span, :] = p
            total = total + fold(p, jnp.add)
        inverse = 1.0 / jnp.sum(total, axis=0, keepdims=True)
        row_delta = delta[0, j, 0:1, :]
        for n in range(cand // JOIN):
            span = slice(n * JOIN * BLOCK, (n + 1) * JOIN * BLOCK)
            weight_grad = jnp.dot(vc[j, span, :], gt[0, j], preferred_element_type=F32)
            w = s_ref[j, span, :] * inverse
            if n * JOIN < nv:
                vert_w[j, span, :] = w.astype(BF16)
            else:
                low_w[0, j] = w.astype(BF16)
            low_ds[0, j, span, :] = (w * (weight_grad - row_delta)).astype(BF16)

        here = slice(0, nv * BLOCK)
        dv = jnp.dot(vert_w[j], gs[0, j], preferred_element_type=F32)
        dk = jnp.dot(low_ds[0, j, here, :], qs[0, j], preferred_element_type=F32) * scaling
        for kv, part in enumerate((dk, dv)):
            vertical_sum[kv] = part if j == 0 else vertical_sum[kv] + part

    first = core == 0
    parts = (
        jnp.where(first, vertical_sum[0], vertical_sum[1]),
        jnp.where(first, vertical_sum[1], vertical_sum[0]),
    )
    for c in range(nv * BLOCK // chunk):
        slot = lax.rem(i * (nv * BLOCK // chunk) + c - far + lines.far, lines.far)
        for n, part in enumerate(parts):
            hold[n, slot] = part[c * chunk : (c + 1) * chunk, :]

    @pl.when(i == pl.num_programs(0) - 1)
    def _():
        share[...] = hold[0].astype(share.dtype)
        give[...] = hold[1].astype(give.dtype)


def attend(
    call, bases, slab_index, verticals, offsets, prepared, gathered, recv, lines, kept_as
):
    half, per_device, deep, head_dim = prepared[0].shape
    heads = 2 * half
    rows, features = per_device * BLOCK, heads * head_dim
    nv, ns = verticals.shape[1], offsets.shape[1]
    cand = nv + 1 + ns
    anywhere = pl.BlockSpec(memory_space=pl.ANY)

    def by_turn(shape):
        return pl.BlockSpec((1,) + shape[1:], lambda i, *_: (i,) + (0,) * (len(shape) - 1))

    window = (2, (WDEV + 1) * rows, features // 2)
    share = (lines.far, half * nv * BLOCK // lines.far, head_dim)
    shares = pl.BlockSpec(share, lambda i, *_: (0, 0, 0))
    low_shapes = [
        (half, per_device, (1 + ns) * BLOCK, deep),
        (half, per_device, cand * BLOCK, deep),
        (half, per_device, cand * BLOCK, head_dim),
    ]
    return pl.pallas_call(
        functools.partial(
            attend_kernel, lines=lines, nv=nv, ns=ns, per_device=per_device, call=call
        ),
        grid_spec=pltpu.PrefetchScalarGridSpec(
            num_scalar_prefetch=4,
            grid=(half,),
            in_specs=[by_turn(array.shape) for array in prepared]
            + [anywhere] * (2 + len(recv)),
            out_specs=[shares] * 2
            + [by_turn(shape) for shape in low_shapes]
            + [anywhere] * (1 - call),
            scratch_shapes=[
                pltpu.VMEM(window, BF16),
                pltpu.VMEM((2, half * nv * BLOCK, head_dim), BF16),
                pltpu.VMEM((per_device, cand * BLOCK, head_dim), BF16),
                pltpu.VMEM((per_device, cand * BLOCK, deep), F32),
                pltpu.VMEM((per_device, nv * BLOCK, deep), BF16),
                pltpu.VMEM((2,) + share, F32),
                pltpu.SemaphoreType.DMA((2 + 2 * WDEV + 2 * lines.far,)),
            ],
        ),
        out_shape=[
            jax.ShapeDtypeStruct(share, kept_as),
            jax.ShapeDtypeStruct(share, BF16),
        ]
        + [jax.ShapeDtypeStruct(shape, BF16) for shape in low_shapes]
        + [jax.ShapeDtypeStruct(window, BF16)] * (1 - call),
        compiler_params=pltpu.CompilerParams(vmem_limit_bytes=18 * MIB),
        cost_estimate=pl.CostEstimate(
            flops=2 * 5 * half * per_device * cand * BLOCK * deep * head_dim,
            bytes_accessed=12 << 20,
            transcendentals=half * per_device * cand * BLOCK * deep,
        ),
    )(bases, slab_index, verticals, offsets, *prepared, *gathered, *recv)


def window_kernel(bases, offs, *rest, lines, half, ns, per_device):
    calls, home, parts, total = (rest[0:4], rest[4:8]), rest[8], rest[9 : 9 + WDEV], rest[9 + WDEV]
    t = pl.program_id(0)
    h = turn_to_head(t, bases, half)
    _, _, core = lines.place(lax.axis_index("ctx"))
    head_dim = rest[0].shape[3]
    rows = per_device * BLOCK
    scaling = 1.0 / math.sqrt(head_dim)
    lanes = pl.ds(pl.multiple_of(h * head_dim, head_dim), head_dim)
    total[...] = jnp.zeros_like(total)
    for call, (qs, gs, low_w, low_ds) in enumerate(calls):

        @pl.when(lax.div(t, half) == call)
        def _():
            for j in range(per_device):
                dv = jnp.dot(low_w[0, j], gs[0, j], preferred_element_type=F32)
                dk = jnp.dot(low_ds[0, j], qs[0, j], preferred_element_type=F32) * scaling
                own_at = (WDEV * per_device + j) * BLOCK
                for kv, part in enumerate((dk, dv)):
                    total[kv, own_at : own_at + BLOCK, :] += part[0:BLOCK]
                    for s in range(ns):
                        at = slash_rows(offs, h, j, s, per_device)
                        total[kv, pl.ds(at, BLOCK), :] += part[(1 + s) * BLOCK : (2 + s) * BLOCK]

    for kv in range(2):
        home[kv, :, lanes] = total[kv, WDEV * rows :, :]
        for part, d in zip(parts, distances(core)):
            at = pl.multiple_of((WDEV - d) * rows, rows)
            part[kv, :, lanes] = total[kv, pl.ds(at, rows), :].astype(part.dtype)


def window_gradients(bases, offsets, prepared, lows, lines, nv):
    half, per_device, deep, head_dim = prepared[0][0].shape
    heads = 2 * half
    ns = offsets.shape[1]
    rows, features = per_device * BLOCK, heads * head_dim
    shard = (2, rows, features)
    whole = pl.BlockSpec(shard, lambda t, *_: (0, 0, 0))
    stacked = (per_device, deep, head_dim)
    tail = (1 + ns) * BLOCK
    block = (per_device, tail, deep)
    specs = []
    for call in range(2):
        specs += [of_call(call, half, stacked)] * 2
        specs += [of_call(call, half, block), of_call(call, half, block, nv * BLOCK // tail)]
    return pl.pallas_call(
        functools.partial(window_kernel, lines=lines, half=half, ns=ns, per_device=per_device),
        grid_spec=pltpu.PrefetchScalarGridSpec(
            num_scalar_prefetch=2,
            grid=(heads,),
            in_specs=specs,
            out_specs=[whole] * (1 + WDEV),
            scratch_shapes=[pltpu.VMEM((2, (WDEV + 1) * rows, head_dim), F32)],
        ),
        out_shape=[jax.ShapeDtypeStruct(shard, F32)] * 3 + [jax.ShapeDtypeStruct(shard, BF16)] * 3,
        compiler_params=pltpu.CompilerParams(vmem_limit_bytes=16 * MIB),
        cost_estimate=pl.CostEstimate(flops=0, bytes_accessed=9 << 20, transcendentals=0),
    )(bases, offsets, *prepared[0][:2], *lows[0][:2], *prepared[1][:2], *lows[1][:2])


def query_kernel(bases, *rest):
    calls, dq = (rest[0:2], rest[2:4]), rest[4]
    t = pl.program_id(0)
    per_device, _, head_dim = rest[0].shape[1:]
    scaling = 1.0 / math.sqrt(head_dim)
    half = pl.num_programs(0) // 2
    for call, (cand_keys, low_ds) in enumerate(calls):

        @pl.when(lax.div(t, half) == call)
        def _():
            for j in range(per_device):
                turned = lax.dot_general(
                    cand_keys[0, j],
                    low_ds[0, j],
                    (((0,), (0,)), ((), ())),
                    preferred_element_type=F32,
                )
                stacked = (jnp.transpose(turned) * scaling).astype(BF16)
                for g in range(dq.shape[1] // head_dim):
                    dq[j * BLOCK : (j + 1) * BLOCK, g * head_dim : (g + 1) * head_dim] = stacked[
                        g * BLOCK : (g + 1) * BLOCK, :
                    ]


def query_gradients(bases, lows):
    half, per_device, _, head_dim = lows[0][2].shape
    deep = lows[0][1].shape[3]
    rows, width = per_device * BLOCK, deep // BLOCK * head_dim
    specs = []
    for call in range(2):
        specs += [of_call(call, half, lows[0][n].shape[1:]) for n in (2, 1)]
    return pl.pallas_call(
        query_kernel,
        grid_spec=pltpu.PrefetchScalarGridSpec(
            num_scalar_prefetch=1,
            grid=(2 * half,),
            in_specs=specs,
            out_specs=pl.BlockSpec(
                (rows, width), lambda t, bases: (0, turn_to_head(t, bases, half))
            ),
        ),
        out_shape=jax.ShapeDtypeStruct((rows, 2 * half * width), BF16),
        compiler_params=pltpu.CompilerParams(vmem_limit_bytes=16 * MIB),
        cost_estimate=pl.CostEstimate(flops=0, bytes_accessed=10 << 20, transcendentals=0),
    )(bases, lows[0][2], lows[0][1], lows[1][2], lows[1][1])


def zeros_kernel(_, key_out, value_out, blank, sems):
    blank[...] = jnp.zeros_like(blank)
    copies = [
        pltpu.make_async_copy(blank, out.at[r], sems.at[n, r])
        for n, out in enumerate((key_out, value_out))
        for r in range(out.shape[0])
    ]
    for copy in copies:
        copy.start()
    for copy in copies:
        copy.wait()


def zeros(ahead, shape):
    hbm = pl.BlockSpec(memory_space=pltpu.HBM)
    return pl.pallas_call(
        zeros_kernel,
        in_specs=[pl.BlockSpec(memory_space=pl.ANY)],
        out_specs=[hbm] * 2,
        out_shape=[jax.ShapeDtypeStruct(shape, BF16)] * 2,
        scratch_shapes=[pltpu.VMEM(shape[1:], BF16), pltpu.SemaphoreType.DMA((2, shape[0]))],
        compiler_params=pltpu.CompilerParams(vmem_limit_bytes=2 * MIB),
        cost_estimate=pl.CostEstimate(flops=0, bytes_accessed=5 << 20, transcendentals=0),
    )(ahead)


def assemble_kernel(slab_index, verts, home, *rest, lines, heads, nv, per_device):
    from_near, arrived, gathered = rest[0], rest[1:3], rest[3:7]
    outs, vert, acc, low, sems, out_sems, unit_sems = rest[9:11], *rest[11:]
    slab, me = slab_index[0], lax.axis_index("ctx")
    _, near, _ = lines.place(me)
    devices = lines.devices
    chunk, head_dim = gathered[0].shape[1:]
    slab_blocks = per_device * devices
    copies = vertical_copies(lines, me, 1 - near, chunk, gathered[0::2], vert, sems, 0)
    copies += vertical_copies(lines, me, near, chunk, gathered[1::2], vert, sems, 2 * lines.far)
    for copy in copies:
        copy.start()
    acc[0] = home[...]
    acc[1] = jnp.zeros_like(home)

    @pl.when(near == 0)
    def _():
        acc[0] += from_near[...].astype(F32)

    for part, wrapped in zip(arrived, wraps(me, devices)):
        acc[wrapped.astype(jnp.int32)] += part[...].astype(F32)
    for copy in copies:
        copy.wait()

    def unit(h, m):
        inner = lax.rem(verts[h, m], slab_blocks)
        region = lax.div(verts[h, m], slab_blocks)
        row = pl.multiple_of(lax.rem(inner, per_device) * BLOCK, BLOCK)
        close = (region == slab) | (region == slab - 1)
        return lax.div(inner, per_device) == me, close, region, row

    def unit_copies(h, m, region, row):
        at = (h * nv + m) * BLOCK
        for kv in range(2):
            yield pltpu.make_async_copy(
                vert.at[kv, pl.ds(at, BLOCK), :],
                outs[kv].at[region, pl.ds(row, BLOCK), pl.ds(h * head_dim, head_dim)],
                unit_sems.at[kv, h * nv + m],
            )

    for h in range(heads):
        lanes = slice(h * head_dim, (h + 1) * head_dim)
        for m in range(nv):
            mine, close, region, row = unit(h, m)
            at = (h * nv + m) * BLOCK

            @pl.when(mine & close)
            def _():
                for kv in range(2):
                    acc[slab - region, kv, pl.ds(row, BLOCK), lanes] += vert[
                        kv, at : at + BLOCK, :
                    ].astype(F32)

            @pl.when(mine & jnp.logical_not(close))
            def _():
                for copy in unit_copies(h, m, region, row):
                    copy.start()

    low[...] = acc[...].astype(BF16)
    copies = [
        pltpu.make_async_copy(low.at[n, kv], outs[kv].at[slab - n], out_sems.at[n, kv])
        for n in range(2)
        for kv in range(2)
    ]
    for copy in copies:
        copy.start()
    for h in range(heads):
        for m in range(nv):
            mine, close, region, row = unit(h, m)

            @pl.when(mine & jnp.logical_not(close))
            def _():
                for copy in unit_copies(h, m, region, row):
                    copy.wait()

    for copy in copies:
        copy.wait()


def assemble(slab_index, verticals, home, from_near, arrived, gathered, blank, lines):
    _, rows, features = home.shape
    heads, nv = verticals.shape
    smem = pl.BlockSpec(memory_space=pltpu.SMEM)
    vmem = pl.BlockSpec(memory_space=pltpu.VMEM)
    anywhere = pl.BlockSpec(memory_space=pl.ANY)
    hbm = pl.BlockSpec(memory_space=pltpu.HBM)
    return pl.pallas_call(
        functools.partial(
            assemble_kernel, lines=lines, heads=heads, nv=nv, per_device=rows // BLOCK
        ),
        in_specs=[smem] * 2 + [vmem] * 4 + [anywhere] * 4 + [hbm] * 2,
        out_specs=[hbm] * 2,
        out_shape=[jax.ShapeDtypeStruct(blank[0].shape, BF16)] * 2,
        input_output_aliases={10: 0, 11: 1},
        scratch_shapes=[
            pltpu.VMEM((2, heads * nv * BLOCK, features // heads), BF16),
            pltpu.VMEM((2, 2, rows, features), F32),
            pltpu.VMEM((2, 2, rows, features), BF16),
            pltpu.SemaphoreType.DMA((4 * lines.far,)),
            pltpu.SemaphoreType.DMA((2, 2)),
            pltpu.SemaphoreType.DMA((2, heads * nv)),
        ],
        compiler_params=pltpu.CompilerParams(vmem_limit_bytes=12 * MIB),
    )(slab_index, verticals, home, from_near, *arrived, *gathered, *blank)


def shards(
    queries,
    context_keys,
    context_values,
    forward_output,
    output_cotangent,
    verticals,
    offsets,
    slab_index,
):
    lines = Lines(lax.axis_size("ctx"))
    heads, nv = verticals.shape
    head_dim = context_keys.shape[2] // heads
    _, near, _ = lines.place(lax.axis_index("ctx"))

    own, send4, mixed, mine, to_near, to_core, to_both = pack(
        slab_index, verticals, context_keys, context_values, lines
    )
    recv4 = move(send4, lines.shift_pairs(4))
    to_near = core_sum(lines, to_near, to_both)
    quarter = near_sum(lines, mine, move(to_near, lines.near_pairs()), to_core)
    bases = (jnp.stack([near, 1 - near]) * (heads // 2)).astype(jnp.int32)
    prepared = prepare(
        bases, after(queries, to_near), output_cotangent, forward_output, heads, head_dim
    )
    quarter = after(quarter, recv4, *prepared[0], *prepared[1])
    share = far_sum(lines, quarter)
    recv_mixed = move(after(mixed, quarter), lines.mixed_pairs())
    recv2 = move(jnp.where(near == 1, recv4, own), lines.near_pairs())
    other4 = move(recv4, lines.core_pairs())
    blank = zeros(share, context_keys.shape)
    gathered = far_gather(lines, after(share, other4))
    other2 = move(recv2, lines.core_pairs())
    gathered = after(gathered, other2, recv_mixed, *blank)
    gathered = plane_gather(lines, gathered)
    recv = [own, recv2, recv4, recv_mixed, other2, other4]

    def attend_line(call, gathered, recv, kept_as):
        return attend(
            call, bases, slab_index, verticals, offsets, prepared[call], gathered, recv, lines,
            kept_as,
        )

    to_near, to_both, *first_lows, window = attend_line(0, gathered[0::2], recv, BF16)
    to_near = core_sum(lines, to_near, to_both)
    from_near = move(to_near, lines.near_pairs())
    mine, to_core, *second_lows = attend_line(1, gathered[1::2], [window], F32)
    lows = (first_lows, second_lows)

    home, part2, part4, mixed, give2, give4 = window_gradients(
        bases, after(offsets, from_near), prepared, lows, lines, nv
    )
    quarter = after(near_sum(lines, mine, from_near, to_core), home)
    share = far_sum(lines, quarter)
    arrived_mixed = move(mixed, back(lines.mixed_pairs()))
    sum2 = (part2 + move(give2, lines.core_pairs()).astype(F32)).astype(BF16)
    sum4 = part4 + move(give4, lines.core_pairs()).astype(F32)
    from_near = move(sum2, lines.near_pairs())
    totals = after(far_gather(lines, share), from_near, arrived_mixed)
    sum4 = (sum4 + jnp.where(near == 1, from_near.astype(F32), 0.0)).astype(BF16)
    arrived4 = move(after(sum4, totals), back(lines.shift_pairs(4)))
    query_grad = query_gradients(after(bases, totals), lows)
    totals = plane_gather(lines, totals)
    key_gradient, value_gradient = assemble(
        slab_index, verticals, after(home, query_grad), from_near, (arrived4, arrived_mixed),
        totals, blank, lines,
    )
    return query_grad, key_gradient, value_gradient


def solution(mesh):
    in_specs = (
        P(("groups", "ctx"), None),
        P("groups", "ctx", None),
        P("groups", "ctx", None),
        P(("groups", "ctx"), None),
        P(("groups", "ctx"), None),
        P("groups", None),
        P("groups", None),
        P("groups"),
    )
    out_specs = (P(("groups", "ctx"), None), P("groups", "ctx", None), P("groups", "ctx", None))
    return jax.shard_map(shards, mesh=mesh, in_specs=in_specs, out_specs=out_specs, check_vma=False)
```

```python
import functools
import math

import jax
import jax.numpy as jnp
from jax import lax
from jax.experimental import pallas as pl
from jax.experimental.pallas import tpu as pltpu
from jax.sharding import PartitionSpec as P

BLOCK = 64
WDEV = 5
MIB = 1024 * 1024
PACK_VMEM = 60 * MIB
JOIN = 4
BF16 = jnp.bfloat16
F32 = jnp.float32


class Lines:
    def __init__(self, devices):
        self.devices = devices
        self.far = devices // 4

    def place(self, me):
        return lax.div(me, 4), lax.rem(lax.div(me, 2), 2), lax.rem(me, 2)

    def core_pairs(self):
        return [(i, i ^ 1) for i in range(self.devices)]

    def near_pairs(self):
        return [(i, i ^ 2) for i in range(self.devices)]

    def both_pairs(self):
        return [(i, i ^ 3) for i in range(self.devices)]

    def far_pairs(self, by):
        return [(i, (i + 4 * by) % self.devices) for i in range(self.devices)]

    def shift_pairs(self, by):
        return [(i, (i + by) % self.devices) for i in range(self.devices)]

    def mixed_pairs(self):
        return [(i, (i + (5 if i % 2 else 1)) % self.devices) for i in range(self.devices)]


def back(pairs):
    return [(b, a) for a, b in pairs]


def move(array, pairs):
    return lax.ppermute(array, "ctx", pairs)


def after(array, *others):
    return lax.optimization_barrier((array, *others))[0]


def core_sum(lines, to_near, to_both):
    return (to_near.astype(F32) + move(to_both, lines.core_pairs()).astype(F32)).astype(BF16)


def near_sum(lines, mine, from_near, to_core):
    from_core = move(to_core, lines.core_pairs())
    return mine.astype(F32) + from_core.astype(F32) + from_near.astype(F32)


def far_sum(lines, quarter):
    parts = [
        move(quarter[by].astype(BF16), lines.far_pairs(by)) for by in range(1, lines.far)
    ]
    share = quarter[0]
    for part in parts:
        share = share + part.astype(F32)
    return share.astype(BF16)


def far_gather(lines, share):
    parts = [share] + [move(share, lines.far_pairs(by)) for by in range(1, lines.far)]
    return jnp.stack(parts)


def plane_gather(lines, mine):
    across = move(mine, lines.near_pairs())
    core_mine = move(mine, lines.core_pairs())
    core_across = move(across, lines.core_pairs())
    return mine, across, core_mine, core_across


def wraps(me, devices):
    return [me + 4 >= devices, (lax.rem(me, 2) == 1) & (me + 5 >= devices)]


def pack_kernel(slab_index, verts, keys, values, *rest, lines, heads, nv, per_device):
    sends = rest[:3]
    shares = rest[3:7]
    picked, sems, pick_sems = rest[7:]
    slab, me = slab_index[0], lax.axis_index("ctx")
    far, near, core = lines.place(me)
    _, chunk, head_dim = shares[0].shape
    copies = []
    wrapped4, wrapped_mixed = wraps(me, lines.devices)
    for n, region in enumerate(
        (slab, slab - wrapped4.astype(jnp.int32), slab - wrapped_mixed.astype(jnp.int32))
    ):
        for kv, source in enumerate((keys, values)):
            copy = pltpu.make_async_copy(source.at[region], sends[n].at[kv], sems.at[n, kv])
            copy.start()
            copies.append(copy)
    picked[...] = jnp.zeros_like(picked)
    slab_blocks = per_device * lines.devices
    piece = min(BLOCK, chunk)

    def unit_copies(h, m):
        inner = lax.rem(verts[h, m], slab_blocks)
        region = lax.div(verts[h, m], slab_blocks)
        row = lax.rem(inner, per_device) * BLOCK
        for p in range(BLOCK // piece):
            at = (h * nv + m) * BLOCK + p * piece
            line, at = at // (lines.far * chunk), at % (lines.far * chunk)
            slot, at = at // chunk, at % chunk
            line = lax.rem(line + near, 2)
            slot = lax.rem(slot - far + lines.far, lines.far)
            for kv, source in enumerate((keys, values)):
                yield pltpu.make_async_copy(
                    source.at[
                        region,
                        pl.ds(pl.multiple_of(row + p * piece, piece), piece),
                        pl.ds(h * head_dim, head_dim),
                    ],
                    picked.at[lax.rem(kv + core, 2), line, slot, pl.ds(at, piece), :],
                    pick_sems.at[kv, (h * nv + m) * (BLOCK // piece) + p],
                )

    def owned(h, m):
        return lax.div(lax.rem(verts[h, m], slab_blocks), per_device) == me

    for h in range(heads):
        for m in range(nv):

            @pl.when(owned(h, m))
            def _():
                for copy in unit_copies(h, m):
                    copy.start()

    for h in range(heads):
        for m in range(nv):

            @pl.when(owned(h, m))
            def _():
                for copy in unit_copies(h, m):
                    copy.wait()

    for n, share in enumerate(shares):
        share[...] = picked[n // 2, n % 2]
    for copy in copies:
        copy.wait()


def pack(slab_index, verticals, keys, values, lines):
    regions, rows, features = keys.shape
    heads, nv = verticals.shape
    head_dim = features // heads
    chunk = heads * nv * BLOCK // (2 * lines.far)
    smem = pl.BlockSpec(memory_space=pltpu.SMEM)
    hbm = pl.BlockSpec(memory_space=pltpu.HBM)
    share = (lines.far, chunk, head_dim)
    return pl.pallas_call(
        functools.partial(pack_kernel, lines=lines, heads=heads, nv=nv, per_device=rows // BLOCK),
        in_specs=[smem, smem, hbm, hbm],
        out_specs=[pl.BlockSpec(memory_space=pltpu.VMEM)] * 7,
        out_shape=[jax.ShapeDtypeStruct((2, rows, features), BF16)] * 3
        + [jax.ShapeDtypeStruct(share, BF16)] * 4,
        scratch_shapes=[
            pltpu.VMEM((2, 2) + share, BF16),
            pltpu.SemaphoreType.DMA((3, 2)),
            pltpu.SemaphoreType.DMA((2, heads * nv * max(1, BLOCK // chunk))),
        ],
        compiler_params=pltpu.CompilerParams(vmem_limit_bytes=PACK_VMEM),
    )(slab_index, verticals, keys, values)


def distances(core):
    return [2, 4, 5 - 4 * core, 1 + 2 * core, 3 + 2 * core]


def vertical_copies(lines, me, line, chunk, gathered, to, sems, first):
    far, _, core = lines.place(me)
    copies = []
    for kv, source in zip((core, 1 - core), gathered):
        for s in range(lines.far):
            slot = lax.rem(far - s + lines.far, lines.far)
            row = pl.multiple_of((line * lines.far + slot) * chunk, chunk)
            copies.append(
                pltpu.make_async_copy(
                    source.at[s], to.at[kv, pl.ds(row, chunk), :], sems.at[first + len(copies)]
                )
            )
    return copies


NT = (((1,), (1,)), ((), ()))


def turn_to_head(t, bases, half):
    return bases[lax.div(t, half)] + lax.rem(t, half)


def of_call(call, half, shape, block=0):
    def index(t, *_):
        turn = jnp.minimum(t, half - 1) if call == 0 else jnp.maximum(t - half, 0)
        return (turn, 0, block, 0)

    return pl.BlockSpec((1,) + tuple(shape), index)


def prepare_kernel(bases, q, grad, out, *sets, head_dim):
    t = pl.program_id(0)
    half = pl.num_programs(0) // 2
    for call in range(2):

        @pl.when(lax.div(t, half) == call)
        def _():
            prepare_head(q, grad, out, *sets[5 * call : 5 * call + 5], head_dim=head_dim)


def prepare_head(q, grad, out, qs, gs, qt, gt, delta, *, head_dim):
    per_device = qs.shape[1]
    group = q.shape[1] // head_dim
    ones = jnp.ones((8, 2 * head_dim), BF16)
    for j in range(per_device):
        rows = slice(j * BLOCK, (j + 1) * BLOCK)
        split = []
        for g in range(group):
            cols = slice(g * head_dim, (g + 1) * head_dim)
            here = slice(g * BLOCK, (g + 1) * BLOCK)
            qs[0, j, here, :] = q[rows, cols]
            gs[0, j, here, :] = grad[rows, cols]
            product = grad[rows, cols].astype(F32) * out[rows, cols].astype(F32)
            upper = product.astype(BF16)
            lower = (product - upper.astype(F32)).astype(BF16)
            split.append(jnp.concatenate([upper, lower], axis=1))
        qt[0, j] = jnp.transpose(qs[0, j])
        gt[0, j] = jnp.transpose(gs[0, j])
        delta[0, j] = lax.dot_general(
            ones, jnp.concatenate(split, axis=0), NT, preferred_element_type=F32
        )


def prepare(bases, queries, cotangent, output, heads, head_dim):
    rows, width = queries.shape
    per_device = rows // BLOCK
    deep = width // heads // head_dim * BLOCK
    half = heads // 2
    tile = pl.BlockSpec(
        (rows, width // heads), lambda t, bases: (0, turn_to_head(t, bases, half))
    )
    stacked = (per_device, deep, head_dim)
    turned = (per_device, head_dim, deep)
    shapes = [stacked, stacked, turned, turned, (per_device, 8, deep)]
    types = [BF16] * 4 + [F32]
    arrays = pl.pallas_call(
        functools.partial(prepare_kernel, head_dim=head_dim),
        grid_spec=pltpu.PrefetchScalarGridSpec(
            num_scalar_prefetch=1,
            grid=(heads,),
            in_specs=[tile] * 3,
            out_specs=[of_call(call, half, shape) for call in range(2) for shape in shapes],
        ),
        out_shape=[
            jax.ShapeDtypeStruct((half,) + shape, kind) for shape, kind in zip(shapes, types)
        ]
        * 2,
        compiler_params=pltpu.CompilerParams(vmem_limit_bytes=16 * MIB),
        cost_estimate=pl.CostEstimate(flops=0, bytes_accessed=7 << 20, transcendentals=0),
    )(bases, queries, cotangent, output)
    return arrays[:5], arrays[5:]


def slash_rows(offs, h, j, s, per_device):
    return pl.multiple_of((WDEV * per_device + j - offs[h, s]) * BLOCK, BLOCK)


def attend_kernel(
    bases, slab_index, verts, offs, qs, gs, qt, gt, delta, *rest,
    lines, nv, ns, per_device, call,
):
    sources = 1 if call else 1 + WDEV
    gathered, recv, rest = rest[:2], rest[2 : 2 + sources], rest[2 + sources :]
    (share, give, low_w, low_ds, cand_keys), rest = rest[:5], rest[5:]
    scratch = rest if call else rest[1:]
    win, vkv, vc, s_ref, vert_w, hold, sems = scratch
    i = pl.program_id(0)
    base = bases[call]
    h = base + i
    slab, me = slab_index[0], lax.axis_index("ctx")
    far, near, core = lines.place(me)
    _, chunk, head_dim = share.shape
    cand = nv + 1 + ns
    scaling = 1.0 / math.sqrt(head_dim)
    rows = per_device * BLOCK
    width = qs.shape[2]
    first_block = slab * (per_device * lines.devices) + me * per_device
    lanes = pl.ds(pl.multiple_of(i * head_dim, head_dim), head_dim)

    def window_row(d):
        return pl.multiple_of((WDEV - d) * rows, rows)

    @pl.when(i == 0)
    def _():
        half = win.shape[2]
        copies = []
        if call:
            copies.append(pltpu.make_async_copy(recv[0], win, sems.at[0]))
        else:
            for m, to in enumerate((win, rest[0])):
                side = pl.ds(pl.multiple_of(bases[m] * head_dim, half), half)
                for n, d in enumerate([0] + distances(core)):
                    copies.append(
                        pltpu.make_async_copy(
                            recv[n].at[:, :, side],
                            to.at[:, pl.ds(window_row(d), rows), :],
                            sems.at[m * (1 + WDEV) + n],
                        )
                    )
        copies += vertical_copies(lines, me, 0, chunk, gathered, vkv, sems, 2 + 2 * WDEV)
        for copy in copies:
            copy.start()
        for copy in copies:
            copy.wait()

    vert_rows = pl.ds(pl.multiple_of(i * (nv * BLOCK), nv * BLOCK), nv * BLOCK)
    neg, posinf = jnp.float32(-jnp.inf), jnp.float32(jnp.inf)
    log2_scale = scaling * math.log2(math.e)
    key_at = lax.broadcasted_iota(jnp.int32, (BLOCK, width), 0)
    row_at = lax.broadcasted_iota(jnp.int32, (BLOCK, width), 1) % BLOCK

    def fold(x, op):
        y = x[0:8, :]
        for r in range(1, BLOCK // 8):
            y = op(y, x[r * 8 : (r + 1) * 8, :])
        return y

    vertical_sum = [None, None]
    for j in range(per_device):
        block = first_block + j
        own_at = (WDEV * per_device + j) * BLOCK
        valid = [verts[h, m] < block for m in range(nv)] + [None]
        for s in range(ns):
            collide = verts[h, 0] == block - offs[h, s]
            for m in range(1, nv):
                collide = collide | (verts[h, m] == block - offs[h, s])
            valid.append((offs[h, s] > 0) & jnp.logical_not(collide))
        for kv, to in enumerate((cand_keys.at[0], vc)):
            to[j, 0 : nv * BLOCK, :] = vkv[kv, vert_rows, :]
            to[j, nv * BLOCK : (nv + 1) * BLOCK, :] = win[kv, own_at : own_at + BLOCK, lanes]
            for s in range(ns):
                to[j, (nv + 1 + s) * BLOCK : (nv + 2 + s) * BLOCK, :] = win[
                    kv, pl.ds(slash_rows(offs, h, j, s, per_device), BLOCK), lanes
                ]

        top = None
        for n in range(cand // JOIN):
            span = slice(n * JOIN * BLOCK, (n + 1) * JOIN * BLOCK)
            scores = jnp.dot(cand_keys[0, j, span, :], qt[0, j], preferred_element_type=F32)
            for k in range(JOIN):
                c = n * JOIN + k
                part = scores[k * BLOCK : (k + 1) * BLOCK, :]
                if c == nv:
                    part = jnp.where(key_at <= row_at, part, neg)
                s_ref[j, c * BLOCK : (c + 1) * BLOCK, :] = part
                best = fold(part, jnp.maximum)
                if c != nv:
                    best = best + jnp.where(valid[c], jnp.float32(0), neg)
                top = best if top is None else jnp.maximum(top, best)
        top = jnp.max(top, axis=0, keepdims=True) * log2_scale
        total = jnp.zeros((8, width), F32)
        for c in range(cand):
            span = slice(c * BLOCK, (c + 1) * BLOCK)
            less = top if c == nv else top + jnp.where(valid[c], jnp.float32(0), posinf)
            p = jnp.exp2(s_ref[j, span, :] * log2_scale - less)
            s_ref[j, span, :] = p
            total = total + fold(p, jnp.add)
        inverse = 1.0 / jnp.sum(total, axis=0, keepdims=True)
        row_delta = delta[0, j, 0:1, :]
        for n in range(cand // JOIN):
            span = slice(n * JOIN * BLOCK, (n + 1) * JOIN * BLOCK)
            weight_grad = jnp.dot(vc[j, span, :], gt[0, j], preferred_element_type=F32)
            w = s_ref[j, span, :] * inverse
            if n * JOIN < nv:
                vert_w[j, span, :] = w.astype(BF16)
            else:
                low_w[0, j] = w.astype(BF16)
            low_ds[0, j, span, :] = (w * (weight_grad - row_delta)).astype(BF16)

        here = slice(0, nv * BLOCK)
        dv = jnp.dot(vert_w[j], gs[0, j], preferred_element_type=F32)
        dk = jnp.dot(low_ds[0, j, here, :], qs[0, j], preferred_element_type=F32) * scaling
        for kv, part in enumerate((dk, dv)):
            vertical_sum[kv] = part if j == 0 else vertical_sum[kv] + part

    first = core == 0
    parts = (
        jnp.where(first, vertical_sum[0], vertical_sum[1]),
        jnp.where(first, vertical_sum[1], vertical_sum[0]),
    )
    for c in range(nv * BLOCK // chunk):
        slot = lax.rem(i * (nv * BLOCK // chunk) + c - far + lines.far, lines.far)
        for n, part in enumerate(parts):
            hold[n, slot] = part[c * chunk : (c + 1) * chunk, :]

    @pl.when(i == pl.num_programs(0) - 1)
    def _():
        share[...] = hold[0].astype(share.dtype)
        give[...] = hold[1].astype(give.dtype)


def attend(
    call, bases, slab_index, verticals, offsets, prepared, gathered, recv, lines, kept_as
):
    half, per_device, deep, head_dim = prepared[0].shape
    heads = 2 * half
    rows, features = per_device * BLOCK, heads * head_dim
    nv, ns = verticals.shape[1], offsets.shape[1]
    cand = nv + 1 + ns
    anywhere = pl.BlockSpec(memory_space=pl.ANY)

    def by_turn(shape):
        return pl.BlockSpec((1,) + shape[1:], lambda i, *_: (i,) + (0,) * (len(shape) - 1))

    window = (2, (WDEV + 1) * rows, features // 2)
    share = (lines.far, half * nv * BLOCK // lines.far, head_dim)
    shares = pl.BlockSpec(share, lambda i, *_: (0, 0, 0))
    low_shapes = [
        (half, per_device, (1 + ns) * BLOCK, deep),
        (half, per_device, cand * BLOCK, deep),
        (half, per_device, cand * BLOCK, head_dim),
    ]
    return pl.pallas_call(
        functools.partial(
            attend_kernel, lines=lines, nv=nv, ns=ns, per_device=per_device, call=call
        ),
        grid_spec=pltpu.PrefetchScalarGridSpec(
            num_scalar_prefetch=4,
            grid=(half,),
            in_specs=[by_turn(array.shape) for array in prepared]
            + [anywhere] * (2 + len(recv)),
            out_specs=[shares] * 2
            + [by_turn(shape) for shape in low_shapes]
            + [anywhere] * (1 - call),
            scratch_shapes=[
                pltpu.VMEM(window, BF16),
                pltpu.VMEM((2, half * nv * BLOCK, head_dim), BF16),
                pltpu.VMEM((per_device, cand * BLOCK, head_dim), BF16),
                pltpu.VMEM((per_device, cand * BLOCK, deep), F32),
                pltpu.VMEM((per_device, nv * BLOCK, deep), BF16),
                pltpu.VMEM((2,) + share, F32),
                pltpu.SemaphoreType.DMA((2 + 2 * WDEV + 2 * lines.far,)),
            ],
        ),
        out_shape=[
            jax.ShapeDtypeStruct(share, kept_as),
            jax.ShapeDtypeStruct(share, BF16),
        ]
        + [jax.ShapeDtypeStruct(shape, BF16) for shape in low_shapes]
        + [jax.ShapeDtypeStruct(window, BF16)] * (1 - call),
        compiler_params=pltpu.CompilerParams(vmem_limit_bytes=18 * MIB),
        cost_estimate=pl.CostEstimate(
            flops=2 * 5 * half * per_device * cand * BLOCK * deep * head_dim,
            bytes_accessed=12 << 20,
            transcendentals=half * per_device * cand * BLOCK * deep,
        ),
    )(bases, slab_index, verticals, offsets, *prepared, *gathered, *recv)


def window_kernel(bases, offs, *rest, lines, half, ns, per_device):
    calls, home, parts, total = (rest[0:4], rest[4:8]), rest[8], rest[9 : 9 + WDEV], rest[9 + WDEV]
    t = pl.program_id(0)
    h = turn_to_head(t, bases, half)
    _, _, core = lines.place(lax.axis_index("ctx"))
    head_dim = rest[0].shape[3]
    rows = per_device * BLOCK
    scaling = 1.0 / math.sqrt(head_dim)
    lanes = pl.ds(pl.multiple_of(h * head_dim, head_dim), head_dim)
    total[...] = jnp.zeros_like(total)
    for call, (qs, gs, low_w, low_ds) in enumerate(calls):

        @pl.when(lax.div(t, half) == call)
        def _():
            for j in range(per_device):
                dv = jnp.dot(low_w[0, j], gs[0, j], preferred_element_type=F32)
                dk = jnp.dot(low_ds[0, j], qs[0, j], preferred_element_type=F32) * scaling
                own_at = (WDEV * per_device + j) * BLOCK
                for kv, part in enumerate((dk, dv)):
                    total[kv, own_at : own_at + BLOCK, :] += part[0:BLOCK]
                    for s in range(ns):
                        at = slash_rows(offs, h, j, s, per_device)
                        total[kv, pl.ds(at, BLOCK), :] += part[(1 + s) * BLOCK : (2 + s) * BLOCK]

    for kv in range(2):
        home[kv, :, lanes] = total[kv, WDEV * rows :, :]
        for part, d in zip(parts, distances(core)):
            at = pl.multiple_of((WDEV - d) * rows, rows)
            part[kv, :, lanes] = total[kv, pl.ds(at, rows), :].astype(part.dtype)


def window_gradients(bases, offsets, prepared, lows, lines, nv):
    half, per_device, deep, head_dim = prepared[0][0].shape
    heads = 2 * half
    ns = offsets.shape[1]
    rows, features = per_device * BLOCK, heads * head_dim
    shard = (2, rows, features)
    whole = pl.BlockSpec(shard, lambda t, *_: (0, 0, 0))
    stacked = (per_device, deep, head_dim)
    tail = (1 + ns) * BLOCK
    block = (per_device, tail, deep)
    specs = []
    for call in range(2):
        specs += [of_call(call, half, stacked)] * 2
        specs += [of_call(call, half, block), of_call(call, half, block, nv * BLOCK // tail)]
    return pl.pallas_call(
        functools.partial(window_kernel, lines=lines, half=half, ns=ns, per_device=per_device),
        grid_spec=pltpu.PrefetchScalarGridSpec(
            num_scalar_prefetch=2,
            grid=(heads,),
            in_specs=specs,
            out_specs=[whole] * (1 + WDEV),
            scratch_shapes=[pltpu.VMEM((2, (WDEV + 1) * rows, head_dim), F32)],
        ),
        out_shape=[jax.ShapeDtypeStruct(shard, F32)] * 3 + [jax.ShapeDtypeStruct(shard, BF16)] * 3,
        compiler_params=pltpu.CompilerParams(vmem_limit_bytes=16 * MIB),
        cost_estimate=pl.CostEstimate(flops=0, bytes_accessed=9 << 20, transcendentals=0),
    )(bases, offsets, *prepared[0][:2], *lows[0][:2], *prepared[1][:2], *lows[1][:2])


def query_kernel(bases, *rest):
    calls, dq = (rest[0:2], rest[2:4]), rest[4]
    t = pl.program_id(0)
    per_device, _, head_dim = rest[0].shape[1:]
    scaling = 1.0 / math.sqrt(head_dim)
    half = pl.num_programs(0) // 2
    for call, (cand_keys, low_ds) in enumerate(calls):

        @pl.when(lax.div(t, half) == call)
        def _():
            for j in range(per_device):
                turned = lax.dot_general(
                    cand_keys[0, j],
                    low_ds[0, j],
                    (((0,), (0,)), ((), ())),
                    preferred_element_type=F32,
                )
                stacked = (jnp.transpose(turned) * scaling).astype(BF16)
                for g in range(dq.shape[1] // head_dim):
                    dq[j * BLOCK : (j + 1) * BLOCK, g * head_dim : (g + 1) * head_dim] = stacked[
                        g * BLOCK : (g + 1) * BLOCK, :
                    ]


def query_gradients(bases, lows):
    half, per_device, _, head_dim = lows[0][2].shape
    deep = lows[0][1].shape[3]
    rows, width = per_device * BLOCK, deep // BLOCK * head_dim
    specs = []
    for call in range(2):
        specs += [of_call(call, half, lows[0][n].shape[1:]) for n in (2, 1)]
    return pl.pallas_call(
        query_kernel,
        grid_spec=pltpu.PrefetchScalarGridSpec(
            num_scalar_prefetch=1,
            grid=(2 * half,),
            in_specs=specs,
            out_specs=pl.BlockSpec(
                (rows, width), lambda t, bases: (0, turn_to_head(t, bases, half))
            ),
        ),
        out_shape=jax.ShapeDtypeStruct((rows, 2 * half * width), BF16),
        compiler_params=pltpu.CompilerParams(vmem_limit_bytes=16 * MIB),
        cost_estimate=pl.CostEstimate(flops=0, bytes_accessed=10 << 20, transcendentals=0),
    )(bases, lows[0][2], lows[0][1], lows[1][2], lows[1][1])


def zeros_kernel(_, key_out, value_out, blank, sems):
    blank[...] = jnp.zeros_like(blank)
    copies = [
        pltpu.make_async_copy(blank, out.at[r], sems.at[n, r])
        for n, out in enumerate((key_out, value_out))
        for r in range(out.shape[0])
    ]
    for copy in copies:
        copy.start()
    for copy in copies:
        copy.wait()


def zeros(ahead, shape):
    hbm = pl.BlockSpec(memory_space=pltpu.HBM)
    return pl.pallas_call(
        zeros_kernel,
        in_specs=[pl.BlockSpec(memory_space=pl.ANY)],
        out_specs=[hbm] * 2,
        out_shape=[jax.ShapeDtypeStruct(shape, BF16)] * 2,
        scratch_shapes=[pltpu.VMEM(shape[1:], BF16), pltpu.SemaphoreType.DMA((2, shape[0]))],
        compiler_params=pltpu.CompilerParams(vmem_limit_bytes=2 * MIB),
        cost_estimate=pl.CostEstimate(flops=0, bytes_accessed=5 << 20, transcendentals=0),
    )(ahead)


def assemble_kernel(slab_index, verts, home, *rest, lines, heads, nv, per_device):
    from_near, arrived, gathered = rest[0], rest[1:3], rest[3:7]
    outs, vert, acc, low, sems, out_sems, unit_sems = rest[9:11], *rest[11:]
    slab, me = slab_index[0], lax.axis_index("ctx")
    _, near, _ = lines.place(me)
    devices = lines.devices
    chunk, head_dim = gathered[0].shape[1:]
    slab_blocks = per_device * devices
    copies = vertical_copies(lines, me, 1 - near, chunk, gathered[0::2], vert, sems, 0)
    copies += vertical_copies(lines, me, near, chunk, gathered[1::2], vert, sems, 2 * lines.far)
    for copy in copies:
        copy.start()
    acc[0] = home[...]
    acc[1] = jnp.zeros_like(home)

    @pl.when(near == 0)
    def _():
        acc[0] += from_near[...].astype(F32)

    for part, wrapped in zip(arrived, wraps(me, devices)):
        acc[wrapped.astype(jnp.int32)] += part[...].astype(F32)
    for copy in copies:
        copy.wait()

    def unit(h, m):
        inner = lax.rem(verts[h, m], slab_blocks)
        region = lax.div(verts[h, m], slab_blocks)
        row = pl.multiple_of(lax.rem(inner, per_device) * BLOCK, BLOCK)
        close = (region == slab) | (region == slab - 1)
        return lax.div(inner, per_device) == me, close, region, row

    def unit_copies(h, m, region, row):
        at = (h * nv + m) * BLOCK
        for kv in range(2):
            yield pltpu.make_async_copy(
                vert.at[kv, pl.ds(at, BLOCK), :],
                outs[kv].at[region, pl.ds(row, BLOCK), pl.ds(h * head_dim, head_dim)],
                unit_sems.at[kv, h * nv + m],
            )

    for h in range(heads):
        lanes = slice(h * head_dim, (h + 1) * head_dim)
        for m in range(nv):
            mine, close, region, row = unit(h, m)
            at = (h * nv + m) * BLOCK

            @pl.when(mine & close)
            def _():
                for kv in range(2):
                    acc[slab - region, kv, pl.ds(row, BLOCK), lanes] += vert[
                        kv, at : at + BLOCK, :
                    ].astype(F32)

            @pl.when(mine & jnp.logical_not(close))
            def _():
                for copy in unit_copies(h, m, region, row):
                    copy.start()

    low[...] = acc[...].astype(BF16)
    copies = [
        pltpu.make_async_copy(low.at[n, kv], outs[kv].at[slab - n], out_sems.at[n, kv])
        for n in range(2)
        for kv in range(2)
    ]
    for copy in copies:
        copy.start()
    for h in range(heads):
        for m in range(nv):
            mine, close, region, row = unit(h, m)

            @pl.when(mine & jnp.logical_not(close))
            def _():
                for copy in unit_copies(h, m, region, row):
                    copy.wait()

    for copy in copies:
        copy.wait()


def assemble(slab_index, verticals, home, from_near, arrived, gathered, blank, lines):
    _, rows, features = home.shape
    heads, nv = verticals.shape
    smem = pl.BlockSpec(memory_space=pltpu.SMEM)
    vmem = pl.BlockSpec(memory_space=pltpu.VMEM)
    anywhere = pl.BlockSpec(memory_space=pl.ANY)
    hbm = pl.BlockSpec(memory_space=pltpu.HBM)
    return pl.pallas_call(
        functools.partial(
            assemble_kernel, lines=lines, heads=heads, nv=nv, per_device=rows // BLOCK
        ),
        in_specs=[smem] * 2 + [vmem] * 4 + [anywhere] * 4 + [hbm] * 2,
        out_specs=[hbm] * 2,
        out_shape=[jax.ShapeDtypeStruct(blank[0].shape, BF16)] * 2,
        input_output_aliases={10: 0, 11: 1},
        scratch_shapes=[
            pltpu.VMEM((2, heads * nv * BLOCK, features // heads), BF16),
            pltpu.VMEM((2, 2, rows, features), F32),
            pltpu.VMEM((2, 2, rows, features), BF16),
            pltpu.SemaphoreType.DMA((4 * lines.far,)),
            pltpu.SemaphoreType.DMA((2, 2)),
            pltpu.SemaphoreType.DMA((2, heads * nv)),
        ],
        compiler_params=pltpu.CompilerParams(vmem_limit_bytes=12 * MIB),
    )(slab_index, verticals, home, from_near, *arrived, *gathered, *blank)


def shards(
    queries,
    context_keys,
    context_values,
    forward_output,
    output_cotangent,
    verticals,
    offsets,
    slab_index,
):
    lines = Lines(lax.axis_size("ctx"))
    heads, nv = verticals.shape
    head_dim = context_keys.shape[2] // heads
    _, near, _ = lines.place(lax.axis_index("ctx"))

    own, send4, mixed, mine, to_near, to_core, to_both = pack(
        slab_index, verticals, context_keys, context_values, lines
    )
    to_near = core_sum(lines, to_near, to_both)
    recv4 = move(after(send4, to_near), lines.shift_pairs(4))
    quarter = near_sum(lines, mine, move(to_near, lines.near_pairs()), to_core)
    bases = (jnp.stack([near, 1 - near]) * (heads // 2)).astype(jnp.int32)
    prepared = prepare(
        bases, after(queries, to_near), output_cotangent, forward_output, heads, head_dim
    )
    recv4 = after(recv4, *prepared[0], *prepared[1])
    quarter = after(quarter, recv4)
    share = far_sum(lines, quarter)
    recv_mixed = move(after(mixed, quarter), lines.mixed_pairs())
    recv2 = move(jnp.where(near == 1, recv4, own), lines.near_pairs())
    other4 = move(recv4, lines.core_pairs())
    blank = zeros(share, context_keys.shape)
    gathered = far_gather(lines, after(share, other4))
    other2 = move(recv2, lines.core_pairs())
    gathered = after(gathered, other2, recv_mixed, *blank)
    gathered = plane_gather(lines, gathered)
    recv = [own, recv2, recv4, recv_mixed, other2, other4]

    def attend_line(call, gathered, recv, kept_as):
        return attend(
            call, bases, slab_index, verticals, offsets, prepared[call], gathered, recv, lines,
            kept_as,
        )

    to_near, to_both, *first_lows, window = attend_line(0, gathered[0::2], recv, BF16)
    to_near = core_sum(lines, to_near, to_both)
    from_near = move(to_near, lines.near_pairs())
    mine, to_core, *second_lows = attend_line(1, gathered[1::2], [window], F32)
    lows = (first_lows, second_lows)

    home, part2, part4, mixed, give2, give4 = window_gradients(
        bases, after(offsets, from_near), prepared, lows, lines, nv
    )
    quarter = after(near_sum(lines, mine, from_near, to_core), home)
    share = far_sum(lines, quarter)
    arrived_mixed = move(mixed, back(lines.mixed_pairs()))
    sum2 = (part2 + move(give2, lines.core_pairs()).astype(F32)).astype(BF16)
    given4 = move(give4, lines.core_pairs())
    share = after(share, given4)
    sum4 = part4 + given4.astype(F32)
    from_near = move(sum2, lines.near_pairs())
    query_grad = query_gradients(after(bases, share), lows)
    totals = after(far_gather(lines, share), from_near, arrived_mixed, query_grad)
    sum4 = (sum4 + jnp.where(near == 1, from_near.astype(F32), 0.0)).astype(BF16)
    arrived4 = move(after(sum4, totals), back(lines.shift_pairs(4)))
    totals = plane_gather(lines, totals)
    key_gradient, value_gradient = assemble(
        slab_index, verticals, home, from_near, (arrived4, arrived_mixed),
        totals, blank, lines,
    )
    return query_grad, key_gradient, value_gradient


def solution(mesh):
    in_specs = (
        P(("groups", "ctx"), None),
        P("groups", "ctx", None),
        P("groups", "ctx", None),
        P(("groups", "ctx"), None),
        P(("groups", "ctx"), None),
        P("groups", None),
        P("groups", None),
        P("groups"),
    )
    out_specs = (P(("groups", "ctx"), None), P("groups", "ctx", None), P("groups", "ctx", None))
    return jax.shard_map(shards, mesh=mesh, in_specs=in_specs, out_specs=out_specs, check_vma=False)
```

```python
import functools
import math

import jax
import jax.numpy as jnp
from jax import lax
from jax.experimental import pallas as pl
from jax.experimental.pallas import tpu as pltpu
from jax.sharding import PartitionSpec as P

BLOCK = 64
WDEV = 5
MIB = 1024 * 1024
PACK_VMEM = 60 * MIB
JOIN = 4
BF16 = jnp.bfloat16
F32 = jnp.float32


class Lines:
    def __init__(self, devices):
        self.devices = devices
        self.far = devices // 4

    def place(self, me):
        return lax.div(me, 4), lax.rem(lax.div(me, 2), 2), lax.rem(me, 2)

    def core_pairs(self):
        return [(i, i ^ 1) for i in range(self.devices)]

    def near_pairs(self):
        return [(i, i ^ 2) for i in range(self.devices)]

    def both_pairs(self):
        return [(i, i ^ 3) for i in range(self.devices)]

    def far_pairs(self, by):
        return [(i, (i + 4 * by) % self.devices) for i in range(self.devices)]

    def shift_pairs(self, by):
        return [(i, (i + by) % self.devices) for i in range(self.devices)]

    def mixed_pairs(self):
        return [(i, (i + (5 if i % 2 else 1)) % self.devices) for i in range(self.devices)]


def back(pairs):
    return [(b, a) for a, b in pairs]


def move(array, pairs):
    return lax.ppermute(array, "ctx", pairs)


def after(array, *others):
    return lax.optimization_barrier((array, *others))[0]


def core_sum(lines, to_near, to_both):
    return (to_near.astype(F32) + move(to_both, lines.core_pairs()).astype(F32)).astype(BF16)


def near_sum(lines, mine, from_near, to_core):
    from_core = move(to_core, lines.core_pairs())
    return mine.astype(F32) + from_core.astype(F32) + from_near.astype(F32)


def far_sum(lines, quarter):
    parts = [
        move(quarter[by].astype(BF16), lines.far_pairs(by)) for by in range(1, lines.far)
    ]
    share = quarter[0]
    for part in parts:
        share = share + part.astype(F32)
    return share.astype(BF16)


def far_gather(lines, share):
    parts = [share] + [move(share, lines.far_pairs(by)) for by in range(1, lines.far)]
    return jnp.stack(parts)


def plane_gather(lines, mine):
    across = move(mine, lines.near_pairs())
    core_mine = move(mine, lines.core_pairs())
    core_across = move(across, lines.core_pairs())
    return mine, across, core_mine, core_across


def wraps(me, devices):
    return [me + 4 >= devices, (lax.rem(me, 2) == 1) & (me + 5 >= devices)]


def pack_kernel(slab_index, verts, keys, values, *rest, lines, heads, nv, per_device):
    sends = rest[:3]
    shares = rest[3:7]
    picked, sems, pick_sems = rest[7:]
    slab, me = slab_index[0], lax.axis_index("ctx")
    far, near, core = lines.place(me)
    _, chunk, head_dim = shares[0].shape
    copies = []
    wrapped4, wrapped_mixed = wraps(me, lines.devices)
    for n, region in enumerate(
        (slab, slab - wrapped4.astype(jnp.int32), slab - wrapped_mixed.astype(jnp.int32))
    ):
        for kv, source in enumerate((keys, values)):
            copy = pltpu.make_async_copy(source.at[region], sends[n].at[kv], sems.at[n, kv])
            copy.start()
            copies.append(copy)
    picked[...] = jnp.zeros_like(picked)
    slab_blocks = per_device * lines.devices
    piece = min(BLOCK, chunk)

    def unit_copies(h, m):
        inner = lax.rem(verts[h, m], slab_blocks)
        region = lax.div(verts[h, m], slab_blocks)
        row = lax.rem(inner, per_device) * BLOCK
        for p in range(BLOCK // piece):
            at = (h * nv + m) * BLOCK + p * piece
            line, at = at // (lines.far * chunk), at % (lines.far * chunk)
            slot, at = at // chunk, at % chunk
            line = lax.rem(line + near, 2)
            slot = lax.rem(slot - far + lines.far, lines.far)
            for kv, source in enumerate((keys, values)):
                yield pltpu.make_async_copy(
                    source.at[
                        region,
                        pl.ds(pl.multiple_of(row + p * piece, piece), piece),
                        pl.ds(h * head_dim, head_dim),
                    ],
                    picked.at[lax.rem(kv + core, 2), line, slot, pl.ds(at, piece), :],
                    pick_sems.at[kv, (h * nv + m) * (BLOCK // piece) + p],
                )

    def owned(h, m):
        return lax.div(lax.rem(verts[h, m], slab_blocks), per_device) == me

    for h in range(heads):
        for m in range(nv):

            @pl.when(owned(h, m))
            def _():
                for copy in unit_copies(h, m):
                    copy.start()

    for h in range(heads):
        for m in range(nv):

            @pl.when(owned(h, m))
            def _():
                for copy in unit_copies(h, m):
                    copy.wait()

    for n, share in enumerate(shares):
        share[...] = picked[n // 2, n % 2]
    for copy in copies:
        copy.wait()


def pack(slab_index, verticals, keys, values, lines):
    regions, rows, features = keys.shape
    heads, nv = verticals.shape
    head_dim = features // heads
    chunk = heads * nv * BLOCK // (2 * lines.far)
    smem = pl.BlockSpec(memory_space=pltpu.SMEM)
    hbm = pl.BlockSpec(memory_space=pltpu.HBM)
    share = (lines.far, chunk, head_dim)
    return pl.pallas_call(
        functools.partial(pack_kernel, lines=lines, heads=heads, nv=nv, per_device=rows // BLOCK),
        in_specs=[smem, smem, hbm, hbm],
        out_specs=[pl.BlockSpec(memory_space=pltpu.VMEM)] * 7,
        out_shape=[jax.ShapeDtypeStruct((2, rows, features), BF16)] * 3
        + [jax.ShapeDtypeStruct(share, BF16)] * 4,
        scratch_shapes=[
            pltpu.VMEM((2, 2) + share, BF16),
            pltpu.SemaphoreType.DMA((3, 2)),
            pltpu.SemaphoreType.DMA((2, heads * nv * max(1, BLOCK // chunk))),
        ],
        compiler_params=pltpu.CompilerParams(vmem_limit_bytes=PACK_VMEM),
    )(slab_index, verticals, keys, values)


def distances(core):
    return [2, 4, 5 - 4 * core, 1 + 2 * core, 3 + 2 * core]


def vertical_copies(lines, me, line, chunk, gathered, to, sems, first):
    far, _, core = lines.place(me)
    copies = []
    for kv, source in zip((core, 1 - core), gathered):
        for s in range(lines.far):
            slot = lax.rem(far - s + lines.far, lines.far)
            row = pl.multiple_of((line * lines.far + slot) * chunk, chunk)
            copies.append(
                pltpu.make_async_copy(
                    source.at[s], to.at[kv, pl.ds(row, chunk), :], sems.at[first + len(copies)]
                )
            )
    return copies


NT = (((1,), (1,)), ((), ()))


def turn_to_head(t, bases, half):
    return bases[lax.div(t, half)] + lax.rem(t, half)


def of_call(call, half, shape, block=0):
    def index(t, *_):
        turn = jnp.minimum(t, half - 1) if call == 0 else jnp.maximum(t - half, 0)
        return (turn, 0, block, 0)

    return pl.BlockSpec((1,) + tuple(shape), index)


def prepare_kernel(bases, q, grad, out, *sets, head_dim):
    t = pl.program_id(0)
    half = pl.num_programs(0) // 2
    for call in range(2):

        @pl.when(lax.div(t, half) == call)
        def _():
            prepare_head(q, grad, out, *sets[5 * call : 5 * call + 5], head_dim=head_dim)


def prepare_head(q, grad, out, qs, gs, qt, gt, delta, *, head_dim):
    per_device = qs.shape[1]
    group = q.shape[1] // head_dim
    ones = jnp.ones((8, 2 * head_dim), BF16)
    for j in range(per_device):
        rows = slice(j * BLOCK, (j + 1) * BLOCK)
        split = []
        for g in range(group):
            cols = slice(g * head_dim, (g + 1) * head_dim)
            here = slice(g * BLOCK, (g + 1) * BLOCK)
            qs[0, j, here, :] = q[rows, cols]
            gs[0, j, here, :] = grad[rows, cols]
            product = grad[rows, cols].astype(F32) * out[rows, cols].astype(F32)
            upper = product.astype(BF16)
            lower = (product - upper.astype(F32)).astype(BF16)
            split.append(jnp.concatenate([upper, lower], axis=1))
        qt[0, j] = jnp.transpose(qs[0, j])
        gt[0, j] = jnp.transpose(gs[0, j])
        delta[0, j] = lax.dot_general(
            ones, jnp.concatenate(split, axis=0), NT, preferred_element_type=F32
        )


def prepare(bases, queries, cotangent, output, heads, head_dim):
    rows, width = queries.shape
    per_device = rows // BLOCK
    deep = width // heads // head_dim * BLOCK
    half = heads // 2
    tile = pl.BlockSpec(
        (rows, width // heads), lambda t, bases: (0, turn_to_head(t, bases, half))
    )
    stacked = (per_device, deep, head_dim)
    turned = (per_device, head_dim, deep)
    shapes = [stacked, stacked, turned, turned, (per_device, 8, deep)]
    types = [BF16] * 4 + [F32]
    arrays = pl.pallas_call(
        functools.partial(prepare_kernel, head_dim=head_dim),
        grid_spec=pltpu.PrefetchScalarGridSpec(
            num_scalar_prefetch=1,
            grid=(heads,),
            in_specs=[tile] * 3,
            out_specs=[of_call(call, half, shape) for call in range(2) for shape in shapes],
        ),
        out_shape=[
            jax.ShapeDtypeStruct((half,) + shape, kind) for shape, kind in zip(shapes, types)
        ]
        * 2,
        compiler_params=pltpu.CompilerParams(vmem_limit_bytes=16 * MIB),
        cost_estimate=pl.CostEstimate(flops=0, bytes_accessed=7 << 20, transcendentals=0),
    )(bases, queries, cotangent, output)
    return arrays[:5], arrays[5:]


def slash_rows(offs, h, j, s, per_device):
    return pl.multiple_of((WDEV * per_device + j - offs[h, s]) * BLOCK, BLOCK)


def attend_kernel(
    bases, slab_index, verts, offs, qs, gs, qt, gt, delta, *rest,
    lines, nv, ns, per_device, call,
):
    sources = 1 if call else 1 + WDEV
    gathered, recv, rest = rest[:2], rest[2 : 2 + sources], rest[2 + sources :]
    (share, give, low_w, low_ds, cand_keys), rest = rest[:5], rest[5:]
    scratch = rest if call else rest[1:]
    win, vkv, vc, s_ref, vert_w, hold, sems = scratch
    i = pl.program_id(0)
    base = bases[call]
    h = base + i
    slab, me = slab_index[0], lax.axis_index("ctx")
    far, near, core = lines.place(me)
    _, chunk, head_dim = share.shape
    cand = nv + 1 + ns
    scaling = 1.0 / math.sqrt(head_dim)
    rows = per_device * BLOCK
    width = qs.shape[2]
    first_block = slab * (per_device * lines.devices) + me * per_device
    lanes = pl.ds(pl.multiple_of(i * head_dim, head_dim), head_dim)

    def window_row(d):
        return pl.multiple_of((WDEV - d) * rows, rows)

    @pl.when(i == 0)
    def _():
        half = win.shape[2]
        copies = []
        if call:
            copies.append(pltpu.make_async_copy(recv[0], win, sems.at[0]))
        else:
            for m, to in enumerate((win, rest[0])):
                side = pl.ds(pl.multiple_of(bases[m] * head_dim, half), half)
                for n, d in enumerate([0] + distances(core)):
                    copies.append(
                        pltpu.make_async_copy(
                            recv[n].at[:, :, side],
                            to.at[:, pl.ds(window_row(d), rows), :],
                            sems.at[m * (1 + WDEV) + n],
                        )
                    )
        copies += vertical_copies(lines, me, 0, chunk, gathered, vkv, sems, 2 + 2 * WDEV)
        for copy in copies:
            copy.start()
        for copy in copies:
            copy.wait()

    vert_rows = pl.ds(pl.multiple_of(i * (nv * BLOCK), nv * BLOCK), nv * BLOCK)
    neg, posinf = jnp.float32(-jnp.inf), jnp.float32(jnp.inf)
    log2_scale = scaling * math.log2(math.e)
    key_at = lax.broadcasted_iota(jnp.int32, (BLOCK, width), 0)
    row_at = lax.broadcasted_iota(jnp.int32, (BLOCK, width), 1) % BLOCK

    def fold(x, op):
        y = x[0:8, :]
        for r in range(1, BLOCK // 8):
            y = op(y, x[r * 8 : (r + 1) * 8, :])
        return y

    vertical_sum = [None, None]
    for j in range(per_device):
        block = first_block + j
        own_at = (WDEV * per_device + j) * BLOCK
        valid = [verts[h, m] < block for m in range(nv)] + [None]
        for s in range(ns):
            collide = verts[h, 0] == block - offs[h, s]
            for m in range(1, nv):
                collide = collide | (verts[h, m] == block - offs[h, s])
            valid.append((offs[h, s] > 0) & jnp.logical_not(collide))
        for kv, to in enumerate((cand_keys.at[0], vc)):
            to[j, 0 : nv * BLOCK, :] = vkv[kv, vert_rows, :]
            to[j, nv * BLOCK : (nv + 1) * BLOCK, :] = win[kv, own_at : own_at + BLOCK, lanes]
            for s in range(ns):
                to[j, (nv + 1 + s) * BLOCK : (nv + 2 + s) * BLOCK, :] = win[
                    kv, pl.ds(slash_rows(offs, h, j, s, per_device), BLOCK), lanes
                ]

        top = None
        for n in range(cand // JOIN):
            span = slice(n * JOIN * BLOCK, (n + 1) * JOIN * BLOCK)
            scores = jnp.dot(cand_keys[0, j, span, :], qt[0, j], preferred_element_type=F32)
            for k in range(JOIN):
                c = n * JOIN + k
                part = scores[k * BLOCK : (k + 1) * BLOCK, :]
                if c == nv:
                    part = jnp.where(key_at <= row_at, part, neg)
                s_ref[j, c * BLOCK : (c + 1) * BLOCK, :] = part
                best = fold(part, jnp.maximum)
                if c != nv:
                    best = best + jnp.where(valid[c], jnp.float32(0), neg)
                top = best if top is None else jnp.maximum(top, best)
        top = jnp.max(top, axis=0, keepdims=True) * log2_scale
        total = jnp.zeros((8, width), F32)
        for c in range(cand):
            span = slice(c * BLOCK, (c + 1) * BLOCK)
            less = top if c == nv else top + jnp.where(valid[c], jnp.float32(0), posinf)
            p = jnp.exp2(s_ref[j, span, :] * log2_scale - less)
            s_ref[j, span, :] = p
            total = total + fold(p, jnp.add)
        inverse = 1.0 / jnp.sum(total, axis=0, keepdims=True)
        row_delta = delta[0, j, 0:1, :]
        for n in range(cand // JOIN):
            span = slice(n * JOIN * BLOCK, (n + 1) * JOIN * BLOCK)
            weight_grad = jnp.dot(vc[j, span, :], gt[0, j], preferred_element_type=F32)
            w = s_ref[j, span, :] * inverse
            if n * JOIN < nv:
                vert_w[j, span, :] = w.astype(BF16)
            else:
                low_w[0, j] = w.astype(BF16)
            low_ds[0, j, span, :] = (w * (weight_grad - row_delta)).astype(BF16)

        here = slice(0, nv * BLOCK)
        dv = jnp.dot(vert_w[j], gs[0, j], preferred_element_type=F32)
        dk = jnp.dot(low_ds[0, j, here, :], qs[0, j], preferred_element_type=F32) * scaling
        for kv, part in enumerate((dk, dv)):
            vertical_sum[kv] = part if j == 0 else vertical_sum[kv] + part

    first = core == 0
    parts = (
        jnp.where(first, vertical_sum[0], vertical_sum[1]),
        jnp.where(first, vertical_sum[1], vertical_sum[0]),
    )
    for c in range(nv * BLOCK // chunk):
        slot = lax.rem(i * (nv * BLOCK // chunk) + c - far + lines.far, lines.far)
        for n, part in enumerate(parts):
            hold[n, slot] = part[c * chunk : (c + 1) * chunk, :]

    @pl.when(i == pl.num_programs(0) - 1)
    def _():
        share[...] = hold[0].astype(share.dtype)
        give[...] = hold[1].astype(give.dtype)


def attend(
    call, bases, slab_index, verticals, offsets, prepared, gathered, recv, lines, kept_as
):
    half, per_device, deep, head_dim = prepared[0].shape
    heads = 2 * half
    rows, features = per_device * BLOCK, heads * head_dim
    nv, ns = verticals.shape[1], offsets.shape[1]
    cand = nv + 1 + ns
    anywhere = pl.BlockSpec(memory_space=pl.ANY)

    def by_turn(shape):
        return pl.BlockSpec((1,) + shape[1:], lambda i, *_: (i,) + (0,) * (len(shape) - 1))

    window = (2, (WDEV + 1) * rows, features // 2)
    share = (lines.far, half * nv * BLOCK // lines.far, head_dim)
    shares = pl.BlockSpec(share, lambda i, *_: (0, 0, 0))
    low_shapes = [
        (half, per_device, (1 + ns) * BLOCK, deep),
        (half, per_device, cand * BLOCK, deep),
        (half, per_device, cand * BLOCK, head_dim),
    ]
    return pl.pallas_call(
        functools.partial(
            attend_kernel, lines=lines, nv=nv, ns=ns, per_device=per_device, call=call
        ),
        grid_spec=pltpu.PrefetchScalarGridSpec(
            num_scalar_prefetch=4,
            grid=(half,),
            in_specs=[by_turn(array.shape) for array in prepared]
            + [anywhere] * (2 + len(recv)),
            out_specs=[shares] * 2
            + [by_turn(shape) for shape in low_shapes]
            + [anywhere] * (1 - call),
            scratch_shapes=[
                pltpu.VMEM(window, BF16),
                pltpu.VMEM((2, half * nv * BLOCK, head_dim), BF16),
                pltpu.VMEM((per_device, cand * BLOCK, head_dim), BF16),
                pltpu.VMEM((per_device, cand * BLOCK, deep), F32),
                pltpu.VMEM((per_device, nv * BLOCK, deep), BF16),
                pltpu.VMEM((2,) + share, F32),
                pltpu.SemaphoreType.DMA((2 + 2 * WDEV + 2 * lines.far,)),
            ],
        ),
        out_shape=[
            jax.ShapeDtypeStruct(share, kept_as),
            jax.ShapeDtypeStruct(share, BF16),
        ]
        + [jax.ShapeDtypeStruct(shape, BF16) for shape in low_shapes]
        + [jax.ShapeDtypeStruct(window, BF16)] * (1 - call),
        compiler_params=pltpu.CompilerParams(vmem_limit_bytes=18 * MIB),
        cost_estimate=pl.CostEstimate(
            flops=2 * 5 * half * per_device * cand * BLOCK * deep * head_dim,
            bytes_accessed=12 << 20,
            transcendentals=half * per_device * cand * BLOCK * deep,
        ),
    )(bases, slab_index, verticals, offsets, *prepared, *gathered, *recv)


def window_kernel(bases, offs, *rest, lines, half, ns, per_device):
    calls, home, parts, total = (rest[0:4], rest[4:8]), rest[8], rest[9 : 9 + WDEV], rest[9 + WDEV]
    t = pl.program_id(0)
    h = turn_to_head(t, bases, half)
    _, _, core = lines.place(lax.axis_index("ctx"))
    head_dim = rest[0].shape[3]
    rows = per_device * BLOCK
    scaling = 1.0 / math.sqrt(head_dim)
    lanes = pl.ds(pl.multiple_of(h * head_dim, head_dim), head_dim)
    total[...] = jnp.zeros_like(total)
    for call, (qs, gs, low_w, low_ds) in enumerate(calls):

        @pl.when(lax.div(t, half) == call)
        def _():
            for j in range(per_device):
                dv = jnp.dot(low_w[0, j], gs[0, j], preferred_element_type=F32)
                dk = jnp.dot(low_ds[0, j], qs[0, j], preferred_element_type=F32) * scaling
                own_at = (WDEV * per_device + j) * BLOCK
                for kv, part in enumerate((dk, dv)):
                    total[kv, own_at : own_at + BLOCK, :] += part[0:BLOCK]
                    for s in range(ns):
                        at = slash_rows(offs, h, j, s, per_device)
                        total[kv, pl.ds(at, BLOCK), :] += part[(1 + s) * BLOCK : (2 + s) * BLOCK]

    for kv in range(2):
        home[kv, :, lanes] = total[kv, WDEV * rows :, :]
        for part, d in zip(parts, distances(core)):
            at = pl.multiple_of((WDEV - d) * rows, rows)
            part[kv, :, lanes] = total[kv, pl.ds(at, rows), :].astype(part.dtype)


def window_gradients(bases, offsets, prepared, lows, lines, nv):
    half, per_device, deep, head_dim = prepared[0][0].shape
    heads = 2 * half
    ns = offsets.shape[1]
    rows, features = per_device * BLOCK, heads * head_dim
    shard = (2, rows, features)
    whole = pl.BlockSpec(shard, lambda t, *_: (0, 0, 0))
    stacked = (per_device, deep, head_dim)
    tail = (1 + ns) * BLOCK
    block = (per_device, tail, deep)
    specs = []
    for call in range(2):
        specs += [of_call(call, half, stacked)] * 2
        specs += [of_call(call, half, block), of_call(call, half, block, nv * BLOCK // tail)]
    return pl.pallas_call(
        functools.partial(window_kernel, lines=lines, half=half, ns=ns, per_device=per_device),
        grid_spec=pltpu.PrefetchScalarGridSpec(
            num_scalar_prefetch=2,
            grid=(heads,),
            in_specs=specs,
            out_specs=[whole] * (1 + WDEV),
            scratch_shapes=[pltpu.VMEM((2, (WDEV + 1) * rows, head_dim), F32)],
        ),
        out_shape=[jax.ShapeDtypeStruct(shard, F32)] * 3 + [jax.ShapeDtypeStruct(shard, BF16)] * 3,
        compiler_params=pltpu.CompilerParams(vmem_limit_bytes=16 * MIB),
        cost_estimate=pl.CostEstimate(flops=0, bytes_accessed=9 << 20, transcendentals=0),
    )(bases, offsets, *prepared[0][:2], *lows[0][:2], *prepared[1][:2], *lows[1][:2])


def query_kernel(bases, *rest):
    calls, dq = (rest[0:2], rest[2:4]), rest[4]
    t = pl.program_id(0)
    per_device, _, head_dim = rest[0].shape[1:]
    scaling = 1.0 / math.sqrt(head_dim)
    half = pl.num_programs(0) // 2
    for call, (cand_keys, low_ds) in enumerate(calls):

        @pl.when(lax.div(t, half) == call)
        def _():
            for j in range(per_device):
                turned = lax.dot_general(
                    cand_keys[0, j],
                    low_ds[0, j],
                    (((0,), (0,)), ((), ())),
                    preferred_element_type=F32,
                )
                stacked = (jnp.transpose(turned) * scaling).astype(BF16)
                for g in range(dq.shape[1] // head_dim):
                    dq[j * BLOCK : (j + 1) * BLOCK, g * head_dim : (g + 1) * head_dim] = stacked[
                        g * BLOCK : (g + 1) * BLOCK, :
                    ]


def query_gradients(bases, lows):
    half, per_device, _, head_dim = lows[0][2].shape
    deep = lows[0][1].shape[3]
    rows, width = per_device * BLOCK, deep // BLOCK * head_dim
    specs = []
    for call in range(2):
        specs += [of_call(call, half, lows[0][n].shape[1:]) for n in (2, 1)]
    return pl.pallas_call(
        query_kernel,
        grid_spec=pltpu.PrefetchScalarGridSpec(
            num_scalar_prefetch=1,
            grid=(2 * half,),
            in_specs=specs,
            out_specs=pl.BlockSpec(
                (rows, width), lambda t, bases: (0, turn_to_head(t, bases, half))
            ),
        ),
        out_shape=jax.ShapeDtypeStruct((rows, 2 * half * width), BF16),
        compiler_params=pltpu.CompilerParams(vmem_limit_bytes=16 * MIB),
        cost_estimate=pl.CostEstimate(flops=0, bytes_accessed=10 << 20, transcendentals=0),
    )(bases, lows[0][2], lows[0][1], lows[1][2], lows[1][1])


def zeros_kernel(_, key_out, value_out, blank, sems):
    blank[...] = jnp.zeros_like(blank)
    copies = [
        pltpu.make_async_copy(blank, out.at[r], sems.at[n, r])
        for n, out in enumerate((key_out, value_out))
        for r in range(out.shape[0])
    ]
    for copy in copies:
        copy.start()
    for copy in copies:
        copy.wait()


def zeros(ahead, shape):
    hbm = pl.BlockSpec(memory_space=pltpu.HBM)
    return pl.pallas_call(
        zeros_kernel,
        in_specs=[pl.BlockSpec(memory_space=pl.ANY)],
        out_specs=[hbm] * 2,
        out_shape=[jax.ShapeDtypeStruct(shape, BF16)] * 2,
        scratch_shapes=[pltpu.VMEM(shape[1:], BF16), pltpu.SemaphoreType.DMA((2, shape[0]))],
        compiler_params=pltpu.CompilerParams(vmem_limit_bytes=2 * MIB),
        cost_estimate=pl.CostEstimate(flops=0, bytes_accessed=5 << 20, transcendentals=0),
    )(ahead)


def assemble_kernel(slab_index, verts, home, *rest, lines, heads, nv, per_device):
    from_near, arrived, gathered = rest[0], rest[1:3], rest[3:7]
    outs, vert, acc, low, sems, out_sems, unit_sems = rest[9:11], *rest[11:]
    slab, me = slab_index[0], lax.axis_index("ctx")
    _, near, _ = lines.place(me)
    devices = lines.devices
    chunk, head_dim = gathered[0].shape[1:]
    slab_blocks = per_device * devices
    copies = vertical_copies(lines, me, 1 - near, chunk, gathered[0::2], vert, sems, 0)
    copies += vertical_copies(lines, me, near, chunk, gathered[1::2], vert, sems, 2 * lines.far)
    for copy in copies:
        copy.start()
    acc[0] = home[...]
    acc[1] = jnp.zeros_like(home)

    @pl.when(near == 0)
    def _():
        acc[0] += from_near[...].astype(F32)

    for part, wrapped in zip(arrived, wraps(me, devices)):
        acc[wrapped.astype(jnp.int32)] += part[...].astype(F32)
    for copy in copies:
        copy.wait()

    def unit(h, m):
        inner = lax.rem(verts[h, m], slab_blocks)
        region = lax.div(verts[h, m], slab_blocks)
        row = pl.multiple_of(lax.rem(inner, per_device) * BLOCK, BLOCK)
        close = (region == slab) | (region == slab - 1)
        return lax.div(inner, per_device) == me, close, region, row

    def unit_copies(h, m, region, row):
        at = (h * nv + m) * BLOCK
        for kv in range(2):
            yield pltpu.make_async_copy(
                vert.at[kv, pl.ds(at, BLOCK), :],
                outs[kv].at[region, pl.ds(row, BLOCK), pl.ds(h * head_dim, head_dim)],
                unit_sems.at[kv, h * nv + m],
            )

    for h in range(heads):
        lanes = slice(h * head_dim, (h + 1) * head_dim)
        for m in range(nv):
            mine, close, region, row = unit(h, m)
            at = (h * nv + m) * BLOCK

            @pl.when(mine & close)
            def _():
                for kv in range(2):
                    acc[slab - region, kv, pl.ds(row, BLOCK), lanes] += vert[
                        kv, at : at + BLOCK, :
                    ].astype(F32)

            @pl.when(mine & jnp.logical_not(close))
            def _():
                for copy in unit_copies(h, m, region, row):
                    copy.start()

    low[...] = acc[...].astype(BF16)
    copies = [
        pltpu.make_async_copy(low.at[n, kv], outs[kv].at[slab - n], out_sems.at[n, kv])
        for n in range(2)
        for kv in range(2)
    ]
    for copy in copies:
        copy.start()
    for h in range(heads):
        for m in range(nv):
            mine, close, region, row = unit(h, m)

            @pl.when(mine & jnp.logical_not(close))
            def _():
                for copy in unit_copies(h, m, region, row):
                    copy.wait()

    for copy in copies:
        copy.wait()


def assemble(slab_index, verticals, home, from_near, arrived, gathered, blank, lines):
    _, rows, features = home.shape
    heads, nv = verticals.shape
    smem = pl.BlockSpec(memory_space=pltpu.SMEM)
    vmem = pl.BlockSpec(memory_space=pltpu.VMEM)
    anywhere = pl.BlockSpec(memory_space=pl.ANY)
    hbm = pl.BlockSpec(memory_space=pltpu.HBM)
    return pl.pallas_call(
        functools.partial(
            assemble_kernel, lines=lines, heads=heads, nv=nv, per_device=rows // BLOCK
        ),
        in_specs=[smem] * 2 + [vmem] * 4 + [anywhere] * 4 + [hbm] * 2,
        out_specs=[hbm] * 2,
        out_shape=[jax.ShapeDtypeStruct(blank[0].shape, BF16)] * 2,
        input_output_aliases={10: 0, 11: 1},
        scratch_shapes=[
            pltpu.VMEM((2, heads * nv * BLOCK, features // heads), BF16),
            pltpu.VMEM((2, 2, rows, features), F32),
            pltpu.VMEM((2, 2, rows, features), BF16),
            pltpu.SemaphoreType.DMA((4 * lines.far,)),
            pltpu.SemaphoreType.DMA((2, 2)),
            pltpu.SemaphoreType.DMA((2, heads * nv)),
        ],
        compiler_params=pltpu.CompilerParams(vmem_limit_bytes=12 * MIB),
    )(slab_index, verticals, home, from_near, *arrived, *gathered, *blank)


def shards(
    queries,
    context_keys,
    context_values,
    forward_output,
    output_cotangent,
    verticals,
    offsets,
    slab_index,
):
    lines = Lines(lax.axis_size("ctx"))
    heads, nv = verticals.shape
    head_dim = context_keys.shape[2] // heads
    _, near, _ = lines.place(lax.axis_index("ctx"))

    own, send4, mixed, mine, to_near, to_core, to_both = pack(
        slab_index, verticals, context_keys, context_values, lines
    )
    to_near = core_sum(lines, to_near, to_both)
    recv4 = move(send4, lines.shift_pairs(4))
    quarter = near_sum(lines, mine, move(to_near, lines.near_pairs()), to_core)
    bases = (jnp.stack([near, 1 - near]) * (heads // 2)).astype(jnp.int32)
    prepared = prepare(
        bases, after(queries, to_near), output_cotangent, forward_output, heads, head_dim
    )
    recv4 = after(recv4, *prepared[0], *prepared[1])
    quarter = after(quarter, recv4)
    share = far_sum(lines, quarter)
    recv_mixed = move(after(mixed, quarter), lines.mixed_pairs())
    recv2 = move(jnp.where(near == 1, recv4, own), lines.near_pairs())
    other4 = move(recv4, lines.core_pairs())
    blank = zeros(share, context_keys.shape)
    gathered = far_gather(lines, after(share, other4))
    other2 = move(recv2, lines.core_pairs())
    gathered = after(gathered, other2, recv_mixed, *blank)
    gathered = plane_gather(lines, gathered)
    recv = [own, recv2, recv4, recv_mixed, other2, other4]

    def attend_line(call, gathered, recv, kept_as):
        return attend(
            call, bases, slab_index, verticals, offsets, prepared[call], gathered, recv, lines,
            kept_as,
        )

    to_near, to_both, *first_lows, window = attend_line(0, gathered[0::2], recv, BF16)
    to_near = core_sum(lines, to_near, to_both)
    from_near = move(to_near, lines.near_pairs())
    mine, to_core, *second_lows = attend_line(1, gathered[1::2], [window], F32)
    lows = (first_lows, second_lows)

    home, part2, part4, mixed, give2, give4 = window_gradients(
        bases, after(offsets, from_near), prepared, lows, lines, nv
    )
    quarter = after(near_sum(lines, mine, from_near, to_core), home)
    share = far_sum(lines, quarter)
    arrived_mixed = move(mixed, back(lines.mixed_pairs()))
    sum2 = (part2 + move(give2, lines.core_pairs()).astype(F32)).astype(BF16)
    given4 = move(give4, lines.core_pairs())
    share = after(share, given4)
    sum4 = part4 + given4.astype(F32)
    from_near = move(sum2, lines.near_pairs())
    query_grad = query_gradients(after(bases, share), lows)
    totals = after(far_gather(lines, share), from_near, arrived_mixed, query_grad)
    sum4 = (sum4 + jnp.where(near == 1, from_near.astype(F32), 0.0)).astype(BF16)
    arrived4 = move(after(sum4, totals), back(lines.shift_pairs(4)))
    totals = plane_gather(lines, totals)
    key_gradient, value_gradient = assemble(
        slab_index, verticals, home, from_near, (arrived4, arrived_mixed),
        totals, blank, lines,
    )
    return query_grad, key_gradient, value_gradient


def solution(mesh):
    in_specs = (
        P(("groups", "ctx"), None),
        P("groups", "ctx", None),
        P("groups", "ctx", None),
        P(("groups", "ctx"), None),
        P(("groups", "ctx"), None),
        P("groups", None),
        P("groups", None),
        P("groups"),
    )
    out_specs = (P(("groups", "ctx"), None), P("groups", "ctx", None), P("groups", "ctx", None))
    return jax.shard_map(shards, mesh=mesh, in_specs=in_specs, out_specs=out_specs, check_vma=False)
```
